32 devices in a mesh: dp: 8 (over z, y), tensor: 4 (over x, core).
Axes of the slice: x: 2, y: 2, z: 4, core: 2. Of those that a mesh axis runs over, the one named last changes fastest.
Arguments:
- tokens: bfloat16 [16384, 768], P(('dp', 'tensor')), may hold values from -6 to 6
- w_qkv: bfloat16 [3, 768, 768], P(None, 'dp', 'tensor'), may hold values from -0.3125 to 0.3125
- w_out: bfloat16 [768, 768], P('tensor', 'dp'), may hold values from -0.21875 to 0.21875
- conv_weight: float32 [12, 65], P('tensor'), may hold values from -0.48 to 0.48
- w_up: bfloat16 [768, 3072], P(None, ('dp', 'tensor')), may hold values from -0.21875 to 0.21875
- w_down: bfloat16 [3072, 768], P(('dp', 'tensor')), may hold values from -0.109375 to 0.109375
- norm_gain: bfloat16 [2, 768], P(None, ('dp', 'tensor')), may hold values from 0.5 to 1.5
- norm_bias: bfloat16 [2, 768], P(None, ('dp', 'tensor')), may hold values from -3 to 3
- cotangent: bfloat16 [16384, 768], P(('dp', 'tensor')), may hold values from -6 to 6
- seg_ids: int32 [8, 2048], P('dp'), may hold values from 0 to 3, as said below
- landmark_slot: int32 [8, 2048], P('dp'), may hold values from 0 to 256, as said below
- token_live: int32 [8, 2048], P('dp'), may hold values from 0 to 1, as said below
- slot_live: int32 [8, 256], P('dp'), may hold values from 0 to 1, as said below
Outputs:
- layer_out: bfloat16 [16384, 768], P(('dp', 'tensor'))
- input_grad: float32 [16384, 768], P(('dp', 'tensor'))
- grad_qkv: float32 [3, 768, 768], P(None, 'dp', 'tensor')
- grad_out: float32 [768, 768], P('tensor', 'dp')
- grad_conv: float32 [12, 65], P('tensor')
- grad_up: float32 [768, 3072], P(None, ('dp', 'tensor'))
- grad_down: float32 [3072, 768], P(('dp', 'tensor'))
- grad_gain: float32 [2, 768], P(None, ('dp', 'tensor'))
- grad_bias: float32 [2, 768], P(None, ('dp', 'tensor'))
- proxies: float32 [8, 4, 12], P('dp', None, 'tensor')
The draws below stay inside these ranges and needn't reach their ends.
Inputs may be any that keep to these rules, and one draw needn't show every extreme that they name: `seg_ids`: document numbers never fall along a row; each document of a row has at least 64 tokens; the tail padding carries the number of the row's last document. `landmark_slot`: each document s of a row uses m_s landmark slots, 32 <= m_s <= 64; a token at offset p of document s, which has n tokens, names slot s * 64 + floor(p * m_s / n); tail padding names 256, which is no slot. `token_live`: the zeros form a tail of at most 256 tokens. `slot_live`: slot s is 1 exactly when the row holds document s // 64 and s % 64 < m of that document.
All inputs are finite; a program needn't handle non-finite values.
Results may differ from the reference program's by a relative error of at most 0.014.
The reference program's roundings to bfloat16 on the way count: a program that leaves them out, or rounds other values in their place, can miss the bound.
Values may be sent and summed in bfloat16 or wider, within the bound.
A program may use at most 192 MiB of HBM per device.

```python
import math
import jax
import jax.numpy as jnp
from jax import lax

HEADS = 12
HEAD_DIM = 64
D = 768
FF = 3072
LANDMARKS = 64
KSIZE = 65
NEWTON = 6
DOCS = 4
SEQ = 2048
ROWS = 8
TOKENS = 16384
SLOTS = 256


def packed_layout(key):
    folded = jax.random.fold_in(key, 11)
    key_docs, key_pad, key_cuts, key_marks = jax.random.split(folded, 4)
    row_index = jnp.arange(ROWS, dtype=jnp.int32)
    doc_count = jnp.where(row_index % 2 == 0, DOCS, jax.random.randint(key_docs, (ROWS,), 1, DOCS + 1)).astype(jnp.int32)
    pad_count = jnp.where(row_index % 2 == 1, SEQ // 8, jax.random.randint(key_pad, (ROWS,), 0, SEQ // 8 + 1)).astype(jnp.int32)
    live_count = SEQ - pad_count
    spare_room = live_count - LANDMARKS * doc_count
    cut_draws = jax.random.randint(key_cuts, (ROWS, DOCS - 1), 0, 1 << 20) % (spare_room[:, None] + 1)
    cut_index = jnp.arange(DOCS - 1, dtype=jnp.int32)
    cut_draws = jnp.where(cut_index[None, :] < doc_count[:, None] - 1, cut_draws, spare_room[:, None])
    ordered = jnp.sort(cut_draws, axis=1)
    starts = LANDMARKS * (cut_index[None, :] + 1) + ordered
    starts = jnp.where(cut_index[None, :] + 1 < doc_count[:, None], starts, live_count[:, None])
    positions = jnp.arange(SEQ, dtype=jnp.int32)
    segment = jnp.sum((positions[None, :, None] >= starts[:, None, :]).astype(jnp.int32), axis=2)
    segment = jnp.minimum(segment, doc_count[:, None] - 1).astype(jnp.int32)
    bounds = jnp.concatenate([jnp.zeros((ROWS, 1), jnp.int32), starts.astype(jnp.int32), live_count[:, None].astype(jnp.int32)], axis=1)
    begins = jnp.take_along_axis(bounds, segment, axis=1)
    finishes = jnp.take_along_axis(bounds, segment + 1, axis=1)
    marks = jax.random.randint(key_marks, (ROWS, DOCS), LANDMARKS // 2, LANDMARKS + 1).astype(jnp.int32)
    doc_marks = jnp.take_along_axis(marks, segment, axis=1)
    within = (positions[None, :] - begins) * doc_marks // (finishes - begins)
    padded = positions[None, :] >= live_count[:, None]
    slot_index = jnp.where(padded, DOCS * LANDMARKS, segment * LANDMARKS + within).astype(jnp.int32)
    token_mask = (1 - padded.astype(jnp.int32)).astype(jnp.int32)
    slot_all = jnp.arange(DOCS * LANDMARKS, dtype=jnp.int32)
    slot_doc = slot_all // LANDMARKS
    slot_marks = jnp.take_along_axis(marks, jnp.broadcast_to(slot_doc[None, :], (ROWS, DOCS * LANDMARKS)), axis=1)
    slot_mask = ((slot_doc[None, :] < doc_count[:, None]) & ((slot_all % LANDMARKS)[None, :] < slot_marks)).astype(jnp.int32)
    return (segment, slot_index, token_mask, slot_mask)


def draw_tokens(key, part):
    slot_index = packed_layout(key)[1]
    key = jax.random.fold_in(key, 5)
    key_noise, key_table = jax.random.split(key, 2)
    noise = jax.random.normal(key_noise, (ROWS * SEQ, D), jnp.float32)
    table = jax.random.normal(key_table, (ROWS * (DOCS * LANDMARKS + 1), D), jnp.float32)
    flat_slot = (slot_index + jnp.arange(ROWS, dtype=jnp.int32)[:, None] * (DOCS * LANDMARKS + 1)).reshape(ROWS * SEQ)
    shared = jnp.take(table, flat_slot, axis=0)
    return jnp.clip(0.7 * noise + 0.7 * shared, -6.0, 6.0).astype(jnp.bfloat16)


def draw_seg_ids(key, part):
    return packed_layout(key)[0]


def draw_landmark_slot(key, part):
    return packed_layout(key)[1]


def draw_token_live(key, part):
    return packed_layout(key)[2]


def draw_slot_live(key, part):
    return packed_layout(key)[3]


def level_of(stream_key, shape, cuts, smallest, top_value):
    gain = 1.0
    for position, parts in cuts:
        steps = jax.random.uniform(jax.random.fold_in(jax.random.fold_in(stream_key, 6), position), (parts,), jnp.float32, smallest / len(cuts), top_value / len(cuts))
        gain = gain * jnp.repeat(jnp.exp(steps), shape[position] // parts).reshape((-1,) + (1,) * (len(shape) - 1 - position))
    return gain


def bell_draw(rng, shape, deviation, most, shards=(), kind=jnp.bfloat16):
    array = deviation * jax.random.normal(rng, shape, jnp.float32)
    if shards:
        array = array * level_of(rng, shape, shards, -0.22, 0.18)
    return jnp.clip(array, -most, most).astype(kind)


def setup_inputs(seed: int = 0) -> dict:
    key_list = jax.random.split(jax.random.key(seed), 14)
    return {
        "tokens": draw_tokens(jax.random.fold_in(key_list[13], 71), 0),
        "w_qkv": bell_draw(key_list[1], (3, D, D), (D // 2) ** -0.5, 0.3125, ((1, 8), (2, 4))),
        "w_out": bell_draw(key_list[2], (D, D), D ** -0.5, 0.21875, ((0, 4), (1, 8))),
        "conv_weight": bell_draw(key_list[3], (HEADS, KSIZE), 0.08, 0.48, ((0, 4),), jnp.float32),
        "w_up": bell_draw(key_list[4], (D, FF), D ** -0.5, 0.21875, ((1, 32),)),
        "w_down": bell_draw(key_list[5], (FF, D), FF ** -0.5, 0.109375, ((0, 32),)),
        "norm_gain": jnp.clip(1.0 + 0.1 * jax.random.normal(key_list[6], (2, D), jnp.float32), 0.5, 1.5).astype(jnp.bfloat16),
        "norm_bias": bell_draw(key_list[7], (2, D), 0.5, 3.0, ((1, 32),)),
        "cotangent": bell_draw(key_list[8], (TOKENS, D), 1.0, 6.0, ((0, 32),)),
        "seg_ids": draw_seg_ids(jax.random.fold_in(key_list[13], 71), 0),
        "landmark_slot": draw_landmark_slot(jax.random.fold_in(key_list[13], 71), 0),
        "token_live": draw_token_live(jax.random.fold_in(key_list[13], 71), 0),
        "slot_live": draw_slot_live(jax.random.fold_in(key_list[13], 71), 0),
    }


@jax.custom_vjp
def low(v):
    return lax.optimization_barrier(v.astype(jnp.bfloat16)).astype(jnp.float32)

@jax.custom_vjp
def low_back(v):
    return v

def low_keep(v):
    return (low(v), None)

def low_pass(kept, grad):
    return (grad,)

def back_keep(v):
    return (v, None)

def back_low(kept, grad):
    return (low(grad),)
low.defvjp(low_keep, low_pass)
low_back.defvjp(back_keep, back_low)
highest = lax.Precision.HIGHEST
norm_epsilon = 1e-05

def layer_norm(values, gain_row, bias_row):
    average = lax.optimization_barrier(jnp.mean(values, axis=-1, keepdims=True))
    centered = values - average
    variance = lax.optimization_barrier(jnp.mean(centered * centered, axis=-1, keepdims=True))
    return centered * lax.rsqrt(variance + norm_epsilon) * gain_row + bias_row

def newton_inverse(query_land, key_land, live_slots):
    scaling = 1.0 / math.sqrt(HEAD_DIM)
    logits = jnp.einsum('...ie,...je->...ij', query_land, key_land, precision=highest) * scaling
    allowed = live_slots[..., None, :] > 0
    weights = jax.nn.softmax(jnp.where(allowed, logits, -1000000000.0), axis=-1) * live_slots[..., :, None]
    colsums = lax.optimization_barrier(jnp.sum(weights, axis=-2))
    initial = 1.0 / jnp.maximum(lax.optimization_barrier(jnp.max(colsums, axis=-1)), 1.0)
    inverse = initial[..., None, None] * jnp.swapaxes(weights, -1, -2)
    identity = jnp.eye(LANDMARKS, dtype=jnp.float32)
    for repeat in range(NEWTON):
        product = jnp.einsum('...ij,...jk->...ik', weights, inverse, precision=highest)
        nested = 7.0 * identity - product
        nested = 15.0 * identity - jnp.einsum('...ij,...jk->...ik', product, nested, precision=highest)
        nested = 13.0 * identity - jnp.einsum('...ij,...jk->...ik', product, nested, precision=highest)
        inverse = 0.25 * jnp.einsum('...ij,...jk->...ik', inverse, nested, precision=highest)
    return (weights, inverse)

def depthwise(values_all, seg_row, live_row, conv_wide):
    half_width = KSIZE // 2
    padded = jnp.pad(values_all, ((half_width, half_width), (0, 0), (0, 0)))
    seg_pad = jnp.pad(seg_row, (half_width, half_width), constant_values=-1)
    live_pad = jnp.pad(live_row, (half_width, half_width))
    total = jnp.zeros(values_all.shape, jnp.float32)
    for tap_index in range(KSIZE):
        usable = ((seg_pad[tap_index:tap_index + SEQ] == seg_row) & (live_pad[tap_index:tap_index + SEQ] > 0)).astype(jnp.float32)
        total = total + conv_wide[:, tap_index][None, :, None] * padded[tap_index:tap_index + SEQ] * usable[:, None, None]
    return total

def row_attention(row_pack, conv_wide):
    queries, keys_all, values_all, seg_row, slot_row, live_row, slot_mask = row_pack
    scaling = 1.0 / math.sqrt(HEAD_DIM)
    slot_ids = jnp.arange(SLOTS, dtype=jnp.int32)
    onehot = (slot_row[None, :] == slot_ids[:, None]).astype(jnp.float32)
    counts = jnp.maximum(lax.optimization_barrier(jnp.sum(onehot, axis=1)), 1.0)
    query_land = jnp.einsum('st,the->hse', onehot, queries, precision=highest) / counts[None, :, None]
    key_land = jnp.einsum('st,the->hse', onehot, keys_all, precision=highest) / counts[None, :, None]
    slot_float = slot_mask.astype(jnp.float32)
    token_float = live_row.astype(jnp.float32)
    same_doc = (seg_row[:, None] == (slot_ids // LANDMARKS)[None, :]) & (slot_mask[None, :] > 0)
    allowed_three = same_doc.T & (live_row[None, :] > 0) | (slot_mask[:, None] == 0)
    logit_one = low_back(jnp.einsum('the,hse->hts', queries, key_land, precision=highest) * scaling)
    kern_one = low(jax.nn.softmax(jnp.where(same_doc[None], logit_one, -1000000000.0), axis=-1))
    logit_three = low_back(jnp.einsum('hse,the->hst', query_land, keys_all, precision=highest) * scaling)
    kern_three = low(jax.nn.softmax(jnp.where(allowed_three[None], logit_three, -1000000000.0), axis=-1) * slot_float[None, :, None])
    block_shape = (HEADS, DOCS, LANDMARKS, HEAD_DIM)
    slot_blocks = slot_float.reshape(DOCS, LANDMARKS)
    weights, inverse = newton_inverse(query_land.reshape(block_shape), key_land.reshape(block_shape), slot_blocks)
    carried = low_back(jnp.einsum('hst,the->hse', kern_three, values_all, precision=highest))
    mixed = low(jnp.einsum('hdij,hdje->hdie', inverse, carried.reshape(block_shape), precision=highest).reshape(HEADS, SLOTS, HEAD_DIM))
    attended = jnp.einsum('hts,hse->the', kern_one, mixed, precision=highest)
    conv_out = depthwise(values_all, seg_row, live_row, conv_wide)
    heads_out = (attended + conv_out) * token_float[:, None, None]
    doc_live = slot_blocks[:, 0]
    norm_weights = jnp.sqrt(jnp.where(doc_live > 0, lax.optimization_barrier(jnp.sum(weights * weights, axis=(-2, -1))), 1.0))
    norm_inverse = jnp.sqrt(jnp.where(doc_live > 0, lax.optimization_barrier(jnp.sum(inverse * inverse, axis=(-2, -1))), 1.0))
    proxy_row = (norm_weights * norm_inverse * doc_live / LANDMARKS).T
    return (heads_out.reshape(SEQ, D), proxy_row)

def forward(tokens_wide, qkv_wide, out_wide, conv_wide, up_wide, down_wide, gains_wide, biases_wide, seg_ids, landmark_slot, token_live, slot_live):
    projected = jnp.einsum('td,cde->cte', tokens_wide, qkv_wide, precision=highest)
    queries = low(low_back(projected[0])).reshape(ROWS, SEQ, HEADS, HEAD_DIM)
    keys_all = low(low_back(projected[1])).reshape(ROWS, SEQ, HEADS, HEAD_DIM)
    values_all = low(low_back(projected[2])).reshape(ROWS, SEQ, HEADS, HEAD_DIM)
    mapped = jax.checkpoint(lambda row_pack: row_attention(row_pack, conv_wide))
    heads_all, proxies_rows = lax.map(mapped, (queries, keys_all, values_all, seg_ids, landmark_slot, token_live, slot_live))
    heads_low = low(low_back(heads_all.reshape(TOKENS, D)))
    attention = low_back(jnp.dot(heads_low, out_wide, precision=highest))
    hidden = layer_norm(tokens_wide + attention, gains_wide[0], biases_wide[0])
    hidden_low = low(hidden)
    up_proj = low_back(jnp.dot(hidden_low, up_wide, precision=highest))
    activated = low(jax.nn.gelu(up_proj, approximate=False))
    down_proj = low_back(jnp.dot(activated, down_wide, precision=highest))
    result = layer_norm(hidden + down_proj, gains_wide[1], biases_wide[1])
    return (result, proxies_rows)

def reference(tokens, w_qkv, w_out, conv_weight, w_up, w_down, norm_gain, norm_bias, cotangent, seg_ids, landmark_slot, token_live, slot_live):

    def wrapped(*floats):
        return forward(*floats, seg_ids, landmark_slot, token_live, slot_live)
    primals = (tokens.astype(jnp.float32), w_qkv.astype(jnp.float32), w_out.astype(jnp.float32), conv_weight.astype(jnp.float32), w_up.astype(jnp.float32), w_down.astype(jnp.float32), norm_gain.astype(jnp.float32), norm_bias.astype(jnp.float32))
    result, pullback, proxies = jax.vjp(wrapped, *primals, has_aux=True)
    grads = pullback(cotangent.astype(jnp.float32))
    return (result.astype(jnp.bfloat16), grads[0], grads[1], grads[2], grads[3], grads[4], grads[5], grads[6], grads[7], proxies)
```

```python
import math

import jax
import jax.numpy as jnp
from jax import lax
from jax.sharding import PartitionSpec as P

HEAD_DIM = 64
LANDMARKS = 64
NEWTON = 6


highest = lax.Precision.HIGHEST
norm_epsilon = 1e-05


def split_up(shard, dim, length):
    before, after = (shard.shape[:dim], shard.shape[dim + 1 :])
    return jnp.moveaxis(shard.reshape(*before, length, -1, *after), dim, 0)


def sum_at_owner(shard, axis, dim):
    pieces = split_up(shard, dim, lax.axis_size(axis))
    arrived = lax.all_to_all(pieces, axis, split_axis=0, concat_axis=0, tiled=True)
    return arrived.astype(jnp.float32).sum(axis=0)


def layer_norm(values, gain_row, bias_row):
    average = jnp.mean(values, axis=-1, keepdims=True)
    centered = values - average
    variance = jnp.mean(centered * centered, axis=-1, keepdims=True)
    return centered * lax.rsqrt(variance + norm_epsilon) * gain_row + bias_row


def newton_inverse(query_land, key_land, live_slots):
    scaling = 1.0 / math.sqrt(HEAD_DIM)
    logits = jnp.einsum("...ie,...je->...ij", query_land, key_land, precision=highest) * scaling
    allowed = live_slots[..., None, :] > 0
    weights = (
        jax.nn.softmax(jnp.where(allowed, logits, -1000000000.0), axis=-1)
        * live_slots[..., :, None]
    )
    colsums = jnp.sum(weights, axis=-2)
    initial = 1.0 / jnp.maximum(jnp.max(colsums, axis=-1), 1.0)
    inverse = initial[..., None, None] * jnp.swapaxes(weights, -1, -2)
    identity = jnp.eye(LANDMARKS, dtype=jnp.float32)
    for repeat in range(NEWTON):
        product = jnp.einsum("...ij,...jk->...ik", weights, inverse, precision=highest)
        nested = 7.0 * identity - product
        nested = 15.0 * identity - jnp.einsum(
            "...ij,...jk->...ik", product, nested, precision=highest
        )
        nested = 13.0 * identity - jnp.einsum(
            "...ij,...jk->...ik", product, nested, precision=highest
        )
        inverse = 0.25 * jnp.einsum("...ij,...jk->...ik", inverse, nested, precision=highest)
    return (weights, inverse)


def masked_softmax(logits, allowed):
    filled = jnp.where(allowed, logits, -1000000000.0)
    largest = jnp.max(filled, axis=-1, keepdims=True)
    raised = jnp.exp(filled - largest)
    return raised / jnp.sum(raised, axis=-1, keepdims=True)


TILE = 128


def band_of(kernel, taps_total):
    wide = TILE + taps_total - 1
    row = jnp.pad(kernel, ((0, 0), (0, wide + 1 - taps_total)))
    flat = jnp.tile(row, (1, TILE))[:, : TILE * wide]
    return flat.reshape(kernel.shape[0], TILE, wide)


def taps_of(band, taps_total):
    heads, _, wide = band.shape
    flat = jnp.pad(band.reshape(heads, TILE * wide), ((0, 0), (0, TILE)))
    return flat.reshape(heads, TILE, wide + 1).sum(axis=1)[:, :taps_total]


def windows(rows, half_width):
    count = rows.shape[0] // TILE
    pad = [(half_width, half_width)] + [(0, 0)] * (rows.ndim - 1)
    padded = jnp.pad(rows, pad)
    return jnp.stack(
        [padded[i * TILE : i * TILE + TILE + 2 * half_width] for i in range(count)]
    )


def overlap_add(tiles, half_width):
    count, wide = tiles.shape[:2]
    rest = tiles.shape[2:]
    zero = jnp.zeros((1, half_width) + rest, tiles.dtype)
    body = tiles[:, half_width : half_width + TILE]
    before = jnp.concatenate([tiles[1:, :half_width], zero])
    after = jnp.concatenate([zero, tiles[:-1, half_width + TILE :]])
    gap = jnp.zeros((count, TILE - 2 * half_width) + rest, tiles.dtype)
    total = body + jnp.concatenate([after, gap, before], axis=1)
    return total.reshape((count * TILE,) + rest)


def per_device(
    tokens,
    w_qkv,
    w_out,
    conv_weight,
    w_up,
    w_down,
    norm_gain,
    norm_bias,
    cotangent,
    seg_ids,
    landmark_slot,
    token_live,
    slot_live,
):
    scaling = 1.0 / math.sqrt(HEAD_DIM)
    gathered = lax.all_gather(tokens, "tensor", axis=0, tiled=True)
    projections = lax.all_gather(
        jnp.concatenate([w_qkv, w_out.T[None]]), "dp", axis=1, tiled=True
    )
    qkv_full, out_full = projections[:3], projections[3].T
    up_full, down_full, norms_full = (
        lax.all_gather(w_up, ("dp", "tensor"), axis=1, tiled=True),
        lax.all_gather(w_down, ("dp", "tensor"), axis=0, tiled=True),
        lax.all_gather(
            jnp.concatenate([norm_gain, norm_bias]), ("dp", "tensor"), axis=1, tiled=True
        ),
    )
    gains_full, biases_full = norms_full[:2], norms_full[2:]
    seq_len = gathered.shape[0]
    local_heads = qkv_full.shape[2] // HEAD_DIM
    slot_count = slot_live.shape[1]
    doc_slots = slot_count // LANDMARKS
    projected = jnp.einsum(
        "td,cde->cte", gathered, qkv_full, preferred_element_type=jnp.float32
    ).astype(jnp.bfloat16)
    queries = projected[0].reshape(seq_len, local_heads, HEAD_DIM)
    keys_all = projected[1].reshape(seq_len, local_heads, HEAD_DIM)
    values_all = projected[2].reshape(seq_len, local_heads, HEAD_DIM)
    seg_row = seg_ids[0]
    slot_row = landmark_slot[0]
    live_row = token_live[0]
    slot_mask = slot_live[0]
    slot_ids = jnp.arange(slot_count, dtype=jnp.int32)
    onehot = (slot_row[None, :] == slot_ids[:, None]).astype(jnp.bfloat16)
    onehot_wide = onehot.astype(jnp.float32)
    counts = jnp.maximum(jnp.sum(onehot_wide, axis=1), 1.0)
    query_land = (
        jnp.einsum("st,the->hse", onehot, queries, preferred_element_type=jnp.float32)
        / counts[None, :, None]
    )
    key_land = (
        jnp.einsum("st,the->hse", onehot, keys_all, preferred_element_type=jnp.float32)
        / counts[None, :, None]
    )
    slot_float = slot_mask.astype(jnp.float32)
    token_float = live_row.astype(jnp.float32)
    same_doc = (seg_row[:, None] == (slot_ids // LANDMARKS)[None, :]) & (slot_mask[None, :] > 0)
    allowed_three = same_doc.T & (live_row[None, :] > 0) | (slot_mask[:, None] == 0)
    queries_wide = queries.astype(jnp.float32)
    keys_wide = keys_all.astype(jnp.float32)
    kern_one = masked_softmax(
        jnp.einsum("the,hse->hts", queries_wide, key_land, precision=highest) * scaling,
        same_doc[None],
    )
    kern_one_low = kern_one.astype(jnp.bfloat16)
    kern_three = (
        masked_softmax(
            jnp.einsum("hse,the->hst", query_land, keys_wide, precision=highest) * scaling,
            allowed_three[None],
        )
        * slot_float[None, :, None]
    )
    kern_three_low = kern_three.astype(jnp.bfloat16)
    block_shape = (local_heads, doc_slots, LANDMARKS, HEAD_DIM)
    slot_blocks = slot_float.reshape(doc_slots, LANDMARKS)
    (weights, inverse), newton_pull = jax.vjp(
        lambda query_blocks, key_blocks: newton_inverse(query_blocks, key_blocks, slot_blocks),
        query_land.reshape(block_shape),
        key_land.reshape(block_shape),
    )
    carried = jnp.einsum(
        "hst,the->hse", kern_three_low, values_all, preferred_element_type=jnp.float32
    ).reshape(block_shape)
    mixed_low = (
        jnp.einsum("hdij,hdje->hdie", inverse, carried, precision=highest)
        .reshape(local_heads, slot_count, HEAD_DIM)
        .astype(jnp.bfloat16)
    )
    attended = jnp.einsum(
        "hts,hse->the", kern_one_low, mixed_low, preferred_element_type=jnp.float32
    )
    taps_total = conv_weight.shape[1]
    half_width = taps_total // 2
    seg_windows = windows(seg_row + 1, half_width)
    live_windows = windows(live_row, half_width)
    tap_mask = (
        ((seg_row + 1).reshape(-1, TILE)[:, :, None] == seg_windows[:, None, :])
        & (live_windows[:, None, :] > 0)
    ).astype(jnp.bfloat16)
    band = band_of(conv_weight, taps_total)
    band_low = band.astype(jnp.bfloat16)
    masked_band = band_low[:, None] * tap_mask[None]
    value_windows = windows(values_all, half_width)
    conv_out = jnp.einsum(
        "hntu,nuhe->nthe", masked_band, value_windows, preferred_element_type=jnp.float32
    ).reshape(seq_len, local_heads, HEAD_DIM)
    heads_low = (
        ((attended + conv_out) * token_float[:, None, None])
        .reshape(seq_len, local_heads * HEAD_DIM)
        .astype(jnp.bfloat16)
    )
    partial_out = jnp.dot(heads_low, out_full, preferred_element_type=jnp.float32)
    attention = lax.psum_scatter(
        partial_out.astype(jnp.bfloat16), "tensor", scatter_dimension=0, tiled=True
    ).astype(jnp.float32)
    doc_live = slot_blocks[:, 0]
    norm_weights = jnp.sqrt(jnp.where(doc_live > 0, jnp.sum(weights * weights, axis=(-2, -1)), 1.0))
    norm_inverse = jnp.sqrt(jnp.where(doc_live > 0, jnp.sum(inverse * inverse, axis=(-2, -1)), 1.0))
    proxies = (norm_weights * norm_inverse * doc_live / LANDMARKS).T[None]
    residual_in = tokens.astype(jnp.float32) + attention
    hidden, norm_one_pull = jax.vjp(
        layer_norm,
        residual_in,
        gains_full[0].astype(jnp.float32),
        biases_full[0].astype(jnp.float32),
    )
    hidden_low = hidden.astype(jnp.bfloat16)
    up_proj = jnp.dot(hidden_low, up_full, preferred_element_type=jnp.float32)
    activated, gelu_pull = jax.vjp(lambda inputs: jax.nn.gelu(inputs, approximate=False), up_proj)
    activated_low = activated.astype(jnp.bfloat16)
    down_proj = jnp.dot(activated_low, down_full, preferred_element_type=jnp.float32)
    result, norm_two_pull = jax.vjp(
        layer_norm,
        hidden + down_proj,
        gains_full[1].astype(jnp.float32),
        biases_full[1].astype(jnp.float32),
    )
    layer_out = result.astype(jnp.bfloat16)
    grad_sum, gain_two, bias_two = norm_two_pull(cotangent.astype(jnp.float32))
    grad_sum_low = grad_sum.astype(jnp.bfloat16)
    up_back, down_back = up_full, down_full
    grad_down = jnp.einsum(
        "tf,td->fd", activated_low, grad_sum_low, preferred_element_type=jnp.float32
    )
    grad_act = jnp.einsum("td,fd->tf", grad_sum_low, down_back, preferred_element_type=jnp.float32)
    grad_up_low = gelu_pull(grad_act)[0].astype(jnp.bfloat16)
    grad_up = jnp.einsum("td,tf->df", hidden_low, grad_up_low, preferred_element_type=jnp.float32)
    grad_hidden = grad_sum + jnp.einsum(
        "tf,df->td", grad_up_low, up_back, preferred_element_type=jnp.float32
    )
    grad_pre, gain_one, bias_one = norm_one_pull(grad_hidden)
    grad_attn_low = grad_pre.astype(jnp.bfloat16)
    grad_up_shard, grad_down_shard = (
        lax.psum_scatter(
            grad_up.astype(jnp.bfloat16), ("dp", "tensor"), scatter_dimension=1, tiled=True
        ).astype(jnp.float32),
        lax.psum_scatter(
            grad_down.astype(jnp.bfloat16), ("dp", "tensor"), scatter_dimension=0, tiled=True
        ).astype(jnp.float32),
    )
    norm_grads = lax.all_to_all(
        split_up(
            jnp.stack([gain_one, gain_two, bias_one, bias_two]),
            1,
            lax.axis_size("dp") * lax.axis_size("tensor"),
        ),
        ("dp", "tensor"),
        split_axis=0,
        concat_axis=0,
        tiled=True,
    ).sum(axis=0)
    gain_shard, bias_shard = norm_grads[:2], norm_grads[2:]
    grad_rows = lax.all_gather(grad_attn_low, "tensor", axis=0, tiled=True)
    grad_out_local = jnp.einsum(
        "tk,td->kd", heads_low, grad_rows, preferred_element_type=jnp.float32
    )
    grad_heads = jnp.einsum(
        "td,kd->tk", grad_rows, out_full, preferred_element_type=jnp.float32
    ).astype(jnp.bfloat16)
    grad_heads = (
        grad_heads.reshape(seq_len, local_heads, HEAD_DIM)
        * live_row.astype(jnp.bfloat16)[:, None, None]
    )
    grad_kern_one = jnp.einsum(
        "the,hse->hts", grad_heads, mixed_low, preferred_element_type=jnp.float32
    )
    grad_mixed = jnp.einsum(
        "hts,the->hse", kern_one_low, grad_heads, preferred_element_type=jnp.float32
    ).reshape(block_shape)
    grad_logit_one = (
        kern_one * (grad_kern_one - jnp.sum(grad_kern_one * kern_one, axis=-1, keepdims=True))
    ).astype(jnp.bfloat16)
    grad_inverse = jnp.einsum("hdie,hdje->hdij", grad_mixed, carried, precision=highest)
    grad_carried_low = (
        jnp.einsum("hdij,hdie->hdje", inverse, grad_mixed, precision=highest)
        .reshape(local_heads, slot_count, HEAD_DIM)
        .astype(jnp.bfloat16)
    )
    grad_kern_three = jnp.einsum(
        "hse,the->hst", grad_carried_low, values_all, preferred_element_type=jnp.float32
    )
    grad_values = jnp.einsum(
        "hst,hse->the", kern_three_low, grad_carried_low, preferred_element_type=jnp.float32
    )
    grad_logit_three = (
        kern_three
        * (grad_kern_three - jnp.sum(grad_kern_three * kern_three, axis=-1, keepdims=True))
    ).astype(jnp.bfloat16)
    grad_query_blocks, grad_key_blocks = newton_pull((jnp.zeros_like(weights), grad_inverse))
    grad_query_land = (
        grad_query_blocks.reshape(local_heads, slot_count, HEAD_DIM)
        + jnp.einsum("hst,the->hse", grad_logit_three, keys_all, preferred_element_type=jnp.float32)
        * scaling
    )
    grad_key_land = (
        grad_key_blocks.reshape(local_heads, slot_count, HEAD_DIM)
        + jnp.einsum("hts,the->hse", grad_logit_one, queries, preferred_element_type=jnp.float32)
        * scaling
    )
    grad_queries = (
        jnp.einsum("hts,hse->the", grad_logit_one.astype(jnp.float32), key_land, precision=highest)
        * scaling
    )
    grad_queries = grad_queries + jnp.einsum(
        "st,hse->the", onehot_wide, grad_query_land / counts[None, :, None], precision=highest
    )
    grad_keys = (
        jnp.einsum(
            "hst,hse->the", grad_logit_three.astype(jnp.float32), query_land, precision=highest
        )
        * scaling
    )
    grad_keys = grad_keys + jnp.einsum(
        "st,hse->the", onehot_wide, grad_key_land / counts[None, :, None], precision=highest
    )
    head_tiles = grad_heads.reshape(-1, TILE, local_heads, HEAD_DIM)
    band_grad = jnp.einsum(
        "nthe,nuhe->nhtu", head_tiles, value_windows, preferred_element_type=jnp.float32
    )
    conv_local = taps_of((band_grad * tap_mask[:, None]).sum(axis=0), taps_total)
    grad_values = grad_values + overlap_add(
        jnp.einsum(
            "hntu,nthe->nuhe", masked_band, head_tiles, preferred_element_type=jnp.float32
        ),
        half_width,
    )
    grad_stack = (
        jnp.stack([grad_queries, grad_keys, grad_values])
        .reshape(3, seq_len, local_heads * HEAD_DIM)
        .astype(jnp.bfloat16)
    )
    grad_qkv_local = jnp.einsum(
        "td,cte->cde", gathered, grad_stack, preferred_element_type=jnp.float32
    )
    grad_rows_in = jnp.einsum(
        "cte,cde->td", grad_stack, qkv_full, preferred_element_type=jnp.float32
    )
    input_grad = grad_pre + lax.psum_scatter(
        grad_rows_in.astype(jnp.bfloat16), "tensor", scatter_dimension=0, tiled=True
    ).astype(jnp.float32)
    grad_qkv, grad_out = (
        sum_at_owner(grad_qkv_local.astype(jnp.bfloat16), "dp", 1),
        sum_at_owner(grad_out_local.astype(jnp.bfloat16), "dp", 1),
    )
    grad_conv = lax.all_to_all(
        jnp.broadcast_to(conv_local, (lax.axis_size("dp"),) + conv_local.shape),
        "dp",
        split_axis=0,
        concat_axis=0,
        tiled=True,
    ).sum(axis=0)
    return (
        layer_out,
        input_grad,
        grad_qkv,
        grad_out,
        grad_conv,
        grad_up_shard,
        grad_down_shard,
        gain_shard,
        bias_shard,
        proxies,
    )


def solution(mesh):
    return jax.shard_map(
        per_device,
        mesh=mesh,
        in_specs=(
            P(("dp", "tensor"), None),
            P(None, "dp", "tensor"),
            P("tensor", "dp"),
            P("tensor", None),
            P(None, ("dp", "tensor")),
            P(("dp", "tensor"), None),
            P(None, ("dp", "tensor")),
            P(None, ("dp", "tensor")),
            P(("dp", "tensor"), None),
            P("dp", None),
            P("dp", None),
            P("dp", None),
            P("dp", None),
        ),
        out_specs=(
            P(("dp", "tensor"), None),
            P(("dp", "tensor"), None),
            P(None, "dp", "tensor"),
            P("tensor", "dp"),
            P("tensor", None),
            P(None, ("dp", "tensor")),
            P(("dp", "tensor"), None),
            P(None, ("dp", "tensor")),
            P(None, ("dp", "tensor")),
            P("dp", None, "tensor"),
        ),
        check_vma=False,
    )
```

```python
import functools
import math

import jax
import jax.numpy as jnp
from jax import lax
from jax.experimental import pallas as pl
from jax.experimental.pallas import tpu as pltpu
from jax.sharding import PartitionSpec as P

HEAD_DIM = 64
LANDMARKS = 64
NEWTON = 6
TILE = 128
HALO = TILE // 2
CHUNK = 256
LANES = 128
bf16 = jnp.bfloat16
f32 = jnp.float32
i32 = jnp.int32
norm_epsilon = 1e-05
MESH = pl.DeviceIdType.MESH
LIMIT = 62 * 2**20


def mm(a, b):
    return lax.dot_general(a, b, (((1,), (0,)), ((), ())), preferred_element_type=f32)


def mm_nt(a, b):
    return lax.dot_general(a, b, (((1,), (1,)), ((), ())), preferred_element_type=f32)


def split(a):
    high = a.astype(bf16)
    return high, (a - high.astype(f32)).astype(bf16)


def mm3(a, b, dot=mm):
    return dot(a[0], b[0]) + (dot(a[0], b[1]) + dot(a[1], b[0]))


def left_of(a):
    return jnp.concatenate(split(a), axis=1)


def right_of(b):
    high, low = split(b)
    top = jnp.concatenate([high, low], axis=1)
    bottom = jnp.concatenate([jnp.zeros_like(high), high], axis=1)
    return jnp.concatenate([top, bottom], axis=0)


def right_nt(b):
    high, low = split(b)
    top = jnp.concatenate([high, jnp.zeros_like(high)], axis=1)
    bottom = jnp.concatenate([low, high], axis=1)
    return jnp.concatenate([top, bottom], axis=0)


def tt(left, right):
    both = mm(left, right)
    return both[:, :TILE] + both[:, TILE:]


def tt_nt(left, right):
    both = mm_nt(left, right)
    return both[:, :TILE] + both[:, TILE:]


def iota(shape, dim):
    return lax.broadcasted_iota(i32, shape, dim)


def tile_same():
    shape = (TILE, TILE)
    return iota(shape, 0) // LANDMARKS == iota(shape, 1) // LANDMARKS


def tile_eye():
    shape = (TILE, TILE)
    return (iota(shape, 0) == iota(shape, 1)).astype(f32)


def pack(tile):
    return tile[:LANDMARKS] + tile[LANDMARKS:]


def unpack(packed):
    first = iota(packed.shape, 1) < LANDMARKS
    return jnp.concatenate([jnp.where(first, packed, 0.0), jnp.where(first, 0.0, packed)], axis=0)


def landmark_parts(land):
    first = iota(land.shape, 1) < HEAD_DIM
    turned = pltpu.roll(land, HEAD_DIM, 1)
    return jnp.where(first, turned, 0.0), jnp.where(first, 0.0, turned), jnp.where(first, land, 0.0)


def newton_step(Pm, W, ident):
    Pr = right_of(Pm)
    S = tt(left_of(Pm), Pr)
    N = 13.0 * ident - 15.0 * Pm + tt(left_of(S), right_of(7.0 * ident - Pm))
    Nl = left_of(N)
    return S, N, 0.25 * tt(Nl, Pr), 0.25 * tt(Nl, right_of(W))


def newton_start(A):
    colsum = jnp.sum(A, axis=0, keepdims=True)
    first = iota(colsum.shape, 1) < LANDMARKS
    tops = [
        jnp.max(jnp.where(first, colsum, 0.0), axis=1, keepdims=True),
        jnp.max(jnp.where(first, 0.0, colsum), axis=1, keepdims=True),
    ]
    factor = 1.0 / jnp.maximum(jnp.where(first, tops[0], tops[1]), 1.0)
    return factor, colsum, tops


def column(row):
    return jnp.broadcast_to(row, (LANES, LANES)).T


def band_from(row):
    wide = jnp.broadcast_to(row, (TILE, 2 * TILE))
    return pltpu.roll(wide, 0, 1, stride=1, stride_axis=0)


def diagonal_sums(band):
    where = iota(band.shape, 0)
    step = 1
    while step < TILE:
        turned = pltpu.roll(band, 2 * TILE - step, 1)
        band = jnp.where((where // step) % 2 == 1, turned, band)
        step *= 2
    return jnp.sum(band, axis=0, keepdims=True)


def seg_of(code):
    return (code // 512) % 8


def live_of(code):
    return code // 4096


def slot_of(code):
    return code % 512


class Place:
    def __init__(self):
        self.dp = lax.axis_index("dp")
        self.t = lax.axis_index("tensor")
        self.x = self.t // 2
        self.c = self.t % 2
        self.sibling = self.x * 2 + 1 - self.c
        self.across = (1 - self.x) * 2 + self.c
        self.diagonal = (1 - self.x) * 2 + 1 - self.c
        self.z = self.dp // 2
        self.y = self.dp % 2

    def tensor_peers(self):
        return [(self.dp, t) for t in (self.sibling, self.across, self.diagonal)]

    def dp_at(self, turn_z, turn_y):
        return ((self.z + turn_z) % 4) * 2 + (self.y + turn_y) % 2


def greet(peers):
    barrier = pltpu.get_barrier_semaphore()
    for peer in peers:
        pl.semaphore_signal(barrier, inc=1, device_id=peer, device_id_type=MESH)
    pl.semaphore_wait(barrier, len(peers))


def push(src, dst, sems, index, dp, t):
    return pltpu.make_async_remote_copy(
        src_ref=src,
        dst_ref=dst,
        send_sem=sems.at[0, index],
        recv_sem=sems.at[1, index],
        device_id=(dp, t),
        device_id_type=MESH,
    )


def forward_body(
    gather, taps_total,
    x, w, taps, seg, slot, live, slot_live,
    xall, wfull, tokc, segw, qk, v, kern1, kern3, land, counts, Aout, mixed, carried, heads, prox,
    wsh, wlog, l3, carriedT, state, bands, hsend, segp, xsem, wsem, hsem,
):
    here = Place()
    block = x.shape[0]
    blocks = xall.shape[0]
    seq = block * blocks
    heads_n = qk.shape[1] // LANES
    nslot = land.shape[0]
    wide = v.shape[1]
    nchunk = seq // CHUNK
    per_block = block // CHUNK
    tiles_n = nslot // TILE
    width = heads_n * HEAD_DIM
    scaling = 1.0 / math.sqrt(HEAD_DIM)

    depth = w.shape[1]
    parts = []
    for h in range(heads_n):
        e = slice(HEAD_DIM * h, HEAD_DIM * h + HEAD_DIM)
        parts += [w[0, :, e], w[1, :, e]]
    parts += [w[2], jnp.zeros((depth, wide - width), bf16)]
    wsh[...] = jnp.concatenate(parts, axis=1)

    peers = here.tensor_peers()
    if gather:
        peers = peers + [(here.dp_at(dz, 0), here.t) for dz in (1, 2, 3)] + [(here.dp_at(0, 1), here.t)]
    greet(peers)

    copies = []
    pieces = block // TILE

    def start(copy):
        copy.start()
        copies.append(copy)
        return copy

    crossing = [
        start(push(x.at[pl.ds(p * TILE, TILE)], xall.at[here.t, pl.ds(p * TILE, TILE)], xsem, p, here.dp, here.across))
        for p in range(pieces)
    ]
    beside = start(push(x, xall.at[here.t], xsem, pieces, here.dp, here.sibling))
    if gather:
        mine = wfull.at[pl.ds(pl.multiple_of(here.dp * depth, 16), depth)]
        along = [start(push(wsh, mine, wsem, dz, here.dp_at(dz, 0), here.t)) for dz in (1, 2, 3)]
        along = [start(push(wsh, mine, wsem, 0, here.dp_at(0, 1), here.t))] + along
        wfull[pl.ds(pl.multiple_of(here.dp * depth, 16), depth), :] = wsh[...]
    else:
        wfull[...] = wsh[...]
    xall[here.t] = x[...]

    segp[...] = jnp.full(segp.shape, -1, i32)
    segp[0:1, TILE : TILE + seq] = jnp.where(live[...] > 0, seg[...], -1)
    segp[1:2, TILE : TILE + seq] = seg[...]
    code = (slot[...] + 512 * seg[...] + 4096 * live[...]).astype(f32)
    for i in range(seq // TILE):
        lanes = slice(i * TILE, i * TILE + TILE)
        tokc[lanes, :] = column(code[:, lanes]).astype(i32)
        near = pltpu.roll(segp[:, i * TILE : i * TILE + 3 * TILE], 3 * TILE - HALO, 1)
        segw[i : i + 1, :] = near[0:1, : 2 * TILE]
        segw[seq // TILE + i : seq // TILE + i + 1, :] = near[1:2, : 2 * TILE]
    for h in range(heads_n):
        bands[h] = band_from(taps[h : h + 1, :])
    doc_row = iota((1, nslot), 1) // LANDMARKS
    live_row = slot_live[...]
    live_cols = [column(live_row[:, g * TILE : (g + 1) * TILE].astype(f32)) for g in range(tiles_n)]
    v[0:HALO, :] = jnp.zeros((HALO, wide), bf16)
    v[seq + HALO : seq + 2 * HALO, :] = jnp.zeros((HALO, wide), bf16)

    if gather:
        along[0].wait_recv()
        for dz in (1, 2, 3):
            along[dz].wait_recv()
            got = wfull.at[pl.ds(pl.multiple_of(here.dp_at(4 - dz, 0) * depth, 16), depth)]
            along.append(start(push(got, got, wsem, 3 + dz, here.dp_at(0, 1), here.t)))
        for dz in (1, 2, 3):
            along[3 + dz].wait_recv()

    def project(b, carry):
        def one(i, carry):
            acc, cnt = carry
            c = b * per_block + i
            rows = pl.ds(pl.multiple_of(c * CHUNK, CHUNK), CHUNK)
            out = mm(xall[b, pl.ds(pl.multiple_of(i * CHUNK, CHUNK), CHUNK), :], wfull[...])
            qk_now = out[:, : LANES * heads_n].astype(bf16)
            qk[rows, :] = qk_now
            v[pl.ds(pl.multiple_of(c * CHUNK + HALO, HALO), CHUNK), :] = out[:, LANES * heads_n :].astype(bf16)
            slot_now = slot[:, pl.ds(pl.multiple_of(c * CHUNK, CHUNK), CHUNK)]
            hot = (slot_now == iota((nslot, CHUNK), 0)).astype(f32)
            return acc + mm(hot.astype(bf16), qk_now), cnt + jnp.sum(hot, axis=1, keepdims=True)

        return lax.fori_loop(0, per_block, one, carry)

    carry = (jnp.zeros((nslot, LANES * heads_n), f32), jnp.zeros((nslot, 1), f32))
    carry = project(here.t, carry)
    beside.wait_recv()
    carry = project(here.sibling, carry)
    passed = []
    for p in range(pieces):
        crossing[p].wait_recv()
        got = xall.at[here.across, pl.ds(p * TILE, TILE)]
        passed.append(start(push(got, got, xsem, pieces + 1 + p, here.dp, here.sibling)))
    carry = project(here.across, carry)
    for p in range(pieces):
        passed[p].wait_recv()
    acc, cnt = project(here.diagonal, carry)
    cnt = jnp.maximum(cnt, 1.0)
    counts[...] = jnp.broadcast_to(cnt, counts.shape)
    land[...] = acc / cnt

    same = tile_same()
    ident = tile_eye()
    for h in range(heads_n):
        k0, q1, q0 = landmark_parts(land[:, LANES * h : LANES * h + LANES])
        wlog[h] = jnp.concatenate(split(jnp.concatenate([k0, q1], axis=0) * scaling), axis=1)
        for g in range(tiles_n):
            rows = slice(g * TILE, g * TILE + TILE)
            logit = tt_nt(left_of(q0[rows] * scaling), right_nt(k0[rows]))
            filled = jnp.where(same & (live_row[:, rows] > 0), logit, -1e9)
            raised = jnp.exp(filled - jnp.max(filled, axis=1, keepdims=True))
            A = raised / jnp.sum(raised, axis=1, keepdims=True) * live_cols[g]
            n = h * tiles_n + g
            Aout[n] = A
            factor, _, _ = newton_start(A)
            W = A * factor
            state[0, n] = tt_nt(left_of(A), right_nt(W))
            state[1, n] = W

    def step(i, none):
        for n in range(heads_n * tiles_n):
            _, _, Pm, W = newton_step(state[0, n], state[1, n], ident)
            state[0, n] = Pm
            state[1, n] = W
        return none

    lax.fori_loop(0, NEWTON, step, 0)

    def logits(c, top):
        rows = pl.ds(pl.multiple_of(c * CHUNK, CHUNK), CHUNK)
        now = tokc[rows, 0:1]
        allowed = (seg_of(now) == doc_row) & (live_row > 0)
        alive = allowed & (live_of(now) > 0)
        tops = []
        for h in range(heads_n):
            part = qk[rows, LANES * h : LANES * h + LANES]
            both = mm_nt(jnp.concatenate([part, part], axis=1), wlog[h])
            one = jnp.where(allowed, both[:, :nslot], -1e9)
            raised = jnp.exp(one - jnp.max(one, axis=1, keepdims=True))
            kern1[h, rows, :] = (raised / jnp.sum(raised, axis=1, keepdims=True)).astype(bf16)
            three = jnp.where(alive, both[:, nslot:], -1e9)
            l3[h, rows, :] = three
            tops.append(jnp.maximum(top[h], jnp.max(three, axis=0, keepdims=True)))
        return tuple(tops)

    top = lax.fori_loop(
        0, nchunk, logits, tuple(jnp.full((1, nslot), -1e9, f32) for _ in range(heads_n))
    )

    def raise_three(c, total):
        rows = pl.ds(pl.multiple_of(c * CHUNK, CHUNK), CHUNK)
        totals = []
        for h in range(heads_n):
            raised = jnp.exp(l3[h, rows, :] - top[h])
            l3[h, rows, :] = raised
            totals.append(total[h] + jnp.sum(raised, axis=0, keepdims=True))
        return tuple(totals)

    total = lax.fori_loop(
        0, nchunk, raise_three, tuple(jnp.zeros((1, nslot), f32) for _ in range(heads_n))
    )
    norm = [live_row.astype(f32) / total[h] for h in range(heads_n)]
    carriedT[...] = jnp.zeros_like(carriedT)

    def carry_three(c, none):
        rows = pl.ds(pl.multiple_of(c * CHUNK, CHUNK), CHUNK)
        vT = v[pl.ds(pl.multiple_of(c * CHUNK + HALO, HALO), CHUNK), :].astype(f32).T.astype(bf16)
        for h in range(heads_n):
            low = (l3[h, rows, :] * norm[h]).astype(bf16)
            kern3[h, rows, :] = low
            e = slice(HEAD_DIM * h, HEAD_DIM * h + HEAD_DIM)
            carriedT[e, :] += mm(vT[e, :], low)
        return none

    lax.fori_loop(0, nchunk, carry_three, 0)
    carried_all = carriedT[...].T
    carried[...] = carried_all
    lane = iota((TILE, wide), 1) // HEAD_DIM
    docs = nslot // LANDMARKS
    for h in range(heads_n):
        for g in range(tiles_n):
            rows = slice(g * TILE, g * TILE + TILE)
            n = h * tiles_n + g
            W = state[1, n]
            part = split(jnp.where(lane == h, carried_all[rows], 0.0))
            mixed[h, rows, :] = mm3(split(W.T), part).astype(bf16)
            A = Aout[n]
            A2 = jnp.sum(A * A, axis=0, keepdims=True)
            W2 = jnp.sum(W * W, axis=0, keepdims=True)
            first = iota(A2.shape, 1) < LANDMARKS
            for half in range(2):
                mine = first if half == 0 else jnp.logical_not(first)
                a2 = jnp.sum(jnp.where(mine, A2, 0.0), axis=1, keepdims=True)
                z2 = jnp.sum(jnp.where(mine, W2, 0.0), axis=1, keepdims=True)
                doc = g * 2 + half
                alive = live_row[:, doc * LANDMARKS : doc * LANDMARKS + 1] > 0
                value = jnp.where(alive, jnp.sqrt(a2) * jnp.sqrt(z2) / LANDMARKS, 0.0)
                prox[h * docs + doc : h * docs + doc + 1, :] = jnp.broadcast_to(value, (1, LANES))

    def finish(b, out, out_row):
        def one(k, none):
            c = b * per_block + k
            rows = pl.ds(pl.multiple_of(c * CHUNK, CHUNK), CHUNK)
            total = mm(kern1[0, rows, :], mixed[0])
            for h in range(1, heads_n):
                total = total + mm(kern1[h, rows, :], mixed[h])
            for part in range(CHUNK // TILE):
                i = c * (CHUNK // TILE) + part
                now = tokc[pl.ds(pl.multiple_of(i * TILE, TILE), TILE), 0:1]
                near = seg_of(now) == segw[pl.ds(i, 1), :]
                window = v[pl.ds(pl.multiple_of(i * TILE, TILE), 2 * TILE), :]
                conv = jnp.zeros((TILE, wide), f32)
                for h in range(heads_n):
                    term = mm(jnp.where(near, bands[h], 0.0).astype(bf16), window)
                    conv = jnp.where(lane == h, term, conv)
                got = (total[part * TILE : (part + 1) * TILE, :] + conv) * live_of(now).astype(f32)
                row = pl.multiple_of(k * CHUNK + part * TILE, TILE)
                out[out_row, pl.ds(row, TILE), :] = got.astype(bf16)
            return none

        lax.fori_loop(0, per_block, one, 0)

    sent = []
    for k, to in enumerate((here.diagonal, here.across, here.sibling)):
        finish(to, hsend, k)
        sent.append(start(push(hsend.at[k], heads.at[here.t], hsem, k, here.dp, to)))
    finish(here.t, heads, here.t)
    for copy in sent:
        copy.wait_recv()
    for copy in copies:
        copy.wait_send()


VMEM = pl.BlockSpec(memory_space=pltpu.VMEM)
ANY = pl.BlockSpec(memory_space=pl.ANY)


def dma(*shape):
    return pltpu.SemaphoreType.DMA(shape)


def attention_forward(x, w, taps, seg, slot, live, slot_live, heads_n, blocks, depth, taps_total):
    block, feat = x.shape
    seq, nslot = block * blocks, slot_live.shape[1]
    gather = w.shape[1] < feat
    wide = -(-heads_n * HEAD_DIM // 256) * 256
    tiles_n = heads_n * (nslot // TILE)
    shape = jax.ShapeDtypeStruct
    outs = (
        shape((blocks, block, feat), bf16),
        shape((feat, LANES * heads_n + wide), bf16),
        shape((seq, LANES), i32),
        shape((2 * (seq // TILE), 2 * TILE), i32),
        shape((seq, LANES * heads_n), bf16),
        shape((seq + 2 * HALO, wide), bf16),
        shape((heads_n, seq, nslot), bf16),
        shape((heads_n, seq, nslot), bf16),
        shape((nslot, LANES * heads_n), f32),
        shape((nslot, LANES), f32),
        shape((tiles_n, TILE, TILE), f32),
        shape((heads_n, nslot, wide), bf16),
        shape((nslot, wide), f32),
        shape((blocks, block, wide), bf16),
        shape((heads_n * (nslot // LANDMARKS), LANES), f32),
    )
    return pl.pallas_call(
        functools.partial(forward_body, gather, taps_total),
        out_shape=outs,
        in_specs=[VMEM] * 7,
        out_specs=tuple([VMEM] * len(outs)),
        scratch_shapes=[
            pltpu.VMEM((w.shape[1], LANES * heads_n + wide), bf16),
            pltpu.VMEM((heads_n, 2 * nslot, 256), bf16),
            pltpu.VMEM((heads_n, seq, nslot), f32),
            pltpu.VMEM((wide, nslot), f32),
            pltpu.VMEM((2, tiles_n, TILE, TILE), f32),
            pltpu.VMEM((heads_n, TILE, 2 * TILE), f32),
            pltpu.VMEM((3, block, wide), bf16),
            pltpu.VMEM((8, seq + 2 * TILE), i32),
            dma(2, 2 * (block // TILE) + 1),
            dma(2, 7),
            dma(2, 3),
        ],
        compiler_params=pltpu.CompilerParams(
            vmem_limit_bytes=LIMIT, collective_id=1 if gather else 2, has_side_effects=True
        ),
        cost_estimate=pl.CostEstimate(flops=10**10, bytes_accessed=3 * 10**7, transcendentals=10**7),
        name="attention_forward",
    )(x, w, taps, seg, slot, live, slot_live)


class Summer:
    def __init__(self, here, source, first, count, own, from_core, from_y, from_z, from_x, sems, local):
        self.here, self.source, self.rows = here, source, pl.ds(first, count)
        self.own, self.from_core, self.from_y, self.from_z, self.from_x = (
            own, from_core, from_y, from_z, from_x,
        )
        self.sems, self.local = sems, local
        self.copies = []

    def push(self, src, dst, index, dp, t):
        copy = push(src, dst, self.sems, index, dp, t)
        copy.start()
        self.copies.append(copy)
        return copy

    def begin(self):
        here = self.here
        self.loaded = pltpu.make_async_copy(
            self.source.at[:, :, :, here.c, self.rows], self.own, self.local
        )
        self.loaded.start()
        self.core = self.push(
            self.source.at[:, :, :, 1 - here.c, self.rows], self.from_core, 0, here.dp, here.sibling
        )

    def along_y(self):
        here = self.here
        self.loaded.wait()
        self.core.wait_recv()

        def one(n, none):
            z, x = n // 2, n % 2
            y = 1 - here.y
            total = self.from_core[z, y, x].astype(f32) + self.own[z, y, x].astype(f32)
            self.from_core[z, y, x] = total.astype(self.own.dtype)
            return none

        lax.fori_loop(0, 8, one, 0)
        self.y = self.push(
            self.from_core.at[:, 1 - here.y], self.from_y, 1, here.dp_at(0, 1), here.t
        )

    def along_z(self):
        here = self.here
        self.y.wait_recv()

        def one(n, none):
            z, x = n // 2, n % 2
            total = self.from_core[z, here.y, x].astype(f32) + self.own[z, here.y, x].astype(f32)
            total = total + self.from_y[z, x].astype(f32)
            self.from_y[z, x] = total.astype(self.own.dtype)
            return none

        lax.fori_loop(0, 8, one, 0)
        self.z = [
            self.push(
                self.from_y.at[(here.z + dz) % 4], self.from_z.at[dz - 1], 1 + dz, here.dp_at(dz, 0), here.t
            )
            for dz in (1, 2, 3)
        ]

    def along_x(self):
        here = self.here
        for copy in self.z:
            copy.wait_recv()
        for x in range(2):
            total = self.from_y[here.z, x].astype(f32)
            for n in range(3):
                total = total + self.from_z[n, x].astype(f32)
            self.from_y[here.z, x] = total.astype(self.own.dtype)
        self.x = self.push(
            self.from_y.at[here.z, 1 - here.x], self.from_x, 5, here.dp, here.across
        )

    def finish(self, out):
        self.x.wait_recv()
        here = self.here
        out[self.rows, :] = self.from_y[here.z, here.x].astype(f32) + self.from_x[...].astype(f32)
        for copy in self.copies:
            copy.wait_send()


SUMMER_SEMS = 6


def backward_body(gather, shares, *refs):
    (
        gsend, xall_in, wfull, tokc, segw, qk, v, kern1_in, kern3_in,
        land, counts, Ain, mixed, carried, taps, slot_live, gpre,
    ) = refs[:17]
    refs = refs[17:]
    sources, refs = refs[: len(shares)], refs[len(shares) :]
    (input_grad, gw, gconv), refs = refs[:3], refs[3:]
    sums, refs = refs[: len(shares)], refs[len(shares) :]
    (
        gl1, gl3, xall, xT, gopad, gqk, gv, gband, bands, gmixedT, glandT, hist, gstate, gcar, wback,
        part_out, part_in, part_sum, part_x, piece_v, piece_q, in_v, in_q, in_conv, conv_out,
        gsem, lsem, psem, vsem, csem,
    ) = refs[:30]
    refs = refs[30:]

    here = Place()
    blocks, block, wide = gsend.shape
    seq = blocks * block
    heads_n = gl1.shape[0]
    nslot = land.shape[0]
    nchunk = seq // CHUNK
    per_block = block // CHUNK
    tiles_n = nslot // TILE
    all_tiles = heads_n * tiles_n
    feat = wfull.shape[0]
    doc_row = iota((1, nslot), 1) // LANDMARKS
    live_row = slot_live[...]
    live_cols = [column(live_row[:, g * TILE : (g + 1) * TILE].astype(f32)) for g in range(tiles_n)]
    scaling = 1.0 / math.sqrt(HEAD_DIM)
    same = tile_same()
    ident = tile_eye()

    loads = [
        pltpu.make_async_copy(kern1_in, gl1, lsem.at[0]),
        pltpu.make_async_copy(xall_in, xall, lsem.at[1]),
        pltpu.make_async_copy(kern3_in, gl3, lsem.at[2]),
    ]
    for load in loads:
        load.start()

    peers = here.tensor_peers()
    if gather:
        peers = peers + [
            (here.dp_at(dz, dy), here.t) for dz in range(4) for dy in range(2) if dz or dy
        ]
    greet(peers)
    copies = []

    def start(copy):
        copy.start()
        copies.append(copy)
        return copy

    def landing(t):
        return gopad.at[pl.ds(pl.multiple_of(t * block + HALO, HALO), block)]

    gopad[0:HALO, :] = jnp.zeros((HALO, wide), bf16)
    gopad[seq + HALO : seq + 2 * HALO, :] = jnp.zeros((HALO, wide), bf16)
    arriving = [
        start(push(gsend.at[to], landing(here.t), gsem, k, here.dp, to))
        for k, to in enumerate((here.across, here.diagonal, here.sibling))
    ]
    gopad[pl.ds(pl.multiple_of(here.t * block + HALO, HALO), block), :] = gsend[here.t]

    summers = []
    for n, share in enumerate(shares):
        for first, count in share:
            buffers, refs = refs[:7], refs[7:]
            summers.append((Summer(here, sources[n], first, count, *buffers), sums[n]))
    for summer, _ in summers:
        summer.begin()

    for n in range(all_tiles):
        A = Ain[n]
        factor, _, _ = newton_start(A)
        W = A * factor
        hist[0, 0, n] = pack(tt_nt(left_of(A), right_nt(W)))
        hist[0, 1, n] = pack(W)

    def step(i, none):
        for n in range(all_tiles):
            S, N, Pm, W = newton_step(unpack(hist[i, 0, n]), unpack(hist[i, 1, n]), ident)
            hist[i, 2, n] = pack(S)
            hist[i, 3, n] = pack(N)
            hist[i + 1, 0, n] = pack(Pm)
            hist[i + 1, 1, n] = pack(W)
        return none

    lax.fori_loop(0, NEWTON, step, 0)
    for h in range(2 * heads_n):
        bands[h] = band_from(taps[h : h + 1, :])
    gmixedT[...] = jnp.zeros_like(gmixedT)
    glandT[...] = jnp.zeros_like(glandT)
    gband[...] = jnp.zeros_like(gband)
    for load in loads:
        load.wait()

    def turn(b, none):
        for i in range(block // TILE):
            rows = slice(i * TILE, i * TILE + TILE)
            col = pl.ds(pl.multiple_of(b * block + i * TILE, TILE), TILE)
            xT[:, col] = xall[b, rows, :].astype(f32).T.astype(bf16)
        return none

    lax.fori_loop(0, blocks, turn, 0)
    for summer, _ in summers:
        summer.along_y()
    for copy in arriving:
        copy.wait_recv()

    def one(c, none):
        rows = pl.ds(pl.multiple_of(c * CHUNK, CHUNK), CHUNK)
        g_now = gopad[pl.ds(pl.multiple_of(c * CHUNK + HALO, HALO), CHUNK), :]
        gT = g_now.astype(f32).T.astype(bf16)
        for h in range(heads_n):
            k1 = gl1[h, rows, :]
            gk = mm_nt(g_now, mixed[h])
            k1w = k1.astype(f32)
            gl1[h, rows, :] = (k1w * (gk - jnp.sum(gk * k1w, axis=1, keepdims=True))).astype(bf16)
            e = slice(HEAD_DIM * h, HEAD_DIM * h + HEAD_DIM)
            gmixedT[e, :] += mm(gT[e, :], k1)
        return none

    lax.fori_loop(0, nchunk, one, 0)
    gmixed = gmixedT[...].T
    carried_all = carried[...]
    lane = iota((TILE, wide), 1) // HEAD_DIM
    delta = []
    for h in range(heads_n):
        rows_delta = []
        for g in range(tiles_n):
            n = h * tiles_n + g
            rows = slice(g * TILE, g * TILE + TILE)
            W = unpack(hist[NEWTON, 1, n])
            gm = split(jnp.where(lane == h, gmixed[rows], 0.0))
            near = jnp.where(lane == h, carried_all[rows], 0.0)
            gstate[0, n] = jnp.zeros((TILE, TILE), f32)
            gstate[1, n] = jnp.where(same, mm3(split(near), gm, mm_nt), 0.0)
            gc = mm3(split(W), gm).astype(bf16)
            gcar[h, rows, :] = gc
            rows_delta.append(jnp.sum((gc.astype(f32) * near).T, axis=0, keepdims=True))
        delta.append(jnp.concatenate(rows_delta, axis=1))
    half = max(1, len(summers) // 3)
    for summer, _ in summers[:1]:
        summer.along_z()

    def three(c, none):
        rows = pl.ds(pl.multiple_of(c * CHUNK, CHUNK), CHUNK)
        v_now = v[pl.ds(pl.multiple_of(c * CHUNK + HALO, HALO), CHUNK), :]
        total = jnp.zeros((CHUNK, wide), f32)
        for h in range(heads_n):
            gc = gcar[h]
            k3 = gl3[h, rows, :]
            gk = mm_nt(v_now, gc)
            gl = (k3.astype(f32) * (gk - delta[h])).astype(bf16)
            gl3[h, rows, :] = gl
            total = total + mm(k3, gc)
            partT = qk[rows, LANES * h : LANES * h + LANES].astype(f32).T.astype(bf16)
            glandT[h, :HEAD_DIM, :] += mm(partT[:HEAD_DIM, :], gl1[h, rows, :])
            glandT[h, HEAD_DIM:, :] += mm(partT[HEAD_DIM:, :], gl)
        for part in range(CHUNK // TILE):
            i = c * (CHUNK // TILE) + part
            at = pl.ds(pl.multiple_of(i * TILE, TILE), TILE)
            now = tokc[at, 0:1]
            seg_now = seg_of(now)
            near = seg_now == segw[pl.ds(i, 1), :]
            near_back = (seg_now == segw[pl.ds(seq // TILE + i, 1), :]) & (live_of(now) > 0)
            g_window = gopad[pl.ds(pl.multiple_of(i * TILE, TILE), 2 * TILE), :]
            v_window = v[pl.ds(pl.multiple_of(i * TILE, TILE), 2 * TILE), :]
            g_tile = gopad[pl.ds(pl.multiple_of(i * TILE + HALO, HALO), TILE), :].astype(f32)
            conv = jnp.zeros((TILE, wide), f32)
            for h in range(heads_n):
                back = mm(jnp.where(near_back, bands[heads_n + h], 0.0).astype(bf16), g_window)
                conv = jnp.where(lane == h, back, conv)
                mine = jnp.where(lane == h, g_tile, 0.0).astype(bf16)
                gband[h] += jnp.where(near, mm_nt(mine, v_window), 0.0)
            gv[at, :] = (total[part * TILE : (part + 1) * TILE, :] + conv).astype(bf16)
        return none

    lax.fori_loop(0, nchunk, three, 0)

    conv_out[...] = jnp.zeros_like(conv_out)
    for h in range(heads_n):
        conv_out[h : h + 1, :] = diagonal_sums(gband[h])
    piece_v[...] = mm(xT[...], gv[...]).astype(bf16)
    depth = in_v.shape[1] if gather else feat
    sent_v = []
    others = [(dz, dy) for dz in range(4) for dy in range(2) if dz or dy] if gather else []
    for k, (dz, dy) in enumerate(others):
        to = here.dp_at(dz, dy)
        rows = pl.ds(pl.multiple_of(to * depth, 16), depth)
        sent_v.append(start(push(piece_v.at[rows], in_v.at[k], vsem, k, to, here.t)))
        sent_v.append(start(push(conv_out, in_conv.at[k], csem, k, to, here.t)))

    for summer, _ in summers[1:2]:
        summer.along_z()
    for summer, _ in summers[:1]:
        summer.along_x()

    def unstep(r, none):
        i = NEWTON - 1 - r
        for n in range(all_tiles):
            Pm, W = unpack(hist[i, 0, n]), unpack(hist[i, 1, n])
            S, N = unpack(hist[i, 2, n]), unpack(hist[i, 3, n])
            gP, gW = gstate[0, n], gstate[1, n]
            gPl, gWl, Nl = left_of(gP), left_of(gW), left_of(N)
            Pr = right_of(Pm)
            gN = 0.25 * (tt(gPl, Pr) + tt_nt(gWl, right_nt(W)))
            gNl = left_of(gN)
            gS = tt(gNl, right_of(7.0 * ident - Pm))
            gstate[1, n] = 0.25 * tt(Nl, right_of(gW))
            gstate[0, n] = (
                0.25 * tt(Nl, right_of(gP))
                - 15.0 * gN
                - tt(left_of(S), right_of(gN))
                + tt(left_of(gS), Pr)
                + tt(left_of(Pm), right_of(gS))
            )
        return none

    lax.fori_loop(0, NEWTON, unstep, 0)

    for h in range(heads_n):
        sums_land = pltpu.roll(glandT[h].T * scaling, HEAD_DIM, 1)
        k0, q1, _ = landmark_parts(land[:, LANES * h : LANES * h + LANES])
        for g in range(tiles_n):
            n = h * tiles_n + g
            rows = slice(g * TILE, g * TILE + TILE)
            A = Ain[n]
            factor, colsum, tops = newton_start(A)
            gP, gW = gstate[0, n], gstate[1, n]
            GA = tt(left_of(gP + gP.T), right_of(A))
            gA = factor * (GA + gW)
            gf_cols = jnp.sum((0.5 * GA + gW) * A, axis=0, keepdims=True)
            first = iota(colsum.shape, 1) < LANDMARKS
            gcol = jnp.zeros_like(colsum)
            for k in range(2):
                mine = first if k == 0 else jnp.logical_not(first)
                gf = jnp.sum(jnp.where(mine, gf_cols, 0.0), axis=1, keepdims=True)
                top = tops[k]
                is_top = mine & (colsum == top)
                ties = jnp.sum(is_top.astype(f32), axis=1, keepdims=True)
                share = jnp.where(top > 1.0, 1.0, jnp.where(top == 1.0, 0.5, 0.0))
                floor = jnp.maximum(top, 1.0)
                gcol = jnp.where(is_top, -gf * share / (floor * floor * ties), gcol)
            gA = (gA + gcol) * live_cols[g]
            gl2 = A * (gA - jnp.sum(gA * A, axis=1, keepdims=True)) * scaling
            gl2 = jnp.where(same & (live_row[:, rows] > 0), gl2, 0.0)
            g_land = mm3(split(gl2), split(k0[rows])) + mm3(split(gl2.T), split(q1[rows]))
            g_land = (g_land + sums_land[rows]) / counts[rows, :]
            low = slice(2 * nslot + g * TILE, 2 * nslot + g * TILE + TILE)
            wback[h, low, :] = jnp.concatenate(split(g_land), axis=1)
        wback[h, :nslot, :] = jnp.concatenate(split(k0 * scaling), axis=1)
        wback[h, nslot : 2 * nslot, :] = jnp.concatenate(split(q1 * scaling), axis=1)

    for summer, _ in summers[2:3]:
        summer.along_z()
    for summer, _ in summers[1:2]:
        summer.along_x()

    def last(b, k):
        row = pl.multiple_of(b * block + k * CHUNK, CHUNK)
        rows = pl.ds(row, CHUNK)
        hot = (slot_of(tokc[rows, 0:1]) == iota((CHUNK, nslot), 1)).astype(f32).astype(bf16)
        for h in range(heads_n):
            both = (
                mm(gl1[h, rows, :], wback[h, :nslot, :])
                + mm(gl3[h, rows, :], wback[h, nslot : 2 * nslot, :])
                + mm(hot, wback[h, 2 * nslot :, :])
            )
            gqk[rows, LANES * h : LANES * h + LANES] = (both[:, :LANES] + both[:, LANES:]).astype(bf16)
        return mm_nt(gqk[rows, :], wfull[:, : LANES * heads_n]) + mm_nt(
            gv[rows, :], wfull[:, LANES * heads_n :]
        )

    def chunk_rows(k):
        return pl.ds(k * CHUNK, CHUNK)

    from_sibling, from_across, own_from_sibling = [], [], []
    for k in range(per_block):
        part_out[0, chunk_rows(k), :] = last(here.diagonal, k).astype(bf16)
        from_sibling.append(
            start(push(part_out.at[0, chunk_rows(k)], part_in.at[0, chunk_rows(k)], psem, k, here.dp, here.sibling))
        )
    for k in range(per_block):
        got = last(here.across, k)
        from_sibling[k].wait_recv()
        part_sum[chunk_rows(k), :] = (got + part_in[0, chunk_rows(k), :].astype(f32)).astype(bf16)
        from_across.append(
            start(push(part_sum.at[chunk_rows(k)], part_x.at[chunk_rows(k)], psem, per_block + k, here.dp, here.across))
        )
    for k in range(per_block):
        part_out[1, chunk_rows(k), :] = last(here.sibling, k).astype(bf16)
        own_from_sibling.append(
            start(push(part_out.at[1, chunk_rows(k)], part_in.at[1, chunk_rows(k)], psem, 2 * per_block + k, here.dp, here.sibling))
        )
    for k in range(per_block):
        input_grad[chunk_rows(k), :] = last(here.t, k) + gpre[chunk_rows(k), :]

    piece_q[...] = mm(xT[...], gqk[...]).astype(bf16)
    sent_q = []
    for k, (dz, dy) in enumerate(others):
        to = here.dp_at(dz, dy)
        rows = pl.ds(pl.multiple_of(to * depth, 16), depth)
        sent_q.append(start(push(piece_q.at[rows], in_q.at[k], vsem, len(others) + k, to, here.t)))
    for summer, _ in summers[3:]:
        summer.along_z()
    for summer, _ in summers[2:3]:
        summer.along_x()
    for k in range(per_block):
        own_from_sibling[k].wait_recv()
        from_across[k].wait_recv()
        input_grad[chunk_rows(k), :] += part_in[1, chunk_rows(k), :].astype(f32) + part_x[
            chunk_rows(k), :
        ].astype(f32)
    for copy in sent_v + sent_q:
        copy.wait_recv()
    if gather:
        rows = pl.ds(pl.multiple_of(here.dp * depth, 16), depth)
        total_v = piece_v[rows, :].astype(f32)
        total_q = piece_q[rows, :].astype(f32)
        total_conv = conv_out[...]
        for k in range(len(others)):
            total_v = total_v + in_v[k].astype(f32)
            total_q = total_q + in_q[k].astype(f32)
            total_conv = total_conv + in_conv[k]
        gw[:, : LANES * heads_n] = total_q
        gw[:, LANES * heads_n :] = total_v
        gconv[...] = total_conv
    else:
        gw[:, : LANES * heads_n] = piece_q[...].astype(f32)
        gw[:, LANES * heads_n :] = piece_v[...].astype(f32)
        gconv[...] = conv_out[...]
    for summer, _ in summers[3:]:
        summer.along_x()
    for summer, out in summers:
        summer.finish(out)
    for copy in copies:
        copy.wait_send()


def attention_backward(gsend, xall, wfull, tokc, segw, qk, v, kern1, kern3, land, counts, weights,
                       mixed, carried, taps, slot_live, gpre, sources, shares, gather, depth):
    blocks, block, wide = gsend.shape
    heads_n, seq, nslot = kern1.shape
    feat = wfull.shape[0]
    all_tiles = weights.shape[0]
    shape = jax.ShapeDtypeStruct
    outs = (
        shape((block, feat), f32),
        shape((depth, wfull.shape[1]), f32),
        shape((8, 2 * TILE), f32),
    ) + tuple(shape(s.shape[4:], f32) for s in sources)
    others = 7 if gather else 1
    per_block = block // CHUNK
    scratch = [
        pltpu.VMEM((heads_n, seq, nslot), bf16),
        pltpu.VMEM((heads_n, seq, nslot), bf16),
        pltpu.VMEM(xall.shape, bf16),
        pltpu.VMEM((feat, seq), bf16),
        pltpu.VMEM((seq + 2 * HALO, wide), bf16),
        pltpu.VMEM((seq, LANES * heads_n), bf16),
        pltpu.VMEM((seq, wide), bf16),
        pltpu.VMEM((heads_n, TILE, 2 * TILE), f32),
        pltpu.VMEM((2 * heads_n, TILE, 2 * TILE), f32),
        pltpu.VMEM((wide, nslot), f32),
        pltpu.VMEM((heads_n, LANES, nslot), f32),
        pltpu.VMEM((NEWTON + 1, 4, all_tiles, LANDMARKS, TILE), f32),
        pltpu.VMEM((2, all_tiles, TILE, TILE), f32),
        pltpu.VMEM((heads_n, nslot, wide), bf16),
        pltpu.VMEM((heads_n, 3 * nslot, 256), bf16),
        pltpu.VMEM((2, block, feat), bf16),
        pltpu.VMEM((2, block, feat), bf16),
        pltpu.VMEM((block, feat), bf16),
        pltpu.VMEM((block, feat), bf16),
        pltpu.VMEM((feat, wide), bf16),
        pltpu.VMEM((feat, LANES * heads_n), bf16),
        pltpu.VMEM((others, depth if gather else 16, wide), bf16),
        pltpu.VMEM((others, depth if gather else 16, LANES * heads_n), bf16),
        pltpu.VMEM((others, 8, 2 * TILE), f32),
        pltpu.VMEM((8, 2 * TILE), f32),
        dma(2, 3),
        dma(3),
        dma(2, 3 * per_block),
        dma(2, 2 * others),
        dma(2, others),
    ]
    for source, share in zip(sources, shares):
        lanes, kind = source.shape[-1], source.dtype
        for _, count in share:
            scratch += [
                pltpu.VMEM((4, 2, 2, count, lanes), kind),
                pltpu.VMEM((4, 2, 2, count, lanes), kind),
                pltpu.VMEM((4, 2, count, lanes), kind),
                pltpu.VMEM((3, 2, count, lanes), kind),
                pltpu.VMEM((count, lanes), kind),
                dma(2, SUMMER_SEMS),
                pltpu.SemaphoreType.DMA,
            ]
    specs = [VMEM, ANY] + [VMEM] * 5 + [ANY, ANY] + [VMEM] * 8 + [ANY] * len(sources)
    return pl.pallas_call(
        functools.partial(backward_body, gather, shares),
        out_shape=outs,
        in_specs=specs,
        out_specs=tuple([VMEM] * len(outs)),
        scratch_shapes=scratch,
        compiler_params=pltpu.CompilerParams(
            vmem_limit_bytes=LIMIT, collective_id=3 if gather else 4, has_side_effects=True
        ),
        cost_estimate=pl.CostEstimate(flops=3 * 10**10, bytes_accessed=5 * 10**7, transcendentals=10**6),
        name="attention_backward",
    )(gsend, xall, wfull, tokc, segw, qk, v, kern1, kern3, land, counts, weights, mixed, carried,
      taps, slot_live, gpre, *sources)


def layer_norm(values, gain_row, bias_row):
    average = jnp.mean(values, axis=-1, keepdims=True)
    centered = values - average
    variance = jnp.mean(centered * centered, axis=-1, keepdims=True)
    return centered * lax.rsqrt(variance + norm_epsilon) * gain_row + bias_row


def split_up(shard, dim, length):
    before, after = (shard.shape[:dim], shard.shape[dim + 1 :])
    return jnp.moveaxis(shard.reshape(*before, length, -1, *after), dim, 0)


def exchange(pieces, axis):
    return lax.all_to_all(pieces, axis, split_axis=0, concat_axis=0, tiled=True)


def per_device(
    tokens,
    w_qkv,
    w_out,
    conv_weight,
    w_up,
    w_down,
    norm_gain,
    norm_bias,
    cotangent,
    seg_ids,
    landmark_slot,
    token_live,
    slot_live,
):
    both = ("dp", "tensor")
    dp_size, blocks = lax.axis_size("dp"), lax.axis_size("tensor")
    devices = dp_size * blocks
    heads_n, taps_total = conv_weight.shape
    block, feat = tokens.shape
    depth = w_qkv.shape[1]
    width = heads_n * HEAD_DIM
    wide = -(-width // 256) * 256
    hidden_n = w_up.shape[1]
    docs = slot_live.shape[1] // LANDMARKS
    direct = dp_size == 8 and blocks == 4 and depth % 16 == 0 and hidden_n % 32 == 0

    norms = jnp.concatenate([norm_gain, norm_bias])
    norm_row = jnp.pad(norms.reshape(1, -1), ((0, 15), (0, width - norms.size)))
    out_rows = jnp.concatenate([w_out.T, norm_row])
    up_all = lax.all_gather(w_up.T, both, axis=0, tiled=True)
    down_all = lax.all_gather(w_down, both, axis=0, tiled=True)
    out_all = lax.all_gather(out_rows, both, axis=0, tiled=False)
    norms_all = out_all[:, depth, : norms.size].reshape(devices, 4, -1)
    norms_all = jnp.swapaxes(norms_all, 0, 1).reshape(4, feat).astype(f32)
    out_all = out_all[:, :depth].reshape(dp_size, blocks, depth, width)
    taps = jnp.pad(
        jnp.concatenate([conv_weight, conv_weight[:, ::-1]]),
        ((0, 8 - 2 * heads_n), (HALO - taps_total // 2, 2 * TILE - taps_total - HALO + taps_total // 2)),
    )
    weight = w_qkv if direct else lax.all_gather(w_qkv, "dp", axis=1, tiled=True)
    (
        xall, wfull, tokc, segw, qk, v, kern1, kern3, land, counts, weights, mixed, carried, heads, prox,
    ) = attention_forward(
        tokens, weight, taps, seg_ids, landmark_slot, token_live, slot_live,
        heads_n, blocks, depth, taps_total,
    )
    proxies = prox[:, 0].reshape(heads_n, docs).T[None]
    heads = heads[:, :, :width]
    attention = jnp.einsum(
        "tsk,ptdk->spd", heads, out_all, preferred_element_type=f32
    ).reshape(block, feat)
    gains, biases = norms_all[:2], norms_all[2:]
    hidden, norm_one_pull = jax.vjp(layer_norm, tokens.astype(f32) + attention, gains[0], biases[0])
    hidden_low = hidden.astype(bf16)
    up_proj = jnp.einsum("td,fd->tf", hidden_low, up_all, preferred_element_type=f32)
    activated, gelu_pull = jax.vjp(lambda inputs: jax.nn.gelu(inputs, approximate=False), up_proj)
    activated_low = activated.astype(bf16)
    down_proj = jnp.dot(activated_low, down_all, preferred_element_type=f32)
    result, norm_two_pull = jax.vjp(layer_norm, hidden + down_proj, gains[1], biases[1])
    layer_out = result.astype(bf16)
    grad_sum, gain_two, bias_two = norm_two_pull(cotangent.astype(f32))
    grad_sum_low = grad_sum.astype(bf16)
    grad_down = jnp.einsum("tf,td->fd", activated_low, grad_sum_low, preferred_element_type=f32)
    grad_act = jnp.einsum("td,fd->tf", grad_sum_low, down_all, preferred_element_type=f32)
    grad_up_low = gelu_pull(grad_act)[0].astype(bf16)
    grad_up = jnp.einsum("tf,td->fd", grad_up_low, hidden_low, preferred_element_type=f32)
    grad_hidden = grad_sum + jnp.dot(grad_up_low, up_all, preferred_element_type=f32)
    grad_pre, gain_one, bias_one = norm_one_pull(grad_hidden)
    grad_attn_low = grad_pre.astype(bf16)
    norm_grads = jnp.stack([gain_one, gain_two, bias_one, bias_two])
    grad_out = jnp.einsum("sd,tsk->dtk", grad_attn_low, heads, preferred_element_type=f32)
    grad_heads = jnp.einsum(
        "spd,ptdk->tsk",
        grad_attn_low.reshape(block, dp_size, depth),
        out_all,
        preferred_element_type=f32,
    ).astype(bf16)
    live_here = lax.dynamic_slice_in_dim(token_live[0], lax.axis_index("tensor") * block, block)
    gsend = jnp.pad(
        grad_heads * live_here.astype(bf16)[None, :, None], ((0, 0), (0, 0), (0, wide - width))
    )
    up_pieces = grad_up.astype(bf16)
    down_pieces = grad_down.astype(bf16)
    out_pieces = jnp.swapaxes(
        grad_out.astype(bf16).reshape(dp_size, depth, blocks, width), 1, 2
    ).reshape(devices, depth, width)
    norm_pieces = split_up(norm_grads, 1, devices)
    sources, shares = [], ()
    if direct:
        owners = (4, 2, 2, 2)
        sources = [
            up_pieces.reshape(owners + (hidden_n, feat)),
            down_pieces.reshape(owners + (hidden_n, feat)),
            jnp.pad(out_pieces, ((0, 0), (0, 0), (0, wide - width))).reshape(owners + (depth, wide)),
            jnp.pad(norm_pieces, ((0, 0), (0, 4), (0, LANES - norm_pieces.shape[2]))).reshape(
                owners + (8, LANES)
            ),
        ]
        share = tuple((k * (hidden_n // 2), hidden_n // 2) for k in range(2))
        shares = (share, share, ((0, depth),), ((0, 8),))
    got = attention_backward(
        gsend, xall, wfull, tokc, segw, qk, v, kern1, kern3, land, counts, weights,
        mixed, carried, taps, slot_live, grad_pre, sources, shares, direct,
        depth if direct else feat,
    )
    input_grad, grad_w, grad_conv = got[:3]
    if direct:
        grad_up, grad_down, grad_out, norm_sum = got[3:]
        grad_out, norm_sum = grad_out[:, :width], norm_sum[:4, : norm_gain.shape[1]]
    else:
        grad_w = exchange(grad_w.astype(bf16).reshape(dp_size, depth, -1), "dp").astype(f32).sum(axis=0)
        grad_conv = lax.psum(grad_conv, "dp")
        grad_up = lax.psum_scatter(up_pieces, both, scatter_dimension=0, tiled=True).astype(f32)
        grad_down = lax.psum_scatter(down_pieces, both, scatter_dimension=0, tiled=True).astype(f32)
        grad_out = lax.psum_scatter(out_pieces, both, scatter_dimension=0, tiled=False).astype(f32)
        norm_sum = exchange(norm_pieces, both).sum(axis=0)
    pairs = grad_w[:, : LANES * heads_n].reshape(depth, heads_n, 2, HEAD_DIM)
    grad_qkv = jnp.concatenate(
        [
            jnp.moveaxis(pairs, 2, 0).reshape(2, depth, width),
            grad_w[None, :, LANES * heads_n : LANES * heads_n + width],
        ]
    )
    first = HALO - taps_total // 2
    return (
        layer_out,
        input_grad,
        grad_qkv,
        grad_out.T,
        grad_conv[:heads_n, first : first + taps_total],
        grad_up.T,
        grad_down,
        norm_sum[:2],
        norm_sum[2:],
        proxies,
    )


def solution(mesh):
    return jax.shard_map(
        per_device,
        mesh=mesh,
        in_specs=(
            P(("dp", "tensor"), None),
            P(None, "dp", "tensor"),
            P("tensor", "dp"),
            P("tensor", None),
            P(None, ("dp", "tensor")),
            P(("dp", "tensor"), None),
            P(None, ("dp", "tensor")),
            P(None, ("dp", "tensor")),
            P(("dp", "tensor"), None),
            P("dp", None),
            P("dp", None),
            P("dp", None),
            P("dp", None),
        ),
        out_specs=(
            P(("dp", "tensor"), None),
            P(("dp", "tensor"), None),
            P(None, "dp", "tensor"),
            P("tensor", "dp"),
            P("tensor", None),
            P(None, ("dp", "tensor")),
            P(("dp", "tensor"), None),
            P(None, ("dp", "tensor")),
            P(None, ("dp", "tensor")),
            P("dp", None, "tensor"),
        ),
        check_vma=False,
    )
```

```python
import functools
import math

import jax
import jax.numpy as jnp
from jax import lax
from jax.experimental import pallas as pl
from jax.experimental.pallas import tpu as pltpu
from jax.sharding import PartitionSpec as P

HEAD_DIM = 64
LANDMARKS = 64
NEWTON = 6
TILE = 128
HALO = TILE // 2
CHUNK = 256
LANES = 128
bf16 = jnp.bfloat16
f32 = jnp.float32
i32 = jnp.int32
norm_epsilon = 1e-05
MESH = pl.DeviceIdType.MESH
LIMIT = 62 * 2**20


def mm(a, b):
    return lax.dot_general(a, b, (((1,), (0,)), ((), ())), preferred_element_type=f32)


def mm_nt(a, b):
    return lax.dot_general(a, b, (((1,), (1,)), ((), ())), preferred_element_type=f32)


def split(a):
    high = a.astype(bf16)
    return high, (a - high.astype(f32)).astype(bf16)


def mm3(a, b, dot=mm):
    return dot(a[0], b[0]) + (dot(a[0], b[1]) + dot(a[1], b[0]))


def left_of(a):
    return jnp.concatenate(split(a), axis=1)


def right_of(b):
    high, low = split(b)
    top = jnp.concatenate([high, low], axis=1)
    bottom = jnp.concatenate([jnp.zeros_like(high), high], axis=1)
    return jnp.concatenate([top, bottom], axis=0)


def right_nt(b):
    high, low = split(b)
    top = jnp.concatenate([high, jnp.zeros_like(high)], axis=1)
    bottom = jnp.concatenate([low, high], axis=1)
    return jnp.concatenate([top, bottom], axis=0)


def tt(left, right):
    both = mm(left, right)
    return both[:, :TILE] + both[:, TILE:]


def tt_nt(left, right):
    both = mm_nt(left, right)
    return both[:, :TILE] + both[:, TILE:]


def iota(shape, dim):
    return lax.broadcasted_iota(i32, shape, dim)


def tile_same():
    shape = (TILE, TILE)
    return iota(shape, 0) // LANDMARKS == iota(shape, 1) // LANDMARKS


def tile_eye():
    shape = (TILE, TILE)
    return (iota(shape, 0) == iota(shape, 1)).astype(f32)


def pack(tile):
    return tile[:LANDMARKS] + tile[LANDMARKS:]


def unpack(packed):
    first = iota(packed.shape, 1) < LANDMARKS
    return jnp.concatenate([jnp.where(first, packed, 0.0), jnp.where(first, 0.0, packed)], axis=0)


def landmark_parts(land):
    first = iota(land.shape, 1) < HEAD_DIM
    turned = pltpu.roll(land, HEAD_DIM, 1)
    return jnp.where(first, turned, 0.0), jnp.where(first, 0.0, turned), jnp.where(first, land, 0.0)


def newton_step(Pm, W, ident):
    Pr = right_of(Pm)
    S = tt(left_of(Pm), Pr)
    N = 13.0 * ident - 15.0 * Pm + tt(left_of(S), right_of(7.0 * ident - Pm))
    Nl = left_of(N)
    return S, N, 0.25 * tt(Nl, Pr), 0.25 * tt(Nl, right_of(W))


def newton_start(A):
    colsum = jnp.sum(A, axis=0, keepdims=True)
    first = iota(colsum.shape, 1) < LANDMARKS
    tops = [
        jnp.max(jnp.where(first, colsum, 0.0), axis=1, keepdims=True),
        jnp.max(jnp.where(first, 0.0, colsum), axis=1, keepdims=True),
    ]
    factor = 1.0 / jnp.maximum(jnp.where(first, tops[0], tops[1]), 1.0)
    return factor, colsum, tops


def column(row):
    return jnp.broadcast_to(row, (LANES, LANES)).T


def band_from(row):
    wide = jnp.broadcast_to(row, (TILE, 2 * TILE))
    return pltpu.roll(wide, 0, 1, stride=1, stride_axis=0)


def diagonal_sums(band):
    where = iota(band.shape, 0)
    step = 1
    while step < TILE:
        turned = pltpu.roll(band, 2 * TILE - step, 1)
        band = jnp.where((where // step) % 2 == 1, turned, band)
        step *= 2
    return jnp.sum(band, axis=0, keepdims=True)


def seg_of(code):
    return (code // 512) % 8


def live_of(code):
    return code // 4096


def slot_of(code):
    return code % 512


class Place:
    def __init__(self):
        self.dp = lax.axis_index("dp")
        self.t = lax.axis_index("tensor")
        self.x = self.t // 2
        self.c = self.t % 2
        self.sibling = self.x * 2 + 1 - self.c
        self.across = (1 - self.x) * 2 + self.c
        self.diagonal = (1 - self.x) * 2 + 1 - self.c
        self.z = self.dp // 2
        self.y = self.dp % 2

    def tensor_peers(self):
        return [(self.dp, t) for t in (self.sibling, self.across, self.diagonal)]

    def dp_at(self, turn_z, turn_y):
        return ((self.z + turn_z) % 4) * 2 + (self.y + turn_y) % 2


def greet(peers):
    barrier = pltpu.get_barrier_semaphore()
    for peer in peers:
        pl.semaphore_signal(barrier, inc=1, device_id=peer, device_id_type=MESH)
    pl.semaphore_wait(barrier, len(peers))


def push(src, dst, sems, index, dp, t):
    return pltpu.make_async_remote_copy(
        src_ref=src,
        dst_ref=dst,
        send_sem=sems.at[0, index],
        recv_sem=sems.at[1, index],
        device_id=(dp, t),
        device_id_type=MESH,
    )


class Spreader:
    def __init__(self, here, shard, whole, sems, local, by_rows=False):
        self.here, self.shard, self.whole, self.sems, self.local = here, shard, whole, sems, local
        self.by_rows = by_rows
        self.copies = []

    def at(self, z, y, x):
        c = self.here.c
        if not self.by_rows:
            return self.whole.at[z, y, x, c]
        depth = self.shard.shape[0]
        rows = pl.ds(pl.multiple_of((z * 2 + y) * depth, 16), depth)
        return self.whole.at[x, c, rows]

    def pair(self, z, y):
        return self.at(z, y, slice(None))

    def push(self, src, dst, index, dp, t):
        copy = push(src, dst, self.sems, index, dp, t)
        copy.start()
        self.copies.append(copy)
        return copy

    def pass_on(self, ref, index, dp, t):
        return self.push(ref, ref, index, dp, t)

    def begin(self):
        here = self.here
        mine = self.at(here.z, here.y, here.x)
        self.kept = pltpu.make_async_copy(self.shard, mine, self.local)
        self.kept.start()
        self.first = self.push(self.shard, mine, 0, here.dp, here.across)

    def along_z(self):
        here = self.here
        self.kept.wait()
        self.first.wait_recv()
        mine = self.pair(here.z, here.y)
        self.from_z = [
            self.pass_on(mine, dz, here.dp_at(dz, 0), here.t) for dz in (1, 2, 3)
        ]
        self.from_y = [self.pass_on(mine, 4, here.dp_at(0, 1), here.t)]
        self.from_core = [self.pass_on(mine, 5, here.dp, here.sibling)]

    def along_y(self, dz):
        here = self.here
        self.from_z[dz - 1].wait_recv()
        got = self.pair((here.z + 4 - dz) % 4, here.y)
        self.from_y.append(self.pass_on(got, 5 + dz, here.dp_at(0, 1), here.t))
        self.from_core.append(self.pass_on(got, 8 + dz, here.dp, here.sibling))

    def to_core(self, dz):
        here = self.here
        self.from_y[dz].wait_recv()
        got = self.pair((here.z + 4 - dz) % 4, 1 - here.y)
        self.from_core.append(self.pass_on(got, 12 + dz, here.dp, here.sibling))

    def finish(self):
        for copy in self.from_core:
            copy.wait_recv()
        for copy in self.copies:
            copy.wait_send()


class SpreaderX(Spreader):
    def begin(self):
        here = self.here
        mine = self.at(here.z, here.y, here.x)
        self.kept = pltpu.make_async_copy(self.shard, mine, self.local)
        self.kept.start()
        self.from_z = [
            self.push(self.shard, mine, dz, here.dp_at(dz, 0), here.t) for dz in (1, 2, 3)
        ]
        self.from_y = [self.push(self.shard, mine, 4, here.dp_at(0, 1), here.t)]
        self.from_x = []

    def own_x(self):
        here = self.here
        mine = self.at(here.z, here.y, here.x)
        self.from_x.append(self.push(self.shard, mine, 0, here.dp, here.across))

    def along_y(self, dz):
        here = self.here
        self.from_z[dz - 1].wait_recv()
        got = self.at((here.z + 4 - dz) % 4, here.y, here.x)
        self.from_y.append(self.pass_on(got, 4 + dz, here.dp_at(0, 1), here.t))
        self.from_x.append(self.pass_on(got, 7 + dz, here.dp, here.across))

    def along_x(self, dz):
        here = self.here
        self.from_y[dz].wait_recv()
        got = self.at((here.z + 4 - dz) % 4, 1 - here.y, here.x)
        self.from_x.append(self.pass_on(got, 11 + dz, here.dp, here.across))

    def to_core(self):
        here = self.here
        self.kept.wait()
        near = self.whole.at[:, :, here.x, here.c]
        self.from_core = [self.pass_on(near, 15, here.dp, here.sibling)]

    def to_core_last(self):
        here = self.here
        for copy in self.from_x:
            copy.wait_recv()
        far = self.whole.at[:, :, 1 - here.x, here.c]
        self.from_core.append(self.pass_on(far, 16, here.dp, here.sibling))


def spread_lanes(length, whole):
    shape = (LANES, whole)
    return (iota(shape, 0) == iota(shape, 1) % length).astype(f32)


def forward_body(gather, taps_total, *refs):
    (x, w, taps, seg, slot, live, slot_live), refs = refs[:7], refs[7:]
    if gather:
        (w_up, w_down, w_out, gain, bias), refs = refs[:5], refs[5:]
    (
        xall, wfull, tokc, segw, qk, v, kern1, kern3, land, counts, Aout, mixed, carried, heads, prox,
    ) = refs[:15]
    refs = refs[15:]
    if gather:
        (up_all, down_all, out_all, norms), refs = refs[:4], refs[4:]
    wsh, wlog, l3, carriedT, state, bands, hsend, segp, xsem, wsem, hsem = refs[:11]
    refs = refs[11:]
    here = Place()
    block = x.shape[0]
    blocks = xall.shape[0]
    seq = block * blocks
    heads_n = qk.shape[1] // LANES
    nslot = land.shape[0]
    wide = v.shape[1]
    nchunk = seq // CHUNK
    per_block = block // CHUNK
    tiles_n = nslot // TILE
    width = heads_n * HEAD_DIM
    scaling = 1.0 / math.sqrt(HEAD_DIM)

    depth = w.shape[1]
    parts = []
    for h in range(heads_n):
        e = slice(HEAD_DIM * h, HEAD_DIM * h + HEAD_DIM)
        parts += [w[0, :, e], w[1, :, e]]
    parts += [w[2], jnp.zeros((depth, wide - width), bf16)]
    wsh[...] = jnp.concatenate(parts, axis=1)

    peers = here.tensor_peers()
    if gather:
        peers = peers + [(here.dp_at(dz, 0), here.t) for dz in (1, 2, 3)] + [(here.dp_at(0, 1), here.t)]
        up_sh, out_sh, norm_sh, norm_all = refs[:4]
        up_sh[...] = w_up[...].astype(f32).T.astype(bf16)
        out_sh[...] = jnp.concatenate(
            [w_out[...].astype(f32).T, jnp.zeros((depth, wide - width), f32)], axis=1
        ).astype(bf16)
        norm_sh[...] = jnp.zeros_like(norm_sh)
        norm_sh[0:2, : gain.shape[1]] = gain[...].astype(f32)
        norm_sh[2:4, : gain.shape[1]] = bias[...].astype(f32)
        sems = refs[4:]
        spread_up = Spreader(here, up_sh, up_all, sems[0], sems[1])
        spread_out = Spreader(here, out_sh, out_all, sems[2], sems[3], by_rows=True)
        spread_norm = Spreader(here, norm_sh, norm_all, sems[4], sems[5])
        spread_down = SpreaderX(here, w_down, down_all, sems[6], sems[7])
        spreads = (spread_up, spread_out, spread_norm)
    greet(peers)

    copies = []
    pieces = block // TILE

    def start(copy):
        copy.start()
        copies.append(copy)
        return copy

    crossing = [
        start(push(x.at[pl.ds(p * TILE, TILE)], xall.at[here.t, pl.ds(p * TILE, TILE)], xsem, p, here.dp, here.across))
        for p in range(pieces)
    ]
    beside = start(push(x, xall.at[here.t], xsem, pieces, here.dp, here.sibling))
    if gather:
        mine = wfull.at[pl.ds(pl.multiple_of(here.dp * depth, 16), depth)]
        along = [start(push(wsh, mine, wsem, dz, here.dp_at(dz, 0), here.t)) for dz in (1, 2, 3)]
        along = [start(push(wsh, mine, wsem, 0, here.dp_at(0, 1), here.t))] + along
        wfull[pl.ds(pl.multiple_of(here.dp * depth, 16), depth), :] = wsh[...]
    else:
        wfull[...] = wsh[...]
    xall[here.t] = x[...]

    segp[...] = jnp.full(segp.shape, -1, i32)
    segp[0:1, TILE : TILE + seq] = jnp.where(live[...] > 0, seg[...], -1)
    segp[1:2, TILE : TILE + seq] = seg[...]
    code = (slot[...] + 512 * seg[...] + 4096 * live[...]).astype(f32)
    for i in range(seq // TILE):
        lanes = slice(i * TILE, i * TILE + TILE)
        tokc[lanes, :] = column(code[:, lanes]).astype(i32)
        near = pltpu.roll(segp[:, i * TILE : i * TILE + 3 * TILE], 3 * TILE - HALO, 1)
        segw[i : i + 1, :] = near[0:1, : 2 * TILE]
        segw[seq // TILE + i : seq // TILE + i + 1, :] = near[1:2, : 2 * TILE]
    for h in range(heads_n):
        bands[h] = band_from(taps[h : h + 1, :])
    doc_row = iota((1, nslot), 1) // LANDMARKS
    live_row = slot_live[...]
    live_cols = [column(live_row[:, g * TILE : (g + 1) * TILE].astype(f32)) for g in range(tiles_n)]
    v[0:HALO, :] = jnp.zeros((HALO, wide), bf16)
    v[seq + HALO : seq + 2 * HALO, :] = jnp.zeros((HALO, wide), bf16)

    if gather:
        for spread in spreads:
            spread.begin()
        along[0].wait_recv()
        for dz in (1, 2, 3):
            along[dz].wait_recv()
            got = wfull.at[pl.ds(pl.multiple_of(here.dp_at(4 - dz, 0) * depth, 16), depth)]
            along.append(start(push(got, got, wsem, 3 + dz, here.dp_at(0, 1), here.t)))
        spread_down.begin()
        for spread in spreads:
            spread.along_z()
        for dz in (1, 2, 3):
            along[3 + dz].wait_recv()

    def project(b, carry):
        def one(i, carry):
            acc, cnt = carry
            c = b * per_block + i
            rows = pl.ds(pl.multiple_of(c * CHUNK, CHUNK), CHUNK)
            out = mm(xall[b, pl.ds(pl.multiple_of(i * CHUNK, CHUNK), CHUNK), :], wfull[...])
            qk_now = out[:, : LANES * heads_n].astype(bf16)
            qk[rows, :] = qk_now
            v[pl.ds(pl.multiple_of(c * CHUNK + HALO, HALO), CHUNK), :] = out[:, LANES * heads_n :].astype(bf16)
            slot_now = slot[:, pl.ds(pl.multiple_of(c * CHUNK, CHUNK), CHUNK)]
            hot = (slot_now == iota((nslot, CHUNK), 0)).astype(f32)
            return acc + mm(hot.astype(bf16), qk_now), cnt + jnp.sum(hot, axis=1, keepdims=True)

        return lax.fori_loop(0, per_block, one, carry)

    carry = (jnp.zeros((nslot, LANES * heads_n), f32), jnp.zeros((nslot, 1), f32))
    carry = project(here.t, carry)
    beside.wait_recv()
    carry = project(here.sibling, carry)
    passed = []
    for p in range(pieces):
        crossing[p].wait_recv()
        got = xall.at[here.across, pl.ds(p * TILE, TILE)]
        passed.append(start(push(got, got, xsem, pieces + 1 + p, here.dp, here.sibling)))
    carry = project(here.across, carry)
    if gather:
        spread_down.own_x()
    for p in range(pieces):
        passed[p].wait_recv()
    acc, cnt = project(here.diagonal, carry)
    cnt = jnp.maximum(cnt, 1.0)
    counts[...] = jnp.broadcast_to(cnt, counts.shape)
    land[...] = acc / cnt

    if gather:
        for dz in (1, 2, 3):
            spread_down.along_y(dz)

    same = tile_same()
    ident = tile_eye()
    for h in range(heads_n):
        k0, q1, q0 = landmark_parts(land[:, LANES * h : LANES * h + LANES])
        wlog[h] = jnp.concatenate(split(jnp.concatenate([k0, q1], axis=0) * scaling), axis=1)
        for g in range(tiles_n):
            rows = slice(g * TILE, g * TILE + TILE)
            logit = tt_nt(left_of(q0[rows] * scaling), right_nt(k0[rows]))
            filled = jnp.where(same & (live_row[:, rows] > 0), logit, -1e9)
            raised = jnp.exp(filled - jnp.max(filled, axis=1, keepdims=True))
            A = raised / jnp.sum(raised, axis=1, keepdims=True) * live_cols[g]
            n = h * tiles_n + g
            Aout[n] = A
            factor, _, _ = newton_start(A)
            W = A * factor
            state[0, n] = tt_nt(left_of(A), right_nt(W))
            state[1, n] = W

    def step(i, none):
        for n in range(heads_n * tiles_n):
            _, _, Pm, W = newton_step(state[0, n], state[1, n], ident)
            state[0, n] = Pm
            state[1, n] = W
        return none

    lax.fori_loop(0, NEWTON, step, 0)
    if gather:
        for dz in (1, 2, 3):
            for spread in spreads:
                spread.along_y(dz)
        spread_down.along_x(0)

    def logits(c, top):
        rows = pl.ds(pl.multiple_of(c * CHUNK, CHUNK), CHUNK)
        now = tokc[rows, 0:1]
        allowed = (seg_of(now) == doc_row) & (live_row > 0)
        alive = allowed & (live_of(now) > 0)
        tops = []
        for h in range(heads_n):
            part = qk[rows, LANES * h : LANES * h + LANES]
            both = mm_nt(jnp.concatenate([part, part], axis=1), wlog[h])
            one = jnp.where(allowed, both[:, :nslot], -1e9)
            raised = jnp.exp(one - jnp.max(one, axis=1, keepdims=True))
            kern1[h, rows, :] = (raised / jnp.sum(raised, axis=1, keepdims=True)).astype(bf16)
            three = jnp.where(alive, both[:, nslot:], -1e9)
            l3[h, rows, :] = three
            tops.append(jnp.maximum(top[h], jnp.max(three, axis=0, keepdims=True)))
        return tuple(tops)

    top = lax.fori_loop(
        0, nchunk, logits, tuple(jnp.full((1, nslot), -1e9, f32) for _ in range(heads_n))
    )

    if gather:
        for dz in (1, 2, 3):
            spread_down.along_x(dz)
        for spread in spreads:
            spread.to_core(0)

    def raise_three(c, total):
        rows = pl.ds(pl.multiple_of(c * CHUNK, CHUNK), CHUNK)
        totals = []
        for h in range(heads_n):
            raised = jnp.exp(l3[h, rows, :] - top[h])
            l3[h, rows, :] = raised
            totals.append(total[h] + jnp.sum(raised, axis=0, keepdims=True))
        return tuple(totals)

    total = lax.fori_loop(
        0, nchunk, raise_three, tuple(jnp.zeros((1, nslot), f32) for _ in range(heads_n))
    )
    norm = [live_row.astype(f32) / total[h] for h in range(heads_n)]
    carriedT[...] = jnp.zeros_like(carriedT)

    def carry_three(c, none):
        rows = pl.ds(pl.multiple_of(c * CHUNK, CHUNK), CHUNK)
        vT = v[pl.ds(pl.multiple_of(c * CHUNK + HALO, HALO), CHUNK), :].astype(f32).T.astype(bf16)
        for h in range(heads_n):
            low = (l3[h, rows, :] * norm[h]).astype(bf16)
            kern3[h, rows, :] = low
            e = slice(HEAD_DIM * h, HEAD_DIM * h + HEAD_DIM)
            carriedT[e, :] += mm(vT[e, :], low)
        return none

    lax.fori_loop(0, nchunk, carry_three, 0)
    if gather:
        spread_down.to_core()
        for spread in spreads:
            spread.to_core(1)
    carried_all = carriedT[...].T
    carried[...] = carried_all
    lane = iota((TILE, wide), 1) // HEAD_DIM
    docs = nslot // LANDMARKS
    prox_all = jnp.zeros((8, LANES), f32)
    for h in range(heads_n):
        for g in range(tiles_n):
            rows = slice(g * TILE, g * TILE + TILE)
            n = h * tiles_n + g
            W = state[1, n]
            part = split(jnp.where(lane == h, carried_all[rows], 0.0))
            mixed[h, rows, :] = mm3(split(W.T), part).astype(bf16)
            A = Aout[n]
            A2 = jnp.sum(A * A, axis=0, keepdims=True)
            W2 = jnp.sum(W * W, axis=0, keepdims=True)
            first = iota(A2.shape, 1) < LANDMARKS
            for half in range(2):
                mine = first if half == 0 else jnp.logical_not(first)
                a2 = jnp.sum(jnp.where(mine, A2, 0.0), axis=1, keepdims=True)
                z2 = jnp.sum(jnp.where(mine, W2, 0.0), axis=1, keepdims=True)
                doc = g * 2 + half
                alive = live_row[:, doc * LANDMARKS : doc * LANDMARKS + 1] > 0
                value = jnp.where(alive, jnp.sqrt(a2) * jnp.sqrt(z2) / LANDMARKS, 0.0)
                here_too = (iota(prox_all.shape, 0) == doc) & (iota(prox_all.shape, 1) == h)
                prox_all = jnp.where(here_too, value, prox_all)
    prox[0] = prox_all[:docs, :heads_n]

    def finish(b, out, out_row):
        def one(k, none):
            c = b * per_block + k
            rows = pl.ds(pl.multiple_of(c * CHUNK, CHUNK), CHUNK)
            total = mm(kern1[0, rows, :], mixed[0])
            for h in range(1, heads_n):
                total = total + mm(kern1[h, rows, :], mixed[h])
            for part in range(CHUNK // TILE):
                i = c * (CHUNK // TILE) + part
                now = tokc[pl.ds(pl.multiple_of(i * TILE, TILE), TILE), 0:1]
                near = seg_of(now) == segw[pl.ds(i, 1), :]
                window = v[pl.ds(pl.multiple_of(i * TILE, TILE), 2 * TILE), :]
                conv = jnp.zeros((TILE, wide), f32)
                for h in range(heads_n):
                    term = mm(jnp.where(near, bands[h], 0.0).astype(bf16), window)
                    conv = jnp.where(lane == h, term, conv)
                got = (total[part * TILE : (part + 1) * TILE, :] + conv) * live_of(now).astype(f32)
                row = pl.multiple_of(k * CHUNK + part * TILE, TILE)
                out[out_row, pl.ds(row, TILE), :] = got.astype(bf16)
            return none

        lax.fori_loop(0, per_block, one, 0)

    sent = []
    for k, to in enumerate((here.diagonal, here.across, here.sibling)):
        finish(to, hsend, k)
        sent.append(start(push(hsend.at[k], heads.at[here.t], hsem, k, here.dp, to)))
    finish(here.t, heads, here.t)
    if gather:
        for dz in (2, 3):
            for spread in spreads:
                spread.to_core(dz)
        spread_down.to_core_last()
    for copy in sent:
        copy.wait_recv()
    if gather:
        for spread in spreads + (spread_down,):
            spread.finish()
        length = gain.shape[1]
        far = spread_lanes(length, x.shape[1]).astype(bf16)
        owner = iota((32, x.shape[1]), 1) // length == iota((32, x.shape[1]), 0)
        for r in range(4):
            rows = norm_all[...].reshape(32, 8, LANES)[:, r, :].astype(bf16)
            norms[r : r + 1, :] = jnp.sum(jnp.where(owner, mm(rows, far), 0.0), axis=0, keepdims=True)
        norms[4:8, :] = jnp.zeros((4, x.shape[1]), f32)
    for copy in copies:
        copy.wait_send()


VMEM = pl.BlockSpec(memory_space=pltpu.VMEM)
ANY = pl.BlockSpec(memory_space=pl.ANY)


def dma(*shape):
    return pltpu.SemaphoreType.DMA(shape)


def attention_forward(x, w, taps, seg, slot, live, slot_live, extra, heads_n, blocks, taps_total):
    block, feat = x.shape
    seq, nslot = block * blocks, slot_live.shape[1]
    gather = len(extra) > 0
    depth = w.shape[1]
    wide = -(-heads_n * HEAD_DIM // 256) * 256
    tiles_n = heads_n * (nslot // TILE)
    shape = jax.ShapeDtypeStruct
    outs = [
        shape((blocks, block, feat), bf16),
        shape((feat, LANES * heads_n + wide), bf16),
        shape((seq, LANES), i32),
        shape((2 * (seq // TILE), 2 * TILE), i32),
        shape((seq, LANES * heads_n), bf16),
        shape((seq + 2 * HALO, wide), bf16),
        shape((heads_n, seq, nslot), bf16),
        shape((heads_n, seq, nslot), bf16),
        shape((nslot, LANES * heads_n), f32),
        shape((nslot, LANES), f32),
        shape((tiles_n, TILE, TILE), f32),
        shape((heads_n, nslot, wide), bf16),
        shape((nslot, wide), f32),
        shape((blocks, block, wide), bf16),
        shape((1, nslot // LANDMARKS, heads_n), f32),
    ]
    out_specs = [VMEM] * len(outs)
    scratch = [
        pltpu.VMEM((depth, LANES * heads_n + wide), bf16),
        pltpu.VMEM((heads_n, 2 * nslot, 256), bf16),
        pltpu.VMEM((heads_n, seq, nslot), f32),
        pltpu.VMEM((wide, nslot), f32),
        pltpu.VMEM((2, tiles_n, TILE, TILE), f32),
        pltpu.VMEM((heads_n, TILE, 2 * TILE), f32),
        pltpu.VMEM((3, block, wide), bf16),
        pltpu.VMEM((8, seq + 2 * TILE), i32),
        dma(2, 2 * (block // TILE) + 1),
        dma(2, 7),
        dma(2, 3),
    ]
    if gather:
        hidden_n = extra[0].shape[1]
        outs += [
            shape((4, 2, 2, 2, hidden_n, feat), bf16),
            shape((4, 2, 2, 2, hidden_n, feat), bf16),
            shape((2, 2, feat, wide), bf16),
            shape((8, feat), f32),
        ]
        out_specs += [ANY, ANY, ANY, VMEM]
        scratch += [
            pltpu.VMEM((hidden_n, feat), bf16),
            pltpu.VMEM((depth, wide), bf16),
            pltpu.VMEM((8, LANES), f32),
            pltpu.VMEM((4, 2, 2, 2, 8, LANES), f32),
        ]
        for _ in range(4):
            scratch += [dma(2, 17), pltpu.SemaphoreType.DMA]
    return pl.pallas_call(
        functools.partial(forward_body, gather, taps_total),
        out_shape=tuple(outs),
        in_specs=[VMEM] * (7 + len(extra)),
        out_specs=tuple(out_specs),
        scratch_shapes=scratch,
        compiler_params=pltpu.CompilerParams(
            vmem_limit_bytes=LIMIT, collective_id=1 if gather else 2, has_side_effects=True
        ),
        name="attention_forward",
    )(x, w, taps, seg, slot, live, slot_live, *extra)


def normalized(u):
    mean = jnp.mean(u, axis=-1, keepdims=True)
    centered = u - mean
    scale = lax.rsqrt(jnp.mean(centered * centered, axis=-1, keepdims=True) + norm_epsilon)
    return centered * scale, scale


def normalized_back(g, n, scale):
    return scale * (
        g - jnp.mean(g, axis=-1, keepdims=True) - n * jnp.mean(g * n, axis=-1, keepdims=True)
    )


ROWS = 64
FF_CHUNK = 512


def mm_tn(a, b):
    return lax.dot_general(a, b, (((0,), (0,)), ((), ())), preferred_element_type=f32)


def feed_body(
    direct, x, cot, heads, live, norms, wout, up_in, down_in,
    layer_out, gsend, gpre, gnorm, gout, gup, gdown,
    up, down, act, slope, hidden, hlow, n1, r1, gsum, glow, acc, up_out, down_out, sems,
):
    block, feat = x.shape
    chunks = act.shape[0]
    loads = []
    for j in range(chunks):
        rows = pl.ds(j * FF_CHUNK, FF_CHUNK)
        loads.append(
            (
                pltpu.make_async_copy(up_in.at[rows], up.at[j], sems.at[0, j]),
                pltpu.make_async_copy(down_in.at[rows], down.at[j], sems.at[1, j]),
            )
        )
        for load in loads[-1]:
            load.start()
    gain0, gain1 = norms[0:1, :], norms[1:2, :]
    bias0, bias1 = norms[2:3, :], norms[3:4, :]
    acc[...] = sum(mm_nt(heads[t], wout[t]) for t in range(heads.shape[0]))

    def first_norm(i, none):
        rows = pl.ds(pl.multiple_of(i * ROWS, ROWS), ROWS)
        n, scale = normalized(x[rows, :].astype(f32) + acc[rows, :])
        now = n * gain0 + bias0
        n1[rows, :] = n
        r1[rows, :] = jnp.broadcast_to(scale, (ROWS, LANES))
        hidden[rows, :] = now
        hlow[rows, :] = now.astype(bf16)
        return none

    lax.fori_loop(0, block // ROWS, first_norm, 0)
    acc[...] = hidden[...]
    for j in range(chunks):
        for load in loads[j]:
            load.wait()

    def rise(j, none):
        u = mm_nt(hlow[...], up[j])
        cdf = 0.5 * (1.0 + lax.erf(u * math.sqrt(0.5)))
        act[j] = (u * cdf).astype(bf16)
        slope[j] = cdf + u * (jnp.exp(-0.5 * u * u) * (1.0 / math.sqrt(2.0 * math.pi)))
        acc[...] += mm(act[j], down[j])
        return none

    lax.fori_loop(0, chunks, rise, 0)

    def second_norm(i, sums):
        rows = pl.ds(pl.multiple_of(i * ROWS, ROWS), ROWS)
        n, scale = normalized(acc[rows, :])
        layer_out[rows, :] = (n * gain1 + bias1).astype(bf16)
        c = cot[rows, :].astype(f32)
        g = normalized_back(c * gain1, n, scale)
        gsum[rows, :] = g
        glow[rows, :] = g.astype(bf16)
        return (
            sums[0] + jnp.sum(c * n, axis=0, keepdims=True),
            sums[1] + jnp.sum(c, axis=0, keepdims=True),
        )

    zero = jnp.zeros((1, feat), f32)
    gain_two, bias_two = lax.fori_loop(0, block // ROWS, second_norm, (zero, zero))
    acc[...] = gsum[...]

    def fall(j, none):
        rows = pl.ds(pl.multiple_of(j * FF_CHUNK, FF_CHUNK), FF_CHUNK)
        g_act = mm_nt(glow[...], down[j])
        g_up = (g_act * slope[j]).astype(bf16)
        down_out[j] = mm_tn(act[j], glow[...]).astype(bf16)
        pltpu.make_async_copy(down_out.at[j], gdown.at[rows], sems.at[2, j]).start()
        up_out[j] = mm_tn(g_up, hlow[...]).astype(bf16)
        pltpu.make_async_copy(up_out.at[j], gup.at[rows], sems.at[3, j]).start()
        acc[...] += mm(g_up, up[j])
        return none

    lax.fori_loop(0, chunks, fall, 0)

    def first_back(i, sums):
        rows = pl.ds(pl.multiple_of(i * ROWS, ROWS), ROWS)
        g = acc[rows, :]
        n = n1[rows, :]
        back = normalized_back(g * gain0, n, r1[rows, 0:1])
        gpre[rows, :] = back
        glow[rows, :] = back.astype(bf16)
        return (
            sums[0] + jnp.sum(g * n, axis=0, keepdims=True),
            sums[1] + jnp.sum(g, axis=0, keepdims=True),
        )

    gain_one, bias_one = lax.fori_loop(0, block // ROWS, first_back, (zero, zero))
    gnorm[...] = jnp.concatenate(
        [gain_one, gain_two, bias_one, bias_two, jnp.zeros((4, feat), f32)], axis=0
    )
    for t in range(heads.shape[0]):
        gsend[t] = mm(glow[...], wout[t]).astype(bf16) * live[...]
        grad = mm_tn(glow[...], heads[t]).astype(bf16)
        if direct:
            gout[:, :, t // 2, t % 2] = grad.reshape((4, 2) + gout.shape[4:])
        else:
            gout[t] = grad

    def land(j, none):
        rows = pl.ds(pl.multiple_of(j * FF_CHUNK, FF_CHUNK), FF_CHUNK)
        pltpu.make_async_copy(down_out.at[j], gdown.at[rows], sems.at[2, j]).wait()
        pltpu.make_async_copy(up_out.at[j], gup.at[rows], sems.at[3, j]).wait()
        return none

    lax.fori_loop(0, chunks, land, 0)


def feed_forward(direct, x, cot, heads, live, norms, wout, up_in, down_in, depth):
    block, feat = x.shape
    blocks, _, wide = heads.shape
    hidden_n = up_in.shape[0]
    chunks = hidden_n // FF_CHUNK
    shape = jax.ShapeDtypeStruct
    outs = (
        shape((block, feat), bf16),
        shape((blocks, block, wide), bf16),
        shape((block, feat), f32),
        shape((8, feat), f32),
        shape((4, 2, 2, 2, depth, wide) if direct else (blocks, feat, wide), bf16),
        shape((hidden_n, feat), bf16),
        shape((hidden_n, feat), bf16),
    )
    scratch = [
        pltpu.VMEM((chunks, FF_CHUNK, feat), bf16),
        pltpu.VMEM((chunks, FF_CHUNK, feat), bf16),
        pltpu.VMEM((chunks, block, FF_CHUNK), bf16),
        pltpu.VMEM((chunks, block, FF_CHUNK), f32),
        pltpu.VMEM((block, feat), f32),
        pltpu.VMEM((block, feat), bf16),
        pltpu.VMEM((block, feat), f32),
        pltpu.VMEM((block, LANES), f32),
        pltpu.VMEM((block, feat), f32),
        pltpu.VMEM((block, feat), bf16),
        pltpu.VMEM((block, feat), f32),
        pltpu.VMEM((chunks, FF_CHUNK, feat), bf16),
        pltpu.VMEM((chunks, FF_CHUNK, feat), bf16),
        dma(4, chunks),
    ]
    return pl.pallas_call(
        functools.partial(feed_body, direct),
        out_shape=outs,
        in_specs=[VMEM] * 6 + [ANY, ANY],
        out_specs=tuple([VMEM] * 5 + [ANY, ANY]),
        scratch_shapes=scratch,
        compiler_params=pltpu.CompilerParams(vmem_limit_bytes=LIMIT),
        name="feed_forward",
    )(x, cot, heads, live, norms, wout, up_in, down_in)


class Summer:
    def __init__(self, here, source, first, count, own, from_core, from_y, from_z, from_x, sems, local):
        self.here, self.source, self.rows = here, source, pl.ds(first, count)
        self.own, self.from_core, self.from_y, self.from_z, self.from_x = (
            own, from_core, from_y, from_z, from_x,
        )
        self.sems, self.local = sems, local
        self.copies = []

    def push(self, src, dst, index, dp, t):
        copy = push(src, dst, self.sems, index, dp, t)
        copy.start()
        self.copies.append(copy)
        return copy

    def begin(self):
        here = self.here
        self.loaded = pltpu.make_async_copy(
            self.source.at[:, :, :, here.c, self.rows], self.own, self.local
        )
        self.loaded.start()
        self.core = self.push(
            self.source.at[:, :, :, 1 - here.c, self.rows], self.from_core, 0, here.dp, here.sibling
        )

    def along_y(self):
        here = self.here
        self.loaded.wait()
        self.core.wait_recv()

        def one(n, none):
            z, x = n // 2, n % 2
            y = 1 - here.y
            total = self.from_core[z, y, x].astype(f32) + self.own[z, y, x].astype(f32)
            self.from_core[z, y, x] = total.astype(self.own.dtype)
            return none

        lax.fori_loop(0, 8, one, 0)
        self.y = self.push(
            self.from_core.at[:, 1 - here.y], self.from_y, 1, here.dp_at(0, 1), here.t
        )

    def along_z(self):
        here = self.here
        self.y.wait_recv()

        def one(n, none):
            z, x = n // 2, n % 2
            total = self.from_core[z, here.y, x].astype(f32) + self.own[z, here.y, x].astype(f32)
            total = total + self.from_y[z, x].astype(f32)
            self.from_y[z, x] = total.astype(self.own.dtype)
            return none

        lax.fori_loop(0, 8, one, 0)
        self.z = [
            self.push(
                self.from_y.at[(here.z + dz) % 4], self.from_z.at[dz - 1], 1 + dz, here.dp_at(dz, 0), here.t
            )
            for dz in (1, 2, 3)
        ]

    def along_x(self):
        here = self.here
        for copy in self.z:
            copy.wait_recv()
        for x in range(2):
            total = self.from_y[here.z, x].astype(f32)
            for n in range(3):
                total = total + self.from_z[n, x].astype(f32)
            self.from_y[here.z, x] = total.astype(self.own.dtype)
        self.x = self.push(
            self.from_y.at[here.z, 1 - here.x], self.from_x, 5, here.dp, here.across
        )

    def finish(self, out):
        self.x.wait_recv()
        here = self.here
        out[self.rows, :] = self.from_y[here.z, here.x].astype(f32) + self.from_x[...].astype(f32)
        for copy in self.copies:
            copy.wait_send()


class SummerX(Summer):
    def along_x_first(self):
        here = self.here
        self.loaded.wait()
        self.core.wait_recv()
        x = 1 - here.x

        def one(n, none):
            z, y = n // 2, n % 2
            total = self.from_core[z, y, x].astype(f32) + self.own[z, y, x].astype(f32)
            self.from_core[z, y, x] = total.astype(self.own.dtype)
            return none

        lax.fori_loop(0, 8, one, 0)
        self.x = self.push(self.from_core.at[:, :, x], self.from_x, 1, here.dp, here.across)

    def then_y(self):
        here = self.here
        self.x.wait_recv()
        x = here.x

        def one(n, none):
            z, y = n // 2, n % 2
            total = self.from_core[z, y, x].astype(f32) + self.own[z, y, x].astype(f32)
            self.from_x[z, y] = (total + self.from_x[z, y].astype(f32)).astype(self.own.dtype)
            return none

        lax.fori_loop(0, 8, one, 0)
        self.y = self.push(
            self.from_x.at[:, 1 - here.y], self.from_y, 2, here.dp_at(0, 1), here.t
        )

    def then_z(self):
        here = self.here
        self.y.wait_recv()
        for z in range(4):
            total = self.from_y[z].astype(f32) + self.from_x[z, here.y].astype(f32)
            self.from_y[z] = total.astype(self.own.dtype)
        self.z = [
            self.push(
                self.from_y.at[(here.z + dz) % 4], self.from_z.at[dz - 1], 2 + dz, here.dp_at(dz, 0), here.t
            )
            for dz in (1, 2, 3)
        ]

    def finish(self, out):
        here = self.here
        for copy in self.z:
            copy.wait_recv()
        total = self.from_y[here.z].astype(f32)
        for n in range(3):
            total = total + self.from_z[n].astype(f32)
        out[self.rows, :] = total
        for copy in self.copies:
            copy.wait_send()


SUMMER_SEMS = 6
UP, DOWN, OUT, NORM = range(4)
UP_SHARES = 2


def backward_body(gather, taps_total, *refs):
    (
        gsend, xall_in, wfull, tokc, segw, qk, v, kern1_in, kern3_in,
        land, counts, Ain, mixed, carried, taps, slot_live, gpre,
    ) = refs[:17]
    refs = refs[17:]
    if gather:
        (up_in, down_in, out_in, norm_in), refs = refs[:4], refs[4:]
    (input_grad, gw, gconv), refs = refs[:3], refs[3:]
    if gather:
        (up_out, down_out, out_out, gain_out, bias_out), refs = refs[:5], refs[5:]
    (
        gl1, gl3, xall, xT, gopad, gqk, gv, gband, bands, gmixedT, glandT, hist, gstate, gcar, wback,
        part_out, part_in, part_sum, part_x, piece_v, piece_q, in_v, in_q, in_conv, conv_out,
        gsem, lsem, psem, vsem, csem,
    ) = refs[:30]
    refs = refs[30:]

    here = Place()
    blocks, block, wide = gsend.shape
    seq = blocks * block
    heads_n = gl1.shape[0]
    nslot = land.shape[0]
    nchunk = seq // CHUNK
    per_block = block // CHUNK
    tiles_n = nslot // TILE
    all_tiles = heads_n * tiles_n
    feat = wfull.shape[0]
    doc_row = iota((1, nslot), 1) // LANDMARKS
    live_row = slot_live[...]
    live_cols = [column(live_row[:, g * TILE : (g + 1) * TILE].astype(f32)) for g in range(tiles_n)]
    scaling = 1.0 / math.sqrt(HEAD_DIM)
    same = tile_same()
    ident = tile_eye()

    loads = [
        pltpu.make_async_copy(kern1_in, gl1, lsem.at[0]),
        pltpu.make_async_copy(xall_in, xall, lsem.at[1]),
        pltpu.make_async_copy(kern3_in, gl3, lsem.at[2]),
    ]
    for load in loads:
        load.start()

    peers = here.tensor_peers()
    if gather:
        peers = peers + [
            (here.dp_at(dz, dy), here.t) for dz in range(4) for dy in range(2) if dz or dy
        ]
    greet(peers)
    copies = []

    def start(copy):
        copy.start()
        copies.append(copy)
        return copy

    def landing(t):
        return gopad.at[pl.ds(pl.multiple_of(t * block + HALO, HALO), block)]

    gopad[0:HALO, :] = jnp.zeros((HALO, wide), bf16)
    gopad[seq + HALO : seq + 2 * HALO, :] = jnp.zeros((HALO, wide), bf16)
    arriving = [
        start(push(gsend.at[to], landing(here.t), gsem, k, here.dp, to))
        for k, to in enumerate((here.across, here.diagonal, here.sibling))
    ]
    gopad[pl.ds(pl.multiple_of(here.t * block + HALO, HALO), block), :] = gsend[here.t]

    if gather:
        up_sum, out_sum, norm_sum, norm_pieces = refs[:4]
        refs = refs[4:]
        length = gain_out.shape[1]
        far = spread_lanes(length, feat).astype(bf16)
        owner = iota((32, feat), 1) // length == iota((32, feat), 0)
        for r in range(4):
            high, low = split(jnp.where(owner, norm_in[r : r + 1, :], 0.0))
            norm_pieces[:, r, :] = mm_nt(high, far) + mm_nt(low, far)
        for r in range(4, 8):
            norm_pieces[:, r, :] = jnp.zeros((32, LANES), f32)
        norm_view = norm_pieces.reshape(4, 2, 2, 2, 8, LANES)
        half = up_in.shape[4] // UP_SHARES
        plan = [(Summer, up_in, k * half, half) for k in range(UP_SHARES)]
        plan += [(SummerX, down_in, k * half, half) for k in range(UP_SHARES)]
        plan += [(Summer, out_in, 0, out_in.shape[4]), (Summer, norm_view, 0, 8)]
        summers = []
        for kind, source, first, count in plan:
            buffers, refs = refs[:7], refs[7:]
            summers.append(kind(here, source, first, count, *buffers))
        ups, downs = summers[:UP_SHARES], summers[UP_SHARES : 2 * UP_SHARES]
        smalls = summers[2 * UP_SHARES :]
        for pair in zip(ups, downs):
            for summer in pair:
                summer.begin()
        for summer in smalls:
            summer.begin()

    for n in range(all_tiles):
        A = Ain[n]
        factor, _, _ = newton_start(A)
        W = A * factor
        hist[0, 0, n] = pack(tt_nt(left_of(A), right_nt(W)))
        hist[0, 1, n] = pack(W)

    def step(i, none):
        for n in range(all_tiles):
            S, N, Pm, W = newton_step(unpack(hist[i, 0, n]), unpack(hist[i, 1, n]), ident)
            hist[i, 2, n] = pack(S)
            hist[i, 3, n] = pack(N)
            hist[i + 1, 0, n] = pack(Pm)
            hist[i + 1, 1, n] = pack(W)
        return none

    lax.fori_loop(0, NEWTON, step, 0)
    for h in range(2 * heads_n):
        bands[h] = band_from(taps[h : h + 1, :])
    gmixedT[...] = jnp.zeros_like(gmixedT)
    glandT[...] = jnp.zeros_like(glandT)
    gband[...] = jnp.zeros_like(gband)
    for load in loads:
        load.wait()

    def turn(b, none):
        for i in range(block // TILE):
            rows = slice(i * TILE, i * TILE + TILE)
            col = pl.ds(pl.multiple_of(b * block + i * TILE, TILE), TILE)
            xT[:, col] = xall[b, rows, :].astype(f32).T.astype(bf16)
        return none

    lax.fori_loop(0, blocks, turn, 0)
    if gather:
        for near, far in zip(ups, downs):
            near.along_y()
            far.along_x_first()
        for summer in smalls:
            summer.along_y()
    for copy in arriving:
        copy.wait_recv()

    def one(c, none):
        rows = pl.ds(pl.multiple_of(c * CHUNK, CHUNK), CHUNK)
        g_now = gopad[pl.ds(pl.multiple_of(c * CHUNK + HALO, HALO), CHUNK), :]
        gT = g_now.astype(f32).T.astype(bf16)
        for h in range(heads_n):
            k1 = gl1[h, rows, :]
            gk = mm_nt(g_now, mixed[h])
            k1w = k1.astype(f32)
            gl1[h, rows, :] = (k1w * (gk - jnp.sum(gk * k1w, axis=1, keepdims=True))).astype(bf16)
            e = slice(HEAD_DIM * h, HEAD_DIM * h + HEAD_DIM)
            gmixedT[e, :] += mm(gT[e, :], k1)
        return none

    lax.fori_loop(0, nchunk, one, 0)
    gmixed = gmixedT[...].T
    carried_all = carried[...]
    lane = iota((TILE, wide), 1) // HEAD_DIM
    delta = []
    for h in range(heads_n):
        rows_delta = []
        for g in range(tiles_n):
            n = h * tiles_n + g
            rows = slice(g * TILE, g * TILE + TILE)
            W = unpack(hist[NEWTON, 1, n])
            gm = split(jnp.where(lane == h, gmixed[rows], 0.0))
            near = jnp.where(lane == h, carried_all[rows], 0.0)
            gstate[0, n] = jnp.zeros((TILE, TILE), f32)
            gstate[1, n] = jnp.where(same, mm3(split(near), gm, mm_nt), 0.0)
            gc = mm3(split(W), gm).astype(bf16)
            gcar[h, rows, :] = gc
            rows_delta.append(jnp.sum((gc.astype(f32) * near).T, axis=0, keepdims=True))
        delta.append(jnp.concatenate(rows_delta, axis=1))
    if gather:
        ups[0].along_z()
        downs[0].then_y()

    def three(c, none):
        rows = pl.ds(pl.multiple_of(c * CHUNK, CHUNK), CHUNK)
        v_now = v[pl.ds(pl.multiple_of(c * CHUNK + HALO, HALO), CHUNK), :]
        total = jnp.zeros((CHUNK, wide), f32)
        for h in range(heads_n):
            gc = gcar[h]
            k3 = gl3[h, rows, :]
            gk = mm_nt(v_now, gc)
            gl = (k3.astype(f32) * (gk - delta[h])).astype(bf16)
            gl3[h, rows, :] = gl
            total = total + mm(k3, gc)
            partT = qk[rows, LANES * h : LANES * h + LANES].astype(f32).T.astype(bf16)
            glandT[h, :HEAD_DIM, :] += mm(partT[:HEAD_DIM, :], gl1[h, rows, :])
            glandT[h, HEAD_DIM:, :] += mm(partT[HEAD_DIM:, :], gl)
        for part in range(CHUNK // TILE):
            i = c * (CHUNK // TILE) + part
            at = pl.ds(pl.multiple_of(i * TILE, TILE), TILE)
            now = tokc[at, 0:1]
            seg_now = seg_of(now)
            near = seg_now == segw[pl.ds(i, 1), :]
            near_back = (seg_now == segw[pl.ds(seq // TILE + i, 1), :]) & (live_of(now) > 0)
            g_window = gopad[pl.ds(pl.multiple_of(i * TILE, TILE), 2 * TILE), :]
            v_window = v[pl.ds(pl.multiple_of(i * TILE, TILE), 2 * TILE), :]
            g_tile = gopad[pl.ds(pl.multiple_of(i * TILE + HALO, HALO), TILE), :].astype(f32)
            conv = jnp.zeros((TILE, wide), f32)
            for h in range(heads_n):
                back = mm(jnp.where(near_back, bands[heads_n + h], 0.0).astype(bf16), g_window)
                conv = jnp.where(lane == h, back, conv)
                mine = jnp.where(lane == h, g_tile, 0.0).astype(bf16)
                gband[h] += jnp.where(near, mm_nt(mine, v_window), 0.0)
            gv[at, :] = (total[part * TILE : (part + 1) * TILE, :] + conv).astype(bf16)
        return none

    lax.fori_loop(0, nchunk // 2, three, 0)
    if gather:
        ups[1].along_z()
        downs[1].then_y()
        for summer in smalls:
            summer.along_z()
    lax.fori_loop(nchunk // 2, nchunk, three, 0)

    conv_out[...] = jnp.zeros_like(conv_out)
    for h in range(heads_n):
        conv_out[h : h + 1, :] = diagonal_sums(gband[h])
    piece_v[...] = mm(xT[...], gv[...]).astype(bf16)
    depth = in_v.shape[1] if gather else feat
    sent_v = []
    others = [(dz, dy) for dz in range(4) for dy in range(2) if dz or dy] if gather else []
    for k, (dz, dy) in enumerate(others):
        to = here.dp_at(dz, dy)
        rows = pl.ds(pl.multiple_of(to * depth, 16), depth)
        sent_v.append(start(push(piece_v.at[rows], in_v.at[k], vsem, k, to, here.t)))
        sent_v.append(start(push(conv_out, in_conv.at[k], csem, k, to, here.t)))

    if gather:
        downs[0].then_z()
        ups[0].along_x()

    def unstep(r, none):
        i = NEWTON - 1 - r
        for n in range(all_tiles):
            Pm, W = unpack(hist[i, 0, n]), unpack(hist[i, 1, n])
            S, N = unpack(hist[i, 2, n]), unpack(hist[i, 3, n])
            gP, gW = gstate[0, n], gstate[1, n]
            gPl, gWl, Nl = left_of(gP), left_of(gW), left_of(N)
            Pr = right_of(Pm)
            gN = 0.25 * (tt(gPl, Pr) + tt_nt(gWl, right_nt(W)))
            gNl = left_of(gN)
            gS = tt(gNl, right_of(7.0 * ident - Pm))
            gstate[1, n] = 0.25 * tt(Nl, right_of(gW))
            gstate[0, n] = (
                0.25 * tt(Nl, right_of(gP))
                - 15.0 * gN
                - tt(left_of(S), right_of(gN))
                + tt(left_of(gS), Pr)
                + tt(left_of(Pm), right_of(gS))
            )
        return none

    lax.fori_loop(0, NEWTON, unstep, 0)

    for h in range(heads_n):
        sums_land = pltpu.roll(glandT[h].T * scaling, HEAD_DIM, 1)
        k0, q1, _ = landmark_parts(land[:, LANES * h : LANES * h + LANES])
        for g in range(tiles_n):
            n = h * tiles_n + g
            rows = slice(g * TILE, g * TILE + TILE)
            A = Ain[n]
            factor, colsum, tops = newton_start(A)
            gP, gW = gstate[0, n], gstate[1, n]
            GA = tt(left_of(gP + gP.T), right_of(A))
            gA = factor * (GA + gW)
            gf_cols = jnp.sum((0.5 * GA + gW) * A, axis=0, keepdims=True)
            first = iota(colsum.shape, 1) < LANDMARKS
            gcol = jnp.zeros_like(colsum)
            for k in range(2):
                mine = first if k == 0 else jnp.logical_not(first)
                gf = jnp.sum(jnp.where(mine, gf_cols, 0.0), axis=1, keepdims=True)
                top = tops[k]
                is_top = mine & (colsum == top)
                ties = jnp.sum(is_top.astype(f32), axis=1, keepdims=True)
                share = jnp.where(top > 1.0, 1.0, jnp.where(top == 1.0, 0.5, 0.0))
                floor = jnp.maximum(top, 1.0)
                gcol = jnp.where(is_top, -gf * share / (floor * floor * ties), gcol)
            gA = (gA + gcol) * live_cols[g]
            gl2 = A * (gA - jnp.sum(gA * A, axis=1, keepdims=True)) * scaling
            gl2 = jnp.where(same & (live_row[:, rows] > 0), gl2, 0.0)
            g_land = mm3(split(gl2), split(k0[rows])) + mm3(split(gl2.T), split(q1[rows]))
            g_land = (g_land + sums_land[rows]) / counts[rows, :]
            low = slice(2 * nslot + g * TILE, 2 * nslot + g * TILE + TILE)
            wback[h, low, :] = jnp.concatenate(split(g_land), axis=1)
        wback[h, :nslot, :] = jnp.concatenate(split(k0 * scaling), axis=1)
        wback[h, nslot : 2 * nslot, :] = jnp.concatenate(split(q1 * scaling), axis=1)

    if gather:
        downs[1].then_z()
        ups[1].along_x()
        for summer in smalls:
            summer.along_x()

    def last(b, k):
        row = pl.multiple_of(b * block + k * CHUNK, CHUNK)
        rows = pl.ds(row, CHUNK)
        hot = (slot_of(tokc[rows, 0:1]) == iota((CHUNK, nslot), 1)).astype(f32).astype(bf16)
        for h in range(heads_n):
            both = (
                mm(gl1[h, rows, :], wback[h, :nslot, :])
                + mm(gl3[h, rows, :], wback[h, nslot : 2 * nslot, :])
                + mm(hot, wback[h, 2 * nslot :, :])
            )
            gqk[rows, LANES * h : LANES * h + LANES] = (both[:, :LANES] + both[:, LANES:]).astype(bf16)
        return mm_nt(gqk[rows, :], wfull[:, : LANES * heads_n]) + mm_nt(
            gv[rows, :], wfull[:, LANES * heads_n :]
        )

    def chunk_rows(k):
        return pl.ds(k * CHUNK, CHUNK)

    from_sibling, from_across, own_from_sibling = [], [], []
    for k in range(per_block):
        part_out[0, chunk_rows(k), :] = last(here.diagonal, k).astype(bf16)
        from_sibling.append(
            start(push(part_out.at[0, chunk_rows(k)], part_in.at[0, chunk_rows(k)], psem, k, here.dp, here.sibling))
        )
    for k in range(per_block):
        got = last(here.across, k)
        from_sibling[k].wait_recv()
        part_sum[chunk_rows(k), :] = (got + part_in[0, chunk_rows(k), :].astype(f32)).astype(bf16)
        from_across.append(
            start(push(part_sum.at[chunk_rows(k)], part_x.at[chunk_rows(k)], psem, per_block + k, here.dp, here.across))
        )
    for k in range(per_block):
        part_out[1, chunk_rows(k), :] = last(here.sibling, k).astype(bf16)
        own_from_sibling.append(
            start(push(part_out.at[1, chunk_rows(k)], part_in.at[1, chunk_rows(k)], psem, 2 * per_block + k, here.dp, here.sibling))
        )
    for k in range(per_block):
        input_grad[chunk_rows(k), :] = last(here.t, k) + gpre[chunk_rows(k), :]

    piece_q[...] = mm(xT[...], gqk[...]).astype(bf16)
    sent_q = []
    for k, (dz, dy) in enumerate(others):
        to = here.dp_at(dz, dy)
        rows = pl.ds(pl.multiple_of(to * depth, 16), depth)
        sent_q.append(start(push(piece_q.at[rows], in_q.at[k], vsem, len(others) + k, to, here.t)))
    for k in range(per_block):
        own_from_sibling[k].wait_recv()
        from_across[k].wait_recv()
        input_grad[chunk_rows(k), :] += part_in[1, chunk_rows(k), :].astype(f32) + part_x[
            chunk_rows(k), :
        ].astype(f32)
    for copy in sent_v + sent_q:
        copy.wait_recv()
    if gather:
        rows = pl.ds(pl.multiple_of(here.dp * depth, 16), depth)
        total_v = piece_v[rows, :].astype(f32)
        total_q = piece_q[rows, :].astype(f32)
        total_conv = conv_out[...]
        for k in range(len(others)):
            total_v = total_v + in_v[k].astype(f32)
            total_q = total_q + in_q[k].astype(f32)
            total_conv = total_conv + in_conv[k]
        for h in range(heads_n):
            e = slice(HEAD_DIM * h, HEAD_DIM * h + HEAD_DIM)
            one = total_q[:, LANES * h : LANES * h + LANES]
            gw[0, :, e] = one[:, :HEAD_DIM]
            gw[1, :, e] = one[:, HEAD_DIM:]
        gw[2] = total_v[:, : heads_n * HEAD_DIM]
        first = HALO - taps_total // 2
        turned = pltpu.roll(total_conv, 2 * TILE - first, 1)
        gconv[...] = turned[:heads_n, :taps_total]
        for summer in ups:
            summer.finish(up_sum)
        up_out[...] = up_sum[...].T
        for summer in downs:
            summer.finish(down_out)
        smalls[0].finish(out_sum)
        out_out[...] = out_sum[:, : heads_n * HEAD_DIM].T
        smalls[1].finish(norm_sum)
        gain_out[...] = norm_sum[0:2, :length]
        bias_out[...] = norm_sum[2:4, :length]
    else:
        gw[:, : LANES * heads_n] = piece_q[...].astype(f32)
        gw[:, LANES * heads_n :] = piece_v[...].astype(f32)
        gconv[...] = conv_out[...]
    for copy in copies:
        copy.wait_send()


def attention_backward(gsend, xall, wfull, tokc, segw, qk, v, kern1, kern3, land, counts, weights,
                       mixed, carried, taps, slot_live, gpre, sources, taps_total, depth):
    blocks, block, wide = gsend.shape
    heads_n, seq, nslot = kern1.shape
    feat = wfull.shape[0]
    all_tiles = weights.shape[0]
    shape = jax.ShapeDtypeStruct
    gather = len(sources) > 0
    width = heads_n * HEAD_DIM
    outs = [shape((block, feat), f32)]
    if gather:
        hidden_n = sources[UP].shape[4]
        outs += [
            shape((3, depth, width), f32),
            shape((heads_n, taps_total), f32),
            shape((feat, hidden_n), f32),
            shape((hidden_n, feat), f32),
            shape((width, depth), f32),
            shape((2, feat // 32), f32),
            shape((2, feat // 32), f32),
        ]
    else:
        outs += [shape((feat, wfull.shape[1]), f32), shape((8, 2 * TILE), f32)]
    others = 7 if gather else 1
    per_block = block // CHUNK
    scratch = [
        pltpu.VMEM((heads_n, seq, nslot), bf16),
        pltpu.VMEM((heads_n, seq, nslot), bf16),
        pltpu.VMEM(xall.shape, bf16),
        pltpu.VMEM((feat, seq), bf16),
        pltpu.VMEM((seq + 2 * HALO, wide), bf16),
        pltpu.VMEM((seq, LANES * heads_n), bf16),
        pltpu.VMEM((seq, wide), bf16),
        pltpu.VMEM((heads_n, TILE, 2 * TILE), f32),
        pltpu.VMEM((2 * heads_n, TILE, 2 * TILE), f32),
        pltpu.VMEM((wide, nslot), f32),
        pltpu.VMEM((heads_n, LANES, nslot), f32),
        pltpu.VMEM((NEWTON + 1, 4, all_tiles, LANDMARKS, TILE), f32),
        pltpu.VMEM((2, all_tiles, TILE, TILE), f32),
        pltpu.VMEM((heads_n, nslot, wide), bf16),
        pltpu.VMEM((heads_n, 3 * nslot, 256), bf16),
        pltpu.VMEM((2, block, feat), bf16),
        pltpu.VMEM((2, block, feat), bf16),
        pltpu.VMEM((block, feat), bf16),
        pltpu.VMEM((block, feat), bf16),
        pltpu.VMEM((feat, wide), bf16),
        pltpu.VMEM((feat, LANES * heads_n), bf16),
        pltpu.VMEM((others, depth if gather else 16, wide), bf16),
        pltpu.VMEM((others, depth if gather else 16, LANES * heads_n), bf16),
        pltpu.VMEM((others, 8, 2 * TILE), f32),
        pltpu.VMEM((8, 2 * TILE), f32),
        dma(2, 3),
        dma(3),
        dma(2, 3 * per_block),
        dma(2, 2 * others),
        dma(2, others),
    ]
    if gather:
        scratch += [
            pltpu.VMEM((hidden_n, feat), f32),
            pltpu.VMEM((depth, wide), f32),
            pltpu.VMEM((8, LANES), f32),
            pltpu.VMEM((32, 8, LANES), f32),
        ]
        half = hidden_n // UP_SHARES
        plan = [(False, half, feat, bf16)] * UP_SHARES + [(True, half, feat, bf16)] * UP_SHARES
        plan += [(False, depth, wide, bf16), (False, 8, LANES, f32)]
        for turned, count, lanes, kind in plan:
            scratch += [
                pltpu.VMEM((4, 2, 2, count, lanes), kind),
                pltpu.VMEM((4, 2, 2, count, lanes), kind),
                pltpu.VMEM((4, count, lanes) if turned else (4, 2, count, lanes), kind),
                pltpu.VMEM((3, count, lanes) if turned else (3, 2, count, lanes), kind),
                pltpu.VMEM((4, 2, count, lanes) if turned else (count, lanes), kind),
                dma(2, SUMMER_SEMS),
                pltpu.SemaphoreType.DMA,
            ]
    specs = [VMEM, ANY] + [VMEM] * 5 + [ANY, ANY] + [VMEM] * 8
    if gather:
        specs += [ANY, ANY, ANY, VMEM]
    return pl.pallas_call(
        functools.partial(backward_body, gather, taps_total),
        out_shape=tuple(outs),
        in_specs=specs,
        out_specs=tuple([VMEM] * len(outs)),
        scratch_shapes=scratch,
        compiler_params=pltpu.CompilerParams(
            vmem_limit_bytes=LIMIT, collective_id=3 if gather else 4, has_side_effects=True
        ),
        name="attention_backward",
    )(gsend, xall, wfull, tokc, segw, qk, v, kern1, kern3, land, counts, weights, mixed, carried,
      taps, slot_live, gpre, *sources)


def split_up(shard, dim, length):
    before, after = (shard.shape[:dim], shard.shape[dim + 1 :])
    return jnp.moveaxis(shard.reshape(*before, length, -1, *after), dim, 0)


def exchange(pieces, axis):
    return lax.all_to_all(pieces, axis, split_axis=0, concat_axis=0, tiled=True)


def per_device(
    tokens,
    w_qkv,
    w_out,
    conv_weight,
    w_up,
    w_down,
    norm_gain,
    norm_bias,
    cotangent,
    seg_ids,
    landmark_slot,
    token_live,
    slot_live,
):
    both = ("dp", "tensor")
    dp_size, blocks = lax.axis_size("dp"), lax.axis_size("tensor")
    devices = dp_size * blocks
    heads_n, taps_total = conv_weight.shape
    block, feat = tokens.shape
    depth = w_qkv.shape[1]
    width = heads_n * HEAD_DIM
    wide = -(-width // 256) * 256
    hidden_n = w_up.shape[1]
    docs = slot_live.shape[1] // LANDMARKS
    direct = dp_size == 8 and blocks == 4 and depth % 16 == 0 and hidden_n % 32 == 0

    first = HALO - taps_total // 2
    taps = jnp.pad(
        jnp.concatenate([conv_weight, conv_weight[:, ::-1]]),
        ((0, 8 - 2 * heads_n), (first, 2 * TILE - taps_total - first)),
    )
    weight = w_qkv if direct else lax.all_gather(w_qkv, "dp", axis=1, tiled=True)
    extra = (w_up, w_down, w_out, norm_gain, norm_bias) if direct else ()
    got = attention_forward(
        tokens, weight, taps, seg_ids, landmark_slot, token_live, slot_live,
        extra, heads_n, blocks, taps_total,
    )
    (
        xall, wfull, tokc, segw, qk, v, kern1, kern3, land, counts, weights, mixed, carried, heads, proxies,
    ) = got[:15]
    if direct:
        up_all, down_all, out_all, norms = got[15:]
        up_all, down_all = up_all.reshape(-1, feat), down_all.reshape(-1, feat)
        out_all = out_all.reshape(blocks, feat, wide)
    else:
        up_all = lax.all_gather(w_up.T, both, axis=0, tiled=True)
        down_all = lax.all_gather(w_down, both, axis=0, tiled=True)
        out_all = lax.all_gather(lax.all_gather(w_out.T, "dp", axis=0, tiled=True), "tensor", axis=0)
        out_all = jnp.pad(out_all, ((0, 0), (0, 0), (0, wide - width)))
        norms = jnp.concatenate([norm_gain, norm_bias, jnp.zeros_like(norm_gain), jnp.zeros_like(norm_bias)])
        norms = lax.all_gather(norms, both, axis=1, tiled=True).astype(f32)
    live_here = lax.dynamic_slice_in_dim(token_live[0], lax.axis_index("tensor") * block, block)
    live_here = jnp.broadcast_to(live_here.astype(bf16)[:, None], (block, wide))
    layer_out, gsend, grad_pre, norm_grads, out_pieces, up_pieces, down_pieces = feed_forward(
        direct, tokens, cotangent, heads, live_here, norms, out_all, up_all, down_all, depth
    )
    sources = ()
    if direct:
        owners = (4, 2, 2, 2, hidden_n, feat)
        sources = (up_pieces.reshape(owners), down_pieces.reshape(owners), out_pieces, norm_grads)
    got = attention_backward(
        gsend, xall, wfull, tokc, segw, qk, v, kern1, kern3, land, counts, weights,
        mixed, carried, taps, slot_live, grad_pre, sources, taps_total, depth,
    )
    if direct:
        input_grad, grad_qkv, grad_conv, grad_up, grad_down, grad_out, grad_gain, grad_bias = got
    else:
        input_grad, grad_w, grad_conv = got
        grad_w = exchange(grad_w.astype(bf16).reshape(dp_size, depth, -1), "dp").astype(f32).sum(axis=0)
        pairs = grad_w[:, : LANES * heads_n].reshape(depth, heads_n, 2, HEAD_DIM)
        grad_qkv = jnp.concatenate(
            [
                jnp.moveaxis(pairs, 2, 0).reshape(2, depth, width),
                grad_w[None, :, LANES * heads_n : LANES * heads_n + width],
            ]
        )
        grad_conv = lax.psum(grad_conv, "dp")[:heads_n, first : first + taps_total]
        grad_up = lax.psum_scatter(up_pieces, both, scatter_dimension=0, tiled=True).astype(f32).T
        grad_down = lax.psum_scatter(down_pieces, both, scatter_dimension=0, tiled=True).astype(f32)
        out_pieces = out_pieces[:, :, :width].reshape(blocks, dp_size, depth, width)
        out_pieces = jnp.swapaxes(out_pieces, 0, 1).reshape(devices, depth, width)
        grad_out = lax.psum_scatter(out_pieces, both, scatter_dimension=0, tiled=False).astype(f32).T
        norm_sum = exchange(split_up(norm_grads[:4], 1, devices), both).sum(axis=0)
        grad_gain, grad_bias = norm_sum[:2], norm_sum[2:]
    return (
        layer_out,
        input_grad,
        grad_qkv,
        grad_out,
        grad_conv,
        grad_up,
        grad_down,
        grad_gain,
        grad_bias,
        proxies,
    )


def solution(mesh):
    return jax.shard_map(
        per_device,
        mesh=mesh,
        in_specs=(
            P(("dp", "tensor"), None),
            P(None, "dp", "tensor"),
            P("tensor", "dp"),
            P("tensor", None),
            P(None, ("dp", "tensor")),
            P(("dp", "tensor"), None),
            P(None, ("dp", "tensor")),
            P(None, ("dp", "tensor")),
            P(("dp", "tensor"), None),
            P("dp", None),
            P("dp", None),
            P("dp", None),
            P("dp", None),
        ),
        out_specs=(
            P(("dp", "tensor"), None),
            P(("dp", "tensor"), None),
            P(None, "dp", "tensor"),
            P("tensor", "dp"),
            P("tensor", None),
            P(None, ("dp", "tensor")),
            P(("dp", "tensor"), None),
            P(None, ("dp", "tensor")),
            P(None, ("dp", "tensor")),
            P("dp", None, "tensor"),
        ),
        check_vma=False,
    )
```

```python
import functools
import math

import jax
import jax.numpy as jnp
from jax import lax
from jax.experimental import pallas as pl
from jax.experimental.pallas import tpu as pltpu
from jax.sharding import PartitionSpec as P

HEAD_DIM = 64
LANDMARKS = 64
NEWTON = 6
TILE = 128
HALO = TILE // 2
CHUNK = 256
LANES = 128
bf16 = jnp.bfloat16
f32 = jnp.float32
i32 = jnp.int32
norm_epsilon = 1e-05
MESH = pl.DeviceIdType.MESH
LIMIT = 62 * 2**20


def mm(a, b):
    return lax.dot_general(a, b, (((1,), (0,)), ((), ())), preferred_element_type=f32)


def mm_nt(a, b):
    return lax.dot_general(a, b, (((1,), (1,)), ((), ())), preferred_element_type=f32)


def split(a):
    high = a.astype(bf16)
    return high, (a - high.astype(f32)).astype(bf16)


def mm3(a, b, dot=mm):
    return dot(a[0], b[0]) + (dot(a[0], b[1]) + dot(a[1], b[0]))


def left_of(a):
    return jnp.concatenate(split(a), axis=1)


def right_of(b):
    high, low = split(b)
    top = jnp.concatenate([high, low], axis=1)
    bottom = jnp.concatenate([jnp.zeros_like(high), high], axis=1)
    return jnp.concatenate([top, bottom], axis=0)


def right_nt(b):
    high, low = split(b)
    top = jnp.concatenate([high, jnp.zeros_like(high)], axis=1)
    bottom = jnp.concatenate([low, high], axis=1)
    return jnp.concatenate([top, bottom], axis=0)


def tt(left, right):
    both = mm(left, right)
    return both[:, :TILE] + both[:, TILE:]


def tt_nt(left, right):
    both = mm_nt(left, right)
    return both[:, :TILE] + both[:, TILE:]


def iota(shape, dim):
    return lax.broadcasted_iota(i32, shape, dim)


def tile_same():
    shape = (TILE, TILE)
    return iota(shape, 0) // LANDMARKS == iota(shape, 1) // LANDMARKS


def tile_eye():
    shape = (TILE, TILE)
    return (iota(shape, 0) == iota(shape, 1)).astype(f32)


def pack(tile):
    return tile[:LANDMARKS] + tile[LANDMARKS:]


def unpack(packed):
    first = iota(packed.shape, 1) < LANDMARKS
    return jnp.concatenate([jnp.where(first, packed, 0.0), jnp.where(first, 0.0, packed)], axis=0)


def landmark_parts(land):
    first = iota(land.shape, 1) < HEAD_DIM
    turned = pltpu.roll(land, HEAD_DIM, 1)
    return jnp.where(first, turned, 0.0), jnp.where(first, 0.0, turned), jnp.where(first, land, 0.0)


def lane_masks():
    first = (iota((LANDMARKS, TILE), 1) < LANDMARKS).astype(f32)
    return first.astype(bf16), (1.0 - first).astype(bf16)


def packed_eye():
    shape = (LANDMARKS, TILE)
    return (iota(shape, 0) == iota(shape, 1) % LANDMARKS).astype(f32)


def packed_right(b, masks):
    high, low = split(b)
    high = jnp.concatenate([high * masks[0], high * masks[1]], axis=0)
    low = jnp.concatenate([low * masks[0], low * masks[1]], axis=0)
    top = jnp.concatenate([high, low], axis=1)
    bottom = jnp.concatenate([jnp.zeros_like(high), high], axis=1)
    return jnp.concatenate([top, bottom], axis=0)


def packed_tn(a, b):
    (ah, al), (bh, bl) = split(a), split(b)
    both = lax.dot_general(
        jnp.concatenate([ah, al, ah], axis=0),
        jnp.concatenate([bh, bh, bl], axis=0),
        (((0,), (0,)), ((), ())),
        preferred_element_type=f32,
    )
    first = iota(a.shape, 1) < LANDMARKS
    return jnp.where(first, both[:LANDMARKS], both[LANDMARKS:])


def newton_step(Pm, Z, ident, masks):
    Pl, Pr = left_of(Pm), packed_right(Pm, masks)
    S = tt(Pl, Pr)
    N = 13.0 * ident - 15.0 * Pm + 7.0 * S - tt(left_of(S), Pr)
    both = 0.25 * tt(jnp.concatenate([Pl, left_of(Z)], axis=0), packed_right(N, masks))
    return S, N, both[:LANDMARKS], both[LANDMARKS:]


def newton_start(A):
    colsum = jnp.sum(A, axis=0, keepdims=True)
    first = iota(colsum.shape, 1) < LANDMARKS
    tops = [
        jnp.max(jnp.where(first, colsum, 0.0), axis=1, keepdims=True),
        jnp.max(jnp.where(first, 0.0, colsum), axis=1, keepdims=True),
    ]
    factor = 1.0 / jnp.maximum(jnp.where(first, tops[0], tops[1]), 1.0)
    return factor, colsum, tops


def column(row):
    return jnp.broadcast_to(row, (LANES, LANES)).T


def band_from(row):
    wide = jnp.broadcast_to(row, (TILE, 2 * TILE))
    return pltpu.roll(wide, 0, 1, stride=1, stride_axis=0)


def diagonal_sums(band):
    where = iota(band.shape, 0)
    step = 1
    while step < TILE:
        turned = pltpu.roll(band, 2 * TILE - step, 1)
        band = jnp.where((where // step) % 2 == 1, turned, band)
        step *= 2
    return jnp.sum(band, axis=0, keepdims=True)


def seg_of(code):
    return (code // 512) % 8


def live_of(code):
    return code // 4096


def slot_of(code):
    return code % 512


class Place:
    def __init__(self):
        self.dp = lax.axis_index("dp")
        self.t = lax.axis_index("tensor")
        self.x = self.t // 2
        self.c = self.t % 2
        self.sibling = self.x * 2 + 1 - self.c
        self.across = (1 - self.x) * 2 + self.c
        self.diagonal = (1 - self.x) * 2 + 1 - self.c
        self.z = self.dp // 2
        self.y = self.dp % 2

    def tensor_peers(self):
        return [(self.dp, t) for t in (self.sibling, self.across, self.diagonal)]

    def dp_at(self, turn_z, turn_y):
        return ((self.z + turn_z) % 4) * 2 + (self.y + turn_y) % 2


def greet(peers):
    barrier = pltpu.get_barrier_semaphore()
    for peer in peers:
        pl.semaphore_signal(barrier, inc=1, device_id=peer, device_id_type=MESH)
    pl.semaphore_wait(barrier, len(peers))


def push(src, dst, sems, index, dp, t):
    return pltpu.make_async_remote_copy(
        src_ref=src,
        dst_ref=dst,
        send_sem=sems.at[0, index],
        recv_sem=sems.at[1, index],
        device_id=(dp, t),
        device_id_type=MESH,
    )


class Spreader:
    def __init__(self, here, shard, whole, sems, local, by_rows=False):
        self.here, self.shard, self.whole, self.sems, self.local = here, shard, whole, sems, local
        self.by_rows = by_rows
        self.copies = []

    def at(self, z, y, x):
        c = self.here.c
        if not self.by_rows:
            return self.whole.at[z, y, x, c]
        depth = self.shard.shape[0]
        rows = pl.ds(pl.multiple_of((z * 2 + y) * depth, 16), depth)
        return self.whole.at[x, c, rows]

    def pair(self, z, y):
        return self.at(z, y, slice(None))

    def push(self, src, dst, index, dp, t):
        copy = push(src, dst, self.sems, index, dp, t)
        copy.start()
        self.copies.append(copy)
        return copy

    def pass_on(self, ref, index, dp, t):
        return self.push(ref, ref, index, dp, t)

    def begin(self):
        here = self.here
        mine = self.at(here.z, here.y, here.x)
        self.kept = pltpu.make_async_copy(self.shard, mine, self.local)
        self.kept.start()
        self.first = self.push(self.shard, mine, 0, here.dp, here.across)

    def take_x(self):
        here = self.here
        self.kept.wait()
        self.first.wait_recv()
        mine = self.pair(here.z, here.y)
        self.from_y = {0: self.pass_on(mine, 4, here.dp_at(0, 1), here.t)}
        self.from_core = [self.pass_on(mine, 5, here.dp, here.sibling)]
        self.from_z = {}

    def along_z(self, dz):
        here = self.here
        mine = self.pair(here.z, here.y)
        self.from_z[dz] = self.pass_on(mine, dz, here.dp_at(dz, 0), here.t)

    def along_y(self, dz):
        here = self.here
        self.from_z[dz].wait_recv()
        got = self.pair((here.z + 4 - dz) % 4, here.y)
        self.from_y[dz] = self.pass_on(got, 5 + dz, here.dp_at(0, 1), here.t)
        self.from_core.append(self.pass_on(got, 8 + dz, here.dp, here.sibling))

    def to_core(self, dz):
        here = self.here
        self.from_y[dz].wait_recv()
        got = self.pair((here.z + 4 - dz) % 4, 1 - here.y)
        self.from_core.append(self.pass_on(got, 12 + dz, here.dp, here.sibling))

    def finish(self):
        for copy in self.from_core:
            copy.wait_recv()
        for copy in self.copies:
            copy.wait_send()


class SpreaderX(Spreader):
    def begin(self):
        here = self.here
        mine = self.at(here.z, here.y, here.x)
        self.kept = pltpu.make_async_copy(self.shard, mine, self.local)
        self.kept.start()
        self.from_z = [
            self.push(self.shard, mine, dz, here.dp_at(dz, 0), here.t) for dz in (1, 2, 3)
        ]
        self.from_y = [self.push(self.shard, mine, 4, here.dp_at(0, 1), here.t)]
        self.from_x = []

    def own_x(self):
        here = self.here
        mine = self.at(here.z, here.y, here.x)
        self.from_x.append(self.push(self.shard, mine, 0, here.dp, here.across))

    def along_y(self, dz):
        here = self.here
        self.from_z[dz - 1].wait_recv()
        got = self.at((here.z + 4 - dz) % 4, here.y, here.x)
        self.from_y.append(self.pass_on(got, 4 + dz, here.dp_at(0, 1), here.t))
        self.from_x.append(self.pass_on(got, 7 + dz, here.dp, here.across))

    def along_x(self, dz):
        here = self.here
        self.from_y[dz].wait_recv()
        got = self.at((here.z + 4 - dz) % 4, 1 - here.y, here.x)
        self.from_x.append(self.pass_on(got, 11 + dz, here.dp, here.across))

    def to_core(self):
        here = self.here
        self.kept.wait()
        near = self.whole.at[:, :, here.x, here.c]
        self.from_core = [self.pass_on(near, 15, here.dp, here.sibling)]

    def to_core_last(self):
        here = self.here
        for copy in self.from_x:
            copy.wait_recv()
        far = self.whole.at[:, :, 1 - here.x, here.c]
        self.from_core.append(self.pass_on(far, 16, here.dp, here.sibling))


def spread_lanes(length, whole):
    shape = (LANES, whole)
    return (iota(shape, 0) == iota(shape, 1) % length).astype(f32)


def forward_body(gather, taps_total, *refs):
    (x, w, conv, seg, slot, live, slot_live), refs = refs[:7], refs[7:]
    if gather:
        (w_up, w_down, w_out, gain, bias), refs = refs[:5], refs[5:]
    (
        xall_out, wfull_out, tokc, segw, qk_out, v_out, kern1_out, kern3_out,
        land, counts, Aout, mixed, carried, heads, prox, hist_out,
    ) = refs[:16]
    refs = refs[16:]
    if gather:
        (up_all, down_all, out_all, norms), refs = refs[:4], refs[4:]
    (
        xall, wfull, qk, v, kern1, kern3,
        wsh, wlog, l3, carriedT, hist, bands, hsend, segp, taps, xsem, wsem, hsem, osem,
    ) = refs[:19]
    refs = refs[19:]
    keeping = []

    def keep(src, dst):
        copy = pltpu.make_async_copy(src, dst, osem.at[len(keeping)])
        copy.start()
        keeping.append(copy)

    here = Place()
    block = x.shape[0]
    blocks = xall.shape[0]
    seq = block * blocks
    heads_n = qk.shape[1] // LANES
    nslot = land.shape[0]
    wide = v.shape[1]
    nchunk = seq // CHUNK
    per_block = block // CHUNK
    tiles_n = nslot // TILE
    width = heads_n * HEAD_DIM
    scaling = 1.0 / math.sqrt(HEAD_DIM)

    depth = w.shape[1]
    parts = []
    for h in range(heads_n):
        e = slice(HEAD_DIM * h, HEAD_DIM * h + HEAD_DIM)
        parts += [w[0, :, e], w[1, :, e]]
    parts += [w[2], jnp.zeros((depth, wide - width), bf16)]
    wsh[...] = jnp.concatenate(parts, axis=1)

    peers = here.tensor_peers()
    if gather:
        peers = peers + [(here.dp_at(dz, 0), here.t) for dz in (1, 2, 3)] + [(here.dp_at(0, 1), here.t)]
        out_sh, norm_sh, norm_all = refs[:3]
        out_sh[...] = jnp.concatenate(
            [w_out[...].astype(f32).T, jnp.zeros((depth, wide - width), f32)], axis=1
        ).astype(bf16)
        norm_sh[...] = jnp.zeros_like(norm_sh)
        norm_sh[0:2, : gain.shape[1]] = gain[...].astype(f32)
        norm_sh[2:4, : gain.shape[1]] = bias[...].astype(f32)
        sems = refs[3:]
        spread_up = Spreader(here, w_up, up_all, sems[0], sems[1])
        spread_out = Spreader(here, out_sh, out_all, sems[2], sems[3], by_rows=True)
        spread_norm = Spreader(here, norm_sh, norm_all, sems[4], sems[5])
        spread_down = SpreaderX(here, w_down, down_all, sems[6], sems[7])
        spreads = (spread_up, spread_out, spread_norm)
    greet(peers)

    copies = []
    pieces = block // TILE
    if gather:
        for spread in spreads:
            spread.begin()

    def start(copy):
        copy.start()
        copies.append(copy)
        return copy

    crossing = [
        start(push(x.at[pl.ds(p * TILE, TILE)], xall.at[here.t, pl.ds(p * TILE, TILE)], xsem, p, here.dp, here.across))
        for p in range(pieces)
    ]
    beside = start(push(x, xall.at[here.t], xsem, pieces, here.dp, here.sibling))
    if gather:
        mine = wfull.at[pl.ds(pl.multiple_of(here.dp * depth, 16), depth)]
        along = [start(push(wsh, mine, wsem, dz, here.dp_at(dz, 0), here.t)) for dz in (1, 2, 3)]
        along = [start(push(wsh, mine, wsem, 0, here.dp_at(0, 1), here.t))] + along
        wfull[pl.ds(pl.multiple_of(here.dp * depth, 16), depth), :] = wsh[...]
    else:
        wfull[...] = wsh[...]
    xall[here.t] = x[...]

    segp[...] = jnp.full(segp.shape, -1, i32)
    segp[0:1, TILE : TILE + seq] = jnp.where(live[...] > 0, seg[...], -1)
    segp[1:2, TILE : TILE + seq] = seg[...]
    code = (slot[...] + 512 * seg[...] + 4096 * live[...]).astype(f32)
    for i in range(seq // TILE):
        lanes = slice(i * TILE, i * TILE + TILE)
        tokc[lanes, :] = column(code[:, lanes]).astype(i32)
        near = pltpu.roll(segp[:, i * TILE : i * TILE + 3 * TILE], 3 * TILE - HALO, 1)
        segw[i : i + 1, :] = near[0:1, : 2 * TILE]
        segw[seq // TILE + i : seq // TILE + i + 1, :] = near[1:2, : 2 * TILE]
    taps[...] = jnp.zeros_like(taps)
    taps[:heads_n, :taps_total] = conv[...]
    moved = pltpu.roll(taps[...], HALO - taps_total // 2, 1)
    for h in range(heads_n):
        bands[h] = band_from(moved[h : h + 1, :])
    doc_row = iota((1, nslot), 1) // LANDMARKS
    live_row = slot_live[...]
    live_cols = [column(live_row[:, g * TILE : (g + 1) * TILE].astype(f32)) for g in range(tiles_n)]
    v[0:HALO, :] = jnp.zeros((HALO, wide), bf16)
    v[seq + HALO : seq + 2 * HALO, :] = jnp.zeros((HALO, wide), bf16)

    if gather:
        along[0].wait_recv()
        for dz in (1, 2, 3):
            along[dz].wait_recv()
            got = wfull.at[pl.ds(pl.multiple_of(here.dp_at(4 - dz, 0) * depth, 16), depth)]
            along.append(start(push(got, got, wsem, 3 + dz, here.dp_at(0, 1), here.t)))
        spread_down.begin()
        for spread in spreads:
            spread.take_x()
            spread.along_z(2)
        for dz in (1, 2, 3):
            along[3 + dz].wait_recv()

    def project(b, carry):
        def one(i, carry):
            acc, cnt = carry
            c = b * per_block + i
            rows = pl.ds(pl.multiple_of(c * CHUNK, CHUNK), CHUNK)
            out = mm(xall[b, pl.ds(pl.multiple_of(i * CHUNK, CHUNK), CHUNK), :], wfull[...])
            qk_now = out[:, : LANES * heads_n].astype(bf16)
            qk[rows, :] = qk_now
            v[pl.ds(pl.multiple_of(c * CHUNK + HALO, HALO), CHUNK), :] = out[:, LANES * heads_n :].astype(bf16)
            slot_now = slot[:, pl.ds(pl.multiple_of(c * CHUNK, CHUNK), CHUNK)]
            hot = (slot_now == iota((nslot, CHUNK), 0)).astype(f32)
            return acc + mm(hot.astype(bf16), qk_now), cnt + jnp.sum(hot, axis=1, keepdims=True)

        return lax.fori_loop(0, per_block, one, carry)

    carry = (jnp.zeros((nslot, LANES * heads_n), f32), jnp.zeros((nslot, 1), f32))
    carry = project(here.t, carry)
    beside.wait_recv()
    carry = project(here.sibling, carry)
    passed = []
    for p in range(pieces):
        crossing[p].wait_recv()
        got = xall.at[here.across, pl.ds(p * TILE, TILE)]
        passed.append(start(push(got, got, xsem, pieces + 1 + p, here.dp, here.sibling)))
    carry = project(here.across, carry)
    for p in range(pieces):
        passed[p].wait_recv()
    acc, cnt = project(here.diagonal, carry)
    cnt = jnp.maximum(cnt, 1.0)
    counts[...] = jnp.broadcast_to(cnt, counts.shape)
    land[...] = acc / cnt

    if gather:
        spread_down.own_x()
        for spread in spreads:
            spread.along_z(1)
    keep(xall, xall_out)
    keep(wfull, wfull_out)
    keep(qk, qk_out)
    keep(v, v_out)

    same = tile_same()
    ident = packed_eye()
    masks = lane_masks()
    for h in range(heads_n):
        k0, q1, q0 = landmark_parts(land[:, LANES * h : LANES * h + LANES])
        wlog[h] = jnp.concatenate(split(jnp.concatenate([k0, q1], axis=0) * scaling), axis=1)
        for g in range(tiles_n):
            rows = slice(g * TILE, g * TILE + TILE)
            logit = tt_nt(left_of(q0[rows] * scaling), right_nt(k0[rows]))
            filled = jnp.where(same & (live_row[:, rows] > 0), logit, -1e9)
            raised = jnp.exp(filled - jnp.max(filled, axis=1, keepdims=True))
            A = raised / jnp.sum(raised, axis=1, keepdims=True) * live_cols[g]
            n = h * tiles_n + g
            Aout[n] = A
            factor, _, _ = newton_start(A)
            W = A * factor
            hist[0, 0, n] = pack(tt_nt(left_of(A), right_nt(W)))
            hist[0, 1, n] = pack(W.T)

    def logits(c, top):
        rows = pl.ds(pl.multiple_of(c * CHUNK, CHUNK), CHUNK)
        now = tokc[rows, 0:1]
        allowed = (seg_of(now) == doc_row) & (live_row > 0)
        alive = allowed & (live_of(now) > 0)
        tops = []
        for h in range(heads_n):
            part = qk[rows, LANES * h : LANES * h + LANES]
            both = mm_nt(jnp.concatenate([part, part], axis=1), wlog[h])
            one = jnp.where(allowed, both[:, :nslot], -1e9)
            raised = jnp.exp(one - jnp.max(one, axis=1, keepdims=True))
            kern1[h, rows, :] = (raised / jnp.sum(raised, axis=1, keepdims=True)).astype(bf16)
            three = jnp.where(alive, both[:, nslot:], -1e9)
            l3[h, rows, :] = three
            tops.append(jnp.maximum(top[h], jnp.max(three, axis=0, keepdims=True)))
        return tuple(tops)

    def step_and_logits(i, top):
        for n in range(heads_n * tiles_n):
            S, N, Pm, Z = newton_step(hist[i, 0, n], hist[i, 1, n], ident, masks)
            hist[i, 2, n] = S
            hist[i, 3, n] = N
            hist[i + 1, 0, n] = Pm
            hist[i + 1, 1, n] = Z
        return logits(i, top)

    top = tuple(jnp.full((1, nslot), -1e9, f32) for _ in range(heads_n))
    third = NEWTON // 3
    top = lax.fori_loop(0, third, step_and_logits, top)
    if gather:
        for dz in (1, 2, 3):
            spread_down.along_y(dz)
    top = lax.fori_loop(third, 2 * third, step_and_logits, top)
    if gather:
        for spread in spreads:
            spread.along_z(3)
        spread_down.along_x(0)
    top = lax.fori_loop(2 * third, NEWTON, step_and_logits, top)
    keep(hist, hist_out)
    top = lax.fori_loop(NEWTON, nchunk, logits, top)
    keep(kern1, kern1_out)

    def raise_three(c, total):
        rows = pl.ds(pl.multiple_of(c * CHUNK, CHUNK), CHUNK)
        totals = []
        for h in range(heads_n):
            raised = jnp.exp(l3[h, rows, :] - top[h])
            l3[h, rows, :] = raised
            totals.append(total[h] + jnp.sum(raised, axis=0, keepdims=True))
        return tuple(totals)

    total = lax.fori_loop(
        0, nchunk, raise_three, tuple(jnp.zeros((1, nslot), f32) for _ in range(heads_n))
    )
    norm = [live_row.astype(f32) / total[h] for h in range(heads_n)]
    carriedT[...] = jnp.zeros_like(carriedT)

    def carry_three(c, none):
        rows = pl.ds(pl.multiple_of(c * CHUNK, CHUNK), CHUNK)
        vT = v[pl.ds(pl.multiple_of(c * CHUNK + HALO, HALO), CHUNK), :].astype(f32).T.astype(bf16)
        for h in range(heads_n):
            low = (l3[h, rows, :] * norm[h]).astype(bf16)
            kern3[h, rows, :] = low
            e = slice(HEAD_DIM * h, HEAD_DIM * h + HEAD_DIM)
            carriedT[e, :] += mm(vT[e, :], low)
        return none

    lax.fori_loop(0, nchunk, carry_three, 0)
    keep(kern3, kern3_out)
    carried_all = carriedT[...].T
    carried[...] = carried_all
    lane = iota((TILE, wide), 1) // HEAD_DIM
    docs = nslot // LANDMARKS
    prox_all = jnp.zeros((8, LANES), f32)
    for h in range(heads_n):
        for g in range(tiles_n):
            rows = slice(g * TILE, g * TILE + TILE)
            n = h * tiles_n + g
            Z = hist[NEWTON, 1, n]
            part = split(jnp.where(lane == h, carried_all[rows], 0.0))
            mixed[h, rows, :] = mm3(split(unpack(Z)), part).astype(bf16)
            A = Aout[n]
            A2 = jnp.sum(A * A, axis=0, keepdims=True)
            Z2 = jnp.sum(Z * Z, axis=0, keepdims=True)
            first = iota(A2.shape, 1) < LANDMARKS
            for half in range(2):
                mine = first if half == 0 else jnp.logical_not(first)
                a2 = jnp.sum(jnp.where(mine, A2, 0.0), axis=1, keepdims=True)
                z2 = jnp.sum(jnp.where(mine, Z2, 0.0), axis=1, keepdims=True)
                doc = g * 2 + half
                alive = live_row[:, doc * LANDMARKS : doc * LANDMARKS + 1] > 0
                value = jnp.where(alive, jnp.sqrt(a2) * jnp.sqrt(z2) / LANDMARKS, 0.0)
                here_too = (iota(prox_all.shape, 0) == h) & (iota(prox_all.shape, 1) == doc)
                prox_all = jnp.where(here_too, value, prox_all)
    for h in range(heads_n):
        prox[h] = prox_all[h : h + 1, :docs]

    def finish(b, out, out_row):
        def one(k, none):
            c = b * per_block + k
            rows = pl.ds(pl.multiple_of(c * CHUNK, CHUNK), CHUNK)
            total = mm(kern1[0, rows, :], mixed[0])
            for h in range(1, heads_n):
                total = total + mm(kern1[h, rows, :], mixed[h])
            for part in range(CHUNK // TILE):
                i = c * (CHUNK // TILE) + part
                now = tokc[pl.ds(pl.multiple_of(i * TILE, TILE), TILE), 0:1]
                near = seg_of(now) == segw[pl.ds(i, 1), :]
                window = v[pl.ds(pl.multiple_of(i * TILE, TILE), 2 * TILE), :]
                conv = jnp.zeros((TILE, wide), f32)
                for h in range(heads_n):
                    term = mm(jnp.where(near, bands[h], 0.0).astype(bf16), window)
                    conv = jnp.where(lane == h, term, conv)
                got = (total[part * TILE : (part + 1) * TILE, :] + conv) * live_of(now).astype(f32)
                row = pl.multiple_of(k * CHUNK + part * TILE, TILE)
                out[out_row, pl.ds(row, TILE), :] = got.astype(bf16)
            return none

        lax.fori_loop(0, per_block, one, 0)

    sent = []
    for k, to in enumerate((here.diagonal, here.across, here.sibling)):
        finish(to, hsend, k)
        sent.append(start(push(hsend.at[k], heads.at[here.t], hsem, k, here.dp, to)))
    finish(here.t, heads, here.t)
    if gather:
        for spread in spreads:
            spread.along_y(2)
        for dz in (1, 2, 3):
            spread_down.along_x(dz)
        for spread in spreads:
            spread.along_y(1)
        spread_down.to_core()
        for spread in spreads:
            spread.to_core(0)
        for spread in spreads:
            spread.along_y(3)
        for dz in (2, 1):
            for spread in spreads:
                spread.to_core(dz)
        spread_down.to_core_last()
        for spread in spreads:
            spread.to_core(3)
    for copy in sent:
        copy.wait_recv()
    if gather:
        for spread in spreads + (spread_down,):
            spread.finish()
        length = gain.shape[1]
        far = spread_lanes(length, x.shape[1]).astype(bf16)
        owner = iota((32, x.shape[1]), 1) // length == iota((32, x.shape[1]), 0)
        for r in range(4):
            rows = norm_all[...].reshape(32, 8, LANES)[:, r, :].astype(bf16)
            norms[r : r + 1, :] = jnp.sum(jnp.where(owner, mm(rows, far), 0.0), axis=0, keepdims=True)
        norms[4:8, :] = jnp.zeros((4, x.shape[1]), f32)
    for copy in copies:
        copy.wait_send()
    for copy in keeping:
        copy.wait()


VMEM = pl.BlockSpec(memory_space=pltpu.VMEM)
ANY = pl.BlockSpec(memory_space=pl.ANY)


def dma(*shape):
    return pltpu.SemaphoreType.DMA(shape)


def attention_forward(x, w, conv, seg, slot, live, slot_live, extra, heads_n, blocks, taps_total):
    block, feat = x.shape
    seq, nslot = block * blocks, slot_live.shape[1]
    gather = len(extra) > 0
    depth = w.shape[1]
    wide = -(-heads_n * HEAD_DIM // 256) * 256
    tiles_n = heads_n * (nslot // TILE)
    shape = jax.ShapeDtypeStruct
    outs = [
        shape((blocks, block, feat), bf16),
        shape((feat, LANES * heads_n + wide), bf16),
        shape((seq, LANES), i32),
        shape((2 * (seq // TILE), 2 * TILE), i32),
        shape((seq, LANES * heads_n), bf16),
        shape((seq + 2 * HALO, wide), bf16),
        shape((heads_n, seq, nslot), bf16),
        shape((heads_n, seq, nslot), bf16),
        shape((nslot, LANES * heads_n), f32),
        shape((nslot, LANES), f32),
        shape((tiles_n, TILE, TILE), f32),
        shape((heads_n, nslot, wide), bf16),
        shape((nslot, wide), f32),
        shape((blocks, block, wide), bf16),
        shape((heads_n, 1, nslot // LANDMARKS), f32),
        shape((NEWTON + 1, 4, tiles_n, LANDMARKS, TILE), f32),
    ]
    out_specs = [ANY, ANY, VMEM, VMEM] + [ANY] * 4 + [VMEM] * 7 + [ANY]
    scratch = [pltpu.VMEM(outs[n].shape, bf16) for n in (0, 1, 4, 5, 6, 7)]
    scratch += [
        pltpu.VMEM((depth, LANES * heads_n + wide), bf16),
        pltpu.VMEM((heads_n, 2 * nslot, 256), bf16),
        pltpu.VMEM((heads_n, seq, nslot), f32),
        pltpu.VMEM((wide, nslot), f32),
        pltpu.VMEM(outs[15].shape, f32),
        pltpu.VMEM((heads_n, TILE, 2 * TILE), f32),
        pltpu.VMEM((3, block, wide), bf16),
        pltpu.VMEM((8, seq + 2 * TILE), i32),
        pltpu.VMEM((8, 2 * TILE), f32),
        dma(2, 2 * (block // TILE) + 1),
        dma(2, 7),
        dma(2, 3),
        dma(7),
    ]
    if gather:
        hidden_n = extra[0].shape[0]
        outs += [
            shape((4, 2, 2, 2, hidden_n, feat), bf16),
            shape((4, 2, 2, 2, hidden_n, feat), bf16),
            shape((2, 2, feat, wide), bf16),
            shape((8, feat), f32),
        ]
        out_specs += [ANY, ANY, ANY, VMEM]
        scratch += [
            pltpu.VMEM((depth, wide), bf16),
            pltpu.VMEM((8, LANES), f32),
            pltpu.VMEM((4, 2, 2, 2, 8, LANES), f32),
        ]
        for _ in range(4):
            scratch += [dma(2, 17), pltpu.SemaphoreType.DMA]
    return pl.pallas_call(
        functools.partial(forward_body, gather, taps_total),
        out_shape=tuple(outs),
        in_specs=[VMEM] * (7 + len(extra)),
        out_specs=tuple(out_specs),
        scratch_shapes=scratch,
        compiler_params=pltpu.CompilerParams(
            vmem_limit_bytes=LIMIT, collective_id=1 if gather else 2, has_side_effects=True
        ),
        name="attention_forward",
    )(x, w, conv, seg, slot, live, slot_live, *extra)


def normalized(u):
    mean = jnp.mean(u, axis=-1, keepdims=True)
    centered = u - mean
    scale = lax.rsqrt(jnp.mean(centered * centered, axis=-1, keepdims=True) + norm_epsilon)
    return centered * scale, scale


def normalized_back(g, n, scale):
    return scale * (
        g - jnp.mean(g, axis=-1, keepdims=True) - n * jnp.mean(g * n, axis=-1, keepdims=True)
    )


ROWS = 64
FF_CHUNK = 512


def mm_tn(a, b):
    return lax.dot_general(a, b, (((0,), (0,)), ((), ())), preferred_element_type=f32)


def feed_body(
    direct, x, cot, heads, norms, wout, up_in, down_in,
    layer_out, gsend, gpre, gnorm, gout, gup, gdown,
    up, down, act, slope, hidden, hlow, n1, r1, gsum, glow, acc, up_out, down_out, sems,
):
    block, feat = x.shape
    chunks = act.shape[0]
    loads = []
    for j in range(chunks):
        rows = pl.ds(j * FF_CHUNK, FF_CHUNK)
        loads.append(
            (
                pltpu.make_async_copy(up_in.at[rows], up.at[j], sems.at[0, j]),
                pltpu.make_async_copy(down_in.at[rows], down.at[j], sems.at[1, j]),
            )
        )
        for load in loads[-1]:
            load.start()
    gain0, gain1 = norms[0:1, :], norms[1:2, :]
    bias0, bias1 = norms[2:3, :], norms[3:4, :]
    acc[...] = sum(mm_nt(heads[t], wout[t]) for t in range(heads.shape[0]))

    def first_norm(i, none):
        rows = pl.ds(pl.multiple_of(i * ROWS, ROWS), ROWS)
        n, scale = normalized(x[rows, :].astype(f32) + acc[rows, :])
        now = n * gain0 + bias0
        n1[rows, :] = n
        r1[rows, :] = jnp.broadcast_to(scale, (ROWS, LANES))
        hidden[rows, :] = now
        hlow[rows, :] = now.astype(bf16)
        return none

    lax.fori_loop(0, block // ROWS, first_norm, 0)
    acc[...] = hidden[...]
    for j in range(chunks):
        for load in loads[j]:
            load.wait()

    def rise(j, none):
        u = mm_nt(hlow[...], up[j])
        cdf = 0.5 * (1.0 + lax.erf(u * math.sqrt(0.5)))
        act[j] = (u * cdf).astype(bf16)
        slope[j] = cdf + u * (jnp.exp(-0.5 * u * u) * (1.0 / math.sqrt(2.0 * math.pi)))
        acc[...] += mm(act[j], down[j])
        return none

    lax.fori_loop(0, chunks, rise, 0)

    def second_norm(i, sums):
        rows = pl.ds(pl.multiple_of(i * ROWS, ROWS), ROWS)
        n, scale = normalized(acc[rows, :])
        layer_out[rows, :] = (n * gain1 + bias1).astype(bf16)
        c = cot[rows, :].astype(f32)
        g = normalized_back(c * gain1, n, scale)
        gsum[rows, :] = g
        glow[rows, :] = g.astype(bf16)
        return (
            sums[0] + jnp.sum(c * n, axis=0, keepdims=True),
            sums[1] + jnp.sum(c, axis=0, keepdims=True),
        )

    zero = jnp.zeros((1, feat), f32)
    gain_two, bias_two = lax.fori_loop(0, block // ROWS, second_norm, (zero, zero))
    acc[...] = gsum[...]

    def fall(j, none):
        rows = pl.ds(pl.multiple_of(j * FF_CHUNK, FF_CHUNK), FF_CHUNK)
        g_act = mm_nt(glow[...], down[j])
        g_up = (g_act * slope[j]).astype(bf16)
        down_out[j] = mm_tn(act[j], glow[...]).astype(bf16)
        pltpu.make_async_copy(down_out.at[j], gdown.at[rows], sems.at[2, j]).start()
        up_out[j] = mm_tn(g_up, hlow[...]).astype(bf16)
        pltpu.make_async_copy(up_out.at[j], gup.at[rows], sems.at[3, j]).start()
        acc[...] += mm(g_up, up[j])
        return none

    lax.fori_loop(0, chunks, fall, 0)

    def first_back(i, sums):
        rows = pl.ds(pl.multiple_of(i * ROWS, ROWS), ROWS)
        g = acc[rows, :]
        n = n1[rows, :]
        back = normalized_back(g * gain0, n, r1[rows, 0:1])
        gpre[rows, :] = back
        glow[rows, :] = back.astype(bf16)
        return (
            sums[0] + jnp.sum(g * n, axis=0, keepdims=True),
            sums[1] + jnp.sum(g, axis=0, keepdims=True),
        )

    gain_one, bias_one = lax.fori_loop(0, block // ROWS, first_back, (zero, zero))
    gnorm[...] = jnp.concatenate(
        [gain_one, gain_two, bias_one, bias_two, jnp.zeros((4, feat), f32)], axis=0
    )
    for t in range(heads.shape[0]):
        gsend[t] = mm(glow[...], wout[t]).astype(bf16)
        grad = mm_tn(glow[...], heads[t]).astype(bf16)
        if direct:
            gout[:, :, t // 2, t % 2] = grad.reshape((4, 2) + gout.shape[4:])
        else:
            gout[t] = grad

    def land(j, none):
        rows = pl.ds(pl.multiple_of(j * FF_CHUNK, FF_CHUNK), FF_CHUNK)
        pltpu.make_async_copy(down_out.at[j], gdown.at[rows], sems.at[2, j]).wait()
        pltpu.make_async_copy(up_out.at[j], gup.at[rows], sems.at[3, j]).wait()
        return none

    lax.fori_loop(0, chunks, land, 0)


RISE = (0, 2, 3, 1)
FALL = (2, 1, 3, 0)


def feed_direct_body(
    x, cot, heads, norms, wout, up_in, down_in,
    layer_out, gsend, gpre, gnorm, gout, sum_up, sum_down, part_up, part_down,
    up, down, act, slope, hidden, hlow, n1, r1, gsum, glow, acc,
    gu, gd, cu, cd, yu, xd, lsem, csem, ysem,
):
    here = Place()
    block, feat = x.shape
    units = act.shape[2]
    loads = {}
    for k in RISE:
        z = (here.z + k) % 4
        loads[k] = (
            pltpu.make_async_copy(up_in.at[z], up.at[z], lsem.at[0, k]),
            pltpu.make_async_copy(down_in.at[z], down.at[z], lsem.at[1, k]),
        )
        for load in loads[k]:
            load.start()
    greet(
        [(here.dp, here.sibling), (here.dp, here.across), (here.dp_at(0, 1), here.t)]
    )
    gain0, gain1 = norms[0:1, :], norms[1:2, :]
    bias0, bias1 = norms[2:3, :], norms[3:4, :]
    acc[...] = sum(mm_nt(heads[t], wout[t]) for t in range(heads.shape[0]))

    def first_norm(i, none):
        rows = pl.ds(pl.multiple_of(i * ROWS, ROWS), ROWS)
        n, scale = normalized(x[rows, :].astype(f32) + acc[rows, :])
        now = n * gain0 + bias0
        n1[rows, :] = n
        r1[rows, :] = jnp.broadcast_to(scale, (ROWS, LANES))
        hidden[rows, :] = now
        hlow[rows, :] = now.astype(bf16)
        return none

    lax.fori_loop(0, block // ROWS, first_norm, 0)
    acc[...] = hidden[...]
    flat = (4, units, feat)
    up_of, down_of = up.reshape(flat), down.reshape(flat)
    for k in RISE:
        z = (here.z + k) % 4
        for load in loads[k]:
            load.wait()
        u = mm_nt(hlow[...], up_of[z])
        cdf = 0.5 * (1.0 + lax.erf(u * math.sqrt(0.5)))
        act[k] = (u * cdf).astype(bf16)
        slope[k] = cdf + u * (jnp.exp(-0.5 * u * u) * (1.0 / math.sqrt(2.0 * math.pi)))
        acc[...] += mm(act[k], down_of[z])

    def second_norm(i, sums):
        rows = pl.ds(pl.multiple_of(i * ROWS, ROWS), ROWS)
        n, scale = normalized(acc[rows, :])
        layer_out[rows, :] = (n * gain1 + bias1).astype(bf16)
        c = cot[rows, :].astype(f32)
        g = normalized_back(c * gain1, n, scale)
        gsum[rows, :] = g
        glow[rows, :] = g.astype(bf16)
        return (
            sums[0] + jnp.sum(c * n, axis=0, keepdims=True),
            sums[1] + jnp.sum(c, axis=0, keepdims=True),
        )

    zero = jnp.zeros((1, feat), f32)
    gain_two, bias_two = lax.fori_loop(0, block // ROWS, second_norm, (zero, zero))
    acc[...] = gsum[...]
    copies = []

    def start(copy):
        copy.start()
        copies.append(copy)
        return copy

    core, later = {}, {}

    def after_core(k):
        for copy in core[k]:
            copy.wait_recv()
        cu[k] = cu[k] + gu[k, :, :, here.c]
        cd[k] = cd[k] + gd[k, :, :, here.c]
        if k in FALL[:2]:
            n = FALL.index(k)
            later[k] = (
                start(push(cu.at[k, 1 - here.y], yu.at[n], ysem, n, here.dp_at(0, 1), here.t)),
                start(push(cd.at[k, :, 1 - here.x], xd.at[n], ysem, 2 + n, here.dp, here.across)),
            )

    for n, k in enumerate(FALL):
        z = (here.z + k) % 4
        g_act = mm_nt(glow[...], down_of[z])
        g_up = (g_act * slope[k]).astype(bf16)
        gd[k] = mm_tn(act[k], glow[...]).astype(bf16).reshape(gd.shape[1:])
        gu[k] = mm_tn(g_up, hlow[...]).astype(bf16).reshape(gu.shape[1:])
        core[k] = (
            start(push(gd.at[k, :, :, 1 - here.c], cd.at[k], csem, k, here.dp, here.sibling)),
            start(push(gu.at[k, :, :, 1 - here.c], cu.at[k], csem, 4 + k, here.dp, here.sibling)),
        )
        acc[...] += mm(g_up, up_of[z])
        if n > 0:
            after_core(FALL[n - 1])

    def first_back(i, sums):
        rows = pl.ds(pl.multiple_of(i * ROWS, ROWS), ROWS)
        g = acc[rows, :]
        n = n1[rows, :]
        back = normalized_back(g * gain0, n, r1[rows, 0:1])
        gpre[rows, :] = back
        glow[rows, :] = back.astype(bf16)
        return (
            sums[0] + jnp.sum(g * n, axis=0, keepdims=True),
            sums[1] + jnp.sum(g, axis=0, keepdims=True),
        )

    gain_one, bias_one = lax.fori_loop(0, block // ROWS, first_back, (zero, zero))
    gnorm[...] = jnp.concatenate(
        [gain_one, gain_two, bias_one, bias_two, jnp.zeros((4, feat), f32)], axis=0
    )
    after_core(FALL[3])
    for t in range(heads.shape[0]):
        gsend[t] = mm(glow[...], wout[t]).astype(bf16)
        grad = mm_tn(glow[...], heads[t]).astype(bf16)
        gout[:, :, t // 2, t % 2] = grad.reshape((4, 2) + gout.shape[4:])
    for n, k in enumerate(FALL[2:]):
        part_up[n] = cu[k]
        part_down[n] = cd[k]
    for n, k in enumerate(FALL[:2]):
        for copy in later[k]:
            copy.wait_recv()
        sum_up[n] = cu[k, here.y] + yu[n]
        sum_down[n] = cd[k, :, here.x] + xd[n]
    for copy in copies:
        copy.wait_send()


def feed_direct(x, cot, heads, norms, wout, up_in, down_in, depth):
    block, feat = x.shape
    blocks, _, wide = heads.shape
    owners = up_in.shape
    hidden_n = owners[4]
    units = 8 * hidden_n
    shape = jax.ShapeDtypeStruct
    outs = (
        shape((block, feat), bf16),
        shape((blocks, block, wide), bf16),
        shape((block, feat), f32),
        shape((8, feat), f32),
        shape((4, 2, 2, 2, depth, wide), bf16),
        shape((2, 2, hidden_n, feat), bf16),
        shape((2, 2, hidden_n, feat), bf16),
        shape((2, 2, 2, hidden_n, feat), bf16),
        shape((2, 2, 2, hidden_n, feat), bf16),
    )
    scratch = [
        pltpu.VMEM(owners, bf16),
        pltpu.VMEM(owners, bf16),
        pltpu.VMEM((4, block, units), bf16),
        pltpu.VMEM((4, block, units), f32),
        pltpu.VMEM((block, feat), f32),
        pltpu.VMEM((block, feat), bf16),
        pltpu.VMEM((block, feat), f32),
        pltpu.VMEM((block, LANES), f32),
        pltpu.VMEM((block, feat), f32),
        pltpu.VMEM((block, feat), bf16),
        pltpu.VMEM((block, feat), f32),
        pltpu.VMEM(owners, bf16),
        pltpu.VMEM(owners, bf16),
        pltpu.VMEM((4, 2, 2, hidden_n, feat), bf16),
        pltpu.VMEM((4, 2, 2, hidden_n, feat), bf16),
        pltpu.VMEM((2, 2, hidden_n, feat), bf16),
        pltpu.VMEM((2, 2, hidden_n, feat), bf16),
        dma(2, 4),
        dma(2, 8),
        dma(2, 4),
    ]
    return pl.pallas_call(
        feed_direct_body,
        out_shape=outs,
        in_specs=[VMEM] * 5 + [ANY, ANY],
        out_specs=tuple([VMEM] * len(outs)),
        scratch_shapes=scratch,
        compiler_params=pltpu.CompilerParams(
            vmem_limit_bytes=LIMIT, collective_id=5, has_side_effects=True
        ),
        name="feed_forward",
    )(x, cot, heads, norms, wout, up_in, down_in)


def feed_forward(direct, x, cot, heads, norms, wout, up_in, down_in, depth):
    block, feat = x.shape
    blocks, _, wide = heads.shape
    hidden_n = up_in.shape[0]
    chunks = hidden_n // FF_CHUNK
    shape = jax.ShapeDtypeStruct
    outs = (
        shape((block, feat), bf16),
        shape((blocks, block, wide), bf16),
        shape((block, feat), f32),
        shape((8, feat), f32),
        shape((4, 2, 2, 2, depth, wide) if direct else (blocks, feat, wide), bf16),
        shape((hidden_n, feat), bf16),
        shape((hidden_n, feat), bf16),
    )
    scratch = [
        pltpu.VMEM((chunks, FF_CHUNK, feat), bf16),
        pltpu.VMEM((chunks, FF_CHUNK, feat), bf16),
        pltpu.VMEM((chunks, block, FF_CHUNK), bf16),
        pltpu.VMEM((chunks, block, FF_CHUNK), f32),
        pltpu.VMEM((block, feat), f32),
        pltpu.VMEM((block, feat), bf16),
        pltpu.VMEM((block, feat), f32),
        pltpu.VMEM((block, LANES), f32),
        pltpu.VMEM((block, feat), f32),
        pltpu.VMEM((block, feat), bf16),
        pltpu.VMEM((block, feat), f32),
        pltpu.VMEM((chunks, FF_CHUNK, feat), bf16),
        pltpu.VMEM((chunks, FF_CHUNK, feat), bf16),
        dma(4, chunks),
    ]
    return pl.pallas_call(
        functools.partial(feed_body, direct),
        out_shape=outs,
        in_specs=[VMEM] * 5 + [ANY, ANY],
        out_specs=tuple([VMEM] * 5 + [ANY, ANY]),
        scratch_shapes=scratch,
        compiler_params=pltpu.CompilerParams(vmem_limit_bytes=LIMIT),
        name="feed_forward",
    )(x, cot, heads, norms, wout, up_in, down_in)


class Summer:
    def __init__(self, here, source, first, count, own, from_core, from_y, from_z, from_x, sems, local):
        self.here, self.source, self.rows = here, source, pl.ds(first, count)
        self.own, self.from_core, self.from_y, self.from_z, self.from_x = (
            own, from_core, from_y, from_z, from_x,
        )
        self.sems, self.local = sems, local
        self.copies = []

    def push(self, src, dst, index, dp, t):
        copy = push(src, dst, self.sems, index, dp, t)
        copy.start()
        self.copies.append(copy)
        return copy

    def begin(self):
        here = self.here
        self.loaded = pltpu.make_async_copy(
            self.source.at[:, :, :, here.c, self.rows], self.own, self.local
        )
        self.loaded.start()
        self.core = self.push(
            self.source.at[:, :, :, 1 - here.c, self.rows], self.from_core, 0, here.dp, here.sibling
        )

    def along_y(self):
        here = self.here
        self.loaded.wait()
        self.core.wait_recv()

        def one(n, none):
            z, x = n // 2, n % 2
            y = 1 - here.y
            self.from_core[z, y, x] = self.from_core[z, y, x] + self.own[z, y, x]
            return none

        lax.fori_loop(0, 8, one, 0)
        self.y = self.push(
            self.from_core.at[:, 1 - here.y], self.from_y, 1, here.dp_at(0, 1), here.t
        )

    def along_z(self):
        here = self.here
        self.y.wait_recv()

        def one(n, none):
            z, x = n // 2, n % 2
            total = self.from_core[z, here.y, x].astype(f32) + self.own[z, here.y, x].astype(f32)
            total = total + self.from_y[z, x].astype(f32)
            self.from_y[z, x] = total.astype(self.own.dtype)
            return none

        lax.fori_loop(0, 8, one, 0)
        self.z = [
            self.push(
                self.from_y.at[(here.z + dz) % 4], self.from_z.at[dz - 1], 1 + dz, here.dp_at(dz, 0), here.t
            )
            for dz in (1, 2, 3)
        ]

    def along_x(self):
        here = self.here
        for copy in self.z:
            copy.wait_recv()
        for x in range(2):
            total = self.from_y[here.z, x].astype(f32)
            for n in range(3):
                total = total + self.from_z[n, x].astype(f32)
            self.from_y[here.z, x] = total.astype(self.own.dtype)
        self.x = self.push(
            self.from_y.at[here.z, 1 - here.x], self.from_x, 5, here.dp, here.across
        )

    def finish(self, out):
        self.x.wait_recv()
        here = self.here
        out[self.rows, :] = self.from_y[here.z, here.x].astype(f32) + self.from_x[...].astype(f32)
        for copy in self.copies:
            copy.wait_send()


class UpSum:
    def __init__(self, here, sums, parts, from_y, from_z, from_x, sems):
        self.here, self.sums, self.parts = here, sums, parts
        self.from_y, self.from_z, self.from_x, self.sems = from_y, from_z, from_x, sems
        self.copies = []

    def push(self, src, dst, index, dp, t):
        copy = push(src, dst, self.sems, index, dp, t)
        copy.start()
        self.copies.append(copy)
        return copy

    def along_z(self, src, k):
        here = self.here
        return self.push(src, self.from_z.at[k - 1], k - 1, here.dp_at(k, 0), here.t)

    def begin(self):
        here = self.here
        self.y = [
            self.push(self.parts.at[n, 1 - here.y], self.from_y.at[n], 3 + n, here.dp_at(0, 1), here.t)
            for n in range(2)
        ]
        self.z = [self.along_z(self.sums.at[n], FALL[n]) for n in range(2)]

    def second(self):
        for n in range(2):
            self.y[n].wait_recv()
            self.from_y[n] = self.from_y[n] + self.parts[n, self.here.y]
        self.z.append(self.along_z(self.from_y.at[0], FALL[2]))

    def third(self):
        here = self.here
        for copy in self.z:
            copy.wait_recv()
        total = self.from_y[1].astype(f32)
        for n in range(3):
            total = total + self.from_z[n].astype(f32)
        self.from_y[1] = total.astype(bf16)
        self.x = self.push(self.from_y.at[1, 1 - here.x], self.from_x, 5, here.dp, here.across)

    def finish(self, out):
        self.x.wait_recv()
        out[...] = self.from_y[1, self.here.x].astype(f32) + self.from_x[...].astype(f32)
        for copy in self.copies:
            copy.wait_send()


class DownSum(UpSum):
    def begin(self):
        here = self.here
        self.x = [
            self.push(self.parts.at[n, :, 1 - here.x], self.from_x.at[n], 3 + n, here.dp, here.across)
            for n in range(2)
        ]
        self.y = [self.along_y(self.sums.at[n, 1 - here.y], n) for n in range(2)]

    def along_y(self, src, n):
        here = self.here
        return self.push(src, self.from_y.at[n], 5 + n, here.dp_at(0, 1), here.t)

    def second(self):
        self.z = []
        for n in range(2):
            self.y[n].wait_recv()
            self.from_y[n] = self.from_y[n] + self.sums[n, self.here.y]
            self.z.append(self.along_z(self.from_y.at[n], FALL[n]))

    def third(self):
        here = self.here
        for n in range(2):
            self.x[n].wait_recv()
            self.from_x[n] = self.from_x[n] + self.parts[n, :, here.x]
            self.y.append(self.along_y(self.from_x.at[n, 1 - here.y], 2 + n))

    def fourth(self):
        for n in range(2):
            self.y[2 + n].wait_recv()
            self.from_y[2 + n] = self.from_y[2 + n] + self.from_x[n, self.here.y]
        self.z.append(self.along_z(self.from_y.at[2], FALL[2]))

    def finish(self, out):
        for copy in self.z:
            copy.wait_recv()
        total = self.from_y[3].astype(f32)
        for n in range(3):
            total = total + self.from_z[n].astype(f32)
        out[...] = total
        for copy in self.copies:
            copy.wait_send()


SUMMER_SEMS = 6


def backward_body(gather, taps_total, *refs):
    (
        gsend, xall_in, wfull, tokc, segw, qk, v, kern1_in, kern3_in,
        land, counts, Ain, mixed, carried, conv, slot_live, gpre, hist_in,
    ) = refs[:18]
    refs = refs[18:]
    if gather:
        (sum_up, sum_down, part_up, part_down, out_in, norm_in), refs = refs[:6], refs[6:]
    (input_grad, gw, gconv), refs = refs[:3], refs[3:]
    if gather:
        (up_out, down_out, out_out, gain_out, bias_out), refs = refs[:5], refs[5:]
    (
        taps, gl1, gl3, xall, xT, gopad, gqk, gv, gband, bands, gmixedT, glandT, hist, gstate, gcar, wback,
        part_out, part_in, part_sum, part_x, piece_v, piece_q, in_v, in_q, in_conv, conv_out,
        gsem, lsem, psem, csem,
    ) = refs[:30]
    refs = refs[30:]

    here = Place()
    blocks, block, wide = gsend.shape
    seq = blocks * block
    heads_n = gl1.shape[0]
    nslot = land.shape[0]
    nchunk = seq // CHUNK
    per_block = block // CHUNK
    tiles_n = nslot // TILE
    all_tiles = heads_n * tiles_n
    feat = wfull.shape[0]
    doc_row = iota((1, nslot), 1) // LANDMARKS
    live_row = slot_live[...]
    live_cols = [column(live_row[:, g * TILE : (g + 1) * TILE].astype(f32)) for g in range(tiles_n)]
    scaling = 1.0 / math.sqrt(HEAD_DIM)
    same = tile_same()
    masks = lane_masks()

    loads = [
        pltpu.make_async_copy(kern1_in, gl1, lsem.at[0]),
        pltpu.make_async_copy(xall_in, xall, lsem.at[1]),
        pltpu.make_async_copy(kern3_in, gl3, lsem.at[2]),
        pltpu.make_async_copy(hist_in, hist, lsem.at[3]),
    ]
    for load in loads:
        load.start()

    peers = here.tensor_peers()
    if gather:
        peers = peers + [
            (here.dp_at(dz, dy), here.t) for dz in range(4) for dy in range(2) if dz or dy
        ]
    greet(peers)
    copies = []

    def start(copy):
        copy.start()
        copies.append(copy)
        return copy

    def landing(t):
        return gopad.at[pl.ds(pl.multiple_of(t * block + HALO, HALO), block)]

    gopad[0:HALO, :] = jnp.zeros((HALO, wide), bf16)
    gopad[seq + HALO : seq + 2 * HALO, :] = jnp.zeros((HALO, wide), bf16)
    arriving = [
        start(push(gsend.at[to], landing(here.t), gsem, k, here.dp, to))
        for k, to in enumerate((here.across, here.diagonal, here.sibling))
    ]
    gopad[pl.ds(pl.multiple_of(here.t * block + HALO, HALO), block), :] = gsend[here.t]

    if gather:
        out_sum, norm_sum, norm_pieces, q_sems, v_sems, in_vz, in_qz = refs[:7]
        refs = refs[7:]
        ups = UpSum(here, sum_up, part_up, *refs[:4])
        downs = DownSum(here, sum_down, part_down, *refs[4:8])
        refs = refs[8:]
        ups.begin()
        downs.begin()
        length = gain_out.shape[1]
        far = spread_lanes(length, feat).astype(bf16)
        owner = iota((32, feat), 1) // length == iota((32, feat), 0)
        for r in range(4):
            high, low = split(jnp.where(owner, norm_in[r : r + 1, :], 0.0))
            norm_pieces[:, r, :] = mm_nt(high, far) + mm_nt(low, far)
        for r in range(4, 8):
            norm_pieces[:, r, :] = jnp.zeros((32, LANES), f32)
        norm_view = norm_pieces.reshape(4, 2, 2, 2, 8, LANES)
        smalls = []
        for source, count in ((out_in, out_in.shape[4]), (norm_view, 8)):
            buffers, refs = refs[:7], refs[7:]
            smalls.append(Summer(here, source, 0, count, *buffers))
        for summer in smalls:
            summer.begin()

    taps[...] = jnp.zeros_like(taps)
    taps[:heads_n, :taps_total] = conv[...]
    moved = pltpu.roll(taps[...], HALO - taps_total // 2, 1)
    far_rows = (iota((TILE, TILE), 0) + iota((TILE, TILE), 1) == TILE - 1).astype(f32).astype(bf16)
    turn_cols = iota((2 * TILE, 2 * TILE), 0) + iota((2 * TILE, 2 * TILE), 1) == 2 * TILE - 1
    turn_cols = turn_cols.astype(f32).astype(bf16)
    for h in range(heads_n):
        bands[h] = band_from(moved[h : h + 1, :])
        bands[heads_n + h] = mm(mm(far_rows, bands[h].astype(bf16)).astype(bf16), turn_cols)
    gmixedT[...] = jnp.zeros_like(gmixedT)
    glandT[...] = jnp.zeros_like(glandT)
    gband[...] = jnp.zeros_like(gband)
    loads[1].wait()

    def turn(b, none):
        for i in range(block // TILE):
            rows = slice(i * TILE, i * TILE + TILE)
            col = pl.ds(pl.multiple_of(b * block + i * TILE, TILE), TILE)
            xT[:, col] = xall[b, rows, :].astype(f32).T.astype(bf16)
        return none

    lax.fori_loop(0, blocks, turn, 0)
    if gather:
        for summer in smalls:
            summer.along_y()
    for copy in arriving:
        copy.wait_recv()
    for n in (0, 2, 3):
        loads[n].wait()

    def one(c, none):
        rows = pl.ds(pl.multiple_of(c * CHUNK, CHUNK), CHUNK)
        inner = pl.ds(pl.multiple_of(c * CHUNK + HALO, HALO), CHUNK)
        alive = live_of(tokc[rows, 0:1]) > 0
        g_now = jnp.where(alive, gopad[inner, :].astype(f32), 0.0).astype(bf16)
        gopad[inner, :] = g_now
        gT = g_now.astype(f32).T.astype(bf16)
        for h in range(heads_n):
            k1 = gl1[h, rows, :]
            gk = mm_nt(g_now, mixed[h])
            k1w = k1.astype(f32)
            gl1[h, rows, :] = (k1w * (gk - jnp.sum(gk * k1w, axis=1, keepdims=True))).astype(bf16)
            e = slice(HEAD_DIM * h, HEAD_DIM * h + HEAD_DIM)
            gmixedT[e, :] += mm(gT[e, :], k1)
        return none

    lax.fori_loop(0, nchunk, one, 0)
    if gather:
        downs.second()
        ups.second()
    gmixed = gmixedT[...].T
    carried_all = carried[...]
    lane = iota((TILE, wide), 1) // HEAD_DIM
    delta = []
    for h in range(heads_n):
        rows_delta = []
        for g in range(tiles_n):
            n = h * tiles_n + g
            rows = slice(g * TILE, g * TILE + TILE)
            Z = unpack(hist[NEWTON, 1, n])
            gm = split(jnp.where(lane == h, gmixed[rows], 0.0))
            near = jnp.where(lane == h, carried_all[rows], 0.0)
            gstate[0, n] = jnp.zeros((LANDMARKS, TILE), f32)
            gstate[1, n] = pack(jnp.where(same, mm3(gm, split(near), mm_nt), 0.0))
            gc = mm3(split(Z.T), gm).astype(bf16)
            gcar[h, rows, :] = gc
            rows_delta.append(jnp.sum((gc.astype(f32) * near).T, axis=0, keepdims=True))
        delta.append(jnp.concatenate(rows_delta, axis=1))
    def three(c, none):
        rows = pl.ds(pl.multiple_of(c * CHUNK, CHUNK), CHUNK)
        v_now = v[pl.ds(pl.multiple_of(c * CHUNK + HALO, HALO), CHUNK), :]
        total = jnp.zeros((CHUNK, wide), f32)
        for h in range(heads_n):
            gc = gcar[h]
            k3 = gl3[h, rows, :]
            gk = mm_nt(v_now, gc)
            gl = (k3.astype(f32) * (gk - delta[h])).astype(bf16)
            gl3[h, rows, :] = gl
            total = total + mm(k3, gc)
            partT = qk[rows, LANES * h : LANES * h + LANES].astype(f32).T.astype(bf16)
            glandT[h, :HEAD_DIM, :] += mm(partT[:HEAD_DIM, :], gl1[h, rows, :])
            glandT[h, HEAD_DIM:, :] += mm(partT[HEAD_DIM:, :], gl)
        for part in range(CHUNK // TILE):
            i = c * (CHUNK // TILE) + part
            at = pl.ds(pl.multiple_of(i * TILE, TILE), TILE)
            now = tokc[at, 0:1]
            seg_now = seg_of(now)
            near = seg_now == segw[pl.ds(i, 1), :]
            near_back = (seg_now == segw[pl.ds(seq // TILE + i, 1), :]) & (live_of(now) > 0)
            g_window = gopad[pl.ds(pl.multiple_of(i * TILE, TILE), 2 * TILE), :]
            v_window = v[pl.ds(pl.multiple_of(i * TILE, TILE), 2 * TILE), :]
            g_tile = gopad[pl.ds(pl.multiple_of(i * TILE + HALO, HALO), TILE), :].astype(f32)
            conv = jnp.zeros((TILE, wide), f32)
            for h in range(heads_n):
                back = mm(jnp.where(near_back, bands[heads_n + h], 0.0).astype(bf16), g_window)
                conv = jnp.where(lane == h, back, conv)
                mine = jnp.where(lane == h, g_tile, 0.0).astype(bf16)
                gband[h] += jnp.where(near, mm_nt(mine, v_window), 0.0)
            gv[at, :] = (total[part * TILE : (part + 1) * TILE, :] + conv).astype(bf16)
        return none

    def unstep(r, none):
        i = NEWTON - 1 - r
        for n in range(all_tiles):
            Pm, Z, S, N = hist[i, 0, n], hist[i, 1, n], hist[i, 2, n], hist[i, 3, n]
            gP, gZ = gstate[0, n], gstate[1, n]
            Pl, Pr = left_of(Pm), packed_right(Pm, masks)
            gN = 0.25 * (tt(Pl, packed_right(gP, masks)) + packed_tn(Z, gZ))
            gS = 7.0 * gN - tt(left_of(gN), Pr)
            both = 0.25 * tt(
                jnp.concatenate([left_of(gP), left_of(gZ)], axis=0), packed_right(N, masks)
            )
            gstate[1, n] = both[LANDMARKS:]
            gstate[0, n] = (
                both[:LANDMARKS]
                - 15.0 * gN
                - tt(left_of(S), packed_right(gN, masks))
                + tt(left_of(gS), Pr)
                + tt(Pl, packed_right(gS, masks))
            )
        return none

    def both(i, none):
        unstep(i, none)
        return three(i, none)

    third = NEWTON // 3
    lax.fori_loop(0, 2 * third, both, 0)
    if gather:
        downs.third()
        for summer in smalls:
            summer.along_z()
    lax.fori_loop(2 * third, NEWTON, both, 0)
    lax.fori_loop(NEWTON, nchunk, three, 0)
    if gather:
        downs.fourth()
        ups.third()

    conv_out[...] = jnp.zeros_like(conv_out)
    for h in range(heads_n):
        conv_out[h : h + 1, :] = diagonal_sums(gband[h])
    piece_v[...] = mm(xT[...], gv[...]).astype(bf16)
    others = [(dz, dy) for dz in range(4) for dy in range(2) if dz or dy] if gather else []
    sent_conv = []
    for k, (dz, dy) in enumerate(others):
        sent_conv.append(start(push(conv_out, in_conv.at[k], csem, k, here.dp_at(dz, dy), here.t)))

    def piece_along_y(piece, landing, sems):
        view = piece.reshape((4, 2) + landing.shape[1:])
        return start(push(view.at[:, 1 - here.y], landing, sems, 0, here.dp_at(0, 1), here.t))

    def piece_along_z(copy, piece, landing, last_landing, sems):
        view = piece.reshape((4, 2) + landing.shape[1:])
        copy.wait_recv()
        for z in range(4):
            landing[z] = landing[z] + view[z, here.y]
        return [
            start(push(landing.at[(here.z + dz) % 4], last_landing.at[dz - 1], sems, dz, here.dp_at(dz, 0), here.t))
            for dz in (1, 2, 3)
        ]

    if gather:
        v_along_y = piece_along_y(piece_v, in_v, v_sems)

    for h in range(heads_n):
        sums_land = pltpu.roll(glandT[h].T * scaling, HEAD_DIM, 1)
        k0, q1, _ = landmark_parts(land[:, LANES * h : LANES * h + LANES])
        for g in range(tiles_n):
            n = h * tiles_n + g
            rows = slice(g * TILE, g * TILE + TILE)
            A = Ain[n]
            factor, colsum, tops = newton_start(A)
            gP, gW = unpack(gstate[0, n]), unpack(gstate[1, n]).T
            GA = tt(left_of(gP + gP.T), right_of(A))
            gA = factor * (GA + gW)
            gf_cols = jnp.sum((0.5 * GA + gW) * A, axis=0, keepdims=True)
            first = iota(colsum.shape, 1) < LANDMARKS
            gcol = jnp.zeros_like(colsum)
            for k in range(2):
                mine = first if k == 0 else jnp.logical_not(first)
                gf = jnp.sum(jnp.where(mine, gf_cols, 0.0), axis=1, keepdims=True)
                top = tops[k]
                is_top = mine & (colsum == top)
                ties = jnp.sum(is_top.astype(f32), axis=1, keepdims=True)
                share = jnp.where(top > 1.0, 1.0, jnp.where(top == 1.0, 0.5, 0.0))
                floor = jnp.maximum(top, 1.0)
                gcol = jnp.where(is_top, -gf * share / (floor * floor * ties), gcol)
            gA = (gA + gcol) * live_cols[g]
            gl2 = A * (gA - jnp.sum(gA * A, axis=1, keepdims=True)) * scaling
            gl2 = jnp.where(same & (live_row[:, rows] > 0), gl2, 0.0)
            g_land = mm3(split(gl2), split(k0[rows])) + mm3(split(gl2.T), split(q1[rows]))
            g_land = (g_land + sums_land[rows]) / counts[rows, :]
            low = slice(2 * nslot + g * TILE, 2 * nslot + g * TILE + TILE)
            wback[h, low, :] = jnp.concatenate(split(g_land), axis=1)
        wback[h, :nslot, :] = jnp.concatenate(split(k0 * scaling), axis=1)
        wback[h, nslot : 2 * nslot, :] = jnp.concatenate(split(q1 * scaling), axis=1)

    def last(b, k):
        row = pl.multiple_of(b * block + k * CHUNK, CHUNK)
        rows = pl.ds(row, CHUNK)
        hot = (slot_of(tokc[rows, 0:1]) == iota((CHUNK, nslot), 1)).astype(f32).astype(bf16)
        for h in range(heads_n):
            both = (
                mm(gl1[h, rows, :], wback[h, :nslot, :])
                + mm(gl3[h, rows, :], wback[h, nslot : 2 * nslot, :])
                + mm(hot, wback[h, 2 * nslot :, :])
            )
            gqk[rows, LANES * h : LANES * h + LANES] = (both[:, :LANES] + both[:, LANES:]).astype(bf16)
        return mm_nt(gqk[rows, :], wfull[:, : LANES * heads_n]) + mm_nt(
            gv[rows, :], wfull[:, LANES * heads_n :]
        )

    def chunk_rows(k):
        return pl.ds(k * CHUNK, CHUNK)

    from_sibling, from_across, own_from_sibling = [], [], []
    for k in range(per_block):
        part_out[0, chunk_rows(k), :] = last(here.diagonal, k).astype(bf16)
        from_sibling.append(
            start(push(part_out.at[0, chunk_rows(k)], part_in.at[0, chunk_rows(k)], psem, k, here.dp, here.sibling))
        )
    for k in range(per_block):
        got = last(here.across, k)
        from_sibling[k].wait_recv()
        part_sum[chunk_rows(k), :] = (got + part_in[0, chunk_rows(k), :].astype(f32)).astype(bf16)
        from_across.append(
            start(push(part_sum.at[chunk_rows(k)], part_x.at[chunk_rows(k)], psem, per_block + k, here.dp, here.across))
        )
    if gather:
        for summer in smalls:
            summer.along_x()
        sent_v = piece_along_z(v_along_y, piece_v, in_v, in_vz, v_sems)
    for k in range(per_block):
        part_out[1, chunk_rows(k), :] = last(here.sibling, k).astype(bf16)
        own_from_sibling.append(
            start(push(part_out.at[1, chunk_rows(k)], part_in.at[1, chunk_rows(k)], psem, 2 * per_block + k, here.dp, here.sibling))
        )
    for k in range(per_block):
        input_grad[chunk_rows(k), :] = last(here.t, k) + gpre[chunk_rows(k), :]

    piece_q[...] = mm(xT[...], gqk[...]).astype(bf16)
    if gather:
        q_along_y = piece_along_y(piece_q, in_q, q_sems)
        ups.finish(up_out)
        downs.finish(down_out)
        sent_q = piece_along_z(q_along_y, piece_q, in_q, in_qz, q_sems)
    for k in range(per_block):
        own_from_sibling[k].wait_recv()
        from_across[k].wait_recv()
        input_grad[chunk_rows(k), :] += part_in[1, chunk_rows(k), :].astype(f32) + part_x[
            chunk_rows(k), :
        ].astype(f32)
    if gather:
        for copy in sent_v + sent_q + sent_conv:
            copy.wait_recv()
        total_v = in_v[here.z].astype(f32)
        total_q = in_q[here.z].astype(f32)
        for k in range(3):
            total_v = total_v + in_vz[k].astype(f32)
            total_q = total_q + in_qz[k].astype(f32)
        total_conv = conv_out[...]
        for k in range(len(others)):
            total_conv = total_conv + in_conv[k]
        for h in range(heads_n):
            e = slice(HEAD_DIM * h, HEAD_DIM * h + HEAD_DIM)
            one = total_q[:, LANES * h : LANES * h + LANES]
            gw[0, :, e] = one[:, :HEAD_DIM]
            gw[1, :, e] = one[:, HEAD_DIM:]
        gw[2] = total_v[:, : heads_n * HEAD_DIM]
        first = HALO - taps_total // 2
        turned = pltpu.roll(total_conv, 2 * TILE - first, 1)
        gconv[...] = turned[:heads_n, :taps_total]
        smalls[0].finish(out_sum)
        out_out[...] = out_sum[:, : heads_n * HEAD_DIM].T
        smalls[1].finish(norm_sum)
        gain_out[...] = norm_sum[0:2, :length]
        bias_out[...] = norm_sum[2:4, :length]
    else:
        gw[:, : LANES * heads_n] = piece_q[...].astype(f32)
        gw[:, LANES * heads_n :] = piece_v[...].astype(f32)
        gconv[...] = conv_out[...]
    for copy in copies:
        copy.wait_send()


def attention_backward(gsend, xall, wfull, tokc, segw, qk, v, kern1, kern3, land, counts, weights,
                       mixed, carried, conv, slot_live, gpre, hist, sources, taps_total, depth):
    blocks, block, wide = gsend.shape
    heads_n, seq, nslot = kern1.shape
    feat = wfull.shape[0]
    all_tiles = weights.shape[0]
    shape = jax.ShapeDtypeStruct
    gather = len(sources) > 0
    width = heads_n * HEAD_DIM
    outs = [shape((block, feat), f32)]
    if gather:
        hidden_n = sources[0].shape[2]
        outs += [
            shape((3, depth, width), f32),
            shape((heads_n, taps_total), f32),
            shape((hidden_n, feat), f32),
            shape((hidden_n, feat), f32),
            shape((width, depth), f32),
            shape((2, feat // 32), f32),
            shape((2, feat // 32), f32),
        ]
    else:
        outs += [shape((feat, wfull.shape[1]), f32), shape((8, 2 * TILE), f32)]
    others = 7 if gather else 1
    per_block = block // CHUNK
    scratch = [
        pltpu.VMEM((8, 2 * TILE), f32),
        pltpu.VMEM((heads_n, seq, nslot), bf16),
        pltpu.VMEM((heads_n, seq, nslot), bf16),
        pltpu.VMEM(xall.shape, bf16),
        pltpu.VMEM((feat, seq), bf16),
        pltpu.VMEM((seq + 2 * HALO, wide), bf16),
        pltpu.VMEM((seq, LANES * heads_n), bf16),
        pltpu.VMEM((seq, wide), bf16),
        pltpu.VMEM((heads_n, TILE, 2 * TILE), f32),
        pltpu.VMEM((2 * heads_n, TILE, 2 * TILE), f32),
        pltpu.VMEM((wide, nslot), f32),
        pltpu.VMEM((heads_n, LANES, nslot), f32),
        pltpu.VMEM((NEWTON + 1, 4, all_tiles, LANDMARKS, TILE), f32),
        pltpu.VMEM((2, all_tiles, LANDMARKS, TILE), f32),
        pltpu.VMEM((heads_n, nslot, wide), bf16),
        pltpu.VMEM((heads_n, 3 * nslot, 256), bf16),
        pltpu.VMEM((2, block, feat), bf16),
        pltpu.VMEM((2, block, feat), bf16),
        pltpu.VMEM((block, feat), bf16),
        pltpu.VMEM((block, feat), bf16),
        pltpu.VMEM((feat, wide), bf16),
        pltpu.VMEM((feat, LANES * heads_n), bf16),
        pltpu.VMEM((4, depth if gather else 16, wide), bf16),
        pltpu.VMEM((4, depth if gather else 16, LANES * heads_n), bf16),
        pltpu.VMEM((others, 8, 2 * TILE), f32),
        pltpu.VMEM((8, 2 * TILE), f32),
        dma(2, 3),
        dma(4),
        dma(2, 3 * per_block),
        dma(2, others),
    ]
    if gather:
        scratch += [
            pltpu.VMEM((depth, wide), f32),
            pltpu.VMEM((8, LANES), f32),
            pltpu.VMEM((32, 8, LANES), f32),
            dma(2, 4),
            dma(2, 4),
            pltpu.VMEM((3, depth, wide), bf16),
            pltpu.VMEM((3, depth, LANES * heads_n), bf16),
            pltpu.VMEM((2, 2, hidden_n, feat), bf16),
            pltpu.VMEM((3, 2, hidden_n, feat), bf16),
            pltpu.VMEM((hidden_n, feat), bf16),
            dma(2, 6),
            pltpu.VMEM((4, hidden_n, feat), bf16),
            pltpu.VMEM((3, hidden_n, feat), bf16),
            pltpu.VMEM((2, 2, hidden_n, feat), bf16),
            dma(2, 9),
        ]
        for count, lanes, kind in ((depth, wide, bf16), (8, LANES, f32)):
            scratch += [
                pltpu.VMEM((4, 2, 2, count, lanes), kind),
                pltpu.VMEM((4, 2, 2, count, lanes), kind),
                pltpu.VMEM((4, 2, count, lanes), kind),
                pltpu.VMEM((3, 2, count, lanes), kind),
                pltpu.VMEM((count, lanes), kind),
                dma(2, SUMMER_SEMS),
                pltpu.SemaphoreType.DMA,
            ]
    specs = [VMEM, ANY] + [VMEM] * 5 + [ANY, ANY] + [VMEM] * 8 + [ANY]
    if gather:
        specs += [VMEM] * 4 + [ANY, VMEM]
    return pl.pallas_call(
        functools.partial(backward_body, gather, taps_total),
        out_shape=tuple(outs),
        in_specs=specs,
        out_specs=tuple([VMEM] * len(outs)),
        scratch_shapes=scratch,
        compiler_params=pltpu.CompilerParams(
            vmem_limit_bytes=LIMIT, collective_id=3 if gather else 4, has_side_effects=True
        ),
        name="attention_backward",
    )(gsend, xall, wfull, tokc, segw, qk, v, kern1, kern3, land, counts, weights, mixed, carried,
      conv, slot_live, gpre, hist, *sources)


def hand_over_body(*refs):
    half = len(refs) // 2
    for src, dst in zip(refs[:half], refs[half:]):
        dst[...] = src[...]


def hand_over(*arrays):
    return pl.pallas_call(
        hand_over_body,
        out_shape=tuple(jax.ShapeDtypeStruct(a.shape, a.dtype) for a in arrays),
        in_specs=[VMEM] * len(arrays),
        out_specs=tuple([VMEM] * len(arrays)),
        name="hand_over",
    )(*arrays)


def split_up(shard, dim, length):
    before, after = (shard.shape[:dim], shard.shape[dim + 1 :])
    return jnp.moveaxis(shard.reshape(*before, length, -1, *after), dim, 0)


def exchange(pieces, axis):
    return lax.all_to_all(pieces, axis, split_axis=0, concat_axis=0, tiled=True)


def per_device(
    tokens,
    w_qkv,
    w_out,
    conv_weight,
    w_up,
    w_down,
    norm_gain,
    norm_bias,
    cotangent,
    seg_ids,
    landmark_slot,
    token_live,
    slot_live,
):
    both = ("dp", "tensor")
    dp_size, blocks = lax.axis_size("dp"), lax.axis_size("tensor")
    devices = dp_size * blocks
    heads_n, taps_total = conv_weight.shape
    block, feat = tokens.shape
    depth = w_qkv.shape[1]
    width = heads_n * HEAD_DIM
    wide = -(-width // 256) * 256
    hidden_n = w_up.shape[1]
    docs = slot_live.shape[1] // LANDMARKS
    direct = dp_size == 8 and blocks == 4 and depth % 16 == 0 and hidden_n % 32 == 0

    first = HALO - taps_total // 2
    weight = w_qkv if direct else lax.all_gather(w_qkv, "dp", axis=1, tiled=True)
    extra = (w_up.T, w_down, w_out, norm_gain, norm_bias) if direct else ()
    got = attention_forward(
        tokens, weight, conv_weight, seg_ids, landmark_slot, token_live, slot_live,
        extra, heads_n, blocks, taps_total,
    )
    (
        xall, wfull, tokc, segw, qk, v, kern1, kern3, land, counts, weights, mixed, carried, heads, proxies,
        hist,
    ) = got[:16]
    if direct:
        up_all, down_all, out_all, norms = got[16:]
        out_all = out_all.reshape(blocks, feat, wide)
    else:
        up_all = lax.all_gather(w_up.T, both, axis=0, tiled=True)
        down_all = lax.all_gather(w_down, both, axis=0, tiled=True)
        out_all = lax.all_gather(lax.all_gather(w_out.T, "dp", axis=0, tiled=True), "tensor", axis=0)
        out_all = jnp.pad(out_all, ((0, 0), (0, 0), (0, wide - width)))
        norms = jnp.concatenate([norm_gain, norm_bias, jnp.zeros_like(norm_gain), jnp.zeros_like(norm_bias)])
        norms = lax.all_gather(norms, both, axis=1, tiled=True).astype(f32)
    if direct:
        got = feed_direct(tokens, cotangent, heads, norms, out_all, up_all, down_all, depth)
        layer_out, gsend, grad_pre, norm_grads, out_pieces = got[:5]
        sources = got[5:] + (out_pieces, norm_grads)
    else:
        layer_out, gsend, grad_pre, norm_grads, out_pieces, up_pieces, down_pieces = feed_forward(
            direct, tokens, cotangent, heads, norms, out_all, up_all, down_all, depth
        )
        sources = ()
    got = attention_backward(
        gsend, xall, wfull, tokc, segw, qk, v, kern1, kern3, land, counts, weights,
        mixed, carried, conv_weight, slot_live, grad_pre, hist, sources, taps_total, depth,
    )
    if direct:
        (
            input_grad, grad_qkv, grad_conv, grad_up, grad_down, grad_out, grad_gain, grad_bias, proxies,
        ) = hand_over(*got, proxies)
        grad_up = grad_up.T
    else:
        input_grad, grad_w, grad_conv = got
        grad_w = exchange(grad_w.astype(bf16).reshape(dp_size, depth, -1), "dp").astype(f32).sum(axis=0)
        pairs = grad_w[:, : LANES * heads_n].reshape(depth, heads_n, 2, HEAD_DIM)
        grad_qkv = jnp.concatenate(
            [
                jnp.moveaxis(pairs, 2, 0).reshape(2, depth, width),
                grad_w[None, :, LANES * heads_n : LANES * heads_n + width],
            ]
        )
        grad_conv = lax.psum(grad_conv, "dp")[:heads_n, first : first + taps_total]
        grad_up = lax.psum_scatter(up_pieces, both, scatter_dimension=0, tiled=True).astype(f32).T
        grad_down = lax.psum_scatter(down_pieces, both, scatter_dimension=0, tiled=True).astype(f32)
        out_pieces = out_pieces[:, :, :width].reshape(blocks, dp_size, depth, width)
        out_pieces = jnp.swapaxes(out_pieces, 0, 1).reshape(devices, depth, width)
        grad_out = lax.psum_scatter(out_pieces, both, scatter_dimension=0, tiled=False).astype(f32).T
        norm_sum = exchange(split_up(norm_grads[:4], 1, devices), both).sum(axis=0)
        grad_gain, grad_bias = norm_sum[:2], norm_sum[2:]
    return (
        layer_out,
        input_grad,
        grad_qkv,
        grad_out,
        grad_conv,
        grad_up,
        grad_down,
        grad_gain,
        grad_bias,
        jnp.transpose(proxies, (1, 2, 0)),
    )


def solution(mesh):
    return jax.shard_map(
        per_device,
        mesh=mesh,
        in_specs=(
            P(("dp", "tensor"), None),
            P(None, "dp", "tensor"),
            P("tensor", "dp"),
            P("tensor", None),
            P(None, ("dp", "tensor")),
            P(("dp", "tensor"), None),
            P(None, ("dp", "tensor")),
            P(None, ("dp", "tensor")),
            P(("dp", "tensor"), None),
            P("dp", None),
            P("dp", None),
            P("dp", None),
            P("dp", None),
        ),
        out_specs=(
            P(("dp", "tensor"), None),
            P(("dp", "tensor"), None),
            P(None, "dp", "tensor"),
            P("tensor", "dp"),
            P("tensor", None),
            P(None, ("dp", "tensor")),
            P(("dp", "tensor"), None),
            P(None, ("dp", "tensor")),
            P(None, ("dp", "tensor")),
            P("dp", None, "tensor"),
        ),
        check_vma=False,
    )
```

```python
import functools
import math

import jax
import jax.numpy as jnp
from jax import lax
from jax.experimental import pallas as pl
from jax.experimental.pallas import tpu as pltpu
from jax.sharding import PartitionSpec as P

HEAD_DIM = 64
LANDMARKS = 64
NEWTON = 6
TILE = 128
HALO = TILE // 2
CHUNK = 256
LANES = 128
bf16 = jnp.bfloat16
f32 = jnp.float32
i32 = jnp.int32
norm_epsilon = 1e-05
MESH = pl.DeviceIdType.MESH
LIMIT = 62 * 2**20


def mm(a, b):
    return lax.dot_general(a, b, (((1,), (0,)), ((), ())), preferred_element_type=f32)


def mm_nt(a, b):
    return lax.dot_general(a, b, (((1,), (1,)), ((), ())), preferred_element_type=f32)


def split(a):
    high = a.astype(bf16)
    return high, (a - high.astype(f32)).astype(bf16)


def mm3(a, b, dot=mm):
    return dot(a[0], b[0]) + (dot(a[0], b[1]) + dot(a[1], b[0]))


def left_of(a):
    return jnp.concatenate(split(a), axis=1)


def right_of(b):
    high, low = split(b)
    top = jnp.concatenate([high, low], axis=1)
    bottom = jnp.concatenate([jnp.zeros_like(high), high], axis=1)
    return jnp.concatenate([top, bottom], axis=0)


def right_nt(b):
    high, low = split(b)
    top = jnp.concatenate([high, jnp.zeros_like(high)], axis=1)
    bottom = jnp.concatenate([low, high], axis=1)
    return jnp.concatenate([top, bottom], axis=0)


def tt(left, right):
    both = mm(left, right)
    return both[:, :TILE] + both[:, TILE:]


def tt_nt(left, right):
    both = mm_nt(left, right)
    return both[:, :TILE] + both[:, TILE:]


def iota(shape, dim):
    return lax.broadcasted_iota(i32, shape, dim)


def tile_same():
    shape = (TILE, TILE)
    return iota(shape, 0) // LANDMARKS == iota(shape, 1) // LANDMARKS


def tile_eye():
    shape = (TILE, TILE)
    return (iota(shape, 0) == iota(shape, 1)).astype(f32)


def pack(tile):
    return tile[:LANDMARKS] + tile[LANDMARKS:]


def unpack(packed):
    first = iota(packed.shape, 1) < LANDMARKS
    return jnp.concatenate([jnp.where(first, packed, 0.0), jnp.where(first, 0.0, packed)], axis=0)


def landmark_parts(land):
    first = iota(land.shape, 1) < HEAD_DIM
    turned = pltpu.roll(land, HEAD_DIM, 1)
    return jnp.where(first, turned, 0.0), jnp.where(first, 0.0, turned), jnp.where(first, land, 0.0)


def lane_masks():
    first = (iota((LANDMARKS, TILE), 1) < LANDMARKS).astype(f32)
    return first.astype(bf16), (1.0 - first).astype(bf16)


def packed_eye():
    shape = (LANDMARKS, TILE)
    return (iota(shape, 0) == iota(shape, 1) % LANDMARKS).astype(f32)


def packed_right(b, masks):
    high, low = split(b)
    high = jnp.concatenate([high * masks[0], high * masks[1]], axis=0)
    low = jnp.concatenate([low * masks[0], low * masks[1]], axis=0)
    top = jnp.concatenate([high, low], axis=1)
    bottom = jnp.concatenate([jnp.zeros_like(high), high], axis=1)
    return jnp.concatenate([top, bottom], axis=0)


def packed_tn(a, b):
    (ah, al), (bh, bl) = split(a), split(b)
    both = lax.dot_general(
        jnp.concatenate([ah, al, ah], axis=0),
        jnp.concatenate([bh, bh, bl], axis=0),
        (((0,), (0,)), ((), ())),
        preferred_element_type=f32,
    )
    first = iota(a.shape, 1) < LANDMARKS
    return jnp.where(first, both[:LANDMARKS], both[LANDMARKS:])


def newton_stages(hist, i, ident, masks):
    tiles = range(hist.shape[2])
    P = [hist[i, 0, n] for n in tiles]
    Pl, Pr = [left_of(p) for p in P], [packed_right(p, masks) for p in P]
    S = [tt(Pl[n], Pr[n]) for n in tiles]
    yield
    N = [13.0 * ident - 15.0 * P[n] + 7.0 * S[n] - tt(left_of(S[n]), Pr[n]) for n in tiles]
    yield
    for n in tiles:
        hist[i, 2, n] = S[n]
        hist[i, 3, n] = N[n]
        rows = jnp.concatenate([Pl[n], left_of(hist[i, 1, n])], axis=0)
        both = 0.25 * tt(rows, packed_right(N[n], masks))
        hist[i + 1, 0, n] = both[:LANDMARKS]
        hist[i + 1, 1, n] = both[LANDMARKS:]
    yield


def newton_back_stages(hist, gstate, i, masks):
    tiles = range(hist.shape[2])
    gP, gZ = [gstate[0, n] for n in tiles], [gstate[1, n] for n in tiles]
    P = [hist[i, 0, n] for n in tiles]
    Pl, Pr = [left_of(p) for p in P], [packed_right(p, masks) for p in P]
    gN = [
        0.25 * (tt(Pl[n], packed_right(gP[n], masks)) + packed_tn(hist[i, 1, n], gZ[n])) for n in tiles
    ]
    both = [
        0.25
        * tt(
            jnp.concatenate([left_of(gP[n]), left_of(gZ[n])], axis=0),
            packed_right(hist[i, 3, n], masks),
        )
        for n in tiles
    ]
    yield
    gS = [7.0 * gN[n] - tt(left_of(gN[n]), Pr[n]) for n in tiles]
    kept = [
        both[n][:LANDMARKS] - 15.0 * gN[n] - tt(left_of(hist[i, 2, n]), packed_right(gN[n], masks))
        for n in tiles
    ]
    yield
    for n in tiles:
        gstate[1, n] = both[n][LANDMARKS:]
        gstate[0, n] = kept[n] + tt(left_of(gS[n]), Pr[n]) + tt(Pl[n], packed_right(gS[n], masks))
    yield


def newton_start(A):
    colsum = jnp.sum(A, axis=0, keepdims=True)
    first = iota(colsum.shape, 1) < LANDMARKS
    tops = [
        jnp.max(jnp.where(first, colsum, 0.0), axis=1, keepdims=True),
        jnp.max(jnp.where(first, 0.0, colsum), axis=1, keepdims=True),
    ]
    factor = 1.0 / jnp.maximum(jnp.where(first, tops[0], tops[1]), 1.0)
    return factor, colsum, tops


def column(row):
    return jnp.broadcast_to(row, (LANES, LANES)).T


def band_from(row):
    wide = jnp.broadcast_to(row, (TILE, 2 * TILE))
    return pltpu.roll(wide, 0, 1, stride=1, stride_axis=0)


def diagonal_sums(band):
    where = iota(band.shape, 0)
    step = 1
    while step < TILE:
        turned = pltpu.roll(band, 2 * TILE - step, 1)
        band = jnp.where((where // step) % 2 == 1, turned, band)
        step *= 2
    return jnp.sum(band, axis=0, keepdims=True)


def seg_of(code):
    return (code // 512) % 8


def live_of(code):
    return code // 4096


def slot_of(code):
    return code % 512


class Place:
    def __init__(self):
        self.dp = lax.axis_index("dp")
        self.t = lax.axis_index("tensor")
        self.x = self.t // 2
        self.c = self.t % 2
        self.sibling = self.x * 2 + 1 - self.c
        self.across = (1 - self.x) * 2 + self.c
        self.diagonal = (1 - self.x) * 2 + 1 - self.c
        self.z = self.dp // 2
        self.y = self.dp % 2

    def tensor_peers(self):
        return [(self.dp, t) for t in (self.sibling, self.across, self.diagonal)]

    def dp_at(self, turn_z, turn_y):
        return ((self.z + turn_z) % 4) * 2 + (self.y + turn_y) % 2


def greet(peers):
    barrier = pltpu.get_barrier_semaphore()
    for peer in peers:
        pl.semaphore_signal(barrier, inc=1, device_id=peer, device_id_type=MESH)
    pl.semaphore_wait(barrier, len(peers))


def push(src, dst, sems, index, dp, t):
    return pltpu.make_async_remote_copy(
        src_ref=src,
        dst_ref=dst,
        send_sem=sems.at[0, index],
        recv_sem=sems.at[1, index],
        device_id=(dp, t),
        device_id_type=MESH,
    )


class Spreader:
    def __init__(self, here, shard, whole, sems, local, by_x, by_rows=False):
        self.here, self.shard, self.whole, self.sems, self.local = here, shard, whole, sems, local
        self.by_rows, self.by_x = by_rows, by_x
        first, last = (here.dp, here.across), (here.dp_at(0, 1), here.t)
        self.first, self.last = (first, last) if by_x else (last, first)
        self.copies = []
        self.from_z, self.from_first, self.from_last, self.from_core = {}, {}, {}, []

    def at(self, z, y, x):
        c = self.here.c
        if not self.by_rows:
            return self.whole.at[z, y, x, c]
        depth = self.shard.shape[0]
        rows = pl.ds(pl.multiple_of((z * 2 + y) * depth, 16), depth)
        return self.whole.at[x, c, rows]

    def one(self, dz):
        return self.at((self.here.z + 4 - dz) % 4, self.here.y, self.here.x)

    def pair(self, dz, turned):
        here, z = self.here, (self.here.z + 4 - dz) % 4
        if self.by_x:
            return self.at(z, (here.y + turned) % 2, slice(None))
        return self.at(z, slice(None), (here.x + turned) % 2)

    def push(self, src, dst, index, place):
        copy = push(src, dst, self.sems, index, *place)
        copy.start()
        self.copies.append(copy)
        return copy

    def begin(self):
        self.kept = pltpu.make_async_copy(self.shard, self.one(0), self.local)
        self.kept.start()
        self.from_first[0] = self.push(self.shard, self.one(0), 3, self.first)

    def along_z(self, dz):
        here = self.here
        self.from_z[dz] = self.push(self.shard, self.one(0), dz - 1, (here.dp_at(dz, 0), here.t))

    def along_first(self, dz):
        self.from_z[dz].wait_recv()
        self.from_first[dz] = self.push(self.one(dz), self.one(dz), 3 + dz, self.first)

    def along_last(self, dz):
        if dz == 0:
            self.kept.wait()
        self.from_first[dz].wait_recv()
        got = self.pair(dz, 0)
        self.from_last[dz] = self.push(got, got, 7 + dz, self.last)
        self.from_core.append(self.push(got, got, 11 + dz, (self.here.dp, self.here.sibling)))

    def to_core(self, dz):
        self.from_last[dz].wait_recv()
        got = self.pair(dz, 1)
        self.from_core.append(self.push(got, got, 15 + dz, (self.here.dp, self.here.sibling)))

    def finish(self):
        for dz in self.from_first:
            if dz not in self.from_last:
                self.from_first[dz].wait_recv()
        for copy in self.from_core:
            copy.wait_recv()
        for copy in self.copies:
            copy.wait_send()


LATE = (1, 3)


def spread_lanes(length, whole):
    shape = (LANES, whole)
    return (iota(shape, 0) == iota(shape, 1) % length).astype(f32)


def forward_body(gather, taps_total, *refs):
    (x, w, conv, seg, slot, live, slot_live), refs = refs[:7], refs[7:]
    if gather:
        (w_up, w_down, w_out, gain, bias), refs = refs[:5], refs[5:]
    (
        xall_out, wfull_out, tokc, segw, qk_out, v_out, kern1_out, kern3_out,
        land, counts, Aout, mixed, carried, heads, prox, hist_out,
    ) = refs[:16]
    refs = refs[16:]
    if gather:
        (up_all, down_all, out_all, norms), refs = refs[:4], refs[4:]
    (
        xall, wfull, qk, v, kern1, kern3,
        wsh, wlog, l3, carriedT, hist, bands, hsend, segp, taps, xsem, wsem, hsem, osem,
    ) = refs[:19]
    refs = refs[19:]
    keeping = []

    def keep(src, dst):
        copy = pltpu.make_async_copy(src, dst, osem.at[len(keeping)])
        copy.start()
        keeping.append(copy)

    here = Place()
    block = x.shape[0]
    blocks = xall.shape[0]
    seq = block * blocks
    heads_n = qk.shape[1] // LANES
    nslot = land.shape[0]
    wide = v.shape[1]
    nchunk = seq // CHUNK
    per_block = block // CHUNK
    tiles_n = nslot // TILE
    width = heads_n * HEAD_DIM
    scaling = 1.0 / math.sqrt(HEAD_DIM)

    depth = w.shape[1]
    parts = []
    for h in range(heads_n):
        e = slice(HEAD_DIM * h, HEAD_DIM * h + HEAD_DIM)
        parts += [w[0, :, e], w[1, :, e]]
    parts += [w[2], jnp.zeros((depth, wide - width), bf16)]
    wsh[...] = jnp.concatenate(parts, axis=1)

    peers = here.tensor_peers()
    if gather:
        peers = peers + [(here.dp_at(dz, 0), here.t) for dz in (1, 2, 3)] + [(here.dp_at(0, 1), here.t)]
        out_sh, norm_sh, norm_all = refs[:3]
        out_sh[...] = jnp.concatenate(
            [w_out[...].astype(f32).T, jnp.zeros((depth, wide - width), f32)], axis=1
        ).astype(bf16)
        norm_sh[...] = jnp.zeros_like(norm_sh)
        norm_sh[0:2, : gain.shape[1]] = gain[...].astype(f32)
        norm_sh[2:4, : gain.shape[1]] = bias[...].astype(f32)
        sems = refs[3:]
        spread_out = Spreader(here, out_sh, out_all, sems[2], sems[3], True, by_rows=True)
        spread_norm = Spreader(here, norm_sh, norm_all, sems[4], sems[5], True)
        whole = (spread_out, spread_norm)
        partly = (
            Spreader(here, w_up, up_all, sems[0], sems[1], True),
            Spreader(here, w_down, down_all, sems[6], sems[7], False),
        )
        spreads = whole + partly
    greet(peers)

    copies = []
    pieces = block // TILE

    def start(copy):
        copy.start()
        copies.append(copy)
        return copy

    crossing = [
        start(push(x.at[pl.ds(p * TILE, TILE)], xall.at[here.t, pl.ds(p * TILE, TILE)], xsem, p, here.dp, here.across))
        for p in range(pieces)
    ]
    beside = start(push(x, xall.at[here.t], xsem, pieces, here.dp, here.sibling))
    if gather:
        mine = wfull.at[pl.ds(pl.multiple_of(here.dp * depth, 16), depth)]
        along = [start(push(wsh, mine, wsem, dz, here.dp_at(dz, 0), here.t)) for dz in (1, 2, 3)]
        along = [start(push(wsh, mine, wsem, 0, here.dp_at(0, 1), here.t))] + along
        wfull[pl.ds(pl.multiple_of(here.dp * depth, 16), depth), :] = wsh[...]
    else:
        wfull[...] = wsh[...]
    xall[here.t] = x[...]

    segp[...] = jnp.full(segp.shape, -1, i32)
    segp[0:1, TILE : TILE + seq] = jnp.where(live[...] > 0, seg[...], -1)
    segp[1:2, TILE : TILE + seq] = seg[...]
    code = (slot[...] + 512 * seg[...] + 4096 * live[...]).astype(f32)
    for i in range(seq // TILE):
        lanes = slice(i * TILE, i * TILE + TILE)
        tokc[lanes, :] = column(code[:, lanes]).astype(i32)
        near = pltpu.roll(segp[:, i * TILE : i * TILE + 3 * TILE], 3 * TILE - HALO, 1)
        segw[i : i + 1, :] = near[0:1, : 2 * TILE]
        segw[seq // TILE + i : seq // TILE + i + 1, :] = near[1:2, : 2 * TILE]
    taps[...] = jnp.zeros_like(taps)
    taps[:heads_n, :taps_total] = conv[...]
    moved = pltpu.roll(taps[...], HALO - taps_total // 2, 1)
    for h in range(heads_n):
        bands[h] = band_from(moved[h : h + 1, :])
    doc_row = iota((1, nslot), 1) // LANDMARKS
    live_row = slot_live[...]
    live_cols = [column(live_row[:, g * TILE : (g + 1) * TILE].astype(f32)) for g in range(tiles_n)]
    v[0:HALO, :] = jnp.zeros((HALO, wide), bf16)
    v[seq + HALO : seq + 2 * HALO, :] = jnp.zeros((HALO, wide), bf16)

    if gather:
        along[0].wait_recv()
        for dz in (1, 2, 3):
            along[dz].wait_recv()
            got = wfull.at[pl.ds(pl.multiple_of(here.dp_at(4 - dz, 0) * depth, 16), depth)]
            along.append(start(push(got, got, wsem, 3 + dz, here.dp_at(0, 1), here.t)))
        for spread in spreads:
            spread.begin()
            spread.along_z(2)
        for dz in (1, 2, 3):
            along[3 + dz].wait_recv()

    def project(b, carry):
        def one(i, carry):
            acc, cnt = carry
            c = b * per_block + i
            rows = pl.ds(pl.multiple_of(c * CHUNK, CHUNK), CHUNK)
            out = mm(xall[b, pl.ds(pl.multiple_of(i * CHUNK, CHUNK), CHUNK), :], wfull[...])
            qk_now = out[:, : LANES * heads_n].astype(bf16)
            qk[rows, :] = qk_now
            v[pl.ds(pl.multiple_of(c * CHUNK + HALO, HALO), CHUNK), :] = out[:, LANES * heads_n :].astype(bf16)
            slot_now = slot[:, pl.ds(pl.multiple_of(c * CHUNK, CHUNK), CHUNK)]
            hot = (slot_now == iota((nslot, CHUNK), 0)).astype(f32)
            return acc + mm(hot.astype(bf16), qk_now), cnt + jnp.sum(hot, axis=1, keepdims=True)

        return lax.fori_loop(0, per_block, one, carry)

    carry = (jnp.zeros((nslot, LANES * heads_n), f32), jnp.zeros((nslot, 1), f32))
    carry = project(here.t, carry)
    beside.wait_recv()
    carry = project(here.sibling, carry)
    passed = []
    for p in range(pieces):
        crossing[p].wait_recv()
        got = xall.at[here.across, pl.ds(p * TILE, TILE)]
        passed.append(start(push(got, got, xsem, pieces + 1 + p, here.dp, here.sibling)))
    carry = project(here.across, carry)
    for p in range(pieces):
        passed[p].wait_recv()
    acc, cnt = project(here.diagonal, carry)
    cnt = jnp.maximum(cnt, 1.0)
    counts[...] = jnp.broadcast_to(cnt, counts.shape)
    land[...] = acc / cnt

    if gather:
        for spread in spreads:
            spread.along_z(1)
            spread.along_last(0)
    keep(xall, xall_out)
    keep(wfull, wfull_out)
    keep(qk, qk_out)
    keep(v, v_out)

    same = tile_same()
    ident = packed_eye()
    masks = lane_masks()
    for h in range(heads_n):
        k0, q1, q0 = landmark_parts(land[:, LANES * h : LANES * h + LANES])
        wlog[h] = jnp.concatenate(split(jnp.concatenate([k0, q1], axis=0) * scaling), axis=1)
        for g in range(tiles_n):
            rows = slice(g * TILE, g * TILE + TILE)
            logit = tt_nt(left_of(q0[rows] * scaling), right_nt(k0[rows]))
            filled = jnp.where(same & (live_row[:, rows] > 0), logit, -1e9)
            raised = jnp.exp(filled - jnp.max(filled, axis=1, keepdims=True))
            A = raised / jnp.sum(raised, axis=1, keepdims=True) * live_cols[g]
            n = h * tiles_n + g
            Aout[n] = A
            factor, _, _ = newton_start(A)
            W = A * factor
            hist[0, 0, n] = pack(tt_nt(left_of(A), right_nt(W)))
            hist[0, 1, n] = pack(W.T)

    def logits(c, top, between=lambda: None):
        rows = pl.ds(pl.multiple_of(c * CHUNK, CHUNK), CHUNK)
        now = tokc[rows, 0:1]
        allowed = (seg_of(now) == doc_row) & (live_row > 0)
        alive = allowed & (live_of(now) > 0)
        tops = []
        for h in range(heads_n):
            part = qk[rows, LANES * h : LANES * h + LANES]
            both = mm_nt(jnp.concatenate([part, part], axis=1), wlog[h])
            one = jnp.where(allowed, both[:, :nslot], -1e9)
            raised = jnp.exp(one - jnp.max(one, axis=1, keepdims=True))
            kern1[h, rows, :] = (raised / jnp.sum(raised, axis=1, keepdims=True)).astype(bf16)
            three = jnp.where(alive, both[:, nslot:], -1e9)
            l3[h, rows, :] = three
            tops.append(jnp.maximum(top[h], jnp.max(three, axis=0, keepdims=True)))
            between()
        return tuple(tops)

    def step_and_logits(i, top):
        stages = newton_stages(hist, i, ident, masks)
        next(stages)
        return logits(i, top, lambda: next(stages, None))

    top = tuple(jnp.full((1, nslot), -1e9, f32) for _ in range(heads_n))
    third = NEWTON // 3
    top = lax.fori_loop(0, third, step_and_logits, top)
    if gather:
        for spread in spreads:
            spread.along_first(2)
            spread.along_z(3)
    top = lax.fori_loop(third, 2 * third, step_and_logits, top)
    if gather:
        for spread in spreads:
            spread.along_last(2)
    top = lax.fori_loop(2 * third, NEWTON, step_and_logits, top)
    keep(hist, hist_out)
    top = lax.fori_loop(NEWTON, nchunk, logits, top)
    keep(kern1, kern1_out)
    if gather:
        for spread in spreads:
            spread.along_first(1)
            spread.to_core(0)

    def raise_three(c, total):
        rows = pl.ds(pl.multiple_of(c * CHUNK, CHUNK), CHUNK)
        totals = []
        for h in range(heads_n):
            raised = jnp.exp(l3[h, rows, :] - top[h])
            l3[h, rows, :] = raised
            totals.append(total[h] + jnp.sum(raised, axis=0, keepdims=True))
        return tuple(totals)

    total = lax.fori_loop(
        0, nchunk, raise_three, tuple(jnp.zeros((1, nslot), f32) for _ in range(heads_n))
    )
    norm = [live_row.astype(f32) / total[h] for h in range(heads_n)]
    carriedT[...] = jnp.zeros_like(carriedT)

    def carry_three(c, none):
        rows = pl.ds(pl.multiple_of(c * CHUNK, CHUNK), CHUNK)
        vT = v[pl.ds(pl.multiple_of(c * CHUNK + HALO, HALO), CHUNK), :].astype(f32).T.astype(bf16)
        for h in range(heads_n):
            low = (l3[h, rows, :] * norm[h]).astype(bf16)
            kern3[h, rows, :] = low
            e = slice(HEAD_DIM * h, HEAD_DIM * h + HEAD_DIM)
            carriedT[e, :] += mm(vT[e, :], low)
        return none

    lax.fori_loop(0, nchunk, carry_three, 0)
    keep(kern3, kern3_out)
    if gather:
        for spread in whole:
            spread.along_last(1)
        for spread in spreads:
            spread.to_core(2)
    carried_all = carriedT[...].T
    carried[...] = carried_all
    lane = iota((TILE, wide), 1) // HEAD_DIM
    docs = nslot // LANDMARKS
    prox_all = jnp.zeros((8, LANES), f32)
    for h in range(heads_n):
        for g in range(tiles_n):
            rows = slice(g * TILE, g * TILE + TILE)
            n = h * tiles_n + g
            Z = hist[NEWTON, 1, n]
            part = split(jnp.where(lane == h, carried_all[rows], 0.0))
            mixed[h, rows, :] = mm3(split(unpack(Z)), part).astype(bf16)
            A = Aout[n]
            A2 = jnp.sum(A * A, axis=0, keepdims=True)
            Z2 = jnp.sum(Z * Z, axis=0, keepdims=True)
            first = iota(A2.shape, 1) < LANDMARKS
            for half in range(2):
                mine = first if half == 0 else jnp.logical_not(first)
                a2 = jnp.sum(jnp.where(mine, A2, 0.0), axis=1, keepdims=True)
                z2 = jnp.sum(jnp.where(mine, Z2, 0.0), axis=1, keepdims=True)
                doc = g * 2 + half
                alive = live_row[:, doc * LANDMARKS : doc * LANDMARKS + 1] > 0
                value = jnp.where(alive, jnp.sqrt(a2) * jnp.sqrt(z2) / LANDMARKS, 0.0)
                here_too = (iota(prox_all.shape, 0) == h) & (iota(prox_all.shape, 1) == doc)
                prox_all = jnp.where(here_too, value, prox_all)
    for h in range(heads_n):
        prox[h] = prox_all[h : h + 1, :docs]

    def finish(b, out, out_row):
        def one(k, none):
            c = b * per_block + k
            rows = pl.ds(pl.multiple_of(c * CHUNK, CHUNK), CHUNK)
            total = mm(kern1[0, rows, :], mixed[0])
            for h in range(1, heads_n):
                total = total + mm(kern1[h, rows, :], mixed[h])
            for part in range(CHUNK // TILE):
                i = c * (CHUNK // TILE) + part
                now = tokc[pl.ds(pl.multiple_of(i * TILE, TILE), TILE), 0:1]
                near = seg_of(now) == segw[pl.ds(i, 1), :]
                window = v[pl.ds(pl.multiple_of(i * TILE, TILE), 2 * TILE), :]
                conv = jnp.zeros((TILE, wide), f32)
                for h in range(heads_n):
                    term = mm(jnp.where(near, bands[h], 0.0).astype(bf16), window)
                    conv = jnp.where(lane == h, term, conv)
                got = (total[part * TILE : (part + 1) * TILE, :] + conv) * live_of(now).astype(f32)
                row = pl.multiple_of(k * CHUNK + part * TILE, TILE)
                out[out_row, pl.ds(row, TILE), :] = got.astype(bf16)
            return none

        lax.fori_loop(0, per_block, one, 0)

    if gather:
        for spread in spreads:
            spread.along_first(3)
    sent = []
    for k, to in enumerate((here.diagonal, here.across, here.sibling)):
        finish(to, hsend, k)
        sent.append(start(push(hsend.at[k], heads.at[here.t], hsem, k, here.dp, to)))
    finish(here.t, heads, here.t)
    if gather:
        for spread in whole:
            spread.along_last(3)
            spread.to_core(1)
        for spread in whole:
            spread.to_core(3)
    for copy in sent:
        copy.wait_recv()
    if gather:
        for spread in spreads:
            spread.finish()
        length = gain.shape[1]
        far = spread_lanes(length, x.shape[1]).astype(bf16)
        owner = iota((32, x.shape[1]), 1) // length == iota((32, x.shape[1]), 0)
        for r in range(4):
            rows = norm_all[...].reshape(32, 8, LANES)[:, r, :].astype(bf16)
            norms[r : r + 1, :] = jnp.sum(jnp.where(owner, mm(rows, far), 0.0), axis=0, keepdims=True)
        norms[4:8, :] = jnp.zeros((4, x.shape[1]), f32)
    for copy in copies:
        copy.wait_send()
    for copy in keeping:
        copy.wait()


VMEM = pl.BlockSpec(memory_space=pltpu.VMEM)
ANY = pl.BlockSpec(memory_space=pl.ANY)


def dma(*shape):
    return pltpu.SemaphoreType.DMA(shape)


def attention_forward(x, w, conv, seg, slot, live, slot_live, extra, heads_n, blocks, taps_total):
    block, feat = x.shape
    seq, nslot = block * blocks, slot_live.shape[1]
    gather = len(extra) > 0
    depth = w.shape[1]
    wide = -(-heads_n * HEAD_DIM // 256) * 256
    tiles_n = heads_n * (nslot // TILE)
    shape = jax.ShapeDtypeStruct
    outs = [
        shape((blocks, block, feat), bf16),
        shape((feat, LANES * heads_n + wide), bf16),
        shape((seq, LANES), i32),
        shape((2 * (seq // TILE), 2 * TILE), i32),
        shape((seq, LANES * heads_n), bf16),
        shape((seq + 2 * HALO, wide), bf16),
        shape((heads_n, seq, nslot), bf16),
        shape((heads_n, seq, nslot), bf16),
        shape((nslot, LANES * heads_n), f32),
        shape((nslot, LANES), f32),
        shape((tiles_n, TILE, TILE), f32),
        shape((heads_n, nslot, wide), bf16),
        shape((nslot, wide), f32),
        shape((blocks, block, wide), bf16),
        shape((heads_n, 1, nslot // LANDMARKS), f32),
        shape((NEWTON + 1, 4, tiles_n, LANDMARKS, TILE), f32),
    ]
    out_specs = [ANY, ANY, VMEM, VMEM] + [ANY] * 4 + [VMEM] * 7 + [ANY]
    scratch = [pltpu.VMEM(outs[n].shape, bf16) for n in (0, 1, 4, 5, 6, 7)]
    scratch += [
        pltpu.VMEM((depth, LANES * heads_n + wide), bf16),
        pltpu.VMEM((heads_n, 2 * nslot, 256), bf16),
        pltpu.VMEM((heads_n, seq, nslot), f32),
        pltpu.VMEM((wide, nslot), f32),
        pltpu.VMEM(outs[15].shape, f32),
        pltpu.VMEM((heads_n, TILE, 2 * TILE), f32),
        pltpu.VMEM((3, block, wide), bf16),
        pltpu.VMEM((8, seq + 2 * TILE), i32),
        pltpu.VMEM((8, 2 * TILE), f32),
        dma(2, 2 * (block // TILE) + 1),
        dma(2, 7),
        dma(2, 3),
        dma(7),
    ]
    if gather:
        hidden_n = extra[0].shape[0]
        outs += [
            shape((4, 2, 2, 2, hidden_n, feat), bf16),
            shape((4, 2, 2, 2, hidden_n, feat), bf16),
            shape((2, 2, feat, wide), bf16),
            shape((8, feat), f32),
        ]
        out_specs += [ANY, ANY, ANY, VMEM]
        scratch += [
            pltpu.VMEM((depth, wide), bf16),
            pltpu.VMEM((8, LANES), f32),
            pltpu.VMEM((4, 2, 2, 2, 8, LANES), f32),
        ]
        for _ in range(4):
            scratch += [dma(2, 19), pltpu.SemaphoreType.DMA]
    return pl.pallas_call(
        functools.partial(forward_body, gather, taps_total),
        out_shape=tuple(outs),
        in_specs=[VMEM] * (7 + len(extra)),
        out_specs=tuple(out_specs),
        scratch_shapes=scratch,
        compiler_params=pltpu.CompilerParams(
            vmem_limit_bytes=LIMIT, collective_id=1 if gather else 2, has_side_effects=True
        ),
        name="attention_forward",
    )(x, w, conv, seg, slot, live, slot_live, *extra)


def normalized(u):
    mean = jnp.mean(u, axis=-1, keepdims=True)
    centered = u - mean
    scale = lax.rsqrt(jnp.mean(centered * centered, axis=-1, keepdims=True) + norm_epsilon)
    return centered * scale, scale


def normalized_back(g, n, scale):
    return scale * (
        g - jnp.mean(g, axis=-1, keepdims=True) - n * jnp.mean(g * n, axis=-1, keepdims=True)
    )


ROWS = 256
FF_CHUNK = 512


def mm_tn(a, b):
    return lax.dot_general(a, b, (((0,), (0,)), ((), ())), preferred_element_type=f32)


def feed_body(
    direct, x, cot, heads, norms, wout, up_in, down_in,
    layer_out, gsend, gpre, gnorm, gout, gup, gdown,
    up, down, act, slope, hidden, hlow, n1, r1, gsum, glow, acc, up_out, down_out, sems,
):
    block, feat = x.shape
    chunks = act.shape[0]
    loads = []
    for j in range(chunks):
        rows = pl.ds(j * FF_CHUNK, FF_CHUNK)
        loads.append(
            (
                pltpu.make_async_copy(up_in.at[rows], up.at[j], sems.at[0, j]),
                pltpu.make_async_copy(down_in.at[rows], down.at[j], sems.at[1, j]),
            )
        )
        for load in loads[-1]:
            load.start()
    gain0, gain1 = norms[0:1, :], norms[1:2, :]
    bias0, bias1 = norms[2:3, :], norms[3:4, :]
    acc[...] = sum(mm_nt(heads[t], wout[t]) for t in range(heads.shape[0]))

    def first_norm(i, none):
        rows = pl.ds(pl.multiple_of(i * ROWS, ROWS), ROWS)
        n, scale = normalized(x[rows, :].astype(f32) + acc[rows, :])
        now = n * gain0 + bias0
        n1[rows, :] = n
        r1[rows, :] = jnp.broadcast_to(scale, (ROWS, LANES))
        hidden[rows, :] = now
        hlow[rows, :] = now.astype(bf16)
        return none

    lax.fori_loop(0, block // ROWS, first_norm, 0)
    acc[...] = hidden[...]
    for j in range(chunks):
        for load in loads[j]:
            load.wait()

    def rise(j, none):
        u = mm_nt(hlow[...], up[j])
        cdf = 0.5 * (1.0 + lax.erf(u * math.sqrt(0.5)))
        act[j] = (u * cdf).astype(bf16)
        slope[j] = cdf + u * (jnp.exp(-0.5 * u * u) * (1.0 / math.sqrt(2.0 * math.pi)))
        acc[...] += mm(act[j], down[j])
        return none

    lax.fori_loop(0, chunks, rise, 0)

    def second_norm(i, sums):
        rows = pl.ds(pl.multiple_of(i * ROWS, ROWS), ROWS)
        n, scale = normalized(acc[rows, :])
        layer_out[rows, :] = (n * gain1 + bias1).astype(bf16)
        c = cot[rows, :].astype(f32)
        g = normalized_back(c * gain1, n, scale)
        gsum[rows, :] = g
        glow[rows, :] = g.astype(bf16)
        return (
            sums[0] + jnp.sum(c * n, axis=0, keepdims=True),
            sums[1] + jnp.sum(c, axis=0, keepdims=True),
        )

    zero = jnp.zeros((1, feat), f32)
    gain_two, bias_two = lax.fori_loop(0, block // ROWS, second_norm, (zero, zero))
    acc[...] = gsum[...]

    def fall(j, none):
        rows = pl.ds(pl.multiple_of(j * FF_CHUNK, FF_CHUNK), FF_CHUNK)
        g_act = mm_nt(glow[...], down[j])
        g_up = (g_act * slope[j]).astype(bf16)
        down_out[j] = mm_tn(act[j], glow[...]).astype(bf16)
        pltpu.make_async_copy(down_out.at[j], gdown.at[rows], sems.at[2, j]).start()
        up_out[j] = mm_tn(g_up, hlow[...]).astype(bf16)
        pltpu.make_async_copy(up_out.at[j], gup.at[rows], sems.at[3, j]).start()
        acc[...] += mm(g_up, up[j])
        return none

    lax.fori_loop(0, chunks, fall, 0)

    def first_back(i, sums):
        rows = pl.ds(pl.multiple_of(i * ROWS, ROWS), ROWS)
        g = acc[rows, :]
        n = n1[rows, :]
        back = normalized_back(g * gain0, n, r1[rows, 0:1])
        gpre[rows, :] = back
        glow[rows, :] = back.astype(bf16)
        return (
            sums[0] + jnp.sum(g * n, axis=0, keepdims=True),
            sums[1] + jnp.sum(g, axis=0, keepdims=True),
        )

    gain_one, bias_one = lax.fori_loop(0, block // ROWS, first_back, (zero, zero))
    gnorm[...] = jnp.concatenate(
        [gain_one, gain_two, bias_one, bias_two, jnp.zeros((4, feat), f32)], axis=0
    )
    for t in range(heads.shape[0]):
        gsend[t] = mm(glow[...], wout[t]).astype(bf16)
        grad = mm_tn(glow[...], heads[t]).astype(bf16)
        if direct:
            gout[:, :, t // 2, t % 2] = grad.reshape((4, 2) + gout.shape[4:])
        else:
            gout[t] = grad

    def land(j, none):
        rows = pl.ds(pl.multiple_of(j * FF_CHUNK, FF_CHUNK), FF_CHUNK)
        pltpu.make_async_copy(down_out.at[j], gdown.at[rows], sems.at[2, j]).wait()
        pltpu.make_async_copy(up_out.at[j], gup.at[rows], sems.at[3, j]).wait()
        return none

    lax.fori_loop(0, chunks, land, 0)


RISE = (0, 2, 3, 1)
FALL = (2, 1, 3, 0)


def feed_direct_body(
    x, cot, heads, norms, wout, up_in, down_in,
    layer_out, gsend, gpre, gnorm, gout, sum_up, sum_down, part_up, part_down,
    up, down, act, slope, hidden, hlow, n1, r1, gsum, glow, acc,
    gu, gd, cu, cd, yu, xd, lsem, csem, ysem, upsem, downsem,
):
    here = Place()
    block, feat = x.shape
    units = act.shape[2]
    copies = []

    def start(copy):
        copy.start()
        copies.append(copy)
        return copy

    loads = {}
    for k in RISE:
        z, late = (here.z + k) % 4, 4 - k in LATE
        near_up = (z, here.y, slice(None), here.c) if late else (z,)
        near_down = (z, slice(None), here.x, here.c) if late else (z,)
        loads[k] = [
            pltpu.make_async_copy(up_in.at[near_up], up.at[near_up], lsem.at[0, k]),
            pltpu.make_async_copy(down_in.at[near_down], down.at[near_down], lsem.at[1, k]),
        ]
        for load in loads[k]:
            load.start()
    greet(
        [(here.dp, here.sibling), (here.dp, here.across), (here.dp_at(0, 1), here.t)]
    )
    arriving = {}

    def send_late(dz):
        n, z = LATE.index(dz), (here.z + 4 - dz) % 4
        near_up, near_down = (z, here.y, slice(None), here.c), (z, slice(None), here.x, here.c)
        arriving[dz] = [
            start(push(up_in.at[near_up], up.at[near_up], upsem, n, here.dp_at(0, 1), here.t)),
            start(push(down_in.at[near_down], down.at[near_down], downsem, n, here.dp, here.across)),
            start(push(up_in.at[near_up], up.at[near_up], upsem, 2 + n, here.dp, here.sibling)),
            start(push(down_in.at[near_down], down.at[near_down], downsem, 2 + n, here.dp, here.sibling)),
        ]

    send_late(LATE[0])

    def pass_on(dz):
        n, z = LATE.index(dz), (here.z + 4 - dz) % 4
        for copy in arriving[dz][:2]:
            copy.wait_recv()
        far_up, far_down = (z, 1 - here.y, slice(None), here.c), (z, slice(None), 1 - here.x, here.c)
        arriving[dz] = arriving[dz][2:] + [
            start(push(up.at[far_up], up.at[far_up], upsem, 4 + n, here.dp, here.sibling)),
            start(push(down.at[far_down], down.at[far_down], downsem, 4 + n, here.dp, here.sibling)),
        ]

    gain0, gain1 = norms[0:1, :], norms[1:2, :]
    bias0, bias1 = norms[2:3, :], norms[3:4, :]
    acc[...] = sum(mm_nt(heads[t], wout[t]) for t in range(heads.shape[0]))

    def first_norm(i, none):
        rows = pl.ds(pl.multiple_of(i * ROWS, ROWS), ROWS)
        n, scale = normalized(x[rows, :].astype(f32) + acc[rows, :])
        now = n * gain0 + bias0
        n1[rows, :] = n
        r1[rows, :] = jnp.broadcast_to(scale, (ROWS, LANES))
        hidden[rows, :] = now
        hlow[rows, :] = now.astype(bf16)
        return none

    lax.fori_loop(0, block // ROWS, first_norm, 0)
    acc[...] = hidden[...]
    flat = (4, units, feat)
    up_of, down_of = up.reshape(flat), down.reshape(flat)
    for k in RISE:
        z = (here.z + k) % 4
        for load in loads[k]:
            load.wait()
        if 4 - k in LATE:
            for copy in arriving[4 - k]:
                copy.wait_recv()
        u = mm_nt(hlow[...], up_of[z])
        cdf = 0.5 * (1.0 + lax.erf(u * math.sqrt(0.5)))
        act[k] = (u * cdf).astype(bf16)
        slope[k] = cdf + u * (jnp.exp(-0.5 * u * u) * (1.0 / math.sqrt(2.0 * math.pi)))
        acc[...] += mm(act[k], down_of[z])
        if k == RISE[0]:
            pass_on(LATE[0])
            send_late(LATE[1])
        if k == RISE[2]:
            pass_on(LATE[1])

    def second_norm(i, sums):
        rows = pl.ds(pl.multiple_of(i * ROWS, ROWS), ROWS)
        n, scale = normalized(acc[rows, :])
        layer_out[rows, :] = (n * gain1 + bias1).astype(bf16)
        c = cot[rows, :].astype(f32)
        g = normalized_back(c * gain1, n, scale)
        gsum[rows, :] = g
        glow[rows, :] = g.astype(bf16)
        return (
            sums[0] + jnp.sum(c * n, axis=0, keepdims=True),
            sums[1] + jnp.sum(c, axis=0, keepdims=True),
        )

    zero = jnp.zeros((1, feat), f32)
    gain_two, bias_two = lax.fori_loop(0, block // ROWS, second_norm, (zero, zero))
    acc[...] = gsum[...]
    core, later = {}, {}

    def after_core(k):
        for copy in core[k]:
            copy.wait_recv()
        cu[k] = cu[k] + gu[k, :, :, here.c]
        cd[k] = cd[k] + gd[k, :, :, here.c]
        if k in FALL[:2]:
            n = FALL.index(k)
            later[k] = (
                start(push(cu.at[k, 1 - here.y], yu.at[n], ysem, n, here.dp_at(0, 1), here.t)),
                start(push(cd.at[k, :, 1 - here.x], xd.at[n], ysem, 2 + n, here.dp, here.across)),
            )

    for n, k in enumerate(FALL):
        z = (here.z + k) % 4
        g_act = mm_nt(glow[...], down_of[z])
        g_up = (g_act * slope[k]).astype(bf16)
        gd[k] = mm_tn(act[k], glow[...]).astype(bf16).reshape(gd.shape[1:])
        gu[k] = mm_tn(g_up, hlow[...]).astype(bf16).reshape(gu.shape[1:])
        core[k] = (
            start(push(gd.at[k, :, :, 1 - here.c], cd.at[k], csem, k, here.dp, here.sibling)),
            start(push(gu.at[k, :, :, 1 - here.c], cu.at[k], csem, 4 + k, here.dp, here.sibling)),
        )
        acc[...] += mm(g_up, up_of[z])
        if n > 0:
            after_core(FALL[n - 1])

    def first_back(i, sums):
        rows = pl.ds(pl.multiple_of(i * ROWS, ROWS), ROWS)
        g = acc[rows, :]
        n = n1[rows, :]
        back = normalized_back(g * gain0, n, r1[rows, 0:1])
        gpre[rows, :] = back
        glow[rows, :] = back.astype(bf16)
        return (
            sums[0] + jnp.sum(g * n, axis=0, keepdims=True),
            sums[1] + jnp.sum(g, axis=0, keepdims=True),
        )

    gain_one, bias_one = lax.fori_loop(0, block // ROWS, first_back, (zero, zero))
    gnorm[...] = jnp.concatenate(
        [gain_one, gain_two, bias_one, bias_two, jnp.zeros((4, feat), f32)], axis=0
    )
    after_core(FALL[3])
    for t in range(heads.shape[0]):
        gsend[t] = mm(glow[...], wout[t]).astype(bf16)
        grad = mm_tn(glow[...], heads[t]).astype(bf16)
        gout[:, :, t // 2, t % 2] = grad.reshape((4, 2) + gout.shape[4:])
    for n, k in enumerate(FALL[2:]):
        part_up[n] = cu[k]
        part_down[n] = cd[k]
    for n, k in enumerate(FALL[:2]):
        for copy in later[k]:
            copy.wait_recv()
        sum_up[n] = cu[k, here.y] + yu[n]
        sum_down[n] = cd[k, :, here.x] + xd[n]
    for copy in copies:
        copy.wait_send()


def feed_direct(x, cot, heads, norms, wout, up_in, down_in, depth):
    block, feat = x.shape
    blocks, _, wide = heads.shape
    owners = up_in.shape
    hidden_n = owners[4]
    units = 8 * hidden_n
    shape = jax.ShapeDtypeStruct
    outs = (
        shape((block, feat), bf16),
        shape((blocks, block, wide), bf16),
        shape((block, feat), f32),
        shape((8, feat), f32),
        shape((4, 2, 2, 2, depth, wide), bf16),
        shape((2, 2, hidden_n, feat), bf16),
        shape((2, 2, hidden_n, feat), bf16),
        shape((2, 2, 2, hidden_n, feat), bf16),
        shape((2, 2, 2, hidden_n, feat), bf16),
    )
    scratch = [
        pltpu.VMEM(owners, bf16),
        pltpu.VMEM(owners, bf16),
        pltpu.VMEM((4, block, units), bf16),
        pltpu.VMEM((4, block, units), f32),
        pltpu.VMEM((block, feat), f32),
        pltpu.VMEM((block, feat), bf16),
        pltpu.VMEM((block, feat), f32),
        pltpu.VMEM((block, LANES), f32),
        pltpu.VMEM((block, feat), f32),
        pltpu.VMEM((block, feat), bf16),
        pltpu.VMEM((block, feat), f32),
        pltpu.VMEM(owners, bf16),
        pltpu.VMEM(owners, bf16),
        pltpu.VMEM((4, 2, 2, hidden_n, feat), bf16),
        pltpu.VMEM((4, 2, 2, hidden_n, feat), bf16),
        pltpu.VMEM((2, 2, hidden_n, feat), bf16),
        pltpu.VMEM((2, 2, hidden_n, feat), bf16),
        dma(2, 4),
        dma(2, 8),
        dma(2, 4),
        dma(2, 6),
        dma(2, 6),
    ]
    return pl.pallas_call(
        feed_direct_body,
        out_shape=outs,
        in_specs=[VMEM] * 5 + [ANY, ANY],
        out_specs=tuple([VMEM] * len(outs)),
        scratch_shapes=scratch,
        compiler_params=pltpu.CompilerParams(
            vmem_limit_bytes=LIMIT, collective_id=5, has_side_effects=True
        ),
        name="feed_forward",
    )(x, cot, heads, norms, wout, up_in, down_in)


def feed_forward(direct, x, cot, heads, norms, wout, up_in, down_in, depth):
    block, feat = x.shape
    blocks, _, wide = heads.shape
    hidden_n = up_in.shape[0]
    chunks = hidden_n // FF_CHUNK
    shape = jax.ShapeDtypeStruct
    outs = (
        shape((block, feat), bf16),
        shape((blocks, block, wide), bf16),
        shape((block, feat), f32),
        shape((8, feat), f32),
        shape((4, 2, 2, 2, depth, wide) if direct else (blocks, feat, wide), bf16),
        shape((hidden_n, feat), bf16),
        shape((hidden_n, feat), bf16),
    )
    scratch = [
        pltpu.VMEM((chunks, FF_CHUNK, feat), bf16),
        pltpu.VMEM((chunks, FF_CHUNK, feat), bf16),
        pltpu.VMEM((chunks, block, FF_CHUNK), bf16),
        pltpu.VMEM((chunks, block, FF_CHUNK), f32),
        pltpu.VMEM((block, feat), f32),
        pltpu.VMEM((block, feat), bf16),
        pltpu.VMEM((block, feat), f32),
        pltpu.VMEM((block, LANES), f32),
        pltpu.VMEM((block, feat), f32),
        pltpu.VMEM((block, feat), bf16),
        pltpu.VMEM((block, feat), f32),
        pltpu.VMEM((chunks, FF_CHUNK, feat), bf16),
        pltpu.VMEM((chunks, FF_CHUNK, feat), bf16),
        dma(4, chunks),
    ]
    return pl.pallas_call(
        functools.partial(feed_body, direct),
        out_shape=outs,
        in_specs=[VMEM] * 5 + [ANY, ANY],
        out_specs=tuple([VMEM] * 5 + [ANY, ANY]),
        scratch_shapes=scratch,
        compiler_params=pltpu.CompilerParams(vmem_limit_bytes=LIMIT),
        name="feed_forward",
    )(x, cot, heads, norms, wout, up_in, down_in)


class Summer:
    def __init__(self, here, source, first, count, own, from_core, from_y, from_z, from_x, sems, local):
        self.here, self.source, self.rows = here, source, pl.ds(first, count)
        self.own, self.from_core, self.from_y, self.from_z, self.from_x = (
            own, from_core, from_y, from_z, from_x,
        )
        self.sems, self.local = sems, local
        self.copies = []

    def push(self, src, dst, index, dp, t):
        copy = push(src, dst, self.sems, index, dp, t)
        copy.start()
        self.copies.append(copy)
        return copy

    def begin(self):
        here = self.here
        self.loaded = pltpu.make_async_copy(
            self.source.at[:, :, :, here.c, self.rows], self.own, self.local
        )
        self.loaded.start()
        self.core = self.push(
            self.source.at[:, :, :, 1 - here.c, self.rows], self.from_core, 0, here.dp, here.sibling
        )

    def along_y(self):
        here = self.here
        self.loaded.wait()
        self.core.wait_recv()

        def one(n, none):
            z, x = n // 2, n % 2
            y = 1 - here.y
            self.from_core[z, y, x] = self.from_core[z, y, x] + self.own[z, y, x]
            return none

        lax.fori_loop(0, 8, one, 0)
        self.y = self.push(
            self.from_core.at[:, 1 - here.y], self.from_y, 1, here.dp_at(0, 1), here.t
        )

    def along_z(self):
        here = self.here
        self.y.wait_recv()

        def one(n, none):
            z, x = n // 2, n % 2
            total = self.from_core[z, here.y, x].astype(f32) + self.own[z, here.y, x].astype(f32)
            total = total + self.from_y[z, x].astype(f32)
            self.from_y[z, x] = total.astype(self.own.dtype)
            return none

        lax.fori_loop(0, 8, one, 0)
        self.z = [
            self.push(
                self.from_y.at[(here.z + dz) % 4], self.from_z.at[dz - 1], 1 + dz, here.dp_at(dz, 0), here.t
            )
            for dz in (1, 2, 3)
        ]

    def along_x(self):
        here = self.here
        for copy in self.z:
            copy.wait_recv()
        for x in range(2):
            total = self.from_y[here.z, x].astype(f32)
            for n in range(3):
                total = total + self.from_z[n, x].astype(f32)
            self.from_y[here.z, x] = total.astype(self.own.dtype)
        self.x = self.push(
            self.from_y.at[here.z, 1 - here.x], self.from_x, 5, here.dp, here.across
        )

    def finish(self, out):
        self.x.wait_recv()
        here = self.here
        out[self.rows, :] = self.from_y[here.z, here.x].astype(f32) + self.from_x[...].astype(f32)
        for copy in self.copies:
            copy.wait_send()


class UpSum:
    def __init__(self, here, sums, parts, parts_far, from_y, from_z, from_x, sems, sums_far=None):
        self.here, self.sums, self.parts = here, sums, parts
        self.parts_far, self.sums_far = parts_far, sums_far
        self.from_y, self.from_z, self.from_x, self.sems = from_y, from_z, from_x, sems
        self.copies = []

    def push(self, src, dst, index, dp, t):
        copy = push(src, dst, self.sems, index, dp, t)
        copy.start()
        self.copies.append(copy)
        return copy

    def along_z(self, src, k):
        here = self.here
        return self.push(src, self.from_z.at[k - 1], k - 1, here.dp_at(k, 0), here.t)

    def begin(self):
        here = self.here
        self.y = [
            self.push(self.parts_far.at[n, 1 - here.y], self.from_y.at[n], 3 + n, here.dp_at(0, 1), here.t)
            for n in range(2)
        ]
        self.z = [self.along_z(self.sums.at[n], FALL[n]) for n in range(2)]

    def second(self):
        for n in range(2):
            self.y[n].wait_recv()
            self.from_y[n] = self.from_y[n] + self.parts[n, self.here.y]
        self.z.append(self.along_z(self.from_y.at[0], FALL[2]))

    def third(self):
        here = self.here
        for copy in self.z:
            copy.wait_recv()
        total = self.from_y[1].astype(f32)
        for n in range(3):
            total = total + self.from_z[n].astype(f32)
        self.from_y[1] = total.astype(bf16)
        self.x = self.push(self.from_y.at[1, 1 - here.x], self.from_x, 5, here.dp, here.across)

    def finish(self, out):
        self.x.wait_recv()
        out[...] = self.from_y[1, self.here.x].astype(f32) + self.from_x[...].astype(f32)
        for copy in self.copies:
            copy.wait_send()


class DownSum(UpSum):
    def begin(self):
        here = self.here
        self.x = [
            self.push(self.parts_far.at[n, :, 1 - here.x], self.from_x.at[n], 3 + n, here.dp, here.across)
            for n in range(2)
        ]
        self.y = [self.along_y(self.sums_far.at[n, 1 - here.y], n) for n in range(2)]

    def along_y(self, src, n):
        here = self.here
        return self.push(src, self.from_y.at[n], 5 + n, here.dp_at(0, 1), here.t)

    def second(self):
        self.z = []
        for n in range(2):
            self.y[n].wait_recv()
            self.from_y[n] = self.from_y[n] + self.sums[n, self.here.y]
            self.z.append(self.along_z(self.from_y.at[n], FALL[n]))

    def third(self):
        here = self.here
        for n in range(2):
            self.x[n].wait_recv()
            self.from_x[n] = self.from_x[n] + self.parts[n, :, here.x]
            self.y.append(self.along_y(self.from_x.at[n, 1 - here.y], 2 + n))

    def fourth(self):
        for n in range(2):
            self.y[2 + n].wait_recv()
            self.from_y[2 + n] = self.from_y[2 + n] + self.from_x[n, self.here.y]
        self.z.append(self.along_z(self.from_y.at[2], FALL[2]))

    def finish(self, out):
        for copy in self.z:
            copy.wait_recv()
        total = self.from_y[3].astype(f32)
        for n in range(3):
            total = total + self.from_z[n].astype(f32)
        out[...] = total
        for copy in self.copies:
            copy.wait_send()


SUMMER_SEMS = 6


def backward_body(gather, taps_total, *refs):
    (
        gsend, xall_in, wfull_in, tokc_in, segw, qk_in, v_in, kern1_in, kern3_in,
        land, counts, Ain, mixed, carried, conv, slot_live, gpre_in, hist_in,
    ) = refs[:18]
    refs = refs[18:]
    if gather:
        (sum_up, sum_down_in, part_up_in, part_down_in, out_in, norm_in), refs = refs[:6], refs[6:]
    (input_grad, gw, gconv), refs = refs[:3], refs[3:]
    if gather:
        (up_out, down_out, out_out, gain_out, bias_out), refs = refs[:5], refs[5:]
    (
        wfull, tokc, qk, v, gpre, taps, gl1, gl3, xall, xT, gopad, gqk, gv, gband, bands, gmixedT, glandT, hist, gstate, gcar, wback,
        part_out, part_in, part_sum, part_x, piece_v, piece_q, in_v, in_q, in_conv, conv_out,
        land_sum, x_land, g_high, g_low, land_own, land_out, land_in, land_all,
        gsem, lsem, psem, csem,
    ) = refs[:43]
    refs = refs[43:]

    here = Place()
    blocks, block, wide = gsend.shape
    seq = blocks * block
    heads_n = gl1.shape[0]
    nslot = land.shape[0]
    nchunk = seq // CHUNK
    per_block = block // CHUNK
    tiles_n = nslot // TILE
    all_tiles = heads_n * tiles_n
    feat = wfull.shape[0]
    doc_row = iota((1, nslot), 1) // LANDMARKS
    live_row = slot_live[...]
    live_cols = [column(live_row[:, g * TILE : (g + 1) * TILE].astype(f32)) for g in range(tiles_n)]
    scaling = 1.0 / math.sqrt(HEAD_DIM)
    same = tile_same()
    masks = lane_masks()

    pairs = [
        (tokc_in, tokc), (xall_in, xall), (kern1_in, gl1), (hist_in, hist), (kern3_in, gl3), (qk_in, qk),
        (v_in, v), (wfull_in, wfull), (gpre_in, gpre),
    ]
    if gather:
        sum_down, part_up, part_down = refs[:3]
        refs = refs[3:]
        pairs += [(sum_down_in, sum_down), (part_up_in, part_up), (part_down_in, part_down)]
    loads = [pltpu.make_async_copy(src, dst, lsem.at[n]) for n, (src, dst) in enumerate(pairs)]
    for load in loads:
        load.start()

    peers = here.tensor_peers()
    if gather:
        peers = peers + [
            (here.dp_at(dz, dy), here.t) for dz in range(4) for dy in range(2) if dz or dy
        ]
    greet(peers)
    copies = []

    def start(copy):
        copy.start()
        copies.append(copy)
        return copy

    def landing(t):
        return gopad.at[pl.ds(pl.multiple_of(t * block + HALO, HALO), block)]

    gopad[0:HALO, :] = jnp.zeros((HALO, wide), bf16)
    gopad[seq + HALO : seq + 2 * HALO, :] = jnp.zeros((HALO, wide), bf16)
    arriving = [
        start(push(gsend.at[to], landing(here.t), gsem, k, here.dp, to))
        for k, to in enumerate((here.across, here.diagonal, here.sibling))
    ]
    gopad[pl.ds(pl.multiple_of(here.t * block + HALO, HALO), block), :] = gsend[here.t]

    if gather:
        out_sum, norm_sum, norm_pieces, q_sems, v_sems, in_vz, in_qz = refs[:7]
        refs = refs[7:]
        ups = UpSum(here, sum_up, part_up, part_up_in, *refs[:4])
        downs = DownSum(here, sum_down, part_down, part_down_in, *refs[4:8], sum_down_in)
        refs = refs[8:]
        ups.begin()
        downs.begin()
        length = gain_out.shape[1]
        far = spread_lanes(length, feat).astype(bf16)
        owner = iota((32, feat), 1) // length == iota((32, feat), 0)
        for r in range(4):
            high, low = split(jnp.where(owner, norm_in[r : r + 1, :], 0.0))
            norm_pieces[:, r, :] = mm_nt(high, far) + mm_nt(low, far)
        for r in range(4, 8):
            norm_pieces[:, r, :] = jnp.zeros((32, LANES), f32)
        norm_view = norm_pieces.reshape(4, 2, 2, 2, 8, LANES)
        smalls = []
        for source, count in ((out_in, out_in.shape[4]), (norm_view, 8)):
            buffers, refs = refs[:7], refs[7:]
            smalls.append(Summer(here, source, 0, count, *buffers))
        for summer in smalls:
            summer.begin()

    taps[...] = jnp.zeros_like(taps)
    taps[:heads_n, :taps_total] = conv[...]
    moved = pltpu.roll(taps[...], HALO - taps_total // 2, 1)
    far_rows = (iota((TILE, TILE), 0) + iota((TILE, TILE), 1) == TILE - 1).astype(f32).astype(bf16)
    turn_cols = iota((2 * TILE, 2 * TILE), 0) + iota((2 * TILE, 2 * TILE), 1) == 2 * TILE - 1
    turn_cols = turn_cols.astype(f32).astype(bf16)
    for h in range(heads_n):
        bands[h] = band_from(moved[h : h + 1, :])
        bands[heads_n + h] = mm(mm(far_rows, bands[h].astype(bf16)).astype(bf16), turn_cols)
    gmixedT[...] = jnp.zeros_like(gmixedT)
    glandT[...] = jnp.zeros_like(glandT)
    gband[...] = jnp.zeros_like(gband)
    loads[0].wait()
    loads[1].wait()

    def turn(b, none):
        for i in range(block // TILE):
            rows = slice(i * TILE, i * TILE + TILE)
            col = pl.ds(pl.multiple_of(b * block + i * TILE, TILE), TILE)
            xT[:, col] = xall[b, rows, :].astype(f32).T.astype(bf16)
            slot_now = slot_of(tokc[col, 0:1])
            hot = (slot_now == iota((TILE, nslot), 1)).astype(f32).astype(bf16)
            x_land[...] += mm(xT[:, col], hot)
        return none

    x_land[...] = jnp.zeros_like(x_land)
    lax.fori_loop(0, blocks, turn, 0)
    for h in range(heads_n):
        k0, q1, _ = landmark_parts(land[:, LANES * h : LANES * h + LANES])
        wback[h, :nslot, :] = jnp.concatenate(split(k0 * scaling), axis=1)
        wback[h, nslot:, :] = jnp.concatenate(split(q1 * scaling), axis=1)
    if gather:
        for summer in smalls:
            summer.along_y()
    for copy in arriving:
        copy.wait_recv()
    for load in loads[2:]:
        load.wait()

    def one(c, none):
        rows = pl.ds(pl.multiple_of(c * CHUNK, CHUNK), CHUNK)
        inner = pl.ds(pl.multiple_of(c * CHUNK + HALO, HALO), CHUNK)
        alive = live_of(tokc[rows, 0:1]) > 0
        g_now = jnp.where(alive, gopad[inner, :].astype(f32), 0.0).astype(bf16)
        gopad[inner, :] = g_now
        gT = g_now.astype(f32).T.astype(bf16)
        for h in range(heads_n):
            k1 = gl1[h, rows, :]
            gk = mm_nt(g_now, mixed[h])
            k1w = k1.astype(f32)
            gl1[h, rows, :] = (k1w * (gk - jnp.sum(gk * k1w, axis=1, keepdims=True))).astype(bf16)
            e = slice(HEAD_DIM * h, HEAD_DIM * h + HEAD_DIM)
            gmixedT[e, :] += mm(gT[e, :], k1)
        return none

    lax.fori_loop(0, nchunk, one, 0)
    if gather:
        downs.second()
        ups.second()
    gmixed = gmixedT[...].T
    carried_all = carried[...]
    lane = iota((TILE, wide), 1) // HEAD_DIM
    delta = []
    for h in range(heads_n):
        rows_delta = []
        for g in range(tiles_n):
            n = h * tiles_n + g
            rows = slice(g * TILE, g * TILE + TILE)
            Z = unpack(hist[NEWTON, 1, n])
            gm = split(jnp.where(lane == h, gmixed[rows], 0.0))
            near = jnp.where(lane == h, carried_all[rows], 0.0)
            gstate[0, n] = jnp.zeros((LANDMARKS, TILE), f32)
            gstate[1, n] = pack(jnp.where(same, mm3(gm, split(near), mm_nt), 0.0))
            gc = mm3(split(Z.T), gm).astype(bf16)
            gcar[h, rows, :] = gc
            rows_delta.append(jnp.sum((gc.astype(f32) * near).T, axis=0, keepdims=True))
        delta.append(jnp.concatenate(rows_delta, axis=1))
    def three(c, emit, between=lambda: None):
        rows = pl.ds(pl.multiple_of(c * CHUNK, CHUNK), CHUNK)
        v_now = v[pl.ds(pl.multiple_of(c * CHUNK + HALO, HALO), CHUNK), :]
        total = jnp.zeros((CHUNK, wide), f32)
        for h in range(heads_n):
            gc = gcar[h]
            k3 = gl3[h, rows, :]
            gk = mm_nt(v_now, gc)
            gl = (k3.astype(f32) * (gk - delta[h])).astype(bf16)
            gl3[h, rows, :] = gl
            total = total + mm(k3, gc)
            partT = qk[rows, LANES * h : LANES * h + LANES].astype(f32).T.astype(bf16)
            glandT[h, :HEAD_DIM, :] += mm(partT[:HEAD_DIM, :], gl1[h, rows, :])
            glandT[h, HEAD_DIM:, :] += mm(partT[HEAD_DIM:, :], gl)
            between()
        for part in range(CHUNK // TILE):
            i = c * (CHUNK // TILE) + part
            at = pl.ds(pl.multiple_of(i * TILE, TILE), TILE)
            now = tokc[at, 0:1]
            seg_now = seg_of(now)
            near = seg_now == segw[pl.ds(i, 1), :]
            near_back = (seg_now == segw[pl.ds(seq // TILE + i, 1), :]) & (live_of(now) > 0)
            g_window = gopad[pl.ds(pl.multiple_of(i * TILE, TILE), 2 * TILE), :]
            v_window = v[pl.ds(pl.multiple_of(i * TILE, TILE), 2 * TILE), :]
            g_tile = gopad[pl.ds(pl.multiple_of(i * TILE + HALO, HALO), TILE), :].astype(f32)
            conv = jnp.zeros((TILE, wide), f32)
            for h in range(heads_n):
                back = mm(jnp.where(near_back, bands[heads_n + h], 0.0).astype(bf16), g_window)
                conv = jnp.where(lane == h, back, conv)
                mine = jnp.where(lane == h, g_tile, 0.0).astype(bf16)
                gband[h] += jnp.where(near, mm_nt(mine, v_window), 0.0)
            gv[at, :] = (total[part * TILE : (part + 1) * TILE, :] + conv).astype(bf16)
        for h in range(heads_n):
            both = mm(gl1[h, rows, :], wback[h, :nslot, :]) + mm(gl3[h, rows, :], wback[h, nslot:, :])
            gqk[rows, LANES * h : LANES * h + LANES] = (both[:, :LANES] + both[:, LANES:]).astype(bf16)
        emit(
            mm_nt(gqk[rows, :], wfull[:, : LANES * heads_n])
            + mm_nt(gv[rows, :], wfull[:, LANES * heads_n :])
        )

    def dyn_rows(k):
        return pl.ds(pl.multiple_of(k * CHUNK, CHUNK), CHUNK)

    def chunk_rows(k):
        return pl.ds(k * CHUNK, CHUNK)

    def landmark_stages():
        tiles = range(all_tiles)
        A = [Ain[n] for n in tiles]
        starts = [newton_start(a) for a in A]
        gW = [unpack(gstate[1, n]).T for n in tiles]
        gP = [unpack(gstate[0, n]) for n in tiles]
        GA = [tt(left_of(gP[n] + gP[n].T), right_of(A[n])) for n in tiles]
        yield
        gl2 = []
        for n in tiles:
            factor, colsum, tops = starts[n]
            gf_cols = jnp.sum((0.5 * GA[n] + gW[n]) * A[n], axis=0, keepdims=True)
            first = iota(colsum.shape, 1) < LANDMARKS
            gcol = jnp.zeros_like(colsum)
            for k in range(2):
                mine = first if k == 0 else jnp.logical_not(first)
                gf = jnp.sum(jnp.where(mine, gf_cols, 0.0), axis=1, keepdims=True)
                top = tops[k]
                is_top = mine & (colsum == top)
                ties = jnp.sum(is_top.astype(f32), axis=1, keepdims=True)
                share = jnp.where(top > 1.0, 1.0, jnp.where(top == 1.0, 0.5, 0.0))
                floor = jnp.maximum(top, 1.0)
                gcol = jnp.where(is_top, -gf * share / (floor * floor * ties), gcol)
            gA = (factor * (GA[n] + gW[n]) + gcol) * live_cols[n % tiles_n]
            one = A[n] * (gA - jnp.sum(gA * A[n], axis=1, keepdims=True)) * scaling
            rows = slice((n % tiles_n) * TILE, (n % tiles_n) * TILE + TILE)
            gl2.append(jnp.where(same & (live_row[:, rows] > 0), one, 0.0))
        yield
        for n in tiles:
            h, g = n // tiles_n, n % tiles_n
            rows = slice(g * TILE, g * TILE + TILE)
            k0, q1, _ = landmark_parts(land[rows, LANES * h : LANES * h + LANES])
            land_sum[h, rows, :] = mm3(split(gl2[n]), split(k0)) + mm3(split(gl2[n].T), split(q1))
        yield

    def walk(q, b, emit):
        def both(k, none):
            stages = newton_back_stages(hist, gstate, NEWTON - 1 - q * per_block - k, masks)
            next(stages)
            three(b * per_block + k, functools.partial(emit, k), lambda: next(stages, None))
            return none

        def alone(k, none):
            three(b * per_block + k, functools.partial(emit, k))
            return none

        ends = min(max(NEWTON - q * per_block, 0), per_block)
        lax.fori_loop(0, ends, both, 0)
        if NEWTON <= q * per_block < NEWTON + per_block:
            stages = landmark_stages()
            next(stages)
            three(b * per_block, functools.partial(emit, 0), lambda: next(stages, None))
            ends = 1
        lax.fori_loop(ends, per_block, alone, 0)

    def to_part(n, k, value):
        part_out[n, dyn_rows(k), :] = value.astype(bf16)

    def to_grad(k, value):
        input_grad[dyn_rows(k), :] = value

    def to_own_grad(k, value):
        input_grad[dyn_rows(k), :] = value + gpre[dyn_rows(k), :]

    walk(0, here.diagonal, functools.partial(to_part, 0))
    from_sibling = start(push(part_out.at[0], part_in.at[0], psem, 0, here.dp, here.sibling))
    walk(1, here.across, to_grad)
    from_sibling.wait_recv()
    from_across = []
    for k in range(per_block):
        total = input_grad[chunk_rows(k), :] + part_in[0, chunk_rows(k), :].astype(f32)
        part_sum[chunk_rows(k), :] = total.astype(bf16)
        from_across.append(
            start(push(part_sum.at[chunk_rows(k)], part_x.at[chunk_rows(k)], psem, 1 + k, here.dp, here.across))
        )
    if gather:
        downs.third()
        for summer in smalls:
            summer.along_z()
    walk(2, here.sibling, functools.partial(to_part, 1))
    own_from_sibling = start(push(part_out.at[1], part_in.at[1], psem, 1 + per_block, here.dp, here.sibling))
    walk(3, here.t, to_own_grad)
    if gather:
        downs.fourth()
        ups.third()

    conv_out[...] = jnp.zeros_like(conv_out)
    for h in range(heads_n):
        conv_out[h : h + 1, :] = diagonal_sums(gband[h])
    piece_v[...] = mm(xT[...], gv[...]).astype(bf16)
    others = [(dz, dy) for dz in range(4) for dy in range(2) if dz or dy] if gather else []
    sent_conv = []
    for k, (dz, dy) in enumerate(others):
        sent_conv.append(start(push(conv_out, in_conv.at[k], csem, k, here.dp_at(dz, dy), here.t)))

    def piece_along_y(piece, landing, sems):
        view = piece.reshape((4, 2) + landing.shape[1:])
        return start(push(view.at[:, 1 - here.y], landing, sems, 0, here.dp_at(0, 1), here.t))

    def piece_along_z(copy, piece, landing, last_landing, sems):
        view = piece.reshape((4, 2) + landing.shape[1:])
        copy.wait_recv()
        for z in range(4):
            landing[z] = landing[z] + view[z, here.y]
        return [
            start(push(landing.at[(here.z + dz) % 4], last_landing.at[dz - 1], sems, dz, here.dp_at(dz, 0), here.t))
            for dz in (1, 2, 3)
        ]

    if gather:
        v_along_y = piece_along_y(piece_v, in_v, v_sems)

    for h in range(heads_n):
        sums_land = pltpu.roll(glandT[h].T * scaling, HEAD_DIM, 1)
        lanes = slice(LANES * h, LANES * h + LANES)
        total = (land_sum[h] + sums_land) / counts[...]
        g_high[:, lanes], g_low[:, lanes] = split(total)

    weights_qk = wfull[:, : LANES * heads_n]
    spread_land = mm_nt(g_high[...], weights_qk) + mm_nt(g_low[...], weights_qk)
    half = nslot // 2
    land_own[...] = spread_land
    land_out[0] = land_own[pl.ds(pl.multiple_of((1 - here.c) * half, half), half), :].astype(bf16)
    own_half = pl.ds(pl.multiple_of(here.c * half, half), half)
    first = start(push(land_out.at[0], land_in.at[0], psem, 2 + per_block, here.dp, here.sibling))
    high, low = split(x_land[...])
    piece_q[...] = (
        mm(xT[...], gqk[...])
        + (mm(high, g_high[...]) + (mm(high, g_low[...]) + mm(low, g_high[...])))
    ).astype(bf16)
    if gather:
        q_along_y = piece_along_y(piece_q, in_q, q_sems)
    first.wait_recv()
    mine = land_own[own_half, :] + land_in[0].astype(f32)
    land_out[1] = mine.astype(bf16)
    second = start(push(land_out.at[1], land_in.at[1], psem, 3 + per_block, here.dp, here.across))
    if gather:
        for summer in smalls:
            summer.along_x()
        sent_v = piece_along_z(v_along_y, piece_v, in_v, in_vz, v_sems)
    second.wait_recv()
    mine = mine + land_in[1].astype(f32)
    land_all[own_half, :] = mine.astype(bf16)
    third = start(
        push(land_all.at[own_half], land_all.at[own_half], psem, 4 + per_block, here.dp, here.sibling)
    )
    if gather:
        ups.finish(up_out)
        downs.finish(down_out)
        sent_q = piece_along_z(q_along_y, piece_q, in_q, in_qz, q_sems)
    own_from_sibling.wait_recv()
    third.wait_recv()
    for k in range(per_block):
        from_across[k].wait_recv()
        rows = pl.ds(pl.multiple_of(here.t * block + k * CHUNK, CHUNK), CHUNK)
        hot = (slot_of(tokc[rows, 0:1]) == iota((CHUNK, nslot), 1)).astype(f32).astype(bf16)
        input_grad[chunk_rows(k), :] += (
            part_in[1, chunk_rows(k), :].astype(f32)
            + part_x[chunk_rows(k), :].astype(f32)
            + mm(hot, land_all[...])
        )
    if gather:
        for copy in sent_v + sent_q + sent_conv:
            copy.wait_recv()
        total_v = in_v[here.z].astype(f32)
        total_q = in_q[here.z].astype(f32)
        for k in range(3):
            total_v = total_v + in_vz[k].astype(f32)
            total_q = total_q + in_qz[k].astype(f32)
        total_conv = conv_out[...]
        for k in range(len(others)):
            total_conv = total_conv + in_conv[k]
        for h in range(heads_n):
            e = slice(HEAD_DIM * h, HEAD_DIM * h + HEAD_DIM)
            one = total_q[:, LANES * h : LANES * h + LANES]
            gw[0, :, e] = one[:, :HEAD_DIM]
            gw[1, :, e] = one[:, HEAD_DIM:]
        gw[2] = total_v[:, : heads_n * HEAD_DIM]
        first = HALO - taps_total // 2
        turned = pltpu.roll(total_conv, 2 * TILE - first, 1)
        gconv[...] = turned[:heads_n, :taps_total]
        smalls[0].finish(out_sum)
        out_out[...] = out_sum[:, : heads_n * HEAD_DIM].T
        smalls[1].finish(norm_sum)
        gain_out[...] = norm_sum[0:2, :length]
        bias_out[...] = norm_sum[2:4, :length]
    else:
        gw[:, : LANES * heads_n] = piece_q[...].astype(f32)
        gw[:, LANES * heads_n :] = piece_v[...].astype(f32)
        gconv[...] = conv_out[...]
    for copy in copies:
        copy.wait_send()


def attention_backward(gsend, xall, wfull, tokc, segw, qk, v, kern1, kern3, land, counts, weights,
                       mixed, carried, conv, slot_live, gpre, hist, sources, taps_total, depth):
    blocks, block, wide = gsend.shape
    heads_n, seq, nslot = kern1.shape
    feat = wfull.shape[0]
    all_tiles = weights.shape[0]
    shape = jax.ShapeDtypeStruct
    gather = len(sources) > 0
    width = heads_n * HEAD_DIM
    outs = [shape((block, feat), f32)]
    if gather:
        hidden_n = sources[0].shape[2]
        outs += [
            shape((3, depth, width), f32),
            shape((heads_n, taps_total), f32),
            shape((hidden_n, feat), f32),
            shape((hidden_n, feat), f32),
            shape((width, depth), f32),
            shape((2, feat // 32), f32),
            shape((2, feat // 32), f32),
        ]
    else:
        outs += [shape((feat, wfull.shape[1]), f32), shape((8, 2 * TILE), f32)]
    others = 7 if gather else 1
    per_block = block // CHUNK
    scratch = [
        pltpu.VMEM(wfull.shape, bf16),
        pltpu.VMEM(tokc.shape, i32),
        pltpu.VMEM(qk.shape, bf16),
        pltpu.VMEM(v.shape, bf16),
        pltpu.VMEM(gpre.shape, f32),
        pltpu.VMEM((8, 2 * TILE), f32),
        pltpu.VMEM((heads_n, seq, nslot), bf16),
        pltpu.VMEM((heads_n, seq, nslot), bf16),
        pltpu.VMEM(xall.shape, bf16),
        pltpu.VMEM((feat, seq), bf16),
        pltpu.VMEM((seq + 2 * HALO, wide), bf16),
        pltpu.VMEM((seq, LANES * heads_n), bf16),
        pltpu.VMEM((seq, wide), bf16),
        pltpu.VMEM((heads_n, TILE, 2 * TILE), f32),
        pltpu.VMEM((2 * heads_n, TILE, 2 * TILE), f32),
        pltpu.VMEM((wide, nslot), f32),
        pltpu.VMEM((heads_n, LANES, nslot), f32),
        pltpu.VMEM((NEWTON + 1, 4, all_tiles, LANDMARKS, TILE), f32),
        pltpu.VMEM((2, all_tiles, LANDMARKS, TILE), f32),
        pltpu.VMEM((heads_n, nslot, wide), bf16),
        pltpu.VMEM((heads_n, 2 * nslot, 256), bf16),
        pltpu.VMEM((2, block, feat), bf16),
        pltpu.VMEM((2, block, feat), bf16),
        pltpu.VMEM((block, feat), bf16),
        pltpu.VMEM((block, feat), bf16),
        pltpu.VMEM((feat, wide), bf16),
        pltpu.VMEM((feat, LANES * heads_n), bf16),
        pltpu.VMEM((4, depth if gather else 16, wide), bf16),
        pltpu.VMEM((4, depth if gather else 16, LANES * heads_n), bf16),
        pltpu.VMEM((others, 8, 2 * TILE), f32),
        pltpu.VMEM((8, 2 * TILE), f32),
        pltpu.VMEM((heads_n, nslot, LANES), f32),
        pltpu.VMEM((feat, nslot), f32),
        pltpu.VMEM((nslot, LANES * heads_n), bf16),
        pltpu.VMEM((nslot, LANES * heads_n), bf16),
        pltpu.VMEM((nslot, feat), f32),
        pltpu.VMEM((2, nslot // 2, feat), bf16),
        pltpu.VMEM((2, nslot // 2, feat), bf16),
        pltpu.VMEM((nslot, feat), bf16),
        dma(2, 3),
        dma(12),
        dma(2, 5 + per_block),
        dma(2, others),
    ]
    if gather:
        scratch += [pltpu.VMEM(source.shape, bf16) for source in sources[1:4]]
        scratch += [
            pltpu.VMEM((depth, wide), f32),
            pltpu.VMEM((8, LANES), f32),
            pltpu.VMEM((32, 8, LANES), f32),
            dma(2, 4),
            dma(2, 4),
            pltpu.VMEM((3, depth, wide), bf16),
            pltpu.VMEM((3, depth, LANES * heads_n), bf16),
            pltpu.VMEM((2, 2, hidden_n, feat), bf16),
            pltpu.VMEM((3, 2, hidden_n, feat), bf16),
            pltpu.VMEM((hidden_n, feat), bf16),
            dma(2, 6),
            pltpu.VMEM((4, hidden_n, feat), bf16),
            pltpu.VMEM((3, hidden_n, feat), bf16),
            pltpu.VMEM((2, 2, hidden_n, feat), bf16),
            dma(2, 9),
        ]
        for count, lanes, kind in ((depth, wide, bf16), (8, LANES, f32)):
            scratch += [
                pltpu.VMEM((4, 2, 2, count, lanes), kind),
                pltpu.VMEM((4, 2, 2, count, lanes), kind),
                pltpu.VMEM((4, 2, count, lanes), kind),
                pltpu.VMEM((3, 2, count, lanes), kind),
                pltpu.VMEM((count, lanes), kind),
                dma(2, SUMMER_SEMS),
                pltpu.SemaphoreType.DMA,
            ]
    specs = [VMEM, ANY, ANY, ANY, VMEM] + [ANY] * 4 + [VMEM] * 7 + [ANY, ANY]
    if gather:
        specs += [ANY] * 5 + [VMEM]
    return pl.pallas_call(
        functools.partial(backward_body, gather, taps_total),
        out_shape=tuple(outs),
        in_specs=specs,
        out_specs=tuple([VMEM] * len(outs)),
        scratch_shapes=scratch,
        compiler_params=pltpu.CompilerParams(
            vmem_limit_bytes=LIMIT, collective_id=3 if gather else 4, has_side_effects=True
        ),
        name="attention_backward",
    )(gsend, xall, wfull, tokc, segw, qk, v, kern1, kern3, land, counts, weights, mixed, carried,
      conv, slot_live, gpre, hist, *sources)


def hand_over_body(*refs):
    half = len(refs) // 2
    for src, dst in zip(refs[:half], refs[half:]):
        dst[...] = src[...]


def hand_over(*arrays):
    return pl.pallas_call(
        hand_over_body,
        out_shape=tuple(jax.ShapeDtypeStruct(a.shape, a.dtype) for a in arrays),
        in_specs=[VMEM] * len(arrays),
        out_specs=tuple([VMEM] * len(arrays)),
        name="hand_over",
    )(*arrays)


def split_up(shard, dim, length):
    before, after = (shard.shape[:dim], shard.shape[dim + 1 :])
    return jnp.moveaxis(shard.reshape(*before, length, -1, *after), dim, 0)


def exchange(pieces, axis):
    return lax.all_to_all(pieces, axis, split_axis=0, concat_axis=0, tiled=True)


def per_device(
    tokens,
    w_qkv,
    w_out,
    conv_weight,
    w_up,
    w_down,
    norm_gain,
    norm_bias,
    cotangent,
    seg_ids,
    landmark_slot,
    token_live,
    slot_live,
):
    both = ("dp", "tensor")
    dp_size, blocks = lax.axis_size("dp"), lax.axis_size("tensor")
    devices = dp_size * blocks
    heads_n, taps_total = conv_weight.shape
    block, feat = tokens.shape
    depth = w_qkv.shape[1]
    width = heads_n * HEAD_DIM
    wide = -(-width // 256) * 256
    hidden_n = w_up.shape[1]
    docs = slot_live.shape[1] // LANDMARKS
    direct = dp_size == 8 and blocks == 4 and depth % 16 == 0 and hidden_n % 32 == 0

    first = HALO - taps_total // 2
    weight = w_qkv if direct else lax.all_gather(w_qkv, "dp", axis=1, tiled=True)
    extra = (w_up.T, w_down, w_out, norm_gain, norm_bias) if direct else ()
    got = attention_forward(
        tokens, weight, conv_weight, seg_ids, landmark_slot, token_live, slot_live,
        extra, heads_n, blocks, taps_total,
    )
    (
        xall, wfull, tokc, segw, qk, v, kern1, kern3, land, counts, weights, mixed, carried, heads, proxies,
        hist,
    ) = got[:16]
    if direct:
        up_all, down_all, out_all, norms = got[16:]
        out_all = out_all.reshape(blocks, feat, wide)
    else:
        up_all = lax.all_gather(w_up.T, both, axis=0, tiled=True)
        down_all = lax.all_gather(w_down, both, axis=0, tiled=True)
        out_all = lax.all_gather(lax.all_gather(w_out.T, "dp", axis=0, tiled=True), "tensor", axis=0)
        out_all = jnp.pad(out_all, ((0, 0), (0, 0), (0, wide - width)))
        norms = jnp.concatenate([norm_gain, norm_bias, jnp.zeros_like(norm_gain), jnp.zeros_like(norm_bias)])
        norms = lax.all_gather(norms, both, axis=1, tiled=True).astype(f32)
    if direct:
        got = feed_direct(tokens, cotangent, heads, norms, out_all, up_all, down_all, depth)
        layer_out, gsend, grad_pre, norm_grads, out_pieces = got[:5]
        sources = got[5:] + (out_pieces, norm_grads)
    else:
        layer_out, gsend, grad_pre, norm_grads, out_pieces, up_pieces, down_pieces = feed_forward(
            direct, tokens, cotangent, heads, norms, out_all, up_all, down_all, depth
        )
        sources = ()
    got = attention_backward(
        gsend, xall, wfull, tokc, segw, qk, v, kern1, kern3, land, counts, weights,
        mixed, carried, conv_weight, slot_live, grad_pre, hist, sources, taps_total, depth,
    )
    if direct:
        (
            input_grad, grad_qkv, grad_conv, grad_up, grad_down, grad_out, grad_gain, grad_bias, proxies,
            layer_out,
        ) = hand_over(*got, proxies, layer_out)
        grad_up = grad_up.T
    else:
        input_grad, grad_w, grad_conv = got
        grad_w = exchange(grad_w.astype(bf16).reshape(dp_size, depth, -1), "dp").astype(f32).sum(axis=0)
        pairs = grad_w[:, : LANES * heads_n].reshape(depth, heads_n, 2, HEAD_DIM)
        grad_qkv = jnp.concatenate(
            [
                jnp.moveaxis(pairs, 2, 0).reshape(2, depth, width),
                grad_w[None, :, LANES * heads_n : LANES * heads_n + width],
            ]
        )
        grad_conv = lax.psum(grad_conv, "dp")[:heads_n, first : first + taps_total]
        grad_up = lax.psum_scatter(up_pieces, both, scatter_dimension=0, tiled=True).astype(f32).T
        grad_down = lax.psum_scatter(down_pieces, both, scatter_dimension=0, tiled=True).astype(f32)
        out_pieces = out_pieces[:, :, :width].reshape(blocks, dp_size, depth, width)
        out_pieces = jnp.swapaxes(out_pieces, 0, 1).reshape(devices, depth, width)
        grad_out = lax.psum_scatter(out_pieces, both, scatter_dimension=0, tiled=False).astype(f32).T
        norm_sum = exchange(split_up(norm_grads[:4], 1, devices), both).sum(axis=0)
        grad_gain, grad_bias = norm_sum[:2], norm_sum[2:]
    return (
        layer_out,
        input_grad,
        grad_qkv,
        grad_out,
        grad_conv,
        grad_up,
        grad_down,
        grad_gain,
        grad_bias,
        jnp.transpose(proxies, (1, 2, 0)),
    )


def solution(mesh):
    return jax.shard_map(
        per_device,
        mesh=mesh,
        in_specs=(
            P(("dp", "tensor"), None),
            P(None, "dp", "tensor"),
            P("tensor", "dp"),
            P("tensor", None),
            P(None, ("dp", "tensor")),
            P(("dp", "tensor"), None),
            P(None, ("dp", "tensor")),
            P(None, ("dp", "tensor")),
            P(("dp", "tensor"), None),
            P("dp", None),
            P("dp", None),
            P("dp", None),
            P("dp", None),
        ),
        out_specs=(
            P(("dp", "tensor"), None),
            P(("dp", "tensor"), None),
            P(None, "dp", "tensor"),
            P("tensor", "dp"),
            P("tensor", None),
            P(None, ("dp", "tensor")),
            P(("dp", "tensor"), None),
            P(None, ("dp", "tensor")),
            P(None, ("dp", "tensor")),
            P("dp", None, "tensor"),
        ),
        check_vma=False,
    )
```

```python
import functools
import math

import jax
import jax.numpy as jnp
from jax import lax
from jax.experimental import pallas as pl
from jax.experimental.pallas import tpu as pltpu
from jax.sharding import PartitionSpec as P

HEAD_DIM = 64
LANDMARKS = 64
NEWTON = 6
TILE = 128
HALO = TILE // 2
CHUNK = 256
LANES = 128
bf16 = jnp.bfloat16
f32 = jnp.float32
i32 = jnp.int32
norm_epsilon = 1e-05
MESH = pl.DeviceIdType.MESH
LIMIT = 62 * 2**20


def mm(a, b):
    return lax.dot_general(a, b, (((1,), (0,)), ((), ())), preferred_element_type=f32)


def mm_nt(a, b):
    return lax.dot_general(a, b, (((1,), (1,)), ((), ())), preferred_element_type=f32)


def split(a):
    high = a.astype(bf16)
    return high, (a - high.astype(f32)).astype(bf16)


def mm3(a, b, dot=mm):
    return dot(a[0], b[0]) + (dot(a[0], b[1]) + dot(a[1], b[0]))


def left_of(a):
    return jnp.concatenate(split(a), axis=1)


def right_of(b):
    high, low = split(b)
    top = jnp.concatenate([high, low], axis=1)
    bottom = jnp.concatenate([jnp.zeros_like(high), high], axis=1)
    return jnp.concatenate([top, bottom], axis=0)


def right_nt(b):
    high, low = split(b)
    top = jnp.concatenate([high, jnp.zeros_like(high)], axis=1)
    bottom = jnp.concatenate([low, high], axis=1)
    return jnp.concatenate([top, bottom], axis=0)


def tt(left, right):
    both = mm(left, right)
    return both[:, :TILE] + both[:, TILE:]


def tt_nt(left, right):
    both = mm_nt(left, right)
    return both[:, :TILE] + both[:, TILE:]


def iota(shape, dim):
    return lax.broadcasted_iota(i32, shape, dim)


def tile_same():
    shape = (TILE, TILE)
    return iota(shape, 0) // LANDMARKS == iota(shape, 1) // LANDMARKS


def tile_eye():
    shape = (TILE, TILE)
    return (iota(shape, 0) == iota(shape, 1)).astype(f32)


def pack(tile):
    return tile[:LANDMARKS] + tile[LANDMARKS:]


def unpack(packed):
    first = iota(packed.shape, 1) < LANDMARKS
    return jnp.concatenate([jnp.where(first, packed, 0.0), jnp.where(first, 0.0, packed)], axis=0)


def landmark_parts(land):
    first = iota(land.shape, 1) < HEAD_DIM
    turned = pltpu.roll(land, HEAD_DIM, 1)
    return jnp.where(first, turned, 0.0), jnp.where(first, 0.0, turned), jnp.where(first, land, 0.0)


def lane_masks():
    first = (iota((LANDMARKS, TILE), 1) < LANDMARKS).astype(f32)
    return first.astype(bf16), (1.0 - first).astype(bf16)


def packed_eye():
    shape = (LANDMARKS, TILE)
    return (iota(shape, 0) == iota(shape, 1) % LANDMARKS).astype(f32)


def packed_right(b, masks):
    high, low = split(b)
    high = jnp.concatenate([high * masks[0], high * masks[1]], axis=0)
    low = jnp.concatenate([low * masks[0], low * masks[1]], axis=0)
    top = jnp.concatenate([high, low], axis=1)
    bottom = jnp.concatenate([jnp.zeros_like(high), high], axis=1)
    return jnp.concatenate([top, bottom], axis=0)


def packed_tn(a, b):
    (ah, al), (bh, bl) = split(a), split(b)
    both = lax.dot_general(
        jnp.concatenate([ah, al, ah], axis=0),
        jnp.concatenate([bh, bh, bl], axis=0),
        (((0,), (0,)), ((), ())),
        preferred_element_type=f32,
    )
    first = iota(a.shape, 1) < LANDMARKS
    return jnp.where(first, both[:LANDMARKS], both[LANDMARKS:])


def newton_stages(hist, i, ident, masks):
    tiles = range(hist.shape[2])
    P = [hist[i, 0, n] for n in tiles]
    Pl, Pr = [left_of(p) for p in P], [packed_right(p, masks) for p in P]
    S = [tt(Pl[n], Pr[n]) for n in tiles]
    yield
    N = [13.0 * ident - 15.0 * P[n] + 7.0 * S[n] - tt(left_of(S[n]), Pr[n]) for n in tiles]
    yield
    for n in tiles:
        hist[i, 2, n] = S[n]
        hist[i, 3, n] = N[n]
        rows = jnp.concatenate([Pl[n], left_of(hist[i, 1, n])], axis=0)
        both = 0.25 * tt(rows, packed_right(N[n], masks))
        hist[i + 1, 0, n] = both[:LANDMARKS]
        hist[i + 1, 1, n] = both[LANDMARKS:]
    yield


def newton_back_stages(hist, gstate, i, masks):
    tiles = range(hist.shape[2])
    gP, gZ = [gstate[0, n] for n in tiles], [gstate[1, n] for n in tiles]
    P = [hist[i, 0, n] for n in tiles]
    Pl, Pr = [left_of(p) for p in P], [packed_right(p, masks) for p in P]
    gN = [
        0.25 * (tt(Pl[n], packed_right(gP[n], masks)) + packed_tn(hist[i, 1, n], gZ[n])) for n in tiles
    ]
    both = [
        0.25
        * tt(
            jnp.concatenate([left_of(gP[n]), left_of(gZ[n])], axis=0),
            packed_right(hist[i, 3, n], masks),
        )
        for n in tiles
    ]
    yield
    gS = [7.0 * gN[n] - tt(left_of(gN[n]), Pr[n]) for n in tiles]
    kept = [
        both[n][:LANDMARKS] - 15.0 * gN[n] - tt(left_of(hist[i, 2, n]), packed_right(gN[n], masks))
        for n in tiles
    ]
    yield
    for n in tiles:
        gstate[1, n] = both[n][LANDMARKS:]
        gstate[0, n] = kept[n] + tt(left_of(gS[n]), Pr[n]) + tt(Pl[n], packed_right(gS[n], masks))
    yield


def newton_start(A):
    colsum = jnp.sum(A, axis=0, keepdims=True)
    first = iota(colsum.shape, 1) < LANDMARKS
    tops = [
        jnp.max(jnp.where(first, colsum, 0.0), axis=1, keepdims=True),
        jnp.max(jnp.where(first, 0.0, colsum), axis=1, keepdims=True),
    ]
    factor = 1.0 / jnp.maximum(jnp.where(first, tops[0], tops[1]), 1.0)
    return factor, colsum, tops


def column(row):
    return jnp.broadcast_to(row, (LANES, LANES)).T


def band_from(row):
    wide = jnp.broadcast_to(row, (TILE, 2 * TILE))
    return pltpu.roll(wide, 0, 1, stride=1, stride_axis=0)


def diagonal_sums(band):
    where = iota(band.shape, 0)
    step = 1
    while step < TILE:
        turned = pltpu.roll(band, 2 * TILE - step, 1)
        band = jnp.where((where // step) % 2 == 1, turned, band)
        step *= 2
    return jnp.sum(band, axis=0, keepdims=True)


def seg_of(code):
    return (code // 512) % 8


def live_of(code):
    return code // 4096


def slot_of(code):
    return code % 512


def fold(rows, width):
    half = rows.shape[0] // 2
    far = pltpu.roll(rows[half:], width, 1)
    near = rows[:half]
    return jnp.concatenate(
        [near[:, :LANES], near[:, LANES:] + far[:, LANES:], far[:, :LANES]], axis=1
    )


def unfold(folded, k, width):
    if k == 0:
        return folded[:, : 2 * LANES]
    return pltpu.roll(folded[:, LANES:].astype(f32), width, 1)


class Place:
    def __init__(self):
        self.dp = lax.axis_index("dp")
        self.t = lax.axis_index("tensor")
        self.x = self.t // 2
        self.c = self.t % 2
        self.sibling = self.x * 2 + 1 - self.c
        self.across = (1 - self.x) * 2 + self.c
        self.diagonal = (1 - self.x) * 2 + 1 - self.c
        self.z = self.dp // 2
        self.y = self.dp % 2

    def tensor_peers(self):
        return [(self.dp, t) for t in (self.sibling, self.across, self.diagonal)]

    def dp_at(self, turn_z, turn_y):
        return ((self.z + turn_z) % 4) * 2 + (self.y + turn_y) % 2


def greet(peers):
    barrier = pltpu.get_barrier_semaphore()
    for peer in peers:
        pl.semaphore_signal(barrier, inc=1, device_id=peer, device_id_type=MESH)
    pl.semaphore_wait(barrier, len(peers))


def push(src, dst, sems, index, dp, t):
    return pltpu.make_async_remote_copy(
        src_ref=src,
        dst_ref=dst,
        send_sem=sems.at[0, index],
        recv_sem=sems.at[1, index],
        device_id=(dp, t),
        device_id_type=MESH,
    )


class Spreader:
    def __init__(self, here, shard, whole, sems, local, by_x, by_rows=False):
        self.here, self.shard, self.whole, self.sems, self.local = here, shard, whole, sems, local
        self.by_rows, self.by_x = by_rows, by_x
        first, last = (here.dp, here.across), (here.dp_at(0, 1), here.t)
        self.first, self.last = (first, last) if by_x else (last, first)
        self.copies = []
        self.from_z, self.from_first, self.from_last, self.from_core = {}, {}, {}, []

    def at(self, z, y, x):
        c = self.here.c
        if not self.by_rows:
            return self.whole.at[z, y, x, c]
        depth = self.shard.shape[0]
        rows = pl.ds(pl.multiple_of((z * 2 + y) * depth, 16), depth)
        return self.whole.at[x, c, rows]

    def one(self, dz):
        return self.at((self.here.z + 4 - dz) % 4, self.here.y, self.here.x)

    def pair(self, dz, turned):
        here, z = self.here, (self.here.z + 4 - dz) % 4
        if self.by_x:
            return self.at(z, (here.y + turned) % 2, slice(None))
        return self.at(z, slice(None), (here.x + turned) % 2)

    def push(self, src, dst, index, place):
        copy = push(src, dst, self.sems, index, *place)
        copy.start()
        self.copies.append(copy)
        return copy

    def begin(self):
        self.kept = pltpu.make_async_copy(self.shard, self.one(0), self.local)
        self.kept.start()
        self.from_first[0] = self.push(self.shard, self.one(0), 3, self.first)

    def along_z(self, dz):
        here = self.here
        self.from_z[dz] = self.push(self.shard, self.one(0), dz - 1, (here.dp_at(dz, 0), here.t))

    def along_first(self, dz):
        self.from_z[dz].wait_recv()
        self.from_first[dz] = self.push(self.one(dz), self.one(dz), 3 + dz, self.first)

    def along_last(self, dz):
        if dz == 0:
            self.kept.wait()
        self.from_first[dz].wait_recv()
        got = self.pair(dz, 0)
        self.from_last[dz] = self.push(got, got, 7 + dz, self.last)
        self.from_core.append(self.push(got, got, 11 + dz, (self.here.dp, self.here.sibling)))

    def to_core(self, dz):
        self.from_last[dz].wait_recv()
        got = self.pair(dz, 1)
        self.from_core.append(self.push(got, got, 15 + dz, (self.here.dp, self.here.sibling)))

    def finish(self):
        for dz in self.from_first:
            if dz not in self.from_last:
                self.from_first[dz].wait_recv()
        for copy in self.from_core:
            copy.wait_recv()
        for copy in self.copies:
            copy.wait_send()


LATE = (3, 2)


def spread_lanes(length, whole):
    shape = (LANES, whole)
    return (iota(shape, 0) == iota(shape, 1) % length).astype(f32)


def forward_body(gather, taps_total, *refs):
    (x, w, conv, seg, slot, live, slot_live), refs = refs[:7], refs[7:]
    if gather:
        (w_up, w_down, w_out, gain, bias), refs = refs[:5], refs[5:]
    (
        xall_out, wfull_out, tokc, segw, qk_out, v_out, kern1_out, kern3_out,
        land, counts, Aout, mixed, carried, heads, prox, hist_out,
    ) = refs[:16]
    refs = refs[16:]
    if gather:
        (up_all, down_all, out_all, norms), refs = refs[:4], refs[4:]
    (
        xall, wfull, qk, v, kern1, kern3,
        wsh, wlog, l3, carriedT, hist, bands, hsend, segp, taps, xsem, wsem, hsem, osem,
    ) = refs[:19]
    refs = refs[19:]
    keeping = []

    def keep(src, dst):
        copy = pltpu.make_async_copy(src, dst, osem.at[len(keeping)])
        copy.start()
        keeping.append(copy)

    here = Place()
    block = x.shape[0]
    blocks = xall.shape[0]
    seq = block * blocks
    heads_n = qk.shape[1] // LANES
    nslot = land.shape[0]
    wide = v.shape[1]
    nchunk = seq // CHUNK
    per_block = block // CHUNK
    tiles_n = nslot // TILE
    width = heads_n * HEAD_DIM
    scaling = 1.0 / math.sqrt(HEAD_DIM)

    depth = w.shape[1]
    parts = []
    for h in range(heads_n):
        e = slice(HEAD_DIM * h, HEAD_DIM * h + HEAD_DIM)
        parts += [w[0, :, e], w[1, :, e]]
    parts += [w[2], jnp.zeros((depth, wide - width), bf16)]
    wsh[...] = jnp.concatenate(parts, axis=1)

    peers = here.tensor_peers()
    if gather:
        peers = peers + [(here.dp_at(dz, 0), here.t) for dz in (1, 2, 3)] + [(here.dp_at(0, 1), here.t)]
        out_sh, norm_sh, norm_all = refs[:3]
        out_sh[...] = jnp.concatenate(
            [w_out[...].astype(f32).T, jnp.zeros((depth, wide - width), f32)], axis=1
        ).astype(bf16)
        norm_sh[...] = jnp.zeros_like(norm_sh)
        norm_sh[0:2, : gain.shape[1]] = gain[...].astype(f32)
        norm_sh[2:4, : gain.shape[1]] = bias[...].astype(f32)
        sems = refs[3:]
        spread_out = Spreader(here, out_sh, out_all, sems[2], sems[3], True, by_rows=True)
        spread_norm = Spreader(here, norm_sh, norm_all, sems[4], sems[5], True)
        whole = (spread_out, spread_norm)
        partly = (
            Spreader(here, w_up, up_all, sems[0], sems[1], True),
            Spreader(here, w_down, down_all, sems[6], sems[7], False),
        )
        spreads = whole + partly
    greet(peers)

    copies = []
    pieces = block // TILE

    def start(copy):
        copy.start()
        copies.append(copy)
        return copy

    crossing = [
        start(push(x.at[pl.ds(p * TILE, TILE)], xall.at[here.t, pl.ds(p * TILE, TILE)], xsem, p, here.dp, here.across))
        for p in range(pieces)
    ]
    beside = start(push(x, xall.at[here.t], xsem, pieces, here.dp, here.sibling))
    if gather:
        mine = wfull.at[pl.ds(pl.multiple_of(here.dp * depth, 16), depth)]
        along = [start(push(wsh, mine, wsem, dz, here.dp_at(dz, 0), here.t)) for dz in (1, 2, 3)]
        along = [start(push(wsh, mine, wsem, 0, here.dp_at(0, 1), here.t))] + along
        wfull[pl.ds(pl.multiple_of(here.dp * depth, 16), depth), :] = wsh[...]
    else:
        wfull[...] = wsh[...]
    xall[here.t] = x[...]

    segp[...] = jnp.full(segp.shape, -1, i32)
    segp[0:1, TILE : TILE + seq] = jnp.where(live[...] > 0, seg[...], -1)
    segp[1:2, TILE : TILE + seq] = seg[...]
    code = (slot[...] + 512 * seg[...] + 4096 * live[...]).astype(f32)
    for i in range(seq // TILE):
        lanes = slice(i * TILE, i * TILE + TILE)
        tokc[lanes, :] = column(code[:, lanes]).astype(i32)
        near = pltpu.roll(segp[:, i * TILE : i * TILE + 3 * TILE], 3 * TILE - HALO, 1)
        segw[i : i + 1, :] = near[0:1, : 2 * TILE]
        segw[seq // TILE + i : seq // TILE + i + 1, :] = near[1:2, : 2 * TILE]
    taps[...] = jnp.zeros_like(taps)
    taps[:heads_n, :taps_total] = conv[...]
    moved = pltpu.roll(taps[...], HALO - taps_total // 2, 1)
    for h in range(heads_n):
        bands[h] = band_from(moved[h : h + 1, :])
    doc_row = iota((1, nslot), 1) // LANDMARKS
    live_row = slot_live[...]
    live_cols = [column(live_row[:, g * TILE : (g + 1) * TILE].astype(f32)) for g in range(tiles_n)]
    v[0:HALO, :] = jnp.zeros((HALO, wide), bf16)
    v[seq + HALO : seq + 2 * HALO, :] = jnp.zeros((HALO, wide), bf16)

    if gather:
        along[0].wait_recv()
        for dz in (1, 2, 3):
            along[dz].wait_recv()
            got = wfull.at[pl.ds(pl.multiple_of(here.dp_at(4 - dz, 0) * depth, 16), depth)]
            along.append(start(push(got, got, wsem, 3 + dz, here.dp_at(0, 1), here.t)))
        for spread in spreads:
            spread.begin()
            spread.along_z(1)
            spread.along_z(3)
        for dz in (1, 2, 3):
            along[3 + dz].wait_recv()

    def project(b, carry):
        def one(i, carry):
            acc, cnt = carry
            c = b * per_block + i
            rows = pl.ds(pl.multiple_of(c * CHUNK, CHUNK), CHUNK)
            out = mm(xall[b, pl.ds(pl.multiple_of(i * CHUNK, CHUNK), CHUNK), :], wfull[...])
            qk_now = out[:, : LANES * heads_n].astype(bf16)
            qk[rows, :] = qk_now
            v[pl.ds(pl.multiple_of(c * CHUNK + HALO, HALO), CHUNK), :] = out[:, LANES * heads_n :].astype(bf16)
            slot_now = slot[:, pl.ds(pl.multiple_of(c * CHUNK, CHUNK), CHUNK)]
            hot = (slot_now == iota((nslot, CHUNK), 0)).astype(f32)
            return acc + mm(hot.astype(bf16), qk_now), cnt + jnp.sum(hot, axis=1, keepdims=True)

        return lax.fori_loop(0, per_block, one, carry)

    carry = (jnp.zeros((nslot, LANES * heads_n), f32), jnp.zeros((nslot, 1), f32))
    carry = project(here.t, carry)
    beside.wait_recv()
    carry = project(here.sibling, carry)
    passed = []
    for p in range(pieces):
        crossing[p].wait_recv()
        got = xall.at[here.across, pl.ds(p * TILE, TILE)]
        passed.append(start(push(got, got, xsem, pieces + 1 + p, here.dp, here.sibling)))
    carry = project(here.across, carry)
    for p in range(pieces):
        passed[p].wait_recv()
    acc, cnt = project(here.diagonal, carry)
    cnt = jnp.maximum(cnt, 1.0)
    counts[...] = jnp.broadcast_to(cnt, counts.shape)
    land[...] = acc / cnt

    if gather:
        for spread in spreads:
            spread.along_z(2)
            spread.along_last(0)
    keep(xall, xall_out)
    keep(wfull, wfull_out)
    keep(qk, qk_out)
    keep(v, v_out)

    same = tile_same()
    ident = packed_eye()
    masks = lane_masks()
    for h in range(heads_n):
        k0, q1, q0 = landmark_parts(land[:, LANES * h : LANES * h + LANES])
        wlog[h] = jnp.concatenate(split(jnp.concatenate([k0, q1], axis=0) * scaling), axis=1)
        for g in range(tiles_n):
            rows = slice(g * TILE, g * TILE + TILE)
            logit = tt_nt(left_of(q0[rows] * scaling), right_nt(k0[rows]))
            filled = jnp.where(same & (live_row[:, rows] > 0), logit, -1e9)
            raised = jnp.exp(filled - jnp.max(filled, axis=1, keepdims=True))
            A = raised / jnp.sum(raised, axis=1, keepdims=True) * live_cols[g]
            n = h * tiles_n + g
            Aout[n] = A
            factor, _, _ = newton_start(A)
            W = A * factor
            hist[0, 0, n] = pack(tt_nt(left_of(A), right_nt(W)))
            hist[0, 1, n] = pack(W.T)

    def logits(c, top, between=lambda: None):
        rows = pl.ds(pl.multiple_of(c * CHUNK, CHUNK), CHUNK)
        now = tokc[rows, 0:1]
        allowed = (seg_of(now) == doc_row) & (live_row > 0)
        alive = allowed & (live_of(now) > 0)
        tops = []
        for h in range(heads_n):
            part = qk[rows, LANES * h : LANES * h + LANES]
            both = mm_nt(jnp.concatenate([part, part], axis=1), wlog[h])
            one = jnp.where(allowed, both[:, :nslot], -1e9)
            raised = jnp.exp(one - jnp.max(one, axis=1, keepdims=True))
            kern1[h, rows, :] = (raised / jnp.sum(raised, axis=1, keepdims=True)).astype(bf16)
            three = jnp.where(alive, both[:, nslot:], -1e9)
            l3[h, rows, :] = three
            tops.append(jnp.maximum(top[h], jnp.max(three, axis=0, keepdims=True)))
            between()
        return tuple(tops)

    def step_and_logits(i, top):
        stages = newton_stages(hist, i, ident, masks)
        next(stages)
        return logits(i, top, lambda: next(stages, None))

    top = tuple(jnp.full((1, nslot), -1e9, f32) for _ in range(heads_n))
    third = NEWTON // 3
    top = lax.fori_loop(0, third, step_and_logits, top)
    if gather:
        for spread in spreads:
            spread.along_first(1)
    top = lax.fori_loop(third, 2 * third, step_and_logits, top)
    if gather:
        for spread in spreads:
            spread.along_first(3)
    top = lax.fori_loop(2 * third, NEWTON, step_and_logits, top)
    keep(hist, hist_out)
    top = lax.fori_loop(NEWTON, nchunk, logits, top)
    keep(kern1, kern1_out)
    if gather:
        for spread in spreads:
            spread.along_last(1)
            spread.to_core(0)
        for spread in spreads:
            spread.along_first(2)

    def raise_three(c, total):
        rows = pl.ds(pl.multiple_of(c * CHUNK, CHUNK), CHUNK)
        totals = []
        for h in range(heads_n):
            raised = jnp.exp(l3[h, rows, :] - top[h])
            l3[h, rows, :] = raised
            totals.append(total[h] + jnp.sum(raised, axis=0, keepdims=True))
        return tuple(totals)

    total = lax.fori_loop(
        0, nchunk, raise_three, tuple(jnp.zeros((1, nslot), f32) for _ in range(heads_n))
    )
    norm = [live_row.astype(f32) / total[h] for h in range(heads_n)]
    carriedT[...] = jnp.zeros_like(carriedT)

    def carry_three(c, none):
        rows = pl.ds(pl.multiple_of(c * CHUNK, CHUNK), CHUNK)
        vT = v[pl.ds(pl.multiple_of(c * CHUNK + HALO, HALO), CHUNK), :].astype(f32).T.astype(bf16)
        for h in range(heads_n):
            low = (l3[h, rows, :] * norm[h]).astype(bf16)
            kern3[h, rows, :] = low
            e = slice(HEAD_DIM * h, HEAD_DIM * h + HEAD_DIM)
            carriedT[e, :] += mm(vT[e, :], low)
        return none

    lax.fori_loop(0, nchunk, carry_three, 0)
    keep(kern3, kern3_out)
    if gather:
        for spread in whole:
            spread.along_last(3)
        for spread in spreads:
            spread.to_core(1)
    carried_all = carriedT[...].T
    carried[...] = carried_all
    lane = iota((TILE, wide), 1) // HEAD_DIM
    docs = nslot // LANDMARKS
    prox_all = jnp.zeros((8, LANES), f32)
    for h in range(heads_n):
        for g in range(tiles_n):
            rows = slice(g * TILE, g * TILE + TILE)
            n = h * tiles_n + g
            Z = hist[NEWTON, 1, n]
            part = split(jnp.where(lane == h, carried_all[rows], 0.0))
            mixed[h, rows, :] = mm3(split(unpack(Z)), part).astype(bf16)
            A = Aout[n]
            A2 = jnp.sum(A * A, axis=0, keepdims=True)
            Z2 = jnp.sum(Z * Z, axis=0, keepdims=True)
            first = iota(A2.shape, 1) < LANDMARKS
            for half in range(2):
                mine = first if half == 0 else jnp.logical_not(first)
                a2 = jnp.sum(jnp.where(mine, A2, 0.0), axis=1, keepdims=True)
                z2 = jnp.sum(jnp.where(mine, Z2, 0.0), axis=1, keepdims=True)
                doc = g * 2 + half
                alive = live_row[:, doc * LANDMARKS : doc * LANDMARKS + 1] > 0
                value = jnp.where(alive, jnp.sqrt(a2) * jnp.sqrt(z2) / LANDMARKS, 0.0)
                here_too = (iota(prox_all.shape, 0) == h) & (iota(prox_all.shape, 1) == doc)
                prox_all = jnp.where(here_too, value, prox_all)
    for h in range(heads_n):
        prox[h] = prox_all[h : h + 1, :docs]

    def finish(b, out, out_row):
        for k in range(per_block):
            c = b * per_block + k
            rows = pl.ds(pl.multiple_of(c * CHUNK, CHUNK), CHUNK)
            total = mm(kern1[0, rows, :], mixed[0])
            for h in range(1, heads_n):
                total = total + mm(kern1[h, rows, :], mixed[h])
            for part in range(CHUNK // TILE):
                i = c * (CHUNK // TILE) + part
                now = tokc[pl.ds(pl.multiple_of(i * TILE, TILE), TILE), 0:1]
                near = seg_of(now) == segw[pl.ds(i, 1), :]
                window = v[pl.ds(pl.multiple_of(i * TILE, TILE), 2 * TILE), :]
                conv = jnp.zeros((TILE, wide), f32)
                for h in range(heads_n):
                    term = mm(jnp.where(near, bands[h], 0.0).astype(bf16), window)
                    conv = jnp.where(lane == h, term, conv)
                got = (total[part * TILE : (part + 1) * TILE, :] + conv) * live_of(now).astype(f32)
                at = pl.ds(part * TILE, TILE)
                if k == 0:
                    out[out_row, at, : 2 * LANES] = got.astype(bf16)
                else:
                    far = pltpu.roll(got, width, 1)
                    middle = slice(LANES, 2 * LANES)
                    both = out[out_row, at, middle].astype(f32) + far[:, LANES:]
                    out[out_row, at, middle] = both.astype(bf16)
                    out[out_row, at, 2 * LANES :] = far[:, :LANES].astype(bf16)

    if gather:
        for spread in whole:
            spread.along_last(2)
    sent = []
    for k, to in enumerate((here.diagonal, here.across, here.sibling)):
        finish(to, hsend, k)
        sent.append(start(push(hsend.at[k], heads.at[here.t], hsem, k, here.dp, to)))
    finish(here.t, heads, here.t)
    if gather:
        for spread in whole:
            spread.to_core(3)
            spread.to_core(2)
    for copy in sent:
        copy.wait_recv()
    if gather:
        for spread in spreads:
            spread.finish()
        length = gain.shape[1]
        far = spread_lanes(length, x.shape[1]).astype(bf16)
        owner = iota((32, x.shape[1]), 1) // length == iota((32, x.shape[1]), 0)
        for r in range(4):
            rows = norm_all[...].reshape(32, 8, LANES)[:, r, :].astype(bf16)
            norms[r : r + 1, :] = jnp.sum(jnp.where(owner, mm(rows, far), 0.0), axis=0, keepdims=True)
        norms[4:8, :] = jnp.zeros((4, x.shape[1]), f32)
    for copy in copies:
        copy.wait_send()
    for copy in keeping:
        copy.wait()


VMEM = pl.BlockSpec(memory_space=pltpu.VMEM)
ANY = pl.BlockSpec(memory_space=pl.ANY)


def dma(*shape):
    return pltpu.SemaphoreType.DMA(shape)


def attention_forward(x, w, conv, seg, slot, live, slot_live, extra, heads_n, blocks, taps_total):
    block, feat = x.shape
    seq, nslot = block * blocks, slot_live.shape[1]
    gather = len(extra) > 0
    depth = w.shape[1]
    wide = -(-heads_n * HEAD_DIM // 256) * 256
    tiles_n = heads_n * (nslot // TILE)
    shape = jax.ShapeDtypeStruct
    outs = [
        shape((blocks, block, feat), bf16),
        shape((feat, LANES * heads_n + wide), bf16),
        shape((seq, LANES), i32),
        shape((2 * (seq // TILE), 2 * TILE), i32),
        shape((seq, LANES * heads_n), bf16),
        shape((seq + 2 * HALO, wide), bf16),
        shape((heads_n, seq, nslot), bf16),
        shape((heads_n, seq, nslot), bf16),
        shape((nslot, LANES * heads_n), f32),
        shape((nslot, LANES), f32),
        shape((tiles_n, TILE, TILE), f32),
        shape((heads_n, nslot, wide), bf16),
        shape((nslot, wide), f32),
        shape((blocks, block // 2, 2 * heads_n * HEAD_DIM), bf16),
        shape((heads_n, 1, nslot // LANDMARKS), f32),
        shape((NEWTON + 1, 4, tiles_n, LANDMARKS, TILE), f32),
    ]
    out_specs = [ANY, ANY, VMEM, VMEM] + [ANY] * 4 + [VMEM] * 7 + [ANY]
    scratch = [pltpu.VMEM(outs[n].shape, bf16) for n in (0, 1, 4, 5, 6, 7)]
    scratch += [
        pltpu.VMEM((depth, LANES * heads_n + wide), bf16),
        pltpu.VMEM((heads_n, 2 * nslot, 256), bf16),
        pltpu.VMEM((heads_n, seq, nslot), f32),
        pltpu.VMEM((wide, nslot), f32),
        pltpu.VMEM(outs[15].shape, f32),
        pltpu.VMEM((heads_n, TILE, 2 * TILE), f32),
        pltpu.VMEM((3, block // 2, 2 * heads_n * HEAD_DIM), bf16),
        pltpu.VMEM((8, seq + 2 * TILE), i32),
        pltpu.VMEM((8, 2 * TILE), f32),
        dma(2, 2 * (block // TILE) + 1),
        dma(2, 7),
        dma(2, 3),
        dma(7),
    ]
    if gather:
        hidden_n = extra[0].shape[0]
        outs += [
            shape((4, 2, 2, 2, hidden_n, feat), bf16),
            shape((4, 2, 2, 2, hidden_n, feat), bf16),
            shape((2, 2, feat, wide), bf16),
            shape((8, feat), f32),
        ]
        out_specs += [ANY, ANY, ANY, VMEM]
        scratch += [
            pltpu.VMEM((depth, wide), bf16),
            pltpu.VMEM((8, LANES), f32),
            pltpu.VMEM((4, 2, 2, 2, 8, LANES), f32),
        ]
        for _ in range(4):
            scratch += [dma(2, 19), pltpu.SemaphoreType.DMA]
    return pl.pallas_call(
        functools.partial(forward_body, gather, taps_total),
        out_shape=tuple(outs),
        in_specs=[VMEM] * (7 + len(extra)),
        out_specs=tuple(out_specs),
        scratch_shapes=scratch,
        compiler_params=pltpu.CompilerParams(
            vmem_limit_bytes=LIMIT, collective_id=1 if gather else 2, has_side_effects=True
        ),
        name="attention_forward",
    )(x, w, conv, seg, slot, live, slot_live, *extra)


def normalized(u):
    mean = jnp.mean(u, axis=-1, keepdims=True)
    centered = u - mean
    scale = lax.rsqrt(jnp.mean(centered * centered, axis=-1, keepdims=True) + norm_epsilon)
    return centered * scale, scale


def normalized_back(g, n, scale):
    return scale * (
        g - jnp.mean(g, axis=-1, keepdims=True) - n * jnp.mean(g * n, axis=-1, keepdims=True)
    )


ROWS = 256
FF_CHUNK = 512


def mm_tn(a, b):
    return lax.dot_general(a, b, (((0,), (0,)), ((), ())), preferred_element_type=f32)


def feed_body(
    direct, x, cot, folded, norms, wout, up_in, down_in,
    layer_out, gsend, gpre, gnorm, gout, gup, gdown,
    heads, up, down, act, slope, hidden, hlow, n1, r1, gsum, glow, acc, up_out, down_out, sems,
):
    block, feat = x.shape
    chunks = act.shape[0]
    loads = []
    for j in range(chunks):
        rows = pl.ds(j * FF_CHUNK, FF_CHUNK)
        loads.append(
            (
                pltpu.make_async_copy(up_in.at[rows], up.at[j], sems.at[0, j]),
                pltpu.make_async_copy(down_in.at[rows], down.at[j], sems.at[1, j]),
            )
        )
        for load in loads[-1]:
            load.start()
    gain0, gain1 = norms[0:1, :], norms[1:2, :]
    bias0, bias1 = norms[2:3, :], norms[3:4, :]
    width = folded.shape[2] // 2
    for t in range(folded.shape[0]):
        for k in range(2):
            heads[t, k * (block // 2) : (k + 1) * (block // 2), :] = unfold(folded[t], k, width).astype(bf16)
    acc[...] = sum(mm_nt(heads[t], wout[t]) for t in range(heads.shape[0]))

    def first_norm(i, none):
        rows = pl.ds(pl.multiple_of(i * ROWS, ROWS), ROWS)
        n, scale = normalized(x[rows, :].astype(f32) + acc[rows, :])
        now = n * gain0 + bias0
        n1[rows, :] = n
        r1[rows, :] = jnp.broadcast_to(scale, (ROWS, LANES))
        hidden[rows, :] = now
        hlow[rows, :] = now.astype(bf16)
        return none

    lax.fori_loop(0, block // ROWS, first_norm, 0)
    acc[...] = hidden[...]
    for j in range(chunks):
        for load in loads[j]:
            load.wait()

    def rise(j, none):
        u = mm_nt(hlow[...], up[j])
        cdf = 0.5 * (1.0 + lax.erf(u * math.sqrt(0.5)))
        act[j] = (u * cdf).astype(bf16)
        slope[j] = cdf + u * (jnp.exp(-0.5 * u * u) * (1.0 / math.sqrt(2.0 * math.pi)))
        acc[...] += mm(act[j], down[j])
        return none

    lax.fori_loop(0, chunks, rise, 0)

    def second_norm(i, sums):
        rows = pl.ds(pl.multiple_of(i * ROWS, ROWS), ROWS)
        n, scale = normalized(acc[rows, :])
        layer_out[rows, :] = (n * gain1 + bias1).astype(bf16)
        c = cot[rows, :].astype(f32)
        g = normalized_back(c * gain1, n, scale)
        gsum[rows, :] = g
        glow[rows, :] = g.astype(bf16)
        return (
            sums[0] + jnp.sum(c * n, axis=0, keepdims=True),
            sums[1] + jnp.sum(c, axis=0, keepdims=True),
        )

    zero = jnp.zeros((1, feat), f32)
    gain_two, bias_two = lax.fori_loop(0, block // ROWS, second_norm, (zero, zero))
    acc[...] = gsum[...]

    def fall(j, none):
        rows = pl.ds(pl.multiple_of(j * FF_CHUNK, FF_CHUNK), FF_CHUNK)
        g_act = mm_nt(glow[...], down[j])
        g_up = (g_act * slope[j]).astype(bf16)
        down_out[j] = mm_tn(act[j], glow[...]).astype(bf16)
        pltpu.make_async_copy(down_out.at[j], gdown.at[rows], sems.at[2, j]).start()
        up_out[j] = mm_tn(g_up, hlow[...]).astype(bf16)
        pltpu.make_async_copy(up_out.at[j], gup.at[rows], sems.at[3, j]).start()
        acc[...] += mm(g_up, up[j])
        return none

    lax.fori_loop(0, chunks, fall, 0)

    def first_back(i, sums):
        rows = pl.ds(pl.multiple_of(i * ROWS, ROWS), ROWS)
        g = acc[rows, :]
        n = n1[rows, :]
        back = normalized_back(g * gain0, n, r1[rows, 0:1])
        gpre[rows, :] = back
        glow[rows, :] = back.astype(bf16)
        return (
            sums[0] + jnp.sum(g * n, axis=0, keepdims=True),
            sums[1] + jnp.sum(g, axis=0, keepdims=True),
        )

    gain_one, bias_one = lax.fori_loop(0, block // ROWS, first_back, (zero, zero))
    gnorm[...] = jnp.concatenate(
        [gain_one, gain_two, bias_one, bias_two, jnp.zeros((4, feat), f32)], axis=0
    )
    for t in range(heads.shape[0]):
        gsend[t] = fold(mm(glow[...], wout[t]), width).astype(bf16)
        grad = mm_tn(glow[...], heads[t]).astype(bf16)
        if direct:
            gout[:, :, t // 2, t % 2] = grad.reshape((4, 2) + gout.shape[4:])
        else:
            gout[t] = grad

    def land(j, none):
        rows = pl.ds(pl.multiple_of(j * FF_CHUNK, FF_CHUNK), FF_CHUNK)
        pltpu.make_async_copy(down_out.at[j], gdown.at[rows], sems.at[2, j]).wait()
        pltpu.make_async_copy(up_out.at[j], gup.at[rows], sems.at[3, j]).wait()
        return none

    lax.fori_loop(0, chunks, land, 0)


RISE = (0, 3, 1, 2)
FALL = (2, 1, 3, 0)


def feed_direct_body(
    x, cot, folded, norms, wout, up_in, down_in,
    layer_out, gsend, gpre, gnorm, gout, sum_up, sum_down, part_up, part_down,
    heads, up, down, act, slope, hidden, hlow, n1, r1, gsum, glow, acc,
    gu, gd, cu, cd, yu, xd, lsem, csem, ysem, upsem, downsem,
):
    here = Place()
    block, feat = x.shape
    units = act.shape[2]
    copies = []

    def start(copy):
        copy.start()
        copies.append(copy)
        return copy

    loads = {}
    for k in RISE:
        z, late = (here.z + k) % 4, 4 - k in LATE
        near_up = (z, here.y, slice(None), here.c) if late else (z,)
        near_down = (z, slice(None), here.x, here.c) if late else (z,)
        loads[k] = [
            pltpu.make_async_copy(up_in.at[near_up], up.at[near_up], lsem.at[0, k]),
            pltpu.make_async_copy(down_in.at[near_down], down.at[near_down], lsem.at[1, k]),
        ]
        for load in loads[k]:
            load.start()
    greet(
        [(here.dp, here.sibling), (here.dp, here.across), (here.dp_at(0, 1), here.t)]
    )
    arriving = {}

    def send_late(dz):
        n, z = LATE.index(dz), (here.z + 4 - dz) % 4
        near_up, near_down = (z, here.y, slice(None), here.c), (z, slice(None), here.x, here.c)
        arriving[dz] = [
            start(push(up_in.at[near_up], up.at[near_up], upsem, n, here.dp_at(0, 1), here.t)),
            start(push(down_in.at[near_down], down.at[near_down], downsem, n, here.dp, here.across)),
            start(push(up_in.at[near_up], up.at[near_up], upsem, 2 + n, here.dp, here.sibling)),
            start(push(down_in.at[near_down], down.at[near_down], downsem, 2 + n, here.dp, here.sibling)),
        ]

    send_late(LATE[0])

    def pass_on(dz):
        n, z = LATE.index(dz), (here.z + 4 - dz) % 4
        for copy in arriving[dz][:2]:
            copy.wait_recv()
        far_up, far_down = (z, 1 - here.y, slice(None), here.c), (z, slice(None), 1 - here.x, here.c)
        arriving[dz] = arriving[dz][2:] + [
            start(push(up.at[far_up], up.at[far_up], upsem, 4 + n, here.dp, here.sibling)),
            start(push(down.at[far_down], down.at[far_down], downsem, 4 + n, here.dp, here.sibling)),
        ]

    gain0, gain1 = norms[0:1, :], norms[1:2, :]
    bias0, bias1 = norms[2:3, :], norms[3:4, :]
    width = folded.shape[2] // 2
    for t in range(folded.shape[0]):
        for k in range(2):
            heads[t, k * (block // 2) : (k + 1) * (block // 2), :] = unfold(folded[t], k, width).astype(bf16)
    acc[...] = sum(mm_nt(heads[t], wout[t]) for t in range(heads.shape[0]))

    def first_norm(i, none):
        rows = pl.ds(pl.multiple_of(i * ROWS, ROWS), ROWS)
        n, scale = normalized(x[rows, :].astype(f32) + acc[rows, :])
        now = n * gain0 + bias0
        n1[rows, :] = n
        r1[rows, :] = jnp.broadcast_to(scale, (ROWS, LANES))
        hidden[rows, :] = now
        hlow[rows, :] = now.astype(bf16)
        return none

    lax.fori_loop(0, block // ROWS, first_norm, 0)
    acc[...] = hidden[...]
    flat = (4, units, feat)
    up_of, down_of = up.reshape(flat), down.reshape(flat)
    for k in RISE:
        z = (here.z + k) % 4
        for load in loads[k]:
            load.wait()
        if 4 - k in LATE:
            for copy in arriving[4 - k]:
                copy.wait_recv()
        u = mm_nt(hlow[...], up_of[z])
        cdf = 0.5 * (1.0 + lax.erf(u * math.sqrt(0.5)))
        act[k] = (u * cdf).astype(bf16)
        slope[k] = cdf + u * (jnp.exp(-0.5 * u * u) * (1.0 / math.sqrt(2.0 * math.pi)))
        acc[...] += mm(act[k], down_of[z])
        if k == RISE[0]:
            send_late(LATE[1])
        if k == RISE[1]:
            pass_on(LATE[0])
        if k == RISE[2]:
            pass_on(LATE[1])

    def second_norm(i, sums):
        rows = pl.ds(pl.multiple_of(i * ROWS, ROWS), ROWS)
        n, scale = normalized(acc[rows, :])
        layer_out[rows, :] = (n * gain1 + bias1).astype(bf16)
        c = cot[rows, :].astype(f32)
        g = normalized_back(c * gain1, n, scale)
        gsum[rows, :] = g
        glow[rows, :] = g.astype(bf16)
        return (
            sums[0] + jnp.sum(c * n, axis=0, keepdims=True),
            sums[1] + jnp.sum(c, axis=0, keepdims=True),
        )

    zero = jnp.zeros((1, feat), f32)
    gain_two, bias_two = lax.fori_loop(0, block // ROWS, second_norm, (zero, zero))
    acc[...] = gsum[...]
    core, later = {}, {}

    def after_core(k):
        for copy in core[k]:
            copy.wait_recv()
        cu[k] = cu[k] + gu[k, :, :, here.c]
        cd[k] = cd[k] + gd[k, :, :, here.c]
        if k in FALL[:2]:
            n = FALL.index(k)
            later[k] = (
                start(push(cu.at[k, 1 - here.y], yu.at[n], ysem, n, here.dp_at(0, 1), here.t)),
                start(push(cd.at[k, :, 1 - here.x], xd.at[n], ysem, 2 + n, here.dp, here.across)),
            )

    for n, k in enumerate(FALL):
        z = (here.z + k) % 4
        g_act = mm_nt(glow[...], down_of[z])
        g_up = (g_act * slope[k]).astype(bf16)
        gd[k] = mm_tn(act[k], glow[...]).astype(bf16).reshape(gd.shape[1:])
        gu[k] = mm_tn(g_up, hlow[...]).astype(bf16).reshape(gu.shape[1:])
        core[k] = (
            start(push(gd.at[k, :, :, 1 - here.c], cd.at[k], csem, k, here.dp, here.sibling)),
            start(push(gu.at[k, :, :, 1 - here.c], cu.at[k], csem, 4 + k, here.dp, here.sibling)),
        )
        acc[...] += mm(g_up, up_of[z])
        if n > 0:
            after_core(FALL[n - 1])

    def first_back(i, sums):
        rows = pl.ds(pl.multiple_of(i * ROWS, ROWS), ROWS)
        g = acc[rows, :]
        n = n1[rows, :]
        back = normalized_back(g * gain0, n, r1[rows, 0:1])
        gpre[rows, :] = back
        glow[rows, :] = back.astype(bf16)
        return (
            sums[0] + jnp.sum(g * n, axis=0, keepdims=True),
            sums[1] + jnp.sum(g, axis=0, keepdims=True),
        )

    gain_one, bias_one = lax.fori_loop(0, block // ROWS, first_back, (zero, zero))
    gnorm[...] = jnp.concatenate(
        [gain_one, gain_two, bias_one, bias_two, jnp.zeros((4, feat), f32)], axis=0
    )
    after_core(FALL[3])
    for t in range(heads.shape[0]):
        gsend[t] = fold(mm(glow[...], wout[t]), width).astype(bf16)
        grad = mm_tn(glow[...], heads[t]).astype(bf16)
        gout[:, :, t // 2, t % 2] = grad.reshape((4, 2) + gout.shape[4:])
    for n, k in enumerate(FALL[2:]):
        part_up[n] = cu[k]
        part_down[n] = cd[k]
    for n, k in enumerate(FALL[:2]):
        for copy in later[k]:
            copy.wait_recv()
        sum_up[n] = cu[k, here.y] + yu[n]
        sum_down[n] = cd[k, :, here.x] + xd[n]
    for copy in copies:
        copy.wait_send()


def feed_direct(x, cot, heads, norms, wout, up_in, down_in, depth):
    block, feat = x.shape
    blocks, wide = heads.shape[0], wout.shape[2]
    owners = up_in.shape
    hidden_n = owners[4]
    units = 8 * hidden_n
    shape = jax.ShapeDtypeStruct
    outs = (
        shape((block, feat), bf16),
        shape(heads.shape, bf16),
        shape((block, feat), f32),
        shape((8, feat), f32),
        shape((4, 2, 2, 2, depth, wide), bf16),
        shape((2, 2, hidden_n, feat), bf16),
        shape((2, 2, hidden_n, feat), bf16),
        shape((2, 2, 2, hidden_n, feat), bf16),
        shape((2, 2, 2, hidden_n, feat), bf16),
    )
    scratch = [
        pltpu.VMEM((blocks, block, wide), bf16),
        pltpu.VMEM(owners, bf16),
        pltpu.VMEM(owners, bf16),
        pltpu.VMEM((4, block, units), bf16),
        pltpu.VMEM((4, block, units), f32),
        pltpu.VMEM((block, feat), f32),
        pltpu.VMEM((block, feat), bf16),
        pltpu.VMEM((block, feat), f32),
        pltpu.VMEM((block, LANES), f32),
        pltpu.VMEM((block, feat), f32),
        pltpu.VMEM((block, feat), bf16),
        pltpu.VMEM((block, feat), f32),
        pltpu.VMEM(owners, bf16),
        pltpu.VMEM(owners, bf16),
        pltpu.VMEM((4, 2, 2, hidden_n, feat), bf16),
        pltpu.VMEM((4, 2, 2, hidden_n, feat), bf16),
        pltpu.VMEM((2, 2, hidden_n, feat), bf16),
        pltpu.VMEM((2, 2, hidden_n, feat), bf16),
        dma(2, 4),
        dma(2, 8),
        dma(2, 4),
        dma(2, 6),
        dma(2, 6),
    ]
    return pl.pallas_call(
        feed_direct_body,
        out_shape=outs,
        in_specs=[VMEM] * 5 + [ANY, ANY],
        out_specs=tuple([VMEM] * len(outs)),
        scratch_shapes=scratch,
        compiler_params=pltpu.CompilerParams(
            vmem_limit_bytes=LIMIT, collective_id=5, has_side_effects=True
        ),
        name="feed_forward",
    )(x, cot, heads, norms, wout, up_in, down_in)


def feed_forward(direct, x, cot, heads, norms, wout, up_in, down_in, depth):
    block, feat = x.shape
    blocks, wide = heads.shape[0], wout.shape[2]
    hidden_n = up_in.shape[0]
    chunks = hidden_n // FF_CHUNK
    shape = jax.ShapeDtypeStruct
    outs = (
        shape((block, feat), bf16),
        shape(heads.shape, bf16),
        shape((block, feat), f32),
        shape((8, feat), f32),
        shape((4, 2, 2, 2, depth, wide) if direct else (blocks, feat, wide), bf16),
        shape((hidden_n, feat), bf16),
        shape((hidden_n, feat), bf16),
    )
    scratch = [
        pltpu.VMEM((blocks, block, wide), bf16),
        pltpu.VMEM((chunks, FF_CHUNK, feat), bf16),
        pltpu.VMEM((chunks, FF_CHUNK, feat), bf16),
        pltpu.VMEM((chunks, block, FF_CHUNK), bf16),
        pltpu.VMEM((chunks, block, FF_CHUNK), f32),
        pltpu.VMEM((block, feat), f32),
        pltpu.VMEM((block, feat), bf16),
        pltpu.VMEM((block, feat), f32),
        pltpu.VMEM((block, LANES), f32),
        pltpu.VMEM((block, feat), f32),
        pltpu.VMEM((block, feat), bf16),
        pltpu.VMEM((block, feat), f32),
        pltpu.VMEM((chunks, FF_CHUNK, feat), bf16),
        pltpu.VMEM((chunks, FF_CHUNK, feat), bf16),
        dma(4, chunks),
    ]
    return pl.pallas_call(
        functools.partial(feed_body, direct),
        out_shape=outs,
        in_specs=[VMEM] * 5 + [ANY, ANY],
        out_specs=tuple([VMEM] * 5 + [ANY, ANY]),
        scratch_shapes=scratch,
        compiler_params=pltpu.CompilerParams(vmem_limit_bytes=LIMIT),
        name="feed_forward",
    )(x, cot, heads, norms, wout, up_in, down_in)


class Summer:
    def __init__(self, here, source, first, count, own, from_core, from_y, from_z, from_x, sems, local):
        self.here, self.source, self.rows = here, source, pl.ds(first, count)
        self.own, self.from_core, self.from_y, self.from_z, self.from_x = (
            own, from_core, from_y, from_z, from_x,
        )
        self.sems, self.local = sems, local
        self.copies = []

    def push(self, src, dst, index, dp, t):
        copy = push(src, dst, self.sems, index, dp, t)
        copy.start()
        self.copies.append(copy)
        return copy

    def begin(self):
        here = self.here
        self.loaded = pltpu.make_async_copy(
            self.source.at[:, :, :, here.c, self.rows], self.own, self.local
        )
        self.loaded.start()
        self.core = self.push(
            self.source.at[:, :, :, 1 - here.c, self.rows], self.from_core, 0, here.dp, here.sibling
        )

    def along_y(self):
        here = self.here
        self.loaded.wait()
        self.core.wait_recv()

        def one(n, none):
            z, x = n // 2, n % 2
            y = 1 - here.y
            self.from_core[z, y, x] = self.from_core[z, y, x] + self.own[z, y, x]
            return none

        lax.fori_loop(0, 8, one, 0)
        self.y = self.push(
            self.from_core.at[:, 1 - here.y], self.from_y, 1, here.dp_at(0, 1), here.t
        )

    def along_z(self):
        here = self.here
        self.y.wait_recv()

        def one(n, none):
            z, x = n // 2, n % 2
            total = self.from_core[z, here.y, x].astype(f32) + self.own[z, here.y, x].astype(f32)
            total = total + self.from_y[z, x].astype(f32)
            self.from_y[z, x] = total.astype(self.own.dtype)
            return none

        lax.fori_loop(0, 8, one, 0)
        self.z = [
            self.push(
                self.from_y.at[(here.z + dz) % 4], self.from_z.at[dz - 1], 1 + dz, here.dp_at(dz, 0), here.t
            )
            for dz in (1, 2, 3)
        ]

    def along_x(self):
        here = self.here
        for copy in self.z:
            copy.wait_recv()
        for x in range(2):
            total = self.from_y[here.z, x].astype(f32)
            for n in range(3):
                total = total + self.from_z[n, x].astype(f32)
            self.from_y[here.z, x] = total.astype(self.own.dtype)
        self.x = self.push(
            self.from_y.at[here.z, 1 - here.x], self.from_x, 5, here.dp, here.across
        )

    def finish(self, out):
        self.x.wait_recv()
        here = self.here
        out[self.rows, :] = self.from_y[here.z, here.x].astype(f32) + self.from_x[...].astype(f32)
        for copy in self.copies:
            copy.wait_send()


class UpSum:
    def __init__(self, here, sums, parts, parts_far, from_y, from_z, from_x, sems, sums_far=None):
        self.here, self.sums, self.parts = here, sums, parts
        self.parts_far, self.sums_far = parts_far, sums_far
        self.from_y, self.from_z, self.from_x, self.sems = from_y, from_z, from_x, sems
        self.copies = []

    def push(self, src, dst, index, dp, t):
        copy = push(src, dst, self.sems, index, dp, t)
        copy.start()
        self.copies.append(copy)
        return copy

    def along_z(self, src, k):
        here = self.here
        return self.push(src, self.from_z.at[k - 1], k - 1, here.dp_at(k, 0), here.t)

    def begin(self):
        here = self.here
        self.y = [
            self.push(self.parts_far.at[n, 1 - here.y], self.from_y.at[n], 3 + n, here.dp_at(0, 1), here.t)
            for n in range(2)
        ]
        self.z = [self.along_z(self.sums.at[n], FALL[n]) for n in range(2)]

    def second(self):
        for n in range(2):
            self.y[n].wait_recv()
            self.from_y[n] = self.from_y[n] + self.parts[n, self.here.y]
        self.z.append(self.along_z(self.from_y.at[0], FALL[2]))

    def third(self):
        here = self.here
        for copy in self.z:
            copy.wait_recv()
        total = self.from_y[1].astype(f32)
        for n in range(3):
            total = total + self.from_z[n].astype(f32)
        self.from_y[1] = total.astype(bf16)
        self.x = self.push(self.from_y.at[1, 1 - here.x], self.from_x, 5, here.dp, here.across)

    def finish(self, out):
        self.x.wait_recv()
        out[...] = self.from_y[1, self.here.x].astype(f32) + self.from_x[...].astype(f32)
        for copy in self.copies:
            copy.wait_send()


class DownSum(UpSum):
    def begin(self):
        here = self.here
        self.x = [
            self.push(self.parts_far.at[n, :, 1 - here.x], self.from_x.at[n], 3 + n, here.dp, here.across)
            for n in range(2)
        ]
        self.y = [self.along_y(self.sums_far.at[n, 1 - here.y], n) for n in range(2)]

    def along_y(self, src, n):
        here = self.here
        return self.push(src, self.from_y.at[n], 5 + n, here.dp_at(0, 1), here.t)

    def second(self):
        self.z = []
        for n in range(2):
            self.y[n].wait_recv()
            self.from_y[n] = self.from_y[n] + self.sums[n, self.here.y]
            self.z.append(self.along_z(self.from_y.at[n], FALL[n]))

    def third(self):
        here = self.here
        for n in range(2):
            self.x[n].wait_recv()
            self.from_x[n] = self.from_x[n] + self.parts[n, :, here.x]
            self.y.append(self.along_y(self.from_x.at[n, 1 - here.y], 2 + n))

    def fourth(self):
        for n in range(2):
            self.y[2 + n].wait_recv()
            self.from_y[2 + n] = self.from_y[2 + n] + self.from_x[n, self.here.y]
        self.z.append(self.along_z(self.from_y.at[2], FALL[2]))

    def finish(self, out):
        for copy in self.z:
            copy.wait_recv()
        total = self.from_y[3].astype(f32)
        for n in range(3):
            total = total + self.from_z[n].astype(f32)
        out[...] = total
        for copy in self.copies:
            copy.wait_send()


SUMMER_SEMS = 6


def backward_body(gather, taps_total, *refs):
    (
        gsend, xall_in, wfull_in, tokc_in, segw, qk_in, v_in, kern1_in, kern3_in,
        land, counts, Ain, mixed, carried, conv, slot_live, gpre_in, hist_in,
    ) = refs[:18]
    refs = refs[18:]
    if gather:
        (sum_up, sum_down_in, part_up_in, part_down_in, out_in, norm_in), refs = refs[:6], refs[6:]
    (input_grad, gw, gconv), refs = refs[:3], refs[3:]
    if gather:
        (up_out, down_out, out_out, gain_out, bias_out), refs = refs[:5], refs[5:]
    (
        go_in, wfull, tokc, qk, v, gpre, taps, gl1, gl3, xall, xT, gopad, gqk, gv, gband, bands, gmixedT, glandT, hist, gstate, gcar, wback,
        part_out, part_in, part_sum, part_x, piece_v, piece_q, in_v, in_q, in_conv, conv_out,
        land_sum, x_land, g_high, g_low, land_own, land_out, land_in, land_all,
        gsem, lsem, psem, csem,
    ) = refs[:44]
    refs = refs[44:]

    here = Place()
    blocks, block, wide = gsend.shape[0], 2 * gsend.shape[1], gcar.shape[2]
    seq = blocks * block
    heads_n = gl1.shape[0]
    width = heads_n * HEAD_DIM
    nslot = land.shape[0]
    nchunk = seq // CHUNK
    per_block = block // CHUNK
    tiles_n = nslot // TILE
    all_tiles = heads_n * tiles_n
    feat = wfull.shape[0]
    doc_row = iota((1, nslot), 1) // LANDMARKS
    live_row = slot_live[...]
    live_cols = [column(live_row[:, g * TILE : (g + 1) * TILE].astype(f32)) for g in range(tiles_n)]
    scaling = 1.0 / math.sqrt(HEAD_DIM)
    same = tile_same()
    masks = lane_masks()

    pairs = [
        (tokc_in, tokc), (xall_in, xall), (kern1_in, gl1), (hist_in, hist), (kern3_in, gl3), (qk_in, qk),
        (v_in, v), (wfull_in, wfull), (gpre_in, gpre),
    ]
    if gather:
        sum_down, part_up, part_down = refs[:3]
        refs = refs[3:]
        pairs += [(sum_down_in, sum_down), (part_up_in, part_up), (part_down_in, part_down)]
    loads = [pltpu.make_async_copy(src, dst, lsem.at[n]) for n, (src, dst) in enumerate(pairs)]
    for load in loads:
        load.start()

    peers = here.tensor_peers()
    if gather:
        peers = peers + [
            (here.dp_at(dz, dy), here.t) for dz in range(4) for dy in range(2) if dz or dy
        ]
    greet(peers)
    copies = []

    def start(copy):
        copy.start()
        copies.append(copy)
        return copy

    gopad[0:HALO, :] = jnp.zeros((HALO, wide), bf16)
    gopad[seq + HALO : seq + 2 * HALO, :] = jnp.zeros((HALO, wide), bf16)
    arriving = [
        start(push(gsend.at[to], go_in.at[here.t], gsem, k, here.dp, to))
        for k, to in enumerate((here.across, here.diagonal, here.sibling))
    ]
    go_in[here.t] = gsend[here.t]

    if gather:
        out_sum, norm_sum, norm_pieces, q_sems, v_sems, in_vz, in_qz = refs[:7]
        refs = refs[7:]
        ups = UpSum(here, sum_up, part_up, part_up_in, *refs[:4])
        downs = DownSum(here, sum_down, part_down, part_down_in, *refs[4:8], sum_down_in)
        refs = refs[8:]
        ups.begin()
        downs.begin()
        length = gain_out.shape[1]
        far = spread_lanes(length, feat).astype(bf16)
        owner = iota((32, feat), 1) // length == iota((32, feat), 0)
        for r in range(4):
            high, low = split(jnp.where(owner, norm_in[r : r + 1, :], 0.0))
            norm_pieces[:, r, :] = mm_nt(high, far) + mm_nt(low, far)
        for r in range(4, 8):
            norm_pieces[:, r, :] = jnp.zeros((32, LANES), f32)
        norm_view = norm_pieces.reshape(4, 2, 2, 2, 8, LANES)
        smalls = []
        for source, count in ((out_in, out_in.shape[4]), (norm_view, 8)):
            buffers, refs = refs[:7], refs[7:]
            smalls.append(Summer(here, source, 0, count, *buffers))
        for summer in smalls:
            summer.begin()

    taps[...] = jnp.zeros_like(taps)
    taps[:heads_n, :taps_total] = conv[...]
    moved = pltpu.roll(taps[...], HALO - taps_total // 2, 1)
    far_rows = (iota((TILE, TILE), 0) + iota((TILE, TILE), 1) == TILE - 1).astype(f32).astype(bf16)
    turn_cols = iota((2 * TILE, 2 * TILE), 0) + iota((2 * TILE, 2 * TILE), 1) == 2 * TILE - 1
    turn_cols = turn_cols.astype(f32).astype(bf16)
    for h in range(heads_n):
        bands[h] = band_from(moved[h : h + 1, :])
        bands[heads_n + h] = mm(mm(far_rows, bands[h].astype(bf16)).astype(bf16), turn_cols)
    gmixedT[...] = jnp.zeros_like(gmixedT)
    glandT[...] = jnp.zeros_like(glandT)
    gband[...] = jnp.zeros_like(gband)
    loads[0].wait()
    loads[1].wait()

    def turn(b, none):
        for i in range(block // TILE):
            rows = slice(i * TILE, i * TILE + TILE)
            col = pl.ds(pl.multiple_of(b * block + i * TILE, TILE), TILE)
            xT[:, col] = xall[b, rows, :].astype(f32).T.astype(bf16)
            slot_now = slot_of(tokc[col, 0:1])
            hot = (slot_now == iota((TILE, nslot), 1)).astype(f32).astype(bf16)
            x_land[...] += mm(xT[:, col], hot)
        return none

    x_land[...] = jnp.zeros_like(x_land)
    lax.fori_loop(0, blocks, turn, 0)
    for h in range(heads_n):
        k0, q1, _ = landmark_parts(land[:, LANES * h : LANES * h + LANES])
        wback[h, :nslot, :] = jnp.concatenate(split(k0 * scaling), axis=1)
        wback[h, nslot:, :] = jnp.concatenate(split(q1 * scaling), axis=1)
    if gather:
        for summer in smalls:
            summer.along_y()
    for copy in arriving:
        copy.wait_recv()
    for load in loads[2:]:
        load.wait()

    def one(b, k):
        c = b * per_block + k
        rows = pl.ds(pl.multiple_of(c * CHUNK, CHUNK), CHUNK)
        inner = pl.ds(pl.multiple_of(c * CHUNK + HALO, HALO), CHUNK)
        alive = (live_of(tokc[rows, 0:1]) > 0) & (iota((CHUNK, wide), 1) < width)
        g_now = jnp.where(alive, unfold(go_in[b], k, width).astype(f32), 0.0).astype(bf16)
        gopad[inner, :] = g_now
        gT = g_now.astype(f32).T.astype(bf16)
        for h in range(heads_n):
            k1 = gl1[h, rows, :]
            gk = mm_nt(g_now, mixed[h])
            k1w = k1.astype(f32)
            gl1[h, rows, :] = (k1w * (gk - jnp.sum(gk * k1w, axis=1, keepdims=True))).astype(bf16)
            e = slice(HEAD_DIM * h, HEAD_DIM * h + HEAD_DIM)
            gmixedT[e, :] += mm(gT[e, :], k1)

    def one_block(b, none):
        for k in range(per_block):
            one(b, k)
        return none

    lax.fori_loop(0, blocks, one_block, 0)
    if gather:
        downs.second()
        ups.second()
    gmixed = gmixedT[...].T
    carried_all = carried[...]
    lane = iota((TILE, wide), 1) // HEAD_DIM
    delta = []
    for h in range(heads_n):
        rows_delta = []
        for g in range(tiles_n):
            n = h * tiles_n + g
            rows = slice(g * TILE, g * TILE + TILE)
            Z = unpack(hist[NEWTON, 1, n])
            gm = split(jnp.where(lane == h, gmixed[rows], 0.0))
            near = jnp.where(lane == h, carried_all[rows], 0.0)
            gstate[0, n] = jnp.zeros((LANDMARKS, TILE), f32)
            gstate[1, n] = pack(jnp.where(same, mm3(gm, split(near), mm_nt), 0.0))
            gc = mm3(split(Z.T), gm).astype(bf16)
            gcar[h, rows, :] = gc
            rows_delta.append(jnp.sum((gc.astype(f32) * near).T, axis=0, keepdims=True))
        delta.append(jnp.concatenate(rows_delta, axis=1))
    def three(c, emit, between=lambda: None):
        rows = pl.ds(pl.multiple_of(c * CHUNK, CHUNK), CHUNK)
        v_now = v[pl.ds(pl.multiple_of(c * CHUNK + HALO, HALO), CHUNK), :]
        total = jnp.zeros((CHUNK, wide), f32)
        for h in range(heads_n):
            gc = gcar[h]
            k3 = gl3[h, rows, :]
            gk = mm_nt(v_now, gc)
            gl = (k3.astype(f32) * (gk - delta[h])).astype(bf16)
            gl3[h, rows, :] = gl
            total = total + mm(k3, gc)
            partT = qk[rows, LANES * h : LANES * h + LANES].astype(f32).T.astype(bf16)
            glandT[h, :HEAD_DIM, :] += mm(partT[:HEAD_DIM, :], gl1[h, rows, :])
            glandT[h, HEAD_DIM:, :] += mm(partT[HEAD_DIM:, :], gl)
            between()
        for part in range(CHUNK // TILE):
            i = c * (CHUNK // TILE) + part
            at = pl.ds(pl.multiple_of(i * TILE, TILE), TILE)
            now = tokc[at, 0:1]
            seg_now = seg_of(now)
            near = seg_now == segw[pl.ds(i, 1), :]
            near_back = (seg_now == segw[pl.ds(seq // TILE + i, 1), :]) & (live_of(now) > 0)
            g_window = gopad[pl.ds(pl.multiple_of(i * TILE, TILE), 2 * TILE), :]
            v_window = v[pl.ds(pl.multiple_of(i * TILE, TILE), 2 * TILE), :]
            g_tile = gopad[pl.ds(pl.multiple_of(i * TILE + HALO, HALO), TILE), :].astype(f32)
            conv = jnp.zeros((TILE, wide), f32)
            for h in range(heads_n):
                back = mm(jnp.where(near_back, bands[heads_n + h], 0.0).astype(bf16), g_window)
                conv = jnp.where(lane == h, back, conv)
                mine = jnp.where(lane == h, g_tile, 0.0).astype(bf16)
                gband[h] += jnp.where(near, mm_nt(mine, v_window), 0.0)
            gv[at, :] = (total[part * TILE : (part + 1) * TILE, :] + conv).astype(bf16)
        for h in range(heads_n):
            both = mm(gl1[h, rows, :], wback[h, :nslot, :]) + mm(gl3[h, rows, :], wback[h, nslot:, :])
            gqk[rows, LANES * h : LANES * h + LANES] = (both[:, :LANES] + both[:, LANES:]).astype(bf16)
        emit(
            mm_nt(gqk[rows, :], wfull[:, : LANES * heads_n])
            + mm_nt(gv[rows, :], wfull[:, LANES * heads_n :])
        )

    def dyn_rows(k):
        return pl.ds(pl.multiple_of(k * CHUNK, CHUNK), CHUNK)

    def chunk_rows(k):
        return pl.ds(k * CHUNK, CHUNK)

    def landmark_stages():
        tiles = range(all_tiles)
        A = [Ain[n] for n in tiles]
        starts = [newton_start(a) for a in A]
        gW = [unpack(gstate[1, n]).T for n in tiles]
        gP = [unpack(gstate[0, n]) for n in tiles]
        GA = [tt(left_of(gP[n] + gP[n].T), right_of(A[n])) for n in tiles]
        yield
        gl2 = []
        for n in tiles:
            factor, colsum, tops = starts[n]
            gf_cols = jnp.sum((0.5 * GA[n] + gW[n]) * A[n], axis=0, keepdims=True)
            first = iota(colsum.shape, 1) < LANDMARKS
            gcol = jnp.zeros_like(colsum)
            for k in range(2):
                mine = first if k == 0 else jnp.logical_not(first)
                gf = jnp.sum(jnp.where(mine, gf_cols, 0.0), axis=1, keepdims=True)
                top = tops[k]
                is_top = mine & (colsum == top)
                ties = jnp.sum(is_top.astype(f32), axis=1, keepdims=True)
                share = jnp.where(top > 1.0, 1.0, jnp.where(top == 1.0, 0.5, 0.0))
                floor = jnp.maximum(top, 1.0)
                gcol = jnp.where(is_top, -gf * share / (floor * floor * ties), gcol)
            gA = (factor * (GA[n] + gW[n]) + gcol) * live_cols[n % tiles_n]
            one = A[n] * (gA - jnp.sum(gA * A[n], axis=1, keepdims=True)) * scaling
            rows = slice((n % tiles_n) * TILE, (n % tiles_n) * TILE + TILE)
            gl2.append(jnp.where(same & (live_row[:, rows] > 0), one, 0.0))
        yield
        for n in tiles:
            h, g = n // tiles_n, n % tiles_n
            rows = slice(g * TILE, g * TILE + TILE)
            k0, q1, _ = landmark_parts(land[rows, LANES * h : LANES * h + LANES])
            land_sum[h, rows, :] = mm3(split(gl2[n]), split(k0)) + mm3(split(gl2[n].T), split(q1))
        yield

    def walk(q, b, emit):
        def both(k, none):
            stages = newton_back_stages(hist, gstate, NEWTON - 1 - q * per_block - k, masks)
            next(stages)
            three(b * per_block + k, functools.partial(emit, k), lambda: next(stages, None))
            return none

        def alone(k, none):
            three(b * per_block + k, functools.partial(emit, k))
            return none

        ends = min(max(NEWTON - q * per_block, 0), per_block)
        lax.fori_loop(0, ends, both, 0)
        if NEWTON <= q * per_block < NEWTON + per_block:
            stages = landmark_stages()
            next(stages)
            three(b * per_block, functools.partial(emit, 0), lambda: next(stages, None))
            ends = 1
        lax.fori_loop(ends, per_block, alone, 0)

    def to_part(n, k, value):
        part_out[n, dyn_rows(k), :] = value.astype(bf16)

    def to_grad(k, value):
        input_grad[dyn_rows(k), :] = value

    def to_own_grad(k, value):
        input_grad[dyn_rows(k), :] = value + gpre[dyn_rows(k), :]

    walk(0, here.diagonal, functools.partial(to_part, 0))
    from_sibling = start(push(part_out.at[0], part_in.at[0], psem, 0, here.dp, here.sibling))
    walk(1, here.across, to_grad)
    from_sibling.wait_recv()
    from_across = []
    for k in range(per_block):
        total = input_grad[chunk_rows(k), :] + part_in[0, chunk_rows(k), :].astype(f32)
        part_sum[chunk_rows(k), :] = total.astype(bf16)
        from_across.append(
            start(push(part_sum.at[chunk_rows(k)], part_x.at[chunk_rows(k)], psem, 1 + k, here.dp, here.across))
        )
    if gather:
        downs.third()
        for summer in smalls:
            summer.along_z()
    walk(2, here.sibling, functools.partial(to_part, 1))
    own_from_sibling = start(push(part_out.at[1], part_in.at[1], psem, 1 + per_block, here.dp, here.sibling))
    walk(3, here.t, to_own_grad)
    if gather:
        downs.fourth()
        ups.third()

    conv_out[...] = jnp.zeros_like(conv_out)
    for h in range(heads_n):
        conv_out[h : h + 1, :] = diagonal_sums(gband[h])
    piece_v[...] = mm(xT[...], gv[...]).astype(bf16)
    others = [(dz, dy) for dz in range(4) for dy in range(2) if dz or dy] if gather else []
    sent_conv = []
    for k, (dz, dy) in enumerate(others):
        sent_conv.append(start(push(conv_out, in_conv.at[k], csem, k, here.dp_at(dz, dy), here.t)))

    def piece_along_y(piece, landing, sems):
        view = piece.reshape((4, 2) + landing.shape[1:])
        return start(push(view.at[:, 1 - here.y], landing, sems, 0, here.dp_at(0, 1), here.t))

    def piece_along_z(copy, piece, landing, last_landing, sems):
        view = piece.reshape((4, 2) + landing.shape[1:])
        copy.wait_recv()
        for z in range(4):
            landing[z] = landing[z] + view[z, here.y]
        return [
            start(push(landing.at[(here.z + dz) % 4], last_landing.at[dz - 1], sems, dz, here.dp_at(dz, 0), here.t))
            for dz in (1, 2, 3)
        ]

    if gather:
        v_along_y = piece_along_y(piece_v, in_v, v_sems)

    for h in range(heads_n):
        sums_land = pltpu.roll(glandT[h].T * scaling, HEAD_DIM, 1)
        lanes = slice(LANES * h, LANES * h + LANES)
        total = (land_sum[h] + sums_land) / counts[...]
        g_high[:, lanes], g_low[:, lanes] = split(total)

    weights_qk = wfull[:, : LANES * heads_n]
    spread_land = mm_nt(g_high[...], weights_qk) + mm_nt(g_low[...], weights_qk)
    half = nslot // 2
    land_own[...] = spread_land
    land_out[0] = land_own[pl.ds(pl.multiple_of((1 - here.c) * half, half), half), :].astype(bf16)
    own_half = pl.ds(pl.multiple_of(here.c * half, half), half)
    first = start(push(land_out.at[0], land_in.at[0], psem, 2 + per_block, here.dp, here.sibling))
    high, low = split(x_land[...])
    piece_q[...] = (
        mm(xT[...], gqk[...])
        + (mm(high, g_high[...]) + (mm(high, g_low[...]) + mm(low, g_high[...])))
    ).astype(bf16)
    if gather:
        q_along_y = piece_along_y(piece_q, in_q, q_sems)
    first.wait_recv()
    mine = land_own[own_half, :] + land_in[0].astype(f32)
    land_out[1] = mine.astype(bf16)
    second = start(push(land_out.at[1], land_in.at[1], psem, 3 + per_block, here.dp, here.across))
    if gather:
        for summer in smalls:
            summer.along_x()
        sent_v = piece_along_z(v_along_y, piece_v, in_v, in_vz, v_sems)
    second.wait_recv()
    mine = mine + land_in[1].astype(f32)
    land_all[own_half, :] = mine.astype(bf16)
    third = start(
        push(land_all.at[own_half], land_all.at[own_half], psem, 4 + per_block, here.dp, here.sibling)
    )
    if gather:
        ups.finish(up_out)
        downs.finish(down_out)
        sent_q = piece_along_z(q_along_y, piece_q, in_q, in_qz, q_sems)
    own_from_sibling.wait_recv()
    third.wait_recv()
    for k in range(per_block):
        from_across[k].wait_recv()
        rows = pl.ds(pl.multiple_of(here.t * block + k * CHUNK, CHUNK), CHUNK)
        hot = (slot_of(tokc[rows, 0:1]) == iota((CHUNK, nslot), 1)).astype(f32).astype(bf16)
        input_grad[chunk_rows(k), :] += (
            part_in[1, chunk_rows(k), :].astype(f32)
            + part_x[chunk_rows(k), :].astype(f32)
            + mm(hot, land_all[...])
        )
    if gather:
        for copy in sent_v + sent_q + sent_conv:
            copy.wait_recv()
        total_v = in_v[here.z].astype(f32)
        total_q = in_q[here.z].astype(f32)
        for k in range(3):
            total_v = total_v + in_vz[k].astype(f32)
            total_q = total_q + in_qz[k].astype(f32)
        total_conv = conv_out[...]
        for k in range(len(others)):
            total_conv = total_conv + in_conv[k]
        for h in range(heads_n):
            e = slice(HEAD_DIM * h, HEAD_DIM * h + HEAD_DIM)
            one = total_q[:, LANES * h : LANES * h + LANES]
            gw[0, :, e] = one[:, :HEAD_DIM]
            gw[1, :, e] = one[:, HEAD_DIM:]
        gw[2] = total_v[:, : heads_n * HEAD_DIM]
        first = HALO - taps_total // 2
        turned = pltpu.roll(total_conv, 2 * TILE - first, 1)
        gconv[...] = turned[:heads_n, :taps_total]
        smalls[0].finish(out_sum)
        out_out[...] = out_sum[:, : heads_n * HEAD_DIM].T
        smalls[1].finish(norm_sum)
        gain_out[...] = norm_sum[0:2, :length]
        bias_out[...] = norm_sum[2:4, :length]
    else:
        gw[:, : LANES * heads_n] = piece_q[...].astype(f32)
        gw[:, LANES * heads_n :] = piece_v[...].astype(f32)
        gconv[...] = conv_out[...]
    for copy in copies:
        copy.wait_send()


def attention_backward(gsend, xall, wfull, tokc, segw, qk, v, kern1, kern3, land, counts, weights,
                       mixed, carried, conv, slot_live, gpre, hist, sources, taps_total, depth):
    blocks, block, wide = gsend.shape[0], 2 * gsend.shape[1], v.shape[1]
    heads_n, seq, nslot = kern1.shape
    feat = wfull.shape[0]
    all_tiles = weights.shape[0]
    shape = jax.ShapeDtypeStruct
    gather = len(sources) > 0
    width = heads_n * HEAD_DIM
    outs = [shape((block, feat), f32)]
    if gather:
        hidden_n = sources[0].shape[2]
        outs += [
            shape((3, depth, width), f32),
            shape((heads_n, taps_total), f32),
            shape((hidden_n, feat), f32),
            shape((hidden_n, feat), f32),
            shape((width, depth), f32),
            shape((2, feat // 32), f32),
            shape((2, feat // 32), f32),
        ]
    else:
        outs += [shape((feat, wfull.shape[1]), f32), shape((8, 2 * TILE), f32)]
    others = 7 if gather else 1
    per_block = block // CHUNK
    scratch = [
        pltpu.VMEM(gsend.shape, bf16),
        pltpu.VMEM(wfull.shape, bf16),
        pltpu.VMEM(tokc.shape, i32),
        pltpu.VMEM(qk.shape, bf16),
        pltpu.VMEM(v.shape, bf16),
        pltpu.VMEM(gpre.shape, f32),
        pltpu.VMEM((8, 2 * TILE), f32),
        pltpu.VMEM((heads_n, seq, nslot), bf16),
        pltpu.VMEM((heads_n, seq, nslot), bf16),
        pltpu.VMEM(xall.shape, bf16),
        pltpu.VMEM((feat, seq), bf16),
        pltpu.VMEM((seq + 2 * HALO, wide), bf16),
        pltpu.VMEM((seq, LANES * heads_n), bf16),
        pltpu.VMEM((seq, wide), bf16),
        pltpu.VMEM((heads_n, TILE, 2 * TILE), f32),
        pltpu.VMEM((2 * heads_n, TILE, 2 * TILE), f32),
        pltpu.VMEM((wide, nslot), f32),
        pltpu.VMEM((heads_n, LANES, nslot), f32),
        pltpu.VMEM((NEWTON + 1, 4, all_tiles, LANDMARKS, TILE), f32),
        pltpu.VMEM((2, all_tiles, LANDMARKS, TILE), f32),
        pltpu.VMEM((heads_n, nslot, wide), bf16),
        pltpu.VMEM((heads_n, 2 * nslot, 256), bf16),
        pltpu.VMEM((2, block, feat), bf16),
        pltpu.VMEM((2, block, feat), bf16),
        pltpu.VMEM((block, feat), bf16),
        pltpu.VMEM((block, feat), bf16),
        pltpu.VMEM((feat, wide), bf16),
        pltpu.VMEM((feat, LANES * heads_n), bf16),
        pltpu.VMEM((4, depth if gather else 16, wide), bf16),
        pltpu.VMEM((4, depth if gather else 16, LANES * heads_n), bf16),
        pltpu.VMEM((others, 8, 2 * TILE), f32),
        pltpu.VMEM((8, 2 * TILE), f32),
        pltpu.VMEM((heads_n, nslot, LANES), f32),
        pltpu.VMEM((feat, nslot), f32),
        pltpu.VMEM((nslot, LANES * heads_n), bf16),
        pltpu.VMEM((nslot, LANES * heads_n), bf16),
        pltpu.VMEM((nslot, feat), f32),
        pltpu.VMEM((2, nslot // 2, feat), bf16),
        pltpu.VMEM((2, nslot // 2, feat), bf16),
        pltpu.VMEM((nslot, feat), bf16),
        dma(2, 3),
        dma(12),
        dma(2, 5 + per_block),
        dma(2, others),
    ]
    if gather:
        scratch += [pltpu.VMEM(source.shape, bf16) for source in sources[1:4]]
        scratch += [
            pltpu.VMEM((depth, wide), f32),
            pltpu.VMEM((8, LANES), f32),
            pltpu.VMEM((32, 8, LANES), f32),
            dma(2, 4),
            dma(2, 4),
            pltpu.VMEM((3, depth, wide), bf16),
            pltpu.VMEM((3, depth, LANES * heads_n), bf16),
            pltpu.VMEM((2, 2, hidden_n, feat), bf16),
            pltpu.VMEM((3, 2, hidden_n, feat), bf16),
            pltpu.VMEM((hidden_n, feat), bf16),
            dma(2, 6),
            pltpu.VMEM((4, hidden_n, feat), bf16),
            pltpu.VMEM((3, hidden_n, feat), bf16),
            pltpu.VMEM((2, 2, hidden_n, feat), bf16),
            dma(2, 9),
        ]
        for count, lanes, kind in ((depth, wide, bf16), (8, LANES, f32)):
            scratch += [
                pltpu.VMEM((4, 2, 2, count, lanes), kind),
                pltpu.VMEM((4, 2, 2, count, lanes), kind),
                pltpu.VMEM((4, 2, count, lanes), kind),
                pltpu.VMEM((3, 2, count, lanes), kind),
                pltpu.VMEM((count, lanes), kind),
                dma(2, SUMMER_SEMS),
                pltpu.SemaphoreType.DMA,
            ]
    specs = [VMEM, ANY, ANY, ANY, VMEM] + [ANY] * 4 + [VMEM] * 7 + [ANY, ANY]
    if gather:
        specs += [ANY] * 5 + [VMEM]
    return pl.pallas_call(
        functools.partial(backward_body, gather, taps_total),
        out_shape=tuple(outs),
        in_specs=specs,
        out_specs=tuple([VMEM] * len(outs)),
        scratch_shapes=scratch,
        compiler_params=pltpu.CompilerParams(
            vmem_limit_bytes=LIMIT, collective_id=3 if gather else 4, has_side_effects=True
        ),
        name="attention_backward",
    )(gsend, xall, wfull, tokc, segw, qk, v, kern1, kern3, land, counts, weights, mixed, carried,
      conv, slot_live, gpre, hist, *sources)


def hand_over_body(*refs):
    half = len(refs) // 2
    for src, dst in zip(refs[:half], refs[half:]):
        dst[...] = src[...]


def hand_over(*arrays):
    return pl.pallas_call(
        hand_over_body,
        out_shape=tuple(jax.ShapeDtypeStruct(a.shape, a.dtype) for a in arrays),
        in_specs=[VMEM] * len(arrays),
        out_specs=tuple([VMEM] * len(arrays)),
        name="hand_over",
    )(*arrays)


def split_up(shard, dim, length):
    before, after = (shard.shape[:dim], shard.shape[dim + 1 :])
    return jnp.moveaxis(shard.reshape(*before, length, -1, *after), dim, 0)


def exchange(pieces, axis):
    return lax.all_to_all(pieces, axis, split_axis=0, concat_axis=0, tiled=True)


def per_device(
    tokens,
    w_qkv,
    w_out,
    conv_weight,
    w_up,
    w_down,
    norm_gain,
    norm_bias,
    cotangent,
    seg_ids,
    landmark_slot,
    token_live,
    slot_live,
):
    both = ("dp", "tensor")
    dp_size, blocks = lax.axis_size("dp"), lax.axis_size("tensor")
    devices = dp_size * blocks
    heads_n, taps_total = conv_weight.shape
    block, feat = tokens.shape
    depth = w_qkv.shape[1]
    width = heads_n * HEAD_DIM
    wide = -(-width // 256) * 256
    hidden_n = w_up.shape[1]
    docs = slot_live.shape[1] // LANDMARKS
    direct = dp_size == 8 and blocks == 4 and depth % 16 == 0 and hidden_n % 32 == 0

    first = HALO - taps_total // 2
    weight = w_qkv if direct else lax.all_gather(w_qkv, "dp", axis=1, tiled=True)
    extra = (w_up.T, w_down, w_out, norm_gain, norm_bias) if direct else ()
    got = attention_forward(
        tokens, weight, conv_weight, seg_ids, landmark_slot, token_live, slot_live,
        extra, heads_n, blocks, taps_total,
    )
    (
        xall, wfull, tokc, segw, qk, v, kern1, kern3, land, counts, weights, mixed, carried, heads, proxies,
        hist,
    ) = got[:16]
    if direct:
        up_all, down_all, out_all, norms = got[16:]
        out_all = out_all.reshape(blocks, feat, wide)
    else:
        up_all = lax.all_gather(w_up.T, both, axis=0, tiled=True)
        down_all = lax.all_gather(w_down, both, axis=0, tiled=True)
        out_all = lax.all_gather(lax.all_gather(w_out.T, "dp", axis=0, tiled=True), "tensor", axis=0)
        out_all = jnp.pad(out_all, ((0, 0), (0, 0), (0, wide - width)))
        norms = jnp.concatenate([norm_gain, norm_bias, jnp.zeros_like(norm_gain), jnp.zeros_like(norm_bias)])
        norms = lax.all_gather(norms, both, axis=1, tiled=True).astype(f32)
    if direct:
        got = feed_direct(tokens, cotangent, heads, norms, out_all, up_all, down_all, depth)
        layer_out, gsend, grad_pre, norm_grads, out_pieces = got[:5]
        sources = got[5:] + (out_pieces, norm_grads)
    else:
        layer_out, gsend, grad_pre, norm_grads, out_pieces, up_pieces, down_pieces = feed_forward(
            direct, tokens, cotangent, heads, norms, out_all, up_all, down_all, depth
        )
        sources = ()
    got = attention_backward(
        gsend, xall, wfull, tokc, segw, qk, v, kern1, kern3, land, counts, weights,
        mixed, carried, conv_weight, slot_live, grad_pre, hist, sources, taps_total, depth,
    )
    if direct:
        (
            input_grad, grad_qkv, grad_conv, grad_up, grad_down, grad_out, grad_gain, grad_bias, proxies,
            layer_out,
        ) = hand_over(*got, proxies, layer_out)
        grad_up = grad_up.T
    else:
        input_grad, grad_w, grad_conv = got
        grad_w = exchange(grad_w.astype(bf16).reshape(dp_size, depth, -1), "dp").astype(f32).sum(axis=0)
        pairs = grad_w[:, : LANES * heads_n].reshape(depth, heads_n, 2, HEAD_DIM)
        grad_qkv = jnp.concatenate(
            [
                jnp.moveaxis(pairs, 2, 0).reshape(2, depth, width),
                grad_w[None, :, LANES * heads_n : LANES * heads_n + width],
            ]
        )
        grad_conv = lax.psum(grad_conv, "dp")[:heads_n, first : first + taps_total]
        grad_up = lax.psum_scatter(up_pieces, both, scatter_dimension=0, tiled=True).astype(f32).T
        grad_down = lax.psum_scatter(down_pieces, both, scatter_dimension=0, tiled=True).astype(f32)
        out_pieces = out_pieces[:, :, :width].reshape(blocks, dp_size, depth, width)
        out_pieces = jnp.swapaxes(out_pieces, 0, 1).reshape(devices, depth, width)
        grad_out = lax.psum_scatter(out_pieces, both, scatter_dimension=0, tiled=False).astype(f32).T
        norm_sum = exchange(split_up(norm_grads[:4], 1, devices), both).sum(axis=0)
        grad_gain, grad_bias = norm_sum[:2], norm_sum[2:]
    return (
        layer_out,
        input_grad,
        grad_qkv,
        grad_out,
        grad_conv,
        grad_up,
        grad_down,
        grad_gain,
        grad_bias,
        jnp.transpose(proxies, (1, 2, 0)),
    )


def solution(mesh):
    return jax.shard_map(
        per_device,
        mesh=mesh,
        in_specs=(
            P(("dp", "tensor"), None),
            P(None, "dp", "tensor"),
            P("tensor", "dp"),
            P("tensor", None),
            P(None, ("dp", "tensor")),
            P(("dp", "tensor"), None),
            P(None, ("dp", "tensor")),
            P(None, ("dp", "tensor")),
            P(("dp", "tensor"), None),
            P("dp", None),
            P("dp", None),
            P("dp", None),
            P("dp", None),
        ),
        out_specs=(
            P(("dp", "tensor"), None),
            P(("dp", "tensor"), None),
            P(None, "dp", "tensor"),
            P("tensor", "dp"),
            P("tensor", None),
            P(None, ("dp", "tensor")),
            P(("dp", "tensor"), None),
            P(None, ("dp", "tensor")),
            P(None, ("dp", "tensor")),
            P("dp", None, "tensor"),
        ),
        check_vma=False,
    )
```

```python
import functools
import math

import jax
import jax.numpy as jnp
from jax import lax
from jax.experimental import pallas as pl
from jax.experimental.pallas import tpu as pltpu
from jax.sharding import PartitionSpec as P

HEAD_DIM = 64
LANDMARKS = 64
NEWTON = 6
TILE = 128
HALO = TILE // 2
CHUNK = 256
LANES = 128
bf16 = jnp.bfloat16
f32 = jnp.float32
i32 = jnp.int32
norm_epsilon = 1e-05
MESH = pl.DeviceIdType.MESH
LIMIT = 62 * 2**20


def mm(a, b):
    return lax.dot_general(a, b, (((1,), (0,)), ((), ())), preferred_element_type=f32)


def mm_nt(a, b):
    return lax.dot_general(a, b, (((1,), (1,)), ((), ())), preferred_element_type=f32)


def split(a):
    high = a.astype(bf16)
    return high, (a - high.astype(f32)).astype(bf16)


def mm3(a, b, dot=mm):
    return dot(a[0], b[0]) + (dot(a[0], b[1]) + dot(a[1], b[0]))


def left_of(a):
    return jnp.concatenate(split(a), axis=1)


def right_of(b):
    high, low = split(b)
    top = jnp.concatenate([high, low], axis=1)
    bottom = jnp.concatenate([jnp.zeros_like(high), high], axis=1)
    return jnp.concatenate([top, bottom], axis=0)


def right_nt(b):
    high, low = split(b)
    top = jnp.concatenate([high, jnp.zeros_like(high)], axis=1)
    bottom = jnp.concatenate([low, high], axis=1)
    return jnp.concatenate([top, bottom], axis=0)


def tt(left, right):
    both = mm(left, right)
    return both[:, :TILE] + both[:, TILE:]


def tt_nt(left, right):
    both = mm_nt(left, right)
    return both[:, :TILE] + both[:, TILE:]


def iota(shape, dim):
    return lax.broadcasted_iota(i32, shape, dim)


def tile_same():
    shape = (TILE, TILE)
    return iota(shape, 0) // LANDMARKS == iota(shape, 1) // LANDMARKS


def tile_eye():
    shape = (TILE, TILE)
    return (iota(shape, 0) == iota(shape, 1)).astype(f32)


def pack(tile):
    return tile[:LANDMARKS] + tile[LANDMARKS:]


def unpack(packed):
    first = iota(packed.shape, 1) < LANDMARKS
    return jnp.concatenate([jnp.where(first, packed, 0.0), jnp.where(first, 0.0, packed)], axis=0)


def landmark_parts(land):
    first = iota(land.shape, 1) < HEAD_DIM
    turned = pltpu.roll(land, HEAD_DIM, 1)
    return jnp.where(first, turned, 0.0), jnp.where(first, 0.0, turned), jnp.where(first, land, 0.0)


def lane_masks():
    first = (iota((LANDMARKS, TILE), 1) < LANDMARKS).astype(f32)
    return first.astype(bf16), (1.0 - first).astype(bf16)


def packed_eye():
    shape = (LANDMARKS, TILE)
    return (iota(shape, 0) == iota(shape, 1) % LANDMARKS).astype(f32)


def packed_right(b, masks):
    high, low = split(b)
    high = jnp.concatenate([high * masks[0], high * masks[1]], axis=0)
    low = jnp.concatenate([low * masks[0], low * masks[1]], axis=0)
    top = jnp.concatenate([high, low], axis=1)
    bottom = jnp.concatenate([jnp.zeros_like(high), high], axis=1)
    return jnp.concatenate([top, bottom], axis=0)


def packed_tn(a, b):
    (ah, al), (bh, bl) = split(a), split(b)
    both = lax.dot_general(
        jnp.concatenate([ah, al, ah], axis=0),
        jnp.concatenate([bh, bh, bl], axis=0),
        (((0,), (0,)), ((), ())),
        preferred_element_type=f32,
    )
    first = iota(a.shape, 1) < LANDMARKS
    return jnp.where(first, both[:LANDMARKS], both[LANDMARKS:])


def newton_stages(hist, i, ident, masks):
    tiles = range(hist.shape[2])
    P = [hist[i, 0, n] for n in tiles]
    Pl, Pr = [left_of(p) for p in P], [packed_right(p, masks) for p in P]
    S = [tt(Pl[n], Pr[n]) for n in tiles]
    yield
    N = [13.0 * ident - 15.0 * P[n] + 7.0 * S[n] - tt(left_of(S[n]), Pr[n]) for n in tiles]
    yield
    for n in tiles:
        hist[i, 2, n] = S[n]
        hist[i, 3, n] = N[n]
        rows = jnp.concatenate([Pl[n], left_of(hist[i, 1, n])], axis=0)
        both = 0.25 * tt(rows, packed_right(N[n], masks))
        hist[i + 1, 0, n] = both[:LANDMARKS]
        hist[i + 1, 1, n] = both[LANDMARKS:]
    yield


def newton_back_stages(hist, gstate, i, masks):
    tiles = range(hist.shape[2])
    gP, gZ = [gstate[0, n] for n in tiles], [gstate[1, n] for n in tiles]
    P = [hist[i, 0, n] for n in tiles]
    Pl, Pr = [left_of(p) for p in P], [packed_right(p, masks) for p in P]
    gN = [
        0.25 * (tt(Pl[n], packed_right(gP[n], masks)) + packed_tn(hist[i, 1, n], gZ[n])) for n in tiles
    ]
    both = [
        0.25
        * tt(
            jnp.concatenate([left_of(gP[n]), left_of(gZ[n])], axis=0),
            packed_right(hist[i, 3, n], masks),
        )
        for n in tiles
    ]
    yield
    gS = [7.0 * gN[n] - tt(left_of(gN[n]), Pr[n]) for n in tiles]
    kept = [
        both[n][:LANDMARKS] - 15.0 * gN[n] - tt(left_of(hist[i, 2, n]), packed_right(gN[n], masks))
        for n in tiles
    ]
    yield
    for n in tiles:
        gstate[1, n] = both[n][LANDMARKS:]
        gstate[0, n] = kept[n] + tt(left_of(gS[n]), Pr[n]) + tt(Pl[n], packed_right(gS[n], masks))
    yield


def newton_start(A):
    colsum = jnp.sum(A, axis=0, keepdims=True)
    first = iota(colsum.shape, 1) < LANDMARKS
    tops = [
        jnp.max(jnp.where(first, colsum, 0.0), axis=1, keepdims=True),
        jnp.max(jnp.where(first, 0.0, colsum), axis=1, keepdims=True),
    ]
    factor = 1.0 / jnp.maximum(jnp.where(first, tops[0], tops[1]), 1.0)
    return factor, colsum, tops


def column(row):
    return jnp.broadcast_to(row, (LANES, LANES)).T


def band_from(row):
    wide = jnp.broadcast_to(row, (TILE, 2 * TILE))
    return pltpu.roll(wide, 0, 1, stride=1, stride_axis=0)


def diagonal_sums(band):
    where = iota(band.shape, 0)
    step = 1
    while step < TILE:
        turned = pltpu.roll(band, 2 * TILE - step, 1)
        band = jnp.where((where // step) % 2 == 1, turned, band)
        step *= 2
    return jnp.sum(band, axis=0, keepdims=True)


def seg_of(code):
    return (code // 512) % 8


def live_of(code):
    return code // 4096


def slot_of(code):
    return code % 512


def fold(rows, width):
    half = rows.shape[0] // 2
    far = pltpu.roll(rows[half:], width, 1)
    near = rows[:half]
    return jnp.concatenate(
        [near[:, :LANES], near[:, LANES:] + far[:, LANES:], far[:, :LANES]], axis=1
    )


def unfold(folded, k, width):
    if k == 0:
        return folded[:, : 2 * LANES]
    return pltpu.roll(folded[:, LANES:].astype(f32), width, 1)


class Place:
    def __init__(self):
        self.dp = lax.axis_index("dp")
        self.t = lax.axis_index("tensor")
        self.x = self.t // 2
        self.c = self.t % 2
        self.sibling = self.x * 2 + 1 - self.c
        self.across = (1 - self.x) * 2 + self.c
        self.diagonal = (1 - self.x) * 2 + 1 - self.c
        self.z = self.dp // 2
        self.y = self.dp % 2

    def tensor_peers(self):
        return [(self.dp, t) for t in (self.sibling, self.across, self.diagonal)]

    def dp_at(self, turn_z, turn_y):
        return ((self.z + turn_z) % 4) * 2 + (self.y + turn_y) % 2


def greet(peers):
    barrier = pltpu.get_barrier_semaphore()
    for peer in peers:
        pl.semaphore_signal(barrier, inc=1, device_id=peer, device_id_type=MESH)
    pl.semaphore_wait(barrier, len(peers))


def push(src, dst, sems, index, dp, t):
    return pltpu.make_async_remote_copy(
        src_ref=src,
        dst_ref=dst,
        send_sem=sems.at[0, index],
        recv_sem=sems.at[1, index],
        device_id=(dp, t),
        device_id_type=MESH,
    )


class Spreader:
    def __init__(self, here, shard, whole, sems, local, by_x, by_rows=False):
        self.here, self.shard, self.whole, self.sems, self.local = here, shard, whole, sems, local
        self.by_rows, self.by_x = by_rows, by_x
        first, last = (here.dp, here.across), (here.dp_at(0, 1), here.t)
        self.first, self.last = (first, last) if by_x else (last, first)
        self.copies = []
        self.from_z, self.from_first, self.from_last, self.from_core = {}, {}, {}, []

    def at(self, z, y, x):
        c = self.here.c
        if not self.by_rows:
            return self.whole.at[z, y, x, c]
        depth = self.shard.shape[0]
        rows = pl.ds(pl.multiple_of((z * 2 + y) * depth, 16), depth)
        return self.whole.at[x, c, rows]

    def one(self, dz):
        return self.at((self.here.z + 4 - dz) % 4, self.here.y, self.here.x)

    def pair(self, dz, turned):
        here, z = self.here, (self.here.z + 4 - dz) % 4
        if self.by_x:
            return self.at(z, (here.y + turned) % 2, slice(None))
        return self.at(z, slice(None), (here.x + turned) % 2)

    def push(self, src, dst, index, place):
        copy = push(src, dst, self.sems, index, *place)
        copy.start()
        self.copies.append(copy)
        return copy

    def begin(self):
        self.kept = pltpu.make_async_copy(self.shard, self.one(0), self.local)
        self.kept.start()
        if self.by_x:
            self.own_first()

    def own_first(self):
        self.from_first[0] = self.push(self.shard, self.one(0), 3, self.first)

    def along_z(self, dz):
        here = self.here
        self.from_z[dz] = self.push(self.shard, self.one(0), dz - 1, (here.dp_at(dz, 0), here.t))

    def along_first(self, dz):
        self.from_z[dz].wait_recv()
        self.from_first[dz] = self.push(self.one(dz), self.one(dz), 3 + dz, self.first)

    def along_last(self, dz):
        if dz == 0:
            self.kept.wait()
        self.from_first[dz].wait_recv()
        got = self.pair(dz, 0)
        self.from_last[dz] = self.push(got, got, 7 + dz, self.last)
        self.from_core.append(self.push(got, got, 11 + dz, (self.here.dp, self.here.sibling)))

    def to_core(self, dz):
        self.from_last[dz].wait_recv()
        got = self.pair(dz, 1)
        self.from_core.append(self.push(got, got, 15 + dz, (self.here.dp, self.here.sibling)))

    def finish(self):
        for dz in self.from_first:
            if dz not in self.from_last:
                self.from_first[dz].wait_recv()
        for copy in self.from_core:
            copy.wait_recv()
        for copy in self.copies:
            copy.wait_send()


LATE = (3, 2)


def spread_lanes(length, whole):
    shape = (LANES, whole)
    return (iota(shape, 0) == iota(shape, 1) % length).astype(f32)


def forward_body(gather, taps_total, *refs):
    (x, w, conv, seg, slot, live, slot_live), refs = refs[:7], refs[7:]
    if gather:
        (w_up, w_down, w_out, gain, bias), refs = refs[:5], refs[5:]
    (
        xall_out, wfull_out, tokc, segw, qk_out, v_out, kern1_out, kern3_out,
        land, counts, Aout, mixed, carried, heads, prox, hist_out,
    ) = refs[:16]
    refs = refs[16:]
    if gather:
        (up_all, down_all, out_all, norms), refs = refs[:4], refs[4:]
    (
        xall, wfull, qk, v, kern1, kern3,
        wsh, wlog, l3, carriedT, hist, bands, hsend, segp, taps, xsem, wsem, hsem, osem,
    ) = refs[:19]
    refs = refs[19:]
    keeping = []

    def keep(src, dst):
        copy = pltpu.make_async_copy(src, dst, osem.at[len(keeping)])
        copy.start()
        keeping.append(copy)

    here = Place()
    block = x.shape[0]
    blocks = xall.shape[0]
    seq = block * blocks
    heads_n = qk.shape[1] // LANES
    nslot = land.shape[0]
    wide = v.shape[1]
    nchunk = seq // CHUNK
    per_block = block // CHUNK
    tiles_n = nslot // TILE
    width = heads_n * HEAD_DIM
    scaling = 1.0 / math.sqrt(HEAD_DIM)

    depth = w.shape[1]
    parts = []
    for h in range(heads_n):
        e = slice(HEAD_DIM * h, HEAD_DIM * h + HEAD_DIM)
        parts += [w[0, :, e], w[1, :, e]]
    parts += [w[2], jnp.zeros((depth, wide - width), bf16)]
    wsh[...] = jnp.concatenate(parts, axis=1)

    peers = here.tensor_peers()
    if gather:
        peers = peers + [(here.dp_at(dz, 0), here.t) for dz in (1, 2, 3)] + [(here.dp_at(0, 1), here.t)]
        out_sh, norm_sh, norm_all = refs[:3]
        out_sh[...] = jnp.concatenate(
            [w_out[...].astype(f32).T, jnp.zeros((depth, wide - width), f32)], axis=1
        ).astype(bf16)
        norm_sh[...] = jnp.zeros_like(norm_sh)
        norm_sh[0:2, : gain.shape[1]] = gain[...].astype(f32)
        norm_sh[2:4, : gain.shape[1]] = bias[...].astype(f32)
        sems = refs[3:]
        spread_out = Spreader(here, out_sh, out_all, sems[2], sems[3], True, by_rows=True)
        spread_norm = Spreader(here, norm_sh, norm_all, sems[4], sems[5], True)
        whole = (spread_out, spread_norm)
        partly = (
            Spreader(here, w_up, up_all, sems[0], sems[1], True),
            Spreader(here, w_down, down_all, sems[6], sems[7], False),
        )
        spreads = whole + partly
    greet(peers)

    copies = []
    pieces = block // TILE

    def start(copy):
        copy.start()
        copies.append(copy)
        return copy

    crossing = [
        start(push(x.at[pl.ds(p * TILE, TILE)], xall.at[here.t, pl.ds(p * TILE, TILE)], xsem, p, here.dp, here.across))
        for p in range(pieces)
    ]
    beside = start(push(x, xall.at[here.t], xsem, pieces, here.dp, here.sibling))
    if gather:
        mine = wfull.at[pl.ds(pl.multiple_of(here.dp * depth, 16), depth)]
        along = [start(push(wsh, mine, wsem, dz, here.dp_at(dz, 0), here.t)) for dz in (1, 2, 3)]
        along = [start(push(wsh, mine, wsem, 0, here.dp_at(0, 1), here.t))] + along
        wfull[pl.ds(pl.multiple_of(here.dp * depth, 16), depth), :] = wsh[...]
    else:
        wfull[...] = wsh[...]
    xall[here.t] = x[...]

    segp[...] = jnp.full(segp.shape, -1, i32)
    segp[0:1, TILE : TILE + seq] = jnp.where(live[...] > 0, seg[...], -1)
    segp[1:2, TILE : TILE + seq] = seg[...]
    code = (slot[...] + 512 * seg[...] + 4096 * live[...]).astype(f32)
    for i in range(seq // TILE):
        lanes = slice(i * TILE, i * TILE + TILE)
        tokc[lanes, :] = column(code[:, lanes]).astype(i32)
        near = pltpu.roll(segp[:, i * TILE : i * TILE + 3 * TILE], 3 * TILE - HALO, 1)
        segw[i : i + 1, :] = near[0:1, : 2 * TILE]
        segw[seq // TILE + i : seq // TILE + i + 1, :] = near[1:2, : 2 * TILE]
    taps[...] = jnp.zeros_like(taps)
    taps[:heads_n, :taps_total] = conv[...]
    moved = pltpu.roll(taps[...], HALO - taps_total // 2, 1)
    for h in range(heads_n):
        bands[h] = band_from(moved[h : h + 1, :])
    doc_row = iota((1, nslot), 1) // LANDMARKS
    live_row = slot_live[...]
    live_cols = [column(live_row[:, g * TILE : (g + 1) * TILE].astype(f32)) for g in range(tiles_n)]
    v[0:HALO, :] = jnp.zeros((HALO, wide), bf16)
    v[seq + HALO : seq + 2 * HALO, :] = jnp.zeros((HALO, wide), bf16)

    if gather:
        along[0].wait_recv()
        for dz in (1, 2, 3):
            along[dz].wait_recv()
            got = wfull.at[pl.ds(pl.multiple_of(here.dp_at(4 - dz, 0) * depth, 16), depth)]
            along.append(start(push(got, got, wsem, 3 + dz, here.dp_at(0, 1), here.t)))
        for spread in spreads:
            spread.begin()
            spread.along_z(1)
            spread.along_z(3)
        for dz in (1, 2, 3):
            along[3 + dz].wait_recv()
        for spread in spreads:
            if not spread.by_x:
                spread.own_first()

    def project(b, carry):
        def one(i, carry):
            acc, cnt = carry
            c = b * per_block + i
            rows = pl.ds(pl.multiple_of(c * CHUNK, CHUNK), CHUNK)
            out = mm(xall[b, pl.ds(pl.multiple_of(i * CHUNK, CHUNK), CHUNK), :], wfull[...])
            qk_now = out[:, : LANES * heads_n].astype(bf16)
            qk[rows, :] = qk_now
            v[pl.ds(pl.multiple_of(c * CHUNK + HALO, HALO), CHUNK), :] = out[:, LANES * heads_n :].astype(bf16)
            slot_now = slot[:, pl.ds(pl.multiple_of(c * CHUNK, CHUNK), CHUNK)]
            hot = (slot_now == iota((nslot, CHUNK), 0)).astype(f32)
            return acc + mm(hot.astype(bf16), qk_now), cnt + jnp.sum(hot, axis=1, keepdims=True)

        return lax.fori_loop(0, per_block, one, carry)

    carry = (jnp.zeros((nslot, LANES * heads_n), f32), jnp.zeros((nslot, 1), f32))
    carry = project(here.t, carry)
    beside.wait_recv()
    carry = project(here.sibling, carry)
    passed = []
    for p in range(pieces):
        crossing[p].wait_recv()
        got = xall.at[here.across, pl.ds(p * TILE, TILE)]
        passed.append(start(push(got, got, xsem, pieces + 1 + p, here.dp, here.sibling)))
    carry = project(here.across, carry)
    for p in range(pieces):
        passed[p].wait_recv()
    acc, cnt = project(here.diagonal, carry)
    cnt = jnp.maximum(cnt, 1.0)
    counts[...] = jnp.broadcast_to(cnt, counts.shape)
    land[...] = acc / cnt

    if gather:
        for spread in spreads:
            spread.along_z(2)
            spread.along_last(0)
    keep(xall, xall_out)
    keep(wfull, wfull_out)
    keep(qk, qk_out)
    keep(v, v_out)

    same = tile_same()
    ident = packed_eye()
    masks = lane_masks()
    for h in range(heads_n):
        k0, q1, q0 = landmark_parts(land[:, LANES * h : LANES * h + LANES])
        wlog[h] = jnp.concatenate(split(jnp.concatenate([k0, q1], axis=0) * scaling), axis=1)
        for g in range(tiles_n):
            rows = slice(g * TILE, g * TILE + TILE)
            logit = tt_nt(left_of(q0[rows] * scaling), right_nt(k0[rows]))
            filled = jnp.where(same & (live_row[:, rows] > 0), logit, -1e9)
            raised = jnp.exp(filled - jnp.max(filled, axis=1, keepdims=True))
            A = raised / jnp.sum(raised, axis=1, keepdims=True) * live_cols[g]
            n = h * tiles_n + g
            Aout[n] = A
            factor, _, _ = newton_start(A)
            W = A * factor
            hist[0, 0, n] = pack(tt_nt(left_of(A), right_nt(W)))
            hist[0, 1, n] = pack(W.T)

    def logits(c, top, between=lambda: None):
        rows = pl.ds(pl.multiple_of(c * CHUNK, CHUNK), CHUNK)
        now = tokc[rows, 0:1]
        allowed = (seg_of(now) == doc_row) & (live_row > 0)
        alive = allowed & (live_of(now) > 0)
        tops = []
        for h in range(heads_n):
            part = qk[rows, LANES * h : LANES * h + LANES]
            both = mm_nt(jnp.concatenate([part, part], axis=1), wlog[h])
            one = jnp.where(allowed, both[:, :nslot], -1e9)
            raised = jnp.exp(one - jnp.max(one, axis=1, keepdims=True))
            kern1[h, rows, :] = (raised / jnp.sum(raised, axis=1, keepdims=True)).astype(bf16)
            three = jnp.where(alive, both[:, nslot:], -1e9)
            l3[h, rows, :] = three
            tops.append(jnp.maximum(top[h], jnp.max(three, axis=0, keepdims=True)))
            between()
        return tuple(tops)

    def step_and_logits(i, top):
        stages = newton_stages(hist, i, ident, masks)
        next(stages)
        return logits(i, top, lambda: next(stages, None))

    top = tuple(jnp.full((1, nslot), -1e9, f32) for _ in range(heads_n))
    third = NEWTON // 3
    top = lax.fori_loop(0, third, step_and_logits, top)
    if gather:
        for spread in spreads:
            spread.along_first(1)
    top = lax.fori_loop(third, 2 * third, step_and_logits, top)
    if gather:
        for spread in spreads:
            spread.along_first(3)
    top = lax.fori_loop(2 * third, NEWTON, step_and_logits, top)
    keep(hist, hist_out)
    top = lax.fori_loop(NEWTON, nchunk, logits, top)
    keep(kern1, kern1_out)
    if gather:
        for spread in spreads:
            spread.along_last(1)

    def raise_three(c, total):
        rows = pl.ds(pl.multiple_of(c * CHUNK, CHUNK), CHUNK)
        totals = []
        for h in range(heads_n):
            raised = jnp.exp(l3[h, rows, :] - top[h])
            l3[h, rows, :] = raised
            totals.append(total[h] + jnp.sum(raised, axis=0, keepdims=True))
        return tuple(totals)

    total = lax.fori_loop(
        0, nchunk, raise_three, tuple(jnp.zeros((1, nslot), f32) for _ in range(heads_n))
    )
    norm = [live_row.astype(f32) / total[h] for h in range(heads_n)]
    carriedT[...] = jnp.zeros_like(carriedT)

    def carry_three(c, none):
        rows = pl.ds(pl.multiple_of(c * CHUNK, CHUNK), CHUNK)
        vT = v[pl.ds(pl.multiple_of(c * CHUNK + HALO, HALO), CHUNK), :].astype(f32).T.astype(bf16)
        for h in range(heads_n):
            low = (l3[h, rows, :] * norm[h]).astype(bf16)
            kern3[h, rows, :] = low
            e = slice(HEAD_DIM * h, HEAD_DIM * h + HEAD_DIM)
            carriedT[e, :] += mm(vT[e, :], low)
        return none

    lax.fori_loop(0, nchunk, carry_three, 0)
    keep(kern3, kern3_out)
    if gather:
        for spread in spreads:
            spread.along_first(2)
        for spread in whole:
            spread.along_last(3)
        for spread in spreads:
            spread.to_core(0)
    carried_all = carriedT[...].T
    carried[...] = carried_all
    lane = iota((TILE, wide), 1) // HEAD_DIM
    docs = nslot // LANDMARKS
    prox_all = jnp.zeros((8, LANES), f32)
    for h in range(heads_n):
        for g in range(tiles_n):
            rows = slice(g * TILE, g * TILE + TILE)
            n = h * tiles_n + g
            Z = hist[NEWTON, 1, n]
            part = split(jnp.where(lane == h, carried_all[rows], 0.0))
            mixed[h, rows, :] = mm3(split(unpack(Z)), part).astype(bf16)
            A = Aout[n]
            A2 = jnp.sum(A * A, axis=0, keepdims=True)
            Z2 = jnp.sum(Z * Z, axis=0, keepdims=True)
            first = iota(A2.shape, 1) < LANDMARKS
            for half in range(2):
                mine = first if half == 0 else jnp.logical_not(first)
                a2 = jnp.sum(jnp.where(mine, A2, 0.0), axis=1, keepdims=True)
                z2 = jnp.sum(jnp.where(mine, Z2, 0.0), axis=1, keepdims=True)
                doc = g * 2 + half
                alive = live_row[:, doc * LANDMARKS : doc * LANDMARKS + 1] > 0
                value = jnp.where(alive, jnp.sqrt(a2) * jnp.sqrt(z2) / LANDMARKS, 0.0)
                here_too = (iota(prox_all.shape, 0) == h) & (iota(prox_all.shape, 1) == doc)
                prox_all = jnp.where(here_too, value, prox_all)
    for h in range(heads_n):
        prox[h] = prox_all[h : h + 1, :docs]

    def finish(b, out, out_row):
        for k in range(per_block):
            c = b * per_block + k
            rows = pl.ds(pl.multiple_of(c * CHUNK, CHUNK), CHUNK)
            total = mm(kern1[0, rows, :], mixed[0])
            for h in range(1, heads_n):
                total = total + mm(kern1[h, rows, :], mixed[h])
            for part in range(CHUNK // TILE):
                i = c * (CHUNK // TILE) + part
                now = tokc[pl.ds(pl.multiple_of(i * TILE, TILE), TILE), 0:1]
                near = seg_of(now) == segw[pl.ds(i, 1), :]
                window = v[pl.ds(pl.multiple_of(i * TILE, TILE), 2 * TILE), :]
                conv = jnp.zeros((TILE, wide), f32)
                for h in range(heads_n):
                    term = mm(jnp.where(near, bands[h], 0.0).astype(bf16), window)
                    conv = jnp.where(lane == h, term, conv)
                got = (total[part * TILE : (part + 1) * TILE, :] + conv) * live_of(now).astype(f32)
                at = pl.ds(part * TILE, TILE)
                if k == 0:
                    out[out_row, at, : 2 * LANES] = got.astype(bf16)
                else:
                    far = pltpu.roll(got, width, 1)
                    middle = slice(LANES, 2 * LANES)
                    both = out[out_row, at, middle].astype(f32) + far[:, LANES:]
                    out[out_row, at, middle] = both.astype(bf16)
                    out[out_row, at, 2 * LANES :] = far[:, :LANES].astype(bf16)

    if gather:
        for spread in whole:
            spread.along_last(2)
    sent = []
    for k, to in enumerate((here.diagonal, here.across, here.sibling)):
        finish(to, hsend, k)
        sent.append(start(push(hsend.at[k], heads.at[here.t], hsem, k, here.dp, to)))
    finish(here.t, heads, here.t)
    if gather:
        for spread in spreads:
            spread.to_core(1)
        for spread in whole:
            spread.to_core(3)
            spread.to_core(2)
    for copy in sent:
        copy.wait_recv()
    if gather:
        for spread in spreads:
            spread.finish()
        length = gain.shape[1]
        far = spread_lanes(length, x.shape[1]).astype(bf16)
        owner = iota((32, x.shape[1]), 1) // length == iota((32, x.shape[1]), 0)
        for r in range(4):
            rows = norm_all[...].reshape(32, 8, LANES)[:, r, :].astype(bf16)
            norms[r : r + 1, :] = jnp.sum(jnp.where(owner, mm(rows, far), 0.0), axis=0, keepdims=True)
        norms[4:8, :] = jnp.zeros((4, x.shape[1]), f32)
    for copy in copies:
        copy.wait_send()
    for copy in keeping:
        copy.wait()


VMEM = pl.BlockSpec(memory_space=pltpu.VMEM)
ANY = pl.BlockSpec(memory_space=pl.ANY)


def dma(*shape):
    return pltpu.SemaphoreType.DMA(shape)


def attention_forward(x, w, conv, seg, slot, live, slot_live, extra, heads_n, blocks, taps_total):
    block, feat = x.shape
    seq, nslot = block * blocks, slot_live.shape[1]
    gather = len(extra) > 0
    depth = w.shape[1]
    wide = -(-heads_n * HEAD_DIM // 256) * 256
    tiles_n = heads_n * (nslot // TILE)
    shape = jax.ShapeDtypeStruct
    outs = [
        shape((blocks, block, feat), bf16),
        shape((feat, LANES * heads_n + wide), bf16),
        shape((seq, LANES), i32),
        shape((2 * (seq // TILE), 2 * TILE), i32),
        shape((seq, LANES * heads_n), bf16),
        shape((seq + 2 * HALO, wide), bf16),
        shape((heads_n, seq, nslot), bf16),
        shape((heads_n, seq, nslot), bf16),
        shape((nslot, LANES * heads_n), f32),
        shape((nslot, LANES), f32),
        shape((tiles_n, TILE, TILE), f32),
        shape((heads_n, nslot, wide), bf16),
        shape((nslot, wide), f32),
        shape((blocks, block // 2, 2 * heads_n * HEAD_DIM), bf16),
        shape((heads_n, 1, nslot // LANDMARKS), f32),
        shape((NEWTON + 1, 4, tiles_n, LANDMARKS, TILE), f32),
    ]
    out_specs = [ANY, ANY, VMEM, VMEM] + [ANY] * 4 + [VMEM] * 7 + [ANY]
    scratch = [pltpu.VMEM(outs[n].shape, bf16) for n in (0, 1, 4, 5, 6, 7)]
    scratch += [
        pltpu.VMEM((depth, LANES * heads_n + wide), bf16),
        pltpu.VMEM((heads_n, 2 * nslot, 256), bf16),
        pltpu.VMEM((heads_n, seq, nslot), f32),
        pltpu.VMEM((wide, nslot), f32),
        pltpu.VMEM(outs[15].shape, f32),
        pltpu.VMEM((heads_n, TILE, 2 * TILE), f32),
        pltpu.VMEM((3, block // 2, 2 * heads_n * HEAD_DIM), bf16),
        pltpu.VMEM((8, seq + 2 * TILE), i32),
        pltpu.VMEM((8, 2 * TILE), f32),
        dma(2, 2 * (block // TILE) + 1),
        dma(2, 7),
        dma(2, 3),
        dma(7),
    ]
    if gather:
        hidden_n = extra[0].shape[0]
        outs += [
            shape((4, 2, 2, 2, hidden_n, feat), bf16),
            shape((4, 2, 2, 2, hidden_n, feat), bf16),
            shape((2, 2, feat, wide), bf16),
            shape((8, feat), f32),
        ]
        out_specs += [ANY, ANY, ANY, VMEM]
        scratch += [
            pltpu.VMEM((depth, wide), bf16),
            pltpu.VMEM((8, LANES), f32),
            pltpu.VMEM((4, 2, 2, 2, 8, LANES), f32),
        ]
        for _ in range(4):
            scratch += [dma(2, 19), pltpu.SemaphoreType.DMA]
    return pl.pallas_call(
        functools.partial(forward_body, gather, taps_total),
        out_shape=tuple(outs),
        in_specs=[VMEM] * (7 + len(extra)),
        out_specs=tuple(out_specs),
        scratch_shapes=scratch,
        compiler_params=pltpu.CompilerParams(
            vmem_limit_bytes=LIMIT, collective_id=1 if gather else 2, has_side_effects=True
        ),
        name="attention_forward",
    )(x, w, conv, seg, slot, live, slot_live, *extra)


def normalized(u):
    mean = jnp.mean(u, axis=-1, keepdims=True)
    centered = u - mean
    scale = lax.rsqrt(jnp.mean(centered * centered, axis=-1, keepdims=True) + norm_epsilon)
    return centered * scale, scale


def normalized_back(g, n, scale):
    return scale * (
        g - jnp.mean(g, axis=-1, keepdims=True) - n * jnp.mean(g * n, axis=-1, keepdims=True)
    )


ROWS = 256
FF_CHUNK = 512


def mm_tn(a, b):
    return lax.dot_general(a, b, (((0,), (0,)), ((), ())), preferred_element_type=f32)


def feed_body(
    direct, x, cot, folded, norms, wout, up_in, down_in,
    layer_out, gsend, gpre, gnorm, gout, gup, gdown,
    heads, up, down, act, slope, hidden, hlow, n1, r1, gsum, glow, acc, up_out, down_out, sems,
):
    block, feat = x.shape
    chunks = act.shape[0]
    loads = []
    for j in range(chunks):
        rows = pl.ds(j * FF_CHUNK, FF_CHUNK)
        loads.append(
            (
                pltpu.make_async_copy(up_in.at[rows], up.at[j], sems.at[0, j]),
                pltpu.make_async_copy(down_in.at[rows], down.at[j], sems.at[1, j]),
            )
        )
        for load in loads[-1]:
            load.start()
    gain0, gain1 = norms[0:1, :], norms[1:2, :]
    bias0, bias1 = norms[2:3, :], norms[3:4, :]
    width = folded.shape[2] // 2
    for t in range(folded.shape[0]):
        for k in range(2):
            heads[t, k * (block // 2) : (k + 1) * (block // 2), :] = unfold(folded[t], k, width).astype(bf16)
    acc[...] = sum(mm_nt(heads[t], wout[t]) for t in range(heads.shape[0]))

    def first_norm(i, none):
        rows = pl.ds(pl.multiple_of(i * ROWS, ROWS), ROWS)
        n, scale = normalized(x[rows, :].astype(f32) + acc[rows, :])
        now = n * gain0 + bias0
        n1[rows, :] = n
        r1[rows, :] = jnp.broadcast_to(scale, (ROWS, LANES))
        hidden[rows, :] = now
        hlow[rows, :] = now.astype(bf16)
        return none

    lax.fori_loop(0, block // ROWS, first_norm, 0)
    acc[...] = hidden[...]
    for j in range(chunks):
        for load in loads[j]:
            load.wait()

    def rise(j, none):
        u = mm_nt(hlow[...], up[j])
        cdf = 0.5 * (1.0 + lax.erf(u * math.sqrt(0.5)))
        act[j] = (u * cdf).astype(bf16)
        slope[j] = cdf + u * (jnp.exp(-0.5 * u * u) * (1.0 / math.sqrt(2.0 * math.pi)))
        acc[...] += mm(act[j], down[j])
        return none

    lax.fori_loop(0, chunks, rise, 0)

    def second_norm(i, sums):
        rows = pl.ds(pl.multiple_of(i * ROWS, ROWS), ROWS)
        n, scale = normalized(acc[rows, :])
        layer_out[rows, :] = (n * gain1 + bias1).astype(bf16)
        c = cot[rows, :].astype(f32)
        g = normalized_back(c * gain1, n, scale)
        gsum[rows, :] = g
        glow[rows, :] = g.astype(bf16)
        return (
            sums[0] + jnp.sum(c * n, axis=0, keepdims=True),
            sums[1] + jnp.sum(c, axis=0, keepdims=True),
        )

    zero = jnp.zeros((1, feat), f32)
    gain_two, bias_two = lax.fori_loop(0, block // ROWS, second_norm, (zero, zero))
    acc[...] = gsum[...]

    def fall(j, none):
        rows = pl.ds(pl.multiple_of(j * FF_CHUNK, FF_CHUNK), FF_CHUNK)
        g_act = mm_nt(glow[...], down[j])
        g_up = (g_act * slope[j]).astype(bf16)
        down_out[j] = mm_tn(act[j], glow[...]).astype(bf16)
        pltpu.make_async_copy(down_out.at[j], gdown.at[rows], sems.at[2, j]).start()
        up_out[j] = mm_tn(g_up, hlow[...]).astype(bf16)
        pltpu.make_async_copy(up_out.at[j], gup.at[rows], sems.at[3, j]).start()
        acc[...] += mm(g_up, up[j])
        return none

    lax.fori_loop(0, chunks, fall, 0)

    def first_back(i, sums):
        rows = pl.ds(pl.multiple_of(i * ROWS, ROWS), ROWS)
        g = acc[rows, :]
        n = n1[rows, :]
        back = normalized_back(g * gain0, n, r1[rows, 0:1])
        gpre[rows, :] = back
        glow[rows, :] = back.astype(bf16)
        return (
            sums[0] + jnp.sum(g * n, axis=0, keepdims=True),
            sums[1] + jnp.sum(g, axis=0, keepdims=True),
        )

    gain_one, bias_one = lax.fori_loop(0, block // ROWS, first_back, (zero, zero))
    gnorm[...] = jnp.concatenate(
        [gain_one, gain_two, bias_one, bias_two, jnp.zeros((4, feat), f32)], axis=0
    )
    for t in range(heads.shape[0]):
        gsend[t] = fold(mm(glow[...], wout[t]), width).astype(bf16)
        grad = mm_tn(glow[...], heads[t]).astype(bf16)
        if direct:
            gout[:, :, t // 2, t % 2] = grad.reshape((4, 2) + gout.shape[4:])
        else:
            gout[t] = grad

    def land(j, none):
        rows = pl.ds(pl.multiple_of(j * FF_CHUNK, FF_CHUNK), FF_CHUNK)
        pltpu.make_async_copy(down_out.at[j], gdown.at[rows], sems.at[2, j]).wait()
        pltpu.make_async_copy(up_out.at[j], gup.at[rows], sems.at[3, j]).wait()
        return none

    lax.fori_loop(0, chunks, land, 0)


RISE = (0, 3, 1, 2)
FALL = (2, 1, 3, 0)


def feed_direct_body(
    x, cot, folded, norms, wout, up_in, down_in,
    layer_to, gsend, gpre_to, gnorm, gout, sum_up, sum_down, part_up, part_down,
    layer_out, gpre,
    heads, up, down, act, slope, hidden, hlow, n1, r1, gsum, glow, acc,
    gu, gd, cu, cd, yu, xd, lsem, csem, ysem, upsem, downsem, osem,
):
    here = Place()
    block, feat = x.shape
    units = act.shape[2]
    copies, kept = [], []

    def keep(src, dst):
        copy = pltpu.make_async_copy(src, dst, osem.at[len(kept)])
        copy.start()
        kept.append(copy)

    def start(copy):
        copy.start()
        copies.append(copy)
        return copy

    loads = {}
    for k in RISE:
        z, late = (here.z + k) % 4, 4 - k in LATE
        near_up = (z, here.y, slice(None), here.c) if late else (z,)
        near_down = (z, slice(None), here.x, here.c) if late else (z,)
        loads[k] = [
            pltpu.make_async_copy(up_in.at[near_up], up.at[near_up], lsem.at[0, k]),
            pltpu.make_async_copy(down_in.at[near_down], down.at[near_down], lsem.at[1, k]),
        ]
        for load in loads[k]:
            load.start()
    greet(
        [(here.dp, here.sibling), (here.dp, here.across), (here.dp_at(0, 1), here.t)]
    )
    arriving = {}

    def send_late(dz):
        n, z = LATE.index(dz), (here.z + 4 - dz) % 4
        near_up, near_down = (z, here.y, slice(None), here.c), (z, slice(None), here.x, here.c)
        arriving[dz] = [
            start(push(up_in.at[near_up], up.at[near_up], upsem, n, here.dp_at(0, 1), here.t)),
            start(push(down_in.at[near_down], down.at[near_down], downsem, n, here.dp, here.across)),
            start(push(up_in.at[near_up], up.at[near_up], upsem, 2 + n, here.dp, here.sibling)),
            start(push(down_in.at[near_down], down.at[near_down], downsem, 2 + n, here.dp, here.sibling)),
        ]

    send_late(LATE[0])

    def pass_on(dz):
        n, z = LATE.index(dz), (here.z + 4 - dz) % 4
        for copy in arriving[dz][:2]:
            copy.wait_recv()
        far_up, far_down = (z, 1 - here.y, slice(None), here.c), (z, slice(None), 1 - here.x, here.c)
        arriving[dz] = arriving[dz][2:] + [
            start(push(up.at[far_up], up.at[far_up], upsem, 4 + n, here.dp, here.sibling)),
            start(push(down.at[far_down], down.at[far_down], downsem, 4 + n, here.dp, here.sibling)),
        ]

    gain0, gain1 = norms[0:1, :], norms[1:2, :]
    bias0, bias1 = norms[2:3, :], norms[3:4, :]
    width = folded.shape[2] // 2
    for t in range(folded.shape[0]):
        for k in range(2):
            heads[t, k * (block // 2) : (k + 1) * (block // 2), :] = unfold(folded[t], k, width).astype(bf16)
    acc[...] = sum(mm_nt(heads[t], wout[t]) for t in range(heads.shape[0]))

    def first_norm(i, none):
        rows = pl.ds(pl.multiple_of(i * ROWS, ROWS), ROWS)
        n, scale = normalized(x[rows, :].astype(f32) + acc[rows, :])
        now = n * gain0 + bias0
        n1[rows, :] = n
        r1[rows, :] = jnp.broadcast_to(scale, (ROWS, LANES))
        hidden[rows, :] = now
        hlow[rows, :] = now.astype(bf16)
        return none

    lax.fori_loop(0, block // ROWS, first_norm, 0)
    acc[...] = hidden[...]
    flat = (4, units, feat)
    up_of, down_of = up.reshape(flat), down.reshape(flat)
    for k in RISE:
        z = (here.z + k) % 4
        for load in loads[k]:
            load.wait()
        if 4 - k in LATE:
            for copy in arriving[4 - k]:
                copy.wait_recv()
        u = mm_nt(hlow[...], up_of[z])
        cdf = 0.5 * (1.0 + lax.erf(u * math.sqrt(0.5)))
        act[k] = (u * cdf).astype(bf16)
        slope[k] = cdf + u * (jnp.exp(-0.5 * u * u) * (1.0 / math.sqrt(2.0 * math.pi)))
        acc[...] += mm(act[k], down_of[z])
        if k == RISE[0]:
            send_late(LATE[1])
        if k == RISE[1]:
            pass_on(LATE[0])
        if k == RISE[2]:
            pass_on(LATE[1])

    def second_norm(i, sums):
        rows = pl.ds(pl.multiple_of(i * ROWS, ROWS), ROWS)
        n, scale = normalized(acc[rows, :])
        layer_out[rows, :] = (n * gain1 + bias1).astype(bf16)
        c = cot[rows, :].astype(f32)
        g = normalized_back(c * gain1, n, scale)
        gsum[rows, :] = g
        glow[rows, :] = g.astype(bf16)
        return (
            sums[0] + jnp.sum(c * n, axis=0, keepdims=True),
            sums[1] + jnp.sum(c, axis=0, keepdims=True),
        )

    zero = jnp.zeros((1, feat), f32)
    gain_two, bias_two = lax.fori_loop(0, block // ROWS, second_norm, (zero, zero))
    keep(layer_out, layer_to)
    acc[...] = gsum[...]
    core, later = {}, {}

    def after_core(k):
        for copy in core[k]:
            copy.wait_recv()
        cu[k] = cu[k] + gu[k, :, :, here.c]
        cd[k] = cd[k] + gd[k, :, :, here.c]
        if k in FALL[:2]:
            n = FALL.index(k)
            later[k] = (
                start(push(cu.at[k, 1 - here.y], yu.at[n], ysem, n, here.dp_at(0, 1), here.t)),
                start(push(cd.at[k, :, 1 - here.x], xd.at[n], ysem, 2 + n, here.dp, here.across)),
            )
        else:
            n = FALL.index(k) - 2
            keep(cu.at[k], part_up.at[n])
            keep(cd.at[k], part_down.at[n])

    for n, k in enumerate(FALL):
        z = (here.z + k) % 4
        g_act = mm_nt(glow[...], down_of[z])
        g_up = (g_act * slope[k]).astype(bf16)
        gd[k] = mm_tn(act[k], glow[...]).astype(bf16).reshape(gd.shape[1:])
        gu[k] = mm_tn(g_up, hlow[...]).astype(bf16).reshape(gu.shape[1:])
        core[k] = (
            start(push(gd.at[k, :, :, 1 - here.c], cd.at[k], csem, k, here.dp, here.sibling)),
            start(push(gu.at[k, :, :, 1 - here.c], cu.at[k], csem, 4 + k, here.dp, here.sibling)),
        )
        acc[...] += mm(g_up, up_of[z])
        if n > 0:
            after_core(FALL[n - 1])

    def first_back(i, sums):
        rows = pl.ds(pl.multiple_of(i * ROWS, ROWS), ROWS)
        g = acc[rows, :]
        n = n1[rows, :]
        back = normalized_back(g * gain0, n, r1[rows, 0:1])
        gpre[rows, :] = back
        glow[rows, :] = back.astype(bf16)
        return (
            sums[0] + jnp.sum(g * n, axis=0, keepdims=True),
            sums[1] + jnp.sum(g, axis=0, keepdims=True),
        )

    gain_one, bias_one = lax.fori_loop(0, block // ROWS, first_back, (zero, zero))
    keep(gpre, gpre_to)
    gnorm[...] = jnp.concatenate(
        [gain_one, gain_two, bias_one, bias_two, jnp.zeros((4, feat), f32)], axis=0
    )
    after_core(FALL[3])
    for t in range(heads.shape[0]):
        gsend[t] = fold(mm(glow[...], wout[t]), width).astype(bf16)
        grad = mm_tn(glow[...], heads[t]).astype(bf16)
        gout[:, :, t // 2, t % 2] = grad.reshape((4, 2) + gout.shape[4:])
    for n, k in enumerate(FALL[:2]):
        for copy in later[k]:
            copy.wait_recv()
        yu[n] = cu[k, here.y] + yu[n]
        keep(yu.at[n], sum_up.at[n])
        xd[n] = cd[k, :, here.x] + xd[n]
        keep(xd.at[n], sum_down.at[n])
    for copy in copies:
        copy.wait_send()
    for copy in kept:
        copy.wait()


def feed_direct(x, cot, heads, norms, wout, up_in, down_in, depth):
    block, feat = x.shape
    blocks, wide = heads.shape[0], wout.shape[2]
    owners = up_in.shape
    hidden_n = owners[4]
    units = 8 * hidden_n
    shape = jax.ShapeDtypeStruct
    outs = (
        shape((block, feat), bf16),
        shape(heads.shape, bf16),
        shape((block, feat), f32),
        shape((8, feat), f32),
        shape((4, 2, 2, 2, depth, wide), bf16),
        shape((2, 2, hidden_n, feat), bf16),
        shape((2, 2, hidden_n, feat), bf16),
        shape((2, 2, 2, hidden_n, feat), bf16),
        shape((2, 2, 2, hidden_n, feat), bf16),
    )
    scratch = [
        pltpu.VMEM((block, feat), bf16),
        pltpu.VMEM((block, feat), f32),
        pltpu.VMEM((blocks, block, wide), bf16),
        pltpu.VMEM(owners, bf16),
        pltpu.VMEM(owners, bf16),
        pltpu.VMEM((4, block, units), bf16),
        pltpu.VMEM((4, block, units), f32),
        pltpu.VMEM((block, feat), f32),
        pltpu.VMEM((block, feat), bf16),
        pltpu.VMEM((block, feat), f32),
        pltpu.VMEM((block, LANES), f32),
        pltpu.VMEM((block, feat), f32),
        pltpu.VMEM((block, feat), bf16),
        pltpu.VMEM((block, feat), f32),
        pltpu.VMEM(owners, bf16),
        pltpu.VMEM(owners, bf16),
        pltpu.VMEM((4, 2, 2, hidden_n, feat), bf16),
        pltpu.VMEM((4, 2, 2, hidden_n, feat), bf16),
        pltpu.VMEM((2, 2, hidden_n, feat), bf16),
        pltpu.VMEM((2, 2, hidden_n, feat), bf16),
        dma(2, 4),
        dma(2, 8),
        dma(2, 4),
        dma(2, 6),
        dma(2, 6),
        dma(10),
    ]
    return pl.pallas_call(
        feed_direct_body,
        out_shape=outs,
        in_specs=[VMEM] * 5 + [ANY, ANY],
        out_specs=(ANY, VMEM, ANY, VMEM, VMEM) + (ANY,) * 4,
        scratch_shapes=scratch,
        compiler_params=pltpu.CompilerParams(
            vmem_limit_bytes=LIMIT, collective_id=5, has_side_effects=True
        ),
        name="feed_forward",
    )(x, cot, heads, norms, wout, up_in, down_in)


def feed_forward(direct, x, cot, heads, norms, wout, up_in, down_in, depth):
    block, feat = x.shape
    blocks, wide = heads.shape[0], wout.shape[2]
    hidden_n = up_in.shape[0]
    chunks = hidden_n // FF_CHUNK
    shape = jax.ShapeDtypeStruct
    outs = (
        shape((block, feat), bf16),
        shape(heads.shape, bf16),
        shape((block, feat), f32),
        shape((8, feat), f32),
        shape((4, 2, 2, 2, depth, wide) if direct else (blocks, feat, wide), bf16),
        shape((hidden_n, feat), bf16),
        shape((hidden_n, feat), bf16),
    )
    scratch = [
        pltpu.VMEM((blocks, block, wide), bf16),
        pltpu.VMEM((chunks, FF_CHUNK, feat), bf16),
        pltpu.VMEM((chunks, FF_CHUNK, feat), bf16),
        pltpu.VMEM((chunks, block, FF_CHUNK), bf16),
        pltpu.VMEM((chunks, block, FF_CHUNK), f32),
        pltpu.VMEM((block, feat), f32),
        pltpu.VMEM((block, feat), bf16),
        pltpu.VMEM((block, feat), f32),
        pltpu.VMEM((block, LANES), f32),
        pltpu.VMEM((block, feat), f32),
        pltpu.VMEM((block, feat), bf16),
        pltpu.VMEM((block, feat), f32),
        pltpu.VMEM((chunks, FF_CHUNK, feat), bf16),
        pltpu.VMEM((chunks, FF_CHUNK, feat), bf16),
        dma(4, chunks),
    ]
    return pl.pallas_call(
        functools.partial(feed_body, direct),
        out_shape=outs,
        in_specs=[VMEM] * 5 + [ANY, ANY],
        out_specs=tuple([VMEM] * 5 + [ANY, ANY]),
        scratch_shapes=scratch,
        compiler_params=pltpu.CompilerParams(vmem_limit_bytes=LIMIT),
        name="feed_forward",
    )(x, cot, heads, norms, wout, up_in, down_in)


class Summer:
    def __init__(self, here, source, first, count, own, from_core, from_y, from_z, from_x, sems, local):
        self.here, self.source, self.rows = here, source, pl.ds(first, count)
        self.own, self.from_core, self.from_y, self.from_z, self.from_x = (
            own, from_core, from_y, from_z, from_x,
        )
        self.sems, self.local = sems, local
        self.copies = []

    def push(self, src, dst, index, dp, t):
        copy = push(src, dst, self.sems, index, dp, t)
        copy.start()
        self.copies.append(copy)
        return copy

    def begin(self):
        here = self.here
        self.loaded = pltpu.make_async_copy(
            self.source.at[:, :, :, here.c, self.rows], self.own, self.local
        )
        self.loaded.start()
        self.core = self.push(
            self.source.at[:, :, :, 1 - here.c, self.rows], self.from_core, 0, here.dp, here.sibling
        )

    def along_y(self):
        here = self.here
        self.loaded.wait()
        self.core.wait_recv()

        def one(n, none):
            z, x = n // 2, n % 2
            y = 1 - here.y
            self.from_core[z, y, x] = self.from_core[z, y, x] + self.own[z, y, x]
            return none

        lax.fori_loop(0, 8, one, 0)
        self.y = self.push(
            self.from_core.at[:, 1 - here.y], self.from_y, 1, here.dp_at(0, 1), here.t
        )

    def along_z(self):
        here = self.here
        self.y.wait_recv()

        def one(n, none):
            z, x = n // 2, n % 2
            total = self.from_core[z, here.y, x].astype(f32) + self.own[z, here.y, x].astype(f32)
            total = total + self.from_y[z, x].astype(f32)
            self.from_y[z, x] = total.astype(self.own.dtype)
            return none

        lax.fori_loop(0, 8, one, 0)
        self.z = [
            self.push(
                self.from_y.at[(here.z + dz) % 4], self.from_z.at[dz - 1], 1 + dz, here.dp_at(dz, 0), here.t
            )
            for dz in (1, 2, 3)
        ]

    def along_x(self):
        here = self.here
        for copy in self.z:
            copy.wait_recv()
        for x in range(2):
            total = self.from_y[here.z, x].astype(f32)
            for n in range(3):
                total = total + self.from_z[n, x].astype(f32)
            self.from_y[here.z, x] = total.astype(self.own.dtype)
        self.x = self.push(
            self.from_y.at[here.z, 1 - here.x], self.from_x, 5, here.dp, here.across
        )

    def finish(self, out):
        self.x.wait_recv()
        here = self.here
        out[self.rows, :] = self.from_y[here.z, here.x].astype(f32) + self.from_x[...].astype(f32)
        for copy in self.copies:
            copy.wait_send()


class UpSum:
    def __init__(self, here, sums, parts, parts_far, from_y, from_z, from_x, sems, sums_far=None):
        self.here, self.sums, self.parts = here, sums, parts
        self.parts_far, self.sums_far = parts_far, sums_far
        self.from_y, self.from_z, self.from_x, self.sems = from_y, from_z, from_x, sems
        self.copies = []

    def push(self, src, dst, index, dp, t):
        copy = push(src, dst, self.sems, index, dp, t)
        copy.start()
        self.copies.append(copy)
        return copy

    def along_z(self, src, k):
        here = self.here
        return self.push(src, self.from_z.at[k - 1], k - 1, here.dp_at(k, 0), here.t)

    def begin(self):
        here = self.here
        self.y = [
            self.push(self.parts_far.at[n, 1 - here.y], self.from_y.at[n], 3 + n, here.dp_at(0, 1), here.t)
            for n in range(2)
        ]
        self.z = [self.along_z(self.sums.at[n], FALL[n]) for n in range(2)]

    def second(self):
        for n in range(2):
            self.y[n].wait_recv()
            self.from_y[n] = self.from_y[n] + self.parts[n, self.here.y]
        self.z.append(self.along_z(self.from_y.at[0], FALL[2]))

    def third(self):
        here = self.here
        for copy in self.z:
            copy.wait_recv()
        total = self.from_y[1].astype(f32)
        for n in range(3):
            total = total + self.from_z[n].astype(f32)
        self.from_y[1] = total.astype(bf16)
        self.x = self.push(self.from_y.at[1, 1 - here.x], self.from_x, 5, here.dp, here.across)

    def finish(self, out):
        self.x.wait_recv()
        out[...] = self.from_y[1, self.here.x].astype(f32) + self.from_x[...].astype(f32)
        for copy in self.copies:
            copy.wait_send()


class DownSum(UpSum):
    def begin(self):
        here = self.here
        self.x = [
            self.push(self.parts_far.at[n, :, 1 - here.x], self.from_x.at[n], 3 + n, here.dp, here.across)
            for n in range(2)
        ]
        self.y = [self.along_y(self.sums_far.at[n, 1 - here.y], n) for n in range(2)]

    def along_y(self, src, n):
        here = self.here
        return self.push(src, self.from_y.at[n], 5 + n, here.dp_at(0, 1), here.t)

    def second(self):
        self.z = []
        for n in range(2):
            self.y[n].wait_recv()
            self.from_y[n] = self.from_y[n] + self.sums[n, self.here.y]
            self.z.append(self.along_z(self.from_y.at[n], FALL[n]))

    def third(self):
        here = self.here
        for n in range(2):
            self.x[n].wait_recv()
            self.from_x[n] = self.from_x[n] + self.parts[n, :, here.x]
            self.y.append(self.along_y(self.from_x.at[n, 1 - here.y], 2 + n))

    def fourth(self):
        for n in range(2):
            self.y[2 + n].wait_recv()
            self.from_y[2 + n] = self.from_y[2 + n] + self.from_x[n, self.here.y]
        self.z.append(self.along_z(self.from_y.at[2], FALL[2]))

    def finish(self, out):
        for copy in self.z:
            copy.wait_recv()
        total = self.from_y[3].astype(f32)
        for n in range(3):
            total = total + self.from_z[n].astype(f32)
        out[...] = total
        for copy in self.copies:
            copy.wait_send()


SUMMER_SEMS = 6


def backward_body(gather, taps_total, *refs):
    (
        gsend, xall_in, wfull_in, tokc_in, segw, qk_in, v_in, kern1_in, kern3_in,
        land, counts, Ain, mixed, carried, conv, slot_live, gpre_in, hist_in,
    ) = refs[:18]
    refs = refs[18:]
    if gather:
        (sum_up, sum_down_in, part_up_in, part_down_in, out_in, norm_in), refs = refs[:6], refs[6:]
    (input_grad, gw, gconv), refs = refs[:3], refs[3:]
    if gather:
        (up_out, down_out, out_out, gain_out, bias_out), refs = refs[:5], refs[5:]
    (
        go_in, wfull, tokc, qk, v, gpre, taps, gl1, gl3, xall, xT, gopad, gqk, gv, gband, bands, gmixedT, glandT, hist, gstate, gcar, wback,
        part_out, part_in, part_sum, part_x, piece_v, piece_q, in_v, in_q, in_conv, conv_out,
        land_sum, x_land, g_high, g_low, land_own, land_out, land_in, land_all,
        gsem, lsem, psem, csem,
    ) = refs[:44]
    refs = refs[44:]

    here = Place()
    blocks, block, wide = gsend.shape[0], 2 * gsend.shape[1], gcar.shape[2]
    seq = blocks * block
    heads_n = gl1.shape[0]
    width = heads_n * HEAD_DIM
    nslot = land.shape[0]
    nchunk = seq // CHUNK
    per_block = block // CHUNK
    tiles_n = nslot // TILE
    all_tiles = heads_n * tiles_n
    feat = wfull.shape[0]
    doc_row = iota((1, nslot), 1) // LANDMARKS
    live_row = slot_live[...]
    live_cols = [column(live_row[:, g * TILE : (g + 1) * TILE].astype(f32)) for g in range(tiles_n)]
    scaling = 1.0 / math.sqrt(HEAD_DIM)
    same = tile_same()
    masks = lane_masks()

    pairs = [
        (tokc_in, tokc), (xall_in, xall), (kern1_in, gl1), (hist_in, hist), (kern3_in, gl3), (qk_in, qk),
        (v_in, v), (wfull_in, wfull), (gpre_in, gpre),
    ]
    if gather:
        sum_down, part_up, part_down = refs[:3]
        refs = refs[3:]
        pairs += [(sum_down_in, sum_down), (part_up_in, part_up), (part_down_in, part_down)]
    loads = [pltpu.make_async_copy(src, dst, lsem.at[n]) for n, (src, dst) in enumerate(pairs)]
    for load in loads:
        load.start()

    peers = here.tensor_peers()
    if gather:
        peers = peers + [
            (here.dp_at(dz, dy), here.t) for dz in range(4) for dy in range(2) if dz or dy
        ]
    greet(peers)
    copies = []

    def start(copy):
        copy.start()
        copies.append(copy)
        return copy

    gopad[0:HALO, :] = jnp.zeros((HALO, wide), bf16)
    gopad[seq + HALO : seq + 2 * HALO, :] = jnp.zeros((HALO, wide), bf16)
    arriving = [
        start(push(gsend.at[to], go_in.at[here.t], gsem, k, here.dp, to))
        for k, to in enumerate((here.across, here.diagonal, here.sibling))
    ]
    go_in[here.t] = gsend[here.t]

    if gather:
        out_sum, norm_sum, norm_pieces, q_sems, v_sems, in_vz, in_qz = refs[:7]
        refs = refs[7:]
        ups = UpSum(here, sum_up, part_up, part_up_in, *refs[:4])
        downs = DownSum(here, sum_down, part_down, part_down_in, *refs[4:8], sum_down_in)
        refs = refs[8:]
        ups.begin()
        downs.begin()
        length = gain_out.shape[1]
        far = spread_lanes(length, feat).astype(bf16)
        owner = iota((32, feat), 1) // length == iota((32, feat), 0)
        for r in range(4):
            high, low = split(jnp.where(owner, norm_in[r : r + 1, :], 0.0))
            norm_pieces[:, r, :] = mm_nt(high, far) + mm_nt(low, far)
        for r in range(4, 8):
            norm_pieces[:, r, :] = jnp.zeros((32, LANES), f32)
        norm_view = norm_pieces.reshape(4, 2, 2, 2, 8, LANES)
        smalls = []
        for source, count in ((out_in, out_in.shape[4]), (norm_view, 8)):
            buffers, refs = refs[:7], refs[7:]
            smalls.append(Summer(here, source, 0, count, *buffers))
        for summer in smalls:
            summer.begin()

    taps[...] = jnp.zeros_like(taps)
    taps[:heads_n, :taps_total] = conv[...]
    moved = pltpu.roll(taps[...], HALO - taps_total // 2, 1)
    far_rows = (iota((TILE, TILE), 0) + iota((TILE, TILE), 1) == TILE - 1).astype(f32).astype(bf16)
    turn_cols = iota((2 * TILE, 2 * TILE), 0) + iota((2 * TILE, 2 * TILE), 1) == 2 * TILE - 1
    turn_cols = turn_cols.astype(f32).astype(bf16)
    for h in range(heads_n):
        bands[h] = band_from(moved[h : h + 1, :])
        bands[heads_n + h] = mm(mm(far_rows, bands[h].astype(bf16)).astype(bf16), turn_cols)
    gmixedT[...] = jnp.zeros_like(gmixedT)
    glandT[...] = jnp.zeros_like(glandT)
    gband[...] = jnp.zeros_like(gband)
    loads[0].wait()
    loads[1].wait()

    def turn(b, none):
        for i in range(block // TILE):
            rows = slice(i * TILE, i * TILE + TILE)
            col = pl.ds(pl.multiple_of(b * block + i * TILE, TILE), TILE)
            xT[:, col] = xall[b, rows, :].astype(f32).T.astype(bf16)
            slot_now = slot_of(tokc[col, 0:1])
            hot = (slot_now == iota((TILE, nslot), 1)).astype(f32).astype(bf16)
            x_land[...] += mm(xT[:, col], hot)
        return none

    x_land[...] = jnp.zeros_like(x_land)
    lax.fori_loop(0, blocks, turn, 0)
    for h in range(heads_n):
        k0, q1, _ = landmark_parts(land[:, LANES * h : LANES * h + LANES])
        wback[h, :nslot, :] = jnp.concatenate(split(k0 * scaling), axis=1)
        wback[h, nslot:, :] = jnp.concatenate(split(q1 * scaling), axis=1)
    if gather:
        for summer in smalls:
            summer.along_y()
    for copy in arriving:
        copy.wait_recv()
    for load in loads[2:]:
        load.wait()

    def one(b, k):
        c = b * per_block + k
        rows = pl.ds(pl.multiple_of(c * CHUNK, CHUNK), CHUNK)
        inner = pl.ds(pl.multiple_of(c * CHUNK + HALO, HALO), CHUNK)
        alive = (live_of(tokc[rows, 0:1]) > 0) & (iota((CHUNK, wide), 1) < width)
        g_now = jnp.where(alive, unfold(go_in[b], k, width).astype(f32), 0.0).astype(bf16)
        gopad[inner, :] = g_now
        gT = g_now.astype(f32).T.astype(bf16)
        for h in range(heads_n):
            k1 = gl1[h, rows, :]
            gk = mm_nt(g_now, mixed[h])
            k1w = k1.astype(f32)
            gl1[h, rows, :] = (k1w * (gk - jnp.sum(gk * k1w, axis=1, keepdims=True))).astype(bf16)
            e = slice(HEAD_DIM * h, HEAD_DIM * h + HEAD_DIM)
            gmixedT[e, :] += mm(gT[e, :], k1)

    def one_block(b, none):
        for k in range(per_block):
            one(b, k)
        return none

    lax.fori_loop(0, blocks, one_block, 0)
    if gather:
        downs.second()
        ups.second()
    gmixed = gmixedT[...].T
    carried_all = carried[...]
    lane = iota((TILE, wide), 1) // HEAD_DIM
    delta = []
    for h in range(heads_n):
        rows_delta = []
        for g in range(tiles_n):
            n = h * tiles_n + g
            rows = slice(g * TILE, g * TILE + TILE)
            Z = unpack(hist[NEWTON, 1, n])
            gm = split(jnp.where(lane == h, gmixed[rows], 0.0))
            near = jnp.where(lane == h, carried_all[rows], 0.0)
            gstate[0, n] = jnp.zeros((LANDMARKS, TILE), f32)
            gstate[1, n] = pack(jnp.where(same, mm3(gm, split(near), mm_nt), 0.0))
            gc = mm3(split(Z.T), gm).astype(bf16)
            gcar[h, rows, :] = gc
            rows_delta.append(jnp.sum((gc.astype(f32) * near).T, axis=0, keepdims=True))
        delta.append(jnp.concatenate(rows_delta, axis=1))
    def three(c, emit, between=lambda: None):
        rows = pl.ds(pl.multiple_of(c * CHUNK, CHUNK), CHUNK)
        v_now = v[pl.ds(pl.multiple_of(c * CHUNK + HALO, HALO), CHUNK), :]
        total = jnp.zeros((CHUNK, wide), f32)
        for h in range(heads_n):
            gc = gcar[h]
            k3 = gl3[h, rows, :]
            gk = mm_nt(v_now, gc)
            gl = (k3.astype(f32) * (gk - delta[h])).astype(bf16)
            gl3[h, rows, :] = gl
            total = total + mm(k3, gc)
            partT = qk[rows, LANES * h : LANES * h + LANES].astype(f32).T.astype(bf16)
            glandT[h, :HEAD_DIM, :] += mm(partT[:HEAD_DIM, :], gl1[h, rows, :])
            glandT[h, HEAD_DIM:, :] += mm(partT[HEAD_DIM:, :], gl)
            between()
        for part in range(CHUNK // TILE):
            i = c * (CHUNK // TILE) + part
            at = pl.ds(pl.multiple_of(i * TILE, TILE), TILE)
            now = tokc[at, 0:1]
            seg_now = seg_of(now)
            near = seg_now == segw[pl.ds(i, 1), :]
            near_back = (seg_now == segw[pl.ds(seq // TILE + i, 1), :]) & (live_of(now) > 0)
            g_window = gopad[pl.ds(pl.multiple_of(i * TILE, TILE), 2 * TILE), :]
            v_window = v[pl.ds(pl.multiple_of(i * TILE, TILE), 2 * TILE), :]
            g_tile = gopad[pl.ds(pl.multiple_of(i * TILE + HALO, HALO), TILE), :].astype(f32)
            conv = jnp.zeros((TILE, wide), f32)
            for h in range(heads_n):
                back = mm(jnp.where(near_back, bands[heads_n + h], 0.0).astype(bf16), g_window)
                conv = jnp.where(lane == h, back, conv)
                mine = jnp.where(lane == h, g_tile, 0.0).astype(bf16)
                gband[h] += jnp.where(near, mm_nt(mine, v_window), 0.0)
            gv[at, :] = (total[part * TILE : (part + 1) * TILE, :] + conv).astype(bf16)
        for h in range(heads_n):
            both = mm(gl1[h, rows, :], wback[h, :nslot, :]) + mm(gl3[h, rows, :], wback[h, nslot:, :])
            gqk[rows, LANES * h : LANES * h + LANES] = (both[:, :LANES] + both[:, LANES:]).astype(bf16)
        emit(
            mm_nt(gqk[rows, :], wfull[:, : LANES * heads_n])
            + mm_nt(gv[rows, :], wfull[:, LANES * heads_n :])
        )

    def dyn_rows(k):
        return pl.ds(pl.multiple_of(k * CHUNK, CHUNK), CHUNK)

    def chunk_rows(k):
        return pl.ds(k * CHUNK, CHUNK)

    def landmark_stages():
        tiles = range(all_tiles)
        A = [Ain[n] for n in tiles]
        starts = [newton_start(a) for a in A]
        gW = [unpack(gstate[1, n]).T for n in tiles]
        gP = [unpack(gstate[0, n]) for n in tiles]
        GA = [tt(left_of(gP[n] + gP[n].T), right_of(A[n])) for n in tiles]
        yield
        gl2 = []
        for n in tiles:
            factor, colsum, tops = starts[n]
            gf_cols = jnp.sum((0.5 * GA[n] + gW[n]) * A[n], axis=0, keepdims=True)
            first = iota(colsum.shape, 1) < LANDMARKS
            gcol = jnp.zeros_like(colsum)
            for k in range(2):
                mine = first if k == 0 else jnp.logical_not(first)
                gf = jnp.sum(jnp.where(mine, gf_cols, 0.0), axis=1, keepdims=True)
                top = tops[k]
                is_top = mine & (colsum == top)
                ties = jnp.sum(is_top.astype(f32), axis=1, keepdims=True)
                share = jnp.where(top > 1.0, 1.0, jnp.where(top == 1.0, 0.5, 0.0))
                floor = jnp.maximum(top, 1.0)
                gcol = jnp.where(is_top, -gf * share / (floor * floor * ties), gcol)
            gA = (factor * (GA[n] + gW[n]) + gcol) * live_cols[n % tiles_n]
            one = A[n] * (gA - jnp.sum(gA * A[n], axis=1, keepdims=True)) * scaling
            rows = slice((n % tiles_n) * TILE, (n % tiles_n) * TILE + TILE)
            gl2.append(jnp.where(same & (live_row[:, rows] > 0), one, 0.0))
        yield
        for n in tiles:
            h, g = n // tiles_n, n % tiles_n
            rows = slice(g * TILE, g * TILE + TILE)
            k0, q1, _ = landmark_parts(land[rows, LANES * h : LANES * h + LANES])
            land_sum[h, rows, :] = mm3(split(gl2[n]), split(k0)) + mm3(split(gl2[n].T), split(q1))
        yield

    def walk(q, b, emit):
        def both(k, none):
            stages = newton_back_stages(hist, gstate, NEWTON - 1 - q * per_block - k, masks)
            next(stages)
            three(b * per_block + k, functools.partial(emit, k), lambda: next(stages, None))
            return none

        def alone(k, none):
            three(b * per_block + k, functools.partial(emit, k))
            return none

        ends = min(max(NEWTON - q * per_block, 0), per_block)
        lax.fori_loop(0, ends, both, 0)
        if NEWTON <= q * per_block < NEWTON + per_block:
            stages = landmark_stages()
            next(stages)
            three(b * per_block, functools.partial(emit, 0), lambda: next(stages, None))
            ends = 1
        lax.fori_loop(ends, per_block, alone, 0)

    def to_part(n, k, value):
        part_out[n, dyn_rows(k), :] = value.astype(bf16)

    def to_grad(k, value):
        input_grad[dyn_rows(k), :] = value

    def to_own_grad(k, value):
        input_grad[dyn_rows(k), :] = value + gpre[dyn_rows(k), :]

    walk(0, here.diagonal, functools.partial(to_part, 0))
    from_sibling = start(push(part_out.at[0], part_in.at[0], psem, 0, here.dp, here.sibling))
    walk(1, here.across, to_grad)
    from_sibling.wait_recv()
    from_across = []
    for k in range(per_block):
        total = input_grad[chunk_rows(k), :] + part_in[0, chunk_rows(k), :].astype(f32)
        part_sum[chunk_rows(k), :] = total.astype(bf16)
        from_across.append(
            start(push(part_sum.at[chunk_rows(k)], part_x.at[chunk_rows(k)], psem, 1 + k, here.dp, here.across))
        )
    if gather:
        downs.third()
        for summer in smalls:
            summer.along_z()
    walk(2, here.sibling, functools.partial(to_part, 1))
    own_from_sibling = start(push(part_out.at[1], part_in.at[1], psem, 1 + per_block, here.dp, here.sibling))
    walk(3, here.t, to_own_grad)
    if gather:
        downs.fourth()
        ups.third()

    conv_out[...] = jnp.zeros_like(conv_out)
    for h in range(heads_n):
        conv_out[h : h + 1, :] = diagonal_sums(gband[h])
    piece_v[...] = mm(xT[...], gv[...]).astype(bf16)
    others = [(dz, dy) for dz in range(4) for dy in range(2) if dz or dy] if gather else []
    sent_conv = []
    for k, (dz, dy) in enumerate(others):
        sent_conv.append(start(push(conv_out, in_conv.at[k], csem, k, here.dp_at(dz, dy), here.t)))

    def piece_along_y(piece, landing, sems):
        view = piece.reshape((4, 2) + landing.shape[1:])
        return start(push(view.at[:, 1 - here.y], landing, sems, 0, here.dp_at(0, 1), here.t))

    def piece_along_z(copy, piece, landing, last_landing, sems):
        view = piece.reshape((4, 2) + landing.shape[1:])
        copy.wait_recv()
        for z in range(4):
            landing[z] = landing[z] + view[z, here.y]
        return [
            start(push(landing.at[(here.z + dz) % 4], last_landing.at[dz - 1], sems, dz, here.dp_at(dz, 0), here.t))
            for dz in (1, 2, 3)
        ]

    if gather:
        v_along_y = piece_along_y(piece_v, in_v, v_sems)

    for h in range(heads_n):
        sums_land = pltpu.roll(glandT[h].T * scaling, HEAD_DIM, 1)
        lanes = slice(LANES * h, LANES * h + LANES)
        total = (land_sum[h] + sums_land) / counts[...]
        g_high[:, lanes], g_low[:, lanes] = split(total)

    weights_qk = wfull[:, : LANES * heads_n]
    spread_land = mm_nt(g_high[...], weights_qk) + mm_nt(g_low[...], weights_qk)
    half = nslot // 2
    land_own[...] = spread_land
    land_out[0] = land_own[pl.ds(pl.multiple_of((1 - here.c) * half, half), half), :].astype(bf16)
    own_half = pl.ds(pl.multiple_of(here.c * half, half), half)
    first = start(push(land_out.at[0], land_in.at[0], psem, 2 + per_block, here.dp, here.sibling))
    high, low = split(x_land[...])
    piece_q[...] = (
        mm(xT[...], gqk[...])
        + (mm(high, g_high[...]) + (mm(high, g_low[...]) + mm(low, g_high[...])))
    ).astype(bf16)
    if gather:
        q_along_y = piece_along_y(piece_q, in_q, q_sems)
    first.wait_recv()
    mine = land_own[own_half, :] + land_in[0].astype(f32)
    land_out[1] = mine.astype(bf16)
    second = start(push(land_out.at[1], land_in.at[1], psem, 3 + per_block, here.dp, here.across))
    if gather:
        for summer in smalls:
            summer.along_x()
        sent_v = piece_along_z(v_along_y, piece_v, in_v, in_vz, v_sems)
    second.wait_recv()
    mine = mine + land_in[1].astype(f32)
    land_all[own_half, :] = mine.astype(bf16)
    third = start(
        push(land_all.at[own_half], land_all.at[own_half], psem, 4 + per_block, here.dp, here.sibling)
    )
    if gather:
        ups.finish(up_out)
        downs.finish(down_out)
        sent_q = piece_along_z(q_along_y, piece_q, in_q, in_qz, q_sems)
    own_from_sibling.wait_recv()
    third.wait_recv()
    for k in range(per_block):
        from_across[k].wait_recv()
        rows = pl.ds(pl.multiple_of(here.t * block + k * CHUNK, CHUNK), CHUNK)
        hot = (slot_of(tokc[rows, 0:1]) == iota((CHUNK, nslot), 1)).astype(f32).astype(bf16)
        input_grad[chunk_rows(k), :] += (
            part_in[1, chunk_rows(k), :].astype(f32)
            + part_x[chunk_rows(k), :].astype(f32)
            + mm(hot, land_all[...])
        )
    if gather:
        for copy in sent_v + sent_q + sent_conv:
            copy.wait_recv()
        total_v = in_v[here.z].astype(f32)
        total_q = in_q[here.z].astype(f32)
        for k in range(3):
            total_v = total_v + in_vz[k].astype(f32)
            total_q = total_q + in_qz[k].astype(f32)
        total_conv = conv_out[...]
        for k in range(len(others)):
            total_conv = total_conv + in_conv[k]
        for h in range(heads_n):
            e = slice(HEAD_DIM * h, HEAD_DIM * h + HEAD_DIM)
            one = total_q[:, LANES * h : LANES * h + LANES]
            gw[0, :, e] = one[:, :HEAD_DIM]
            gw[1, :, e] = one[:, HEAD_DIM:]
        gw[2] = total_v[:, : heads_n * HEAD_DIM]
        first = HALO - taps_total // 2
        turned = pltpu.roll(total_conv, 2 * TILE - first, 1)
        gconv[...] = turned[:heads_n, :taps_total]
        smalls[0].finish(out_sum)
        out_out[...] = out_sum[:, : heads_n * HEAD_DIM].T
        smalls[1].finish(norm_sum)
        gain_out[...] = norm_sum[0:2, :length]
        bias_out[...] = norm_sum[2:4, :length]
    else:
        gw[:, : LANES * heads_n] = piece_q[...].astype(f32)
        gw[:, LANES * heads_n :] = piece_v[...].astype(f32)
        gconv[...] = conv_out[...]
    for copy in copies:
        copy.wait_send()


def attention_backward(gsend, xall, wfull, tokc, segw, qk, v, kern1, kern3, land, counts, weights,
                       mixed, carried, conv, slot_live, gpre, hist, sources, taps_total, depth):
    blocks, block, wide = gsend.shape[0], 2 * gsend.shape[1], v.shape[1]
    heads_n, seq, nslot = kern1.shape
    feat = wfull.shape[0]
    all_tiles = weights.shape[0]
    shape = jax.ShapeDtypeStruct
    gather = len(sources) > 0
    width = heads_n * HEAD_DIM
    outs = [shape((block, feat), f32)]
    if gather:
        hidden_n = sources[0].shape[2]
        outs += [
            shape((3, depth, width), f32),
            shape((heads_n, taps_total), f32),
            shape((hidden_n, feat), f32),
            shape((hidden_n, feat), f32),
            shape((width, depth), f32),
            shape((2, feat // 32), f32),
            shape((2, feat // 32), f32),
        ]
    else:
        outs += [shape((feat, wfull.shape[1]), f32), shape((8, 2 * TILE), f32)]
    others = 7 if gather else 1
    per_block = block // CHUNK
    scratch = [
        pltpu.VMEM(gsend.shape, bf16),
        pltpu.VMEM(wfull.shape, bf16),
        pltpu.VMEM(tokc.shape, i32),
        pltpu.VMEM(qk.shape, bf16),
        pltpu.VMEM(v.shape, bf16),
        pltpu.VMEM(gpre.shape, f32),
        pltpu.VMEM((8, 2 * TILE), f32),
        pltpu.VMEM((heads_n, seq, nslot), bf16),
        pltpu.VMEM((heads_n, seq, nslot), bf16),
        pltpu.VMEM(xall.shape, bf16),
        pltpu.VMEM((feat, seq), bf16),
        pltpu.VMEM((seq + 2 * HALO, wide), bf16),
        pltpu.VMEM((seq, LANES * heads_n), bf16),
        pltpu.VMEM((seq, wide), bf16),
        pltpu.VMEM((heads_n, TILE, 2 * TILE), f32),
        pltpu.VMEM((2 * heads_n, TILE, 2 * TILE), f32),
        pltpu.VMEM((wide, nslot), f32),
        pltpu.VMEM((heads_n, LANES, nslot), f32),
        pltpu.VMEM((NEWTON + 1, 4, all_tiles, LANDMARKS, TILE), f32),
        pltpu.VMEM((2, all_tiles, LANDMARKS, TILE), f32),
        pltpu.VMEM((heads_n, nslot, wide), bf16),
        pltpu.VMEM((heads_n, 2 * nslot, 256), bf16),
        pltpu.VMEM((2, block, feat), bf16),
        pltpu.VMEM((2, block, feat), bf16),
        pltpu.VMEM((block, feat), bf16),
        pltpu.VMEM((block, feat), bf16),
        pltpu.VMEM((feat, wide), bf16),
        pltpu.VMEM((feat, LANES * heads_n), bf16),
        pltpu.VMEM((4, depth if gather else 16, wide), bf16),
        pltpu.VMEM((4, depth if gather else 16, LANES * heads_n), bf16),
        pltpu.VMEM((others, 8, 2 * TILE), f32),
        pltpu.VMEM((8, 2 * TILE), f32),
        pltpu.VMEM((heads_n, nslot, LANES), f32),
        pltpu.VMEM((feat, nslot), f32),
        pltpu.VMEM((nslot, LANES * heads_n), bf16),
        pltpu.VMEM((nslot, LANES * heads_n), bf16),
        pltpu.VMEM((nslot, feat), f32),
        pltpu.VMEM((2, nslot // 2, feat), bf16),
        pltpu.VMEM((2, nslot // 2, feat), bf16),
        pltpu.VMEM((nslot, feat), bf16),
        dma(2, 3),
        dma(12),
        dma(2, 5 + per_block),
        dma(2, others),
    ]
    if gather:
        scratch += [pltpu.VMEM(source.shape, bf16) for source in sources[1:4]]
        scratch += [
            pltpu.VMEM((depth, wide), f32),
            pltpu.VMEM((8, LANES), f32),
            pltpu.VMEM((32, 8, LANES), f32),
            dma(2, 4),
            dma(2, 4),
            pltpu.VMEM((3, depth, wide), bf16),
            pltpu.VMEM((3, depth, LANES * heads_n), bf16),
            pltpu.VMEM((2, 2, hidden_n, feat), bf16),
            pltpu.VMEM((3, 2, hidden_n, feat), bf16),
            pltpu.VMEM((hidden_n, feat), bf16),
            dma(2, 6),
            pltpu.VMEM((4, hidden_n, feat), bf16),
            pltpu.VMEM((3, hidden_n, feat), bf16),
            pltpu.VMEM((2, 2, hidden_n, feat), bf16),
            dma(2, 9),
        ]
        for count, lanes, kind in ((depth, wide, bf16), (8, LANES, f32)):
            scratch += [
                pltpu.VMEM((4, 2, 2, count, lanes), kind),
                pltpu.VMEM((4, 2, 2, count, lanes), kind),
                pltpu.VMEM((4, 2, count, lanes), kind),
                pltpu.VMEM((3, 2, count, lanes), kind),
                pltpu.VMEM((count, lanes), kind),
                dma(2, SUMMER_SEMS),
                pltpu.SemaphoreType.DMA,
            ]
    specs = [VMEM, ANY, ANY, ANY, VMEM] + [ANY] * 4 + [VMEM] * 7 + [ANY, ANY]
    if gather:
        specs += [ANY] * 5 + [VMEM]
    return pl.pallas_call(
        functools.partial(backward_body, gather, taps_total),
        out_shape=tuple(outs),
        in_specs=specs,
        out_specs=tuple([VMEM] * len(outs)),
        scratch_shapes=scratch,
        compiler_params=pltpu.CompilerParams(
            vmem_limit_bytes=LIMIT, collective_id=3 if gather else 4, has_side_effects=True
        ),
        name="attention_backward",
    )(gsend, xall, wfull, tokc, segw, qk, v, kern1, kern3, land, counts, weights, mixed, carried,
      conv, slot_live, gpre, hist, *sources)


def hand_over_body(*refs):
    half = len(refs) // 2
    for src, dst in zip(refs[:half], refs[half:]):
        dst[...] = src[...]


def hand_over(*arrays):
    return pl.pallas_call(
        hand_over_body,
        out_shape=tuple(jax.ShapeDtypeStruct(a.shape, a.dtype) for a in arrays),
        in_specs=[VMEM] * len(arrays),
        out_specs=tuple([VMEM] * len(arrays)),
        name="hand_over",
    )(*arrays)


def split_up(shard, dim, length):
    before, after = (shard.shape[:dim], shard.shape[dim + 1 :])
    return jnp.moveaxis(shard.reshape(*before, length, -1, *after), dim, 0)


def exchange(pieces, axis):
    return lax.all_to_all(pieces, axis, split_axis=0, concat_axis=0, tiled=True)


def per_device(
    tokens,
    w_qkv,
    w_out,
    conv_weight,
    w_up,
    w_down,
    norm_gain,
    norm_bias,
    cotangent,
    seg_ids,
    landmark_slot,
    token_live,
    slot_live,
):
    both = ("dp", "tensor")
    dp_size, blocks = lax.axis_size("dp"), lax.axis_size("tensor")
    devices = dp_size * blocks
    heads_n, taps_total = conv_weight.shape
    block, feat = tokens.shape
    depth = w_qkv.shape[1]
    width = heads_n * HEAD_DIM
    wide = -(-width // 256) * 256
    hidden_n = w_up.shape[1]
    docs = slot_live.shape[1] // LANDMARKS
    direct = dp_size == 8 and blocks == 4 and depth % 16 == 0 and hidden_n % 32 == 0

    first = HALO - taps_total // 2
    weight = w_qkv if direct else lax.all_gather(w_qkv, "dp", axis=1, tiled=True)
    extra = (w_up.T, w_down, w_out, norm_gain, norm_bias) if direct else ()
    got = attention_forward(
        tokens, weight, conv_weight, seg_ids, landmark_slot, token_live, slot_live,
        extra, heads_n, blocks, taps_total,
    )
    (
        xall, wfull, tokc, segw, qk, v, kern1, kern3, land, counts, weights, mixed, carried, heads, proxies,
        hist,
    ) = got[:16]
    if direct:
        up_all, down_all, out_all, norms = got[16:]
        out_all = out_all.reshape(blocks, feat, wide)
    else:
        up_all = lax.all_gather(w_up.T, both, axis=0, tiled=True)
        down_all = lax.all_gather(w_down, both, axis=0, tiled=True)
        out_all = lax.all_gather(lax.all_gather(w_out.T, "dp", axis=0, tiled=True), "tensor", axis=0)
        out_all = jnp.pad(out_all, ((0, 0), (0, 0), (0, wide - width)))
        norms = jnp.concatenate([norm_gain, norm_bias, jnp.zeros_like(norm_gain), jnp.zeros_like(norm_bias)])
        norms = lax.all_gather(norms, both, axis=1, tiled=True).astype(f32)
    if direct:
        got = feed_direct(tokens, cotangent, heads, norms, out_all, up_all, down_all, depth)
        layer_out, gsend, grad_pre, norm_grads, out_pieces = got[:5]
        sources = got[5:] + (out_pieces, norm_grads)
    else:
        layer_out, gsend, grad_pre, norm_grads, out_pieces, up_pieces, down_pieces = feed_forward(
            direct, tokens, cotangent, heads, norms, out_all, up_all, down_all, depth
        )
        sources = ()
    got = attention_backward(
        gsend, xall, wfull, tokc, segw, qk, v, kern1, kern3, land, counts, weights,
        mixed, carried, conv_weight, slot_live, grad_pre, hist, sources, taps_total, depth,
    )
    if direct:
        (
            input_grad, grad_qkv, grad_conv, grad_up, grad_down, grad_out, grad_gain, grad_bias, proxies,
            layer_out,
        ) = hand_over(*got, proxies, layer_out)
        grad_up = grad_up.T
    else:
        input_grad, grad_w, grad_conv = got
        grad_w = exchange(grad_w.astype(bf16).reshape(dp_size, depth, -1), "dp").astype(f32).sum(axis=0)
        pairs = grad_w[:, : LANES * heads_n].reshape(depth, heads_n, 2, HEAD_DIM)
        grad_qkv = jnp.concatenate(
            [
                jnp.moveaxis(pairs, 2, 0).reshape(2, depth, width),
                grad_w[None, :, LANES * heads_n : LANES * heads_n + width],
            ]
        )
        grad_conv = lax.psum(grad_conv, "dp")[:heads_n, first : first + taps_total]
        grad_up = lax.psum_scatter(up_pieces, both, scatter_dimension=0, tiled=True).astype(f32).T
        grad_down = lax.psum_scatter(down_pieces, both, scatter_dimension=0, tiled=True).astype(f32)
        out_pieces = out_pieces[:, :, :width].reshape(blocks, dp_size, depth, width)
        out_pieces = jnp.swapaxes(out_pieces, 0, 1).reshape(devices, depth, width)
        grad_out = lax.psum_scatter(out_pieces, both, scatter_dimension=0, tiled=False).astype(f32).T
        norm_sum = exchange(split_up(norm_grads[:4], 1, devices), both).sum(axis=0)
        grad_gain, grad_bias = norm_sum[:2], norm_sum[2:]
    return (
        layer_out,
        input_grad,
        grad_qkv,
        grad_out,
        grad_conv,
        grad_up,
        grad_down,
        grad_gain,
        grad_bias,
        jnp.transpose(proxies, (1, 2, 0)),
    )


def solution(mesh):
    return jax.shard_map(
        per_device,
        mesh=mesh,
        in_specs=(
            P(("dp", "tensor"), None),
            P(None, "dp", "tensor"),
            P("tensor", "dp"),
            P("tensor", None),
            P(None, ("dp", "tensor")),
            P(("dp", "tensor"), None),
            P(None, ("dp", "tensor")),
            P(None, ("dp", "tensor")),
            P(("dp", "tensor"), None),
            P("dp", None),
            P("dp", None),
            P("dp", None),
            P("dp", None),
        ),
        out_specs=(
            P(("dp", "tensor"), None),
            P(("dp", "tensor"), None),
            P(None, "dp", "tensor"),
            P("tensor", "dp"),
            P("tensor", None),
            P(None, ("dp", "tensor")),
            P(("dp", "tensor"), None),
            P(None, ("dp", "tensor")),
            P(None, ("dp", "tensor")),
            P("dp", None, "tensor"),
        ),
        check_vma=False,
    )
```

```python
import functools
import math

import jax
import jax.numpy as jnp
from jax import lax
from jax.experimental import pallas as pl
from jax.experimental.pallas import tpu as pltpu
from jax.sharding import PartitionSpec as P

HEAD_DIM = 64
LANDMARKS = 64
NEWTON = 6
TILE = 128
HALO = TILE // 2
CHUNK = 256
LANES = 128
bf16 = jnp.bfloat16
f32 = jnp.float32
i32 = jnp.int32
norm_epsilon = 1e-05
MESH = pl.DeviceIdType.MESH
LIMIT = 62 * 2**20


def mm(a, b):
    return lax.dot_general(a, b, (((1,), (0,)), ((), ())), preferred_element_type=f32)


def mm_nt(a, b):
    return lax.dot_general(a, b, (((1,), (1,)), ((), ())), preferred_element_type=f32)


def split(a):
    high = a.astype(bf16)
    return high, (a - high.astype(f32)).astype(bf16)


def mm3(a, b, dot=mm):
    return dot(a[0], b[0]) + (dot(a[0], b[1]) + dot(a[1], b[0]))


def left_of(a):
    return jnp.concatenate(split(a), axis=1)


def right_of(b):
    high, low = split(b)
    top = jnp.concatenate([high, low], axis=1)
    bottom = jnp.concatenate([jnp.zeros_like(high), high], axis=1)
    return jnp.concatenate([top, bottom], axis=0)


def right_nt(b):
    high, low = split(b)
    top = jnp.concatenate([high, jnp.zeros_like(high)], axis=1)
    bottom = jnp.concatenate([low, high], axis=1)
    return jnp.concatenate([top, bottom], axis=0)


def tt(left, right):
    both = mm(left, right)
    return both[:, :TILE] + both[:, TILE:]


def tt_nt(left, right):
    both = mm_nt(left, right)
    return both[:, :TILE] + both[:, TILE:]


def iota(shape, dim):
    return lax.broadcasted_iota(i32, shape, dim)


def tile_same():
    shape = (TILE, TILE)
    return iota(shape, 0) // LANDMARKS == iota(shape, 1) // LANDMARKS


def tile_eye():
    shape = (TILE, TILE)
    return (iota(shape, 0) == iota(shape, 1)).astype(f32)


def pack(tile):
    return tile[:LANDMARKS] + tile[LANDMARKS:]


def unpack(packed):
    first = iota(packed.shape, 1) < LANDMARKS
    return jnp.concatenate([jnp.where(first, packed, 0.0), jnp.where(first, 0.0, packed)], axis=0)


def landmark_parts(land):
    first = iota(land.shape, 1) < HEAD_DIM
    turned = pltpu.roll(land, HEAD_DIM, 1)
    return jnp.where(first, turned, 0.0), jnp.where(first, 0.0, turned), jnp.where(first, land, 0.0)


def lane_masks():
    first = (iota((LANDMARKS, TILE), 1) < LANDMARKS).astype(f32)
    return first.astype(bf16), (1.0 - first).astype(bf16)


def packed_eye():
    shape = (LANDMARKS, TILE)
    return (iota(shape, 0) == iota(shape, 1) % LANDMARKS).astype(f32)


def packed_right(b, masks):
    high, low = split(b)
    high = jnp.concatenate([high * masks[0], high * masks[1]], axis=0)
    low = jnp.concatenate([low * masks[0], low * masks[1]], axis=0)
    top = jnp.concatenate([high, low], axis=1)
    bottom = jnp.concatenate([jnp.zeros_like(high), high], axis=1)
    return jnp.concatenate([top, bottom], axis=0)


def packed_tn(a, b):
    (ah, al), (bh, bl) = split(a), split(b)
    both = lax.dot_general(
        jnp.concatenate([ah, al, ah], axis=0),
        jnp.concatenate([bh, bh, bl], axis=0),
        (((0,), (0,)), ((), ())),
        preferred_element_type=f32,
    )
    first = iota(a.shape, 1) < LANDMARKS
    return jnp.where(first, both[:LANDMARKS], both[LANDMARKS:])


def newton_stages(hist, i, ident, masks):
    tiles = range(hist.shape[2])
    P = [hist[i, 0, n] for n in tiles]
    Pl, Pr = [left_of(p) for p in P], [packed_right(p, masks) for p in P]
    S = [tt(Pl[n], Pr[n]) for n in tiles]
    yield
    N = [13.0 * ident - 15.0 * P[n] + 7.0 * S[n] - tt(left_of(S[n]), Pr[n]) for n in tiles]
    yield
    for n in tiles:
        hist[i, 2, n] = S[n]
        hist[i, 3, n] = N[n]
        rows = jnp.concatenate([Pl[n], left_of(hist[i, 1, n])], axis=0)
        both = 0.25 * tt(rows, packed_right(N[n], masks))
        hist[i + 1, 0, n] = both[:LANDMARKS]
        hist[i + 1, 1, n] = both[LANDMARKS:]
    yield


def newton_back_stages(hist, gstate, i, masks):
    tiles = range(hist.shape[2])
    gP, gZ = [gstate[0, n] for n in tiles], [gstate[1, n] for n in tiles]
    P = [hist[i, 0, n] for n in tiles]
    Pl, Pr = [left_of(p) for p in P], [packed_right(p, masks) for p in P]
    gN = [
        0.25 * (tt(Pl[n], packed_right(gP[n], masks)) + packed_tn(hist[i, 1, n], gZ[n])) for n in tiles
    ]
    both = [
        0.25
        * tt(
            jnp.concatenate([left_of(gP[n]), left_of(gZ[n])], axis=0),
            packed_right(hist[i, 3, n], masks),
        )
        for n in tiles
    ]
    yield
    gS = [7.0 * gN[n] - tt(left_of(gN[n]), Pr[n]) for n in tiles]
    kept = [
        both[n][:LANDMARKS] - 15.0 * gN[n] - tt(left_of(hist[i, 2, n]), packed_right(gN[n], masks))
        for n in tiles
    ]
    yield
    for n in tiles:
        gstate[1, n] = both[n][LANDMARKS:]
        gstate[0, n] = kept[n] + tt(left_of(gS[n]), Pr[n]) + tt(Pl[n], packed_right(gS[n], masks))
    yield


def newton_start(A):
    colsum = jnp.sum(A, axis=0, keepdims=True)
    first = iota(colsum.shape, 1) < LANDMARKS
    tops = [
        jnp.max(jnp.where(first, colsum, 0.0), axis=1, keepdims=True),
        jnp.max(jnp.where(first, 0.0, colsum), axis=1, keepdims=True),
    ]
    factor = 1.0 / jnp.maximum(jnp.where(first, tops[0], tops[1]), 1.0)
    return factor, colsum, tops


def column(row):
    return jnp.broadcast_to(row, (LANES, LANES)).T


def band_from(row):
    wide = jnp.broadcast_to(row, (TILE, 2 * TILE))
    return pltpu.roll(wide, 0, 1, stride=1, stride_axis=0)


def diagonal_sums(band):
    where = iota(band.shape, 0)
    step = 1
    while step < TILE:
        turned = pltpu.roll(band, 2 * TILE - step, 1)
        band = jnp.where((where // step) % 2 == 1, turned, band)
        step *= 2
    return jnp.sum(band, axis=0, keepdims=True)


def seg_of(code):
    return (code // 512) % 8


def live_of(code):
    return code // 4096


def slot_of(code):
    return code % 512


def fold(rows, width):
    half = rows.shape[0] // 2
    far = pltpu.roll(rows[half:], width, 1)
    near = rows[:half]
    return jnp.concatenate(
        [near[:, :LANES], near[:, LANES:] + far[:, LANES:], far[:, :LANES]], axis=1
    )


def unfold(folded, k, width):
    if k == 0:
        return folded[:, : 2 * LANES]
    return pltpu.roll(folded[:, LANES:].astype(f32), width, 1)


class Place:
    def __init__(self):
        self.dp = lax.axis_index("dp")
        self.t = lax.axis_index("tensor")
        self.x = self.t // 2
        self.c = self.t % 2
        self.sibling = self.x * 2 + 1 - self.c
        self.across = (1 - self.x) * 2 + self.c
        self.diagonal = (1 - self.x) * 2 + 1 - self.c
        self.z = self.dp // 2
        self.y = self.dp % 2

    def tensor_peers(self):
        return [(self.dp, t) for t in (self.sibling, self.across, self.diagonal)]

    def dp_at(self, turn_z, turn_y):
        return ((self.z + turn_z) % 4) * 2 + (self.y + turn_y) % 2


def greet(peers):
    barrier = pltpu.get_barrier_semaphore()
    for peer in peers:
        pl.semaphore_signal(barrier, inc=1, device_id=peer, device_id_type=MESH)
    pl.semaphore_wait(barrier, len(peers))


def push(src, dst, sems, index, dp, t):
    return pltpu.make_async_remote_copy(
        src_ref=src,
        dst_ref=dst,
        send_sem=sems.at[0, index],
        recv_sem=sems.at[1, index],
        device_id=(dp, t),
        device_id_type=MESH,
    )


class Spreader:
    def __init__(self, here, shard, whole, sems, local, by_x, by_rows=False):
        self.here, self.shard, self.whole, self.sems, self.local = here, shard, whole, sems, local
        self.by_rows, self.by_x = by_rows, by_x
        first, last = (here.dp, here.across), (here.dp_at(0, 1), here.t)
        self.first, self.last = (first, last) if by_x else (last, first)
        self.copies = []
        self.from_z, self.from_first, self.from_last, self.from_core = {}, {}, {}, []

    def at(self, z, y, x):
        c = self.here.c
        if not self.by_rows:
            return self.whole.at[z, y, x, c]
        depth = self.shard.shape[0]
        rows = pl.ds(pl.multiple_of((z * 2 + y) * depth, 16), depth)
        return self.whole.at[x, c, rows]

    def one(self, dz):
        return self.at((self.here.z + 4 - dz) % 4, self.here.y, self.here.x)

    def pair(self, dz, turned):
        here, z = self.here, (self.here.z + 4 - dz) % 4
        if self.by_x:
            return self.at(z, (here.y + turned) % 2, slice(None))
        return self.at(z, slice(None), (here.x + turned) % 2)

    def push(self, src, dst, index, place):
        copy = push(src, dst, self.sems, index, *place)
        copy.start()
        self.copies.append(copy)
        return copy

    def begin(self):
        self.kept = pltpu.make_async_copy(self.shard, self.one(0), self.local)
        self.kept.start()
        if self.by_x:
            self.own_first()

    def own_first(self):
        self.from_first[0] = self.push(self.shard, self.one(0), 3, self.first)

    def along_z(self, dz):
        here = self.here
        self.from_z[dz] = self.push(self.shard, self.one(0), dz - 1, (here.dp_at(dz, 0), here.t))

    def along_first(self, dz):
        self.from_z[dz].wait_recv()
        self.from_first[dz] = self.push(self.one(dz), self.one(dz), 3 + dz, self.first)

    def along_last(self, dz):
        if dz == 0:
            self.kept.wait()
        self.from_first[dz].wait_recv()
        got = self.pair(dz, 0)
        self.from_last[dz] = self.push(got, got, 7 + dz, self.last)
        self.from_core.append(self.push(got, got, 11 + dz, (self.here.dp, self.here.sibling)))

    def to_core(self, dz):
        self.from_last[dz].wait_recv()
        got = self.pair(dz, 1)
        self.from_core.append(self.push(got, got, 15 + dz, (self.here.dp, self.here.sibling)))

    def finish(self):
        for dz in self.from_first:
            if dz not in self.from_last:
                self.from_first[dz].wait_recv()
        for copy in self.from_core:
            copy.wait_recv()
        for copy in self.copies:
            copy.wait_send()


LATE = (3, 2)


def spread_lanes(length, whole):
    shape = (LANES, whole)
    return (iota(shape, 0) == iota(shape, 1) % length).astype(f32)


def forward_body(gather, taps_total, *refs):
    (x, w, conv, seg, slot, live, slot_live), refs = refs[:7], refs[7:]
    if gather:
        (w_up, w_down, w_out, gain, bias), refs = refs[:5], refs[5:]
    (
        xall_out, wfull_out, tokc, segw, qk_out, v_out, kern1_out, kern3_out,
        land, counts, Aout, mixed, carried, heads, prox, hist_out,
    ) = refs[:16]
    refs = refs[16:]
    if gather:
        (up_all, down_all, out_all, norms), refs = refs[:4], refs[4:]
    (
        xall, wfull, qk, v, kern1, kern3,
        wsh, wlog, l3, carriedT, hist, bands, hsend, segp, taps, xsem, wsem, hsem, osem,
    ) = refs[:19]
    refs = refs[19:]
    keeping = []

    def keep(src, dst):
        copy = pltpu.make_async_copy(src, dst, osem.at[len(keeping)])
        copy.start()
        keeping.append(copy)

    here = Place()
    block = x.shape[0]
    blocks = xall.shape[0]
    seq = block * blocks
    heads_n = qk.shape[1] // LANES
    nslot = land.shape[0]
    wide = v.shape[1]
    nchunk = seq // CHUNK
    per_block = block // CHUNK
    tiles_n = nslot // TILE
    width = heads_n * HEAD_DIM
    scaling = 1.0 / math.sqrt(HEAD_DIM)

    depth = w.shape[1]
    parts = []
    for h in range(heads_n):
        e = slice(HEAD_DIM * h, HEAD_DIM * h + HEAD_DIM)
        parts += [w[0, :, e], w[1, :, e]]
    parts += [w[2], jnp.zeros((depth, wide - width), bf16)]
    wsh[...] = jnp.concatenate(parts, axis=1)

    peers = here.tensor_peers()
    if gather:
        peers = peers + [(here.dp_at(dz, 0), here.t) for dz in (1, 2, 3)] + [(here.dp_at(0, 1), here.t)]
        out_sh, norm_sh, norm_all = refs[:3]
        out_sh[...] = jnp.concatenate(
            [w_out[...].astype(f32).T, jnp.zeros((depth, wide - width), f32)], axis=1
        ).astype(bf16)
        norm_sh[...] = jnp.zeros_like(norm_sh)
        norm_sh[0:2, : gain.shape[1]] = gain[...].astype(f32)
        norm_sh[2:4, : gain.shape[1]] = bias[...].astype(f32)
        sems = refs[3:]
        spread_out = Spreader(here, out_sh, out_all, sems[2], sems[3], True, by_rows=True)
        spread_norm = Spreader(here, norm_sh, norm_all, sems[4], sems[5], True)
        whole = (spread_out, spread_norm)
        partly = (
            Spreader(here, w_up, up_all, sems[0], sems[1], True),
            Spreader(here, w_down, down_all, sems[6], sems[7], False),
        )
        spreads = whole + partly
    greet(peers)

    copies = []
    pieces = block // TILE

    def start(copy):
        copy.start()
        copies.append(copy)
        return copy

    crossing = [
        start(push(x.at[pl.ds(p * TILE, TILE)], xall.at[here.t, pl.ds(p * TILE, TILE)], xsem, p, here.dp, here.across))
        for p in range(pieces)
    ]
    beside = start(push(x, xall.at[here.t], xsem, pieces, here.dp, here.sibling))
    if gather:
        mine = wfull.at[pl.ds(pl.multiple_of(here.dp * depth, 16), depth)]
        along = [start(push(wsh, mine, wsem, dz, here.dp_at(dz, 0), here.t)) for dz in (1, 2, 3)]
        along = [start(push(wsh, mine, wsem, 0, here.dp_at(0, 1), here.t))] + along
        wfull[pl.ds(pl.multiple_of(here.dp * depth, 16), depth), :] = wsh[...]
    else:
        wfull[...] = wsh[...]
    xall[here.t] = x[...]

    segp[...] = jnp.full(segp.shape, -1, i32)
    segp[0:1, TILE : TILE + seq] = jnp.where(live[...] > 0, seg[...], -1)
    segp[1:2, TILE : TILE + seq] = seg[...]
    code = (slot[...] + 512 * seg[...] + 4096 * live[...]).astype(f32)
    for i in range(seq // TILE):
        lanes = slice(i * TILE, i * TILE + TILE)
        tokc[lanes, :] = column(code[:, lanes]).astype(i32)
        near = pltpu.roll(segp[:, i * TILE : i * TILE + 3 * TILE], 3 * TILE - HALO, 1)
        segw[i : i + 1, :] = near[0:1, : 2 * TILE]
        segw[seq // TILE + i : seq // TILE + i + 1, :] = near[1:2, : 2 * TILE]
    taps[...] = jnp.zeros_like(taps)
    taps[:heads_n, :taps_total] = conv[...]
    moved = pltpu.roll(taps[...], HALO - taps_total // 2, 1)
    for h in range(heads_n):
        bands[h] = band_from(moved[h : h + 1, :])
    doc_row = iota((1, nslot), 1) // LANDMARKS
    live_row = slot_live[...]
    live_cols = [column(live_row[:, g * TILE : (g + 1) * TILE].astype(f32)) for g in range(tiles_n)]
    v[0:HALO, :] = jnp.zeros((HALO, wide), bf16)
    v[seq + HALO : seq + 2 * HALO, :] = jnp.zeros((HALO, wide), bf16)

    if gather:
        along[0].wait_recv()
        for dz in (1, 2, 3):
            along[dz].wait_recv()
            got = wfull.at[pl.ds(pl.multiple_of(here.dp_at(4 - dz, 0) * depth, 16), depth)]
            along.append(start(push(got, got, wsem, 3 + dz, here.dp_at(0, 1), here.t)))
        for spread in spreads:
            spread.begin()
            spread.along_z(1)
            spread.along_z(3)
        for dz in (1, 2, 3):
            along[3 + dz].wait_recv()
        for spread in spreads:
            if not spread.by_x:
                spread.own_first()

    def project(b, carry):
        def one(i, carry):
            acc, cnt = carry
            c = b * per_block + i
            rows = pl.ds(pl.multiple_of(c * CHUNK, CHUNK), CHUNK)
            out = mm(xall[b, pl.ds(pl.multiple_of(i * CHUNK, CHUNK), CHUNK), :], wfull[...])
            qk_now = out[:, : LANES * heads_n].astype(bf16)
            qk[rows, :] = qk_now
            v[pl.ds(pl.multiple_of(c * CHUNK + HALO, HALO), CHUNK), :] = out[:, LANES * heads_n :].astype(bf16)
            slot_now = slot[:, pl.ds(pl.multiple_of(c * CHUNK, CHUNK), CHUNK)]
            hot = (slot_now == iota((nslot, CHUNK), 0)).astype(f32)
            return acc + mm(hot.astype(bf16), qk_now), cnt + jnp.sum(hot, axis=1, keepdims=True)

        return lax.fori_loop(0, per_block, one, carry)

    carry = (jnp.zeros((nslot, LANES * heads_n), f32), jnp.zeros((nslot, 1), f32))
    carry = project(here.t, carry)
    beside.wait_recv()
    carry = project(here.sibling, carry)
    passed = []
    for p in range(pieces):
        crossing[p].wait_recv()
        got = xall.at[here.across, pl.ds(p * TILE, TILE)]
        passed.append(start(push(got, got, xsem, pieces + 1 + p, here.dp, here.sibling)))
    carry = project(here.across, carry)
    for p in range(pieces):
        passed[p].wait_recv()
    acc, cnt = project(here.diagonal, carry)
    cnt = jnp.maximum(cnt, 1.0)
    counts[...] = jnp.broadcast_to(cnt, counts.shape)
    land[...] = acc / cnt

    if gather:
        for spread in spreads:
            spread.along_z(2)
            spread.along_last(0)
    keep(xall, xall_out)
    keep(wfull, wfull_out)
    keep(qk, qk_out)
    keep(v, v_out)

    same = tile_same()
    ident = packed_eye()
    masks = lane_masks()
    for h in range(heads_n):
        k0, q1, q0 = landmark_parts(land[:, LANES * h : LANES * h + LANES])
        wlog[h] = jnp.concatenate(split(jnp.concatenate([k0, q1], axis=0) * scaling), axis=1)
        for g in range(tiles_n):
            rows = slice(g * TILE, g * TILE + TILE)
            logit = tt_nt(left_of(q0[rows] * scaling), right_nt(k0[rows]))
            filled = jnp.where(same & (live_row[:, rows] > 0), logit, -1e9)
            raised = jnp.exp(filled - jnp.max(filled, axis=1, keepdims=True))
            A = raised / jnp.sum(raised, axis=1, keepdims=True) * live_cols[g]
            n = h * tiles_n + g
            Aout[n] = A
            factor, _, _ = newton_start(A)
            W = A * factor
            hist[0, 0, n] = pack(tt_nt(left_of(A), right_nt(W)))
            hist[0, 1, n] = pack(W.T)

    def logits(c, top, between=lambda: None):
        rows = pl.ds(pl.multiple_of(c * CHUNK, CHUNK), CHUNK)
        now = tokc[rows, 0:1]
        allowed = (seg_of(now) == doc_row) & (live_row > 0)
        alive = allowed & (live_of(now) > 0)
        tops = []
        for h in range(heads_n):
            part = qk[rows, LANES * h : LANES * h + LANES]
            both = mm_nt(jnp.concatenate([part, part], axis=1), wlog[h])
            one = jnp.where(allowed, both[:, :nslot], -1e9)
            raised = jnp.exp(one - jnp.max(one, axis=1, keepdims=True))
            kern1[h, rows, :] = (raised / jnp.sum(raised, axis=1, keepdims=True)).astype(bf16)
            three = jnp.where(alive, both[:, nslot:], -1e9)
            l3[h, rows, :] = three
            tops.append(jnp.maximum(top[h], jnp.max(three, axis=0, keepdims=True)))
            between()
        return tuple(tops)

    def step_and_logits(i, top):
        stages = newton_stages(hist, i, ident, masks)
        next(stages)
        return logits(i, top, lambda: next(stages, None))

    top = tuple(jnp.full((1, nslot), -1e9, f32) for _ in range(heads_n))
    third = NEWTON // 3
    top = lax.fori_loop(0, third, step_and_logits, top)
    if gather:
        for spread in spreads:
            spread.along_first(1)
    top = lax.fori_loop(third, 2 * third, step_and_logits, top)
    if gather:
        for spread in spreads:
            spread.along_first(3)
    top = lax.fori_loop(2 * third, NEWTON, step_and_logits, top)
    keep(hist, hist_out)
    top = lax.fori_loop(NEWTON, nchunk, logits, top)
    keep(kern1, kern1_out)
    if gather:
        for spread in spreads:
            spread.along_last(1)

    def raise_three(c, total):
        rows = pl.ds(pl.multiple_of(c * CHUNK, CHUNK), CHUNK)
        totals = []
        for h in range(heads_n):
            raised = jnp.exp(l3[h, rows, :] - top[h])
            l3[h, rows, :] = raised
            totals.append(total[h] + jnp.sum(raised, axis=0, keepdims=True))
        return tuple(totals)

    total = lax.fori_loop(
        0, nchunk, raise_three, tuple(jnp.zeros((1, nslot), f32) for _ in range(heads_n))
    )
    norm = [live_row.astype(f32) / total[h] for h in range(heads_n)]
    carriedT[...] = jnp.zeros_like(carriedT)

    def carry_three(c, none):
        rows = pl.ds(pl.multiple_of(c * CHUNK, CHUNK), CHUNK)
        vT = v[pl.ds(pl.multiple_of(c * CHUNK + HALO, HALO), CHUNK), :].astype(f32).T.astype(bf16)
        for h in range(heads_n):
            low = (l3[h, rows, :] * norm[h]).astype(bf16)
            kern3[h, rows, :] = low
            e = slice(HEAD_DIM * h, HEAD_DIM * h + HEAD_DIM)
            carriedT[e, :] += mm(vT[e, :], low)
        return none

    lax.fori_loop(0, nchunk, carry_three, 0)
    keep(kern3, kern3_out)
    if gather:
        for spread in spreads:
            spread.along_first(2)
        for spread in whole:
            spread.along_last(3)
        for spread in spreads:
            spread.to_core(0)
    carried_all = carriedT[...].T
    carried[...] = carried_all
    lane = iota((TILE, wide), 1) // HEAD_DIM
    docs = nslot // LANDMARKS
    prox_all = jnp.zeros((8, LANES), f32)
    for h in range(heads_n):
        for g in range(tiles_n):
            rows = slice(g * TILE, g * TILE + TILE)
            n = h * tiles_n + g
            Z = hist[NEWTON, 1, n]
            part = split(jnp.where(lane == h, carried_all[rows], 0.0))
            mixed[h, rows, :] = mm3(split(unpack(Z)), part).astype(bf16)
            A = Aout[n]
            A2 = jnp.sum(A * A, axis=0, keepdims=True)
            Z2 = jnp.sum(Z * Z, axis=0, keepdims=True)
            first = iota(A2.shape, 1) < LANDMARKS
            for half in range(2):
                mine = first if half == 0 else jnp.logical_not(first)
                a2 = jnp.sum(jnp.where(mine, A2, 0.0), axis=1, keepdims=True)
                z2 = jnp.sum(jnp.where(mine, Z2, 0.0), axis=1, keepdims=True)
                doc = g * 2 + half
                alive = live_row[:, doc * LANDMARKS : doc * LANDMARKS + 1] > 0
                value = jnp.where(alive, jnp.sqrt(a2) * jnp.sqrt(z2) / LANDMARKS, 0.0)
                here_too = (iota(prox_all.shape, 0) == h) & (iota(prox_all.shape, 1) == doc)
                prox_all = jnp.where(here_too, value, prox_all)
    for h in range(heads_n):
        prox[h] = prox_all[h : h + 1, :docs]

    def finish(b, out, out_row):
        for k in range(per_block):
            c = b * per_block + k
            rows = pl.ds(pl.multiple_of(c * CHUNK, CHUNK), CHUNK)
            total = mm(kern1[0, rows, :], mixed[0])
            for h in range(1, heads_n):
                total = total + mm(kern1[h, rows, :], mixed[h])
            for part in range(CHUNK // TILE):
                i = c * (CHUNK // TILE) + part
                now = tokc[pl.ds(pl.multiple_of(i * TILE, TILE), TILE), 0:1]
                near = seg_of(now) == segw[pl.ds(i, 1), :]
                window = v[pl.ds(pl.multiple_of(i * TILE, TILE), 2 * TILE), :]
                conv = jnp.zeros((TILE, wide), f32)
                for h in range(heads_n):
                    term = mm(jnp.where(near, bands[h], 0.0).astype(bf16), window)
                    conv = jnp.where(lane == h, term, conv)
                got = (total[part * TILE : (part + 1) * TILE, :] + conv) * live_of(now).astype(f32)
                at = pl.ds(part * TILE, TILE)
                if k == 0:
                    out[out_row, at, : 2 * LANES] = got.astype(bf16)
                else:
                    far = pltpu.roll(got, width, 1)
                    middle = slice(LANES, 2 * LANES)
                    both = out[out_row, at, middle].astype(f32) + far[:, LANES:]
                    out[out_row, at, middle] = both.astype(bf16)
                    out[out_row, at, 2 * LANES :] = far[:, :LANES].astype(bf16)

    if gather:
        for spread in whole:
            spread.along_last(2)
    sent = []
    for k, to in enumerate((here.diagonal, here.across, here.sibling)):
        finish(to, hsend, k)
        sent.append(start(push(hsend.at[k], heads.at[here.t], hsem, k, here.dp, to)))
    finish(here.t, heads, here.t)
    if gather:
        for spread in spreads:
            spread.to_core(1)
        for spread in whole:
            spread.to_core(3)
            spread.to_core(2)
    for copy in sent:
        copy.wait_recv()
    if gather:
        for spread in spreads:
            spread.finish()
        length = gain.shape[1]
        far = spread_lanes(length, x.shape[1]).astype(bf16)
        owner = iota((32, x.shape[1]), 1) // length == iota((32, x.shape[1]), 0)
        for r in range(4):
            rows = norm_all[...].reshape(32, 8, LANES)[:, r, :].astype(bf16)
            norms[r : r + 1, :] = jnp.sum(jnp.where(owner, mm(rows, far), 0.0), axis=0, keepdims=True)
        norms[4:8, :] = jnp.zeros((4, x.shape[1]), f32)
    for copy in copies:
        copy.wait_send()
    for copy in keeping:
        copy.wait()


VMEM = pl.BlockSpec(memory_space=pltpu.VMEM)
ANY = pl.BlockSpec(memory_space=pl.ANY)


def dma(*shape):
    return pltpu.SemaphoreType.DMA(shape)


def attention_forward(x, w, conv, seg, slot, live, slot_live, extra, heads_n, blocks, taps_total):
    block, feat = x.shape
    seq, nslot = block * blocks, slot_live.shape[1]
    gather = len(extra) > 0
    depth = w.shape[1]
    wide = -(-heads_n * HEAD_DIM // 256) * 256
    tiles_n = heads_n * (nslot // TILE)
    shape = jax.ShapeDtypeStruct
    outs = [
        shape((blocks, block, feat), bf16),
        shape((feat, LANES * heads_n + wide), bf16),
        shape((seq, LANES), i32),
        shape((2 * (seq // TILE), 2 * TILE), i32),
        shape((seq, LANES * heads_n), bf16),
        shape((seq + 2 * HALO, wide), bf16),
        shape((heads_n, seq, nslot), bf16),
        shape((heads_n, seq, nslot), bf16),
        shape((nslot, LANES * heads_n), f32),
        shape((nslot, LANES), f32),
        shape((tiles_n, TILE, TILE), f32),
        shape((heads_n, nslot, wide), bf16),
        shape((nslot, wide), f32),
        shape((blocks, block // 2, 2 * heads_n * HEAD_DIM), bf16),
        shape((heads_n, 1, nslot // LANDMARKS), f32),
        shape((NEWTON + 1, 4, tiles_n, LANDMARKS, TILE), f32),
    ]
    out_specs = [ANY, ANY, VMEM, VMEM] + [ANY] * 4 + [VMEM] * 7 + [ANY]
    scratch = [pltpu.VMEM(outs[n].shape, bf16) for n in (0, 1, 4, 5, 6, 7)]
    scratch += [
        pltpu.VMEM((depth, LANES * heads_n + wide), bf16),
        pltpu.VMEM((heads_n, 2 * nslot, 256), bf16),
        pltpu.VMEM((heads_n, seq, nslot), f32),
        pltpu.VMEM((wide, nslot), f32),
        pltpu.VMEM(outs[15].shape, f32),
        pltpu.VMEM((heads_n, TILE, 2 * TILE), f32),
        pltpu.VMEM((3, block // 2, 2 * heads_n * HEAD_DIM), bf16),
        pltpu.VMEM((8, seq + 2 * TILE), i32),
        pltpu.VMEM((8, 2 * TILE), f32),
        dma(2, 2 * (block // TILE) + 1),
        dma(2, 7),
        dma(2, 3),
        dma(7),
    ]
    if gather:
        hidden_n = extra[0].shape[0]
        outs += [
            shape((4, 2, 2, 2, hidden_n, feat), bf16),
            shape((4, 2, 2, 2, hidden_n, feat), bf16),
            shape((2, 2, feat, wide), bf16),
            shape((8, feat), f32),
        ]
        out_specs += [ANY, ANY, ANY, VMEM]
        scratch += [
            pltpu.VMEM((depth, wide), bf16),
            pltpu.VMEM((8, LANES), f32),
            pltpu.VMEM((4, 2, 2, 2, 8, LANES), f32),
        ]
        for _ in range(4):
            scratch += [dma(2, 19), pltpu.SemaphoreType.DMA]
    return pl.pallas_call(
        functools.partial(forward_body, gather, taps_total),
        out_shape=tuple(outs),
        in_specs=[VMEM] * (7 + len(extra)),
        out_specs=tuple(out_specs),
        scratch_shapes=scratch,
        compiler_params=pltpu.CompilerParams(
            vmem_limit_bytes=LIMIT, collective_id=1 if gather else 2, has_side_effects=True
        ),
        name="attention_forward",
    )(x, w, conv, seg, slot, live, slot_live, *extra)


def normalized(u):
    mean = jnp.mean(u, axis=-1, keepdims=True)
    centered = u - mean
    scale = lax.rsqrt(jnp.mean(centered * centered, axis=-1, keepdims=True) + norm_epsilon)
    return centered * scale, scale


def normalized_back(g, n, scale):
    return scale * (
        g - jnp.mean(g, axis=-1, keepdims=True) - n * jnp.mean(g * n, axis=-1, keepdims=True)
    )


ROWS = 512
FF_CHUNK = 512


def mm_tn(a, b):
    return lax.dot_general(a, b, (((0,), (0,)), ((), ())), preferred_element_type=f32)


def feed_body(
    direct, x, cot, folded, norms, wout, up_in, down_in,
    layer_out, gsend, gpre, gnorm, gout, gup, gdown,
    heads, up, down, act, slope, hidden, hlow, n1, r1, gsum, glow, acc, up_out, down_out, sems,
):
    block, feat = x.shape
    chunks = act.shape[0]
    loads = []
    for j in range(chunks):
        rows = pl.ds(j * FF_CHUNK, FF_CHUNK)
        loads.append(
            (
                pltpu.make_async_copy(up_in.at[rows], up.at[j], sems.at[0, j]),
                pltpu.make_async_copy(down_in.at[rows], down.at[j], sems.at[1, j]),
            )
        )
        for load in loads[-1]:
            load.start()
    gain0, gain1 = norms[0:1, :], norms[1:2, :]
    bias0, bias1 = norms[2:3, :], norms[3:4, :]
    width = folded.shape[2] // 2
    for t in range(folded.shape[0]):
        for k in range(2):
            heads[t, k * (block // 2) : (k + 1) * (block // 2), :] = unfold(folded[t], k, width).astype(bf16)
    acc[...] = sum(mm_nt(heads[t], wout[t]) for t in range(heads.shape[0]))

    def first_norm(i, none):
        rows = pl.ds(pl.multiple_of(i * ROWS, ROWS), ROWS)
        n, scale = normalized(x[rows, :].astype(f32) + acc[rows, :])
        now = n * gain0 + bias0
        n1[rows, :] = n
        r1[rows, :] = jnp.broadcast_to(scale, (ROWS, LANES))
        hidden[rows, :] = now
        hlow[rows, :] = now.astype(bf16)
        return none

    lax.fori_loop(0, block // ROWS, first_norm, 0)
    acc[...] = hidden[...]
    for j in range(chunks):
        for load in loads[j]:
            load.wait()

    def rise(j, none):
        u = mm_nt(hlow[...], up[j])
        cdf = 0.5 * (1.0 + lax.erf(u * math.sqrt(0.5)))
        act[j] = (u * cdf).astype(bf16)
        slope[j] = cdf + u * (jnp.exp(-0.5 * u * u) * (1.0 / math.sqrt(2.0 * math.pi)))
        acc[...] += mm(act[j], down[j])
        return none

    lax.fori_loop(0, chunks, rise, 0)

    def second_norm(i, sums):
        rows = pl.ds(pl.multiple_of(i * ROWS, ROWS), ROWS)
        n, scale = normalized(acc[rows, :])
        layer_out[rows, :] = (n * gain1 + bias1).astype(bf16)
        c = cot[rows, :].astype(f32)
        g = normalized_back(c * gain1, n, scale)
        gsum[rows, :] = g
        glow[rows, :] = g.astype(bf16)
        return (
            sums[0] + jnp.sum(c * n, axis=0, keepdims=True),
            sums[1] + jnp.sum(c, axis=0, keepdims=True),
        )

    zero = jnp.zeros((1, feat), f32)
    gain_two, bias_two = lax.fori_loop(0, block // ROWS, second_norm, (zero, zero))
    acc[...] = gsum[...]

    def fall(j, none):
        rows = pl.ds(pl.multiple_of(j * FF_CHUNK, FF_CHUNK), FF_CHUNK)
        g_act = mm_nt(glow[...], down[j])
        g_up = (g_act * slope[j]).astype(bf16)
        down_out[j] = mm_tn(act[j], glow[...]).astype(bf16)
        pltpu.make_async_copy(down_out.at[j], gdown.at[rows], sems.at[2, j]).start()
        up_out[j] = mm_tn(g_up, hlow[...]).astype(bf16)
        pltpu.make_async_copy(up_out.at[j], gup.at[rows], sems.at[3, j]).start()
        acc[...] += mm(g_up, up[j])
        return none

    lax.fori_loop(0, chunks, fall, 0)

    def first_back(i, sums):
        rows = pl.ds(pl.multiple_of(i * ROWS, ROWS), ROWS)
        g = acc[rows, :]
        n = n1[rows, :]
        back = normalized_back(g * gain0, n, r1[rows, 0:1])
        gpre[rows, :] = back
        glow[rows, :] = back.astype(bf16)
        return (
            sums[0] + jnp.sum(g * n, axis=0, keepdims=True),
            sums[1] + jnp.sum(g, axis=0, keepdims=True),
        )

    gain_one, bias_one = lax.fori_loop(0, block // ROWS, first_back, (zero, zero))
    gnorm[...] = jnp.concatenate(
        [gain_one, gain_two, bias_one, bias_two, jnp.zeros((4, feat), f32)], axis=0
    )
    for t in range(heads.shape[0]):
        gsend[t] = fold(mm(glow[...], wout[t]), width).astype(bf16)
        grad = mm_tn(glow[...], heads[t]).astype(bf16)
        if direct:
            gout[:, :, t // 2, t % 2] = grad.reshape((4, 2) + gout.shape[4:])
        else:
            gout[t] = grad

    def land(j, none):
        rows = pl.ds(pl.multiple_of(j * FF_CHUNK, FF_CHUNK), FF_CHUNK)
        pltpu.make_async_copy(down_out.at[j], gdown.at[rows], sems.at[2, j]).wait()
        pltpu.make_async_copy(up_out.at[j], gup.at[rows], sems.at[3, j]).wait()
        return none

    lax.fori_loop(0, chunks, land, 0)


RISE = (0, 3, 1, 2)
FALL = (2, 1, 3, 0)


def feed_direct_body(
    x, cot, folded, norms, wout, up_in, down_in,
    layer_to, gsend, gpre_to, gnorm, gout, sum_up, sum_down, part_up, part_down,
    layer_out, gpre,
    heads, up, down, act, slope, hidden, hlow, n1, r1, gsum, glow, acc,
    gu, gd, cu, cd, yu, xd, lsem, csem, ysem, upsem, downsem, osem,
):
    here = Place()
    block, feat = x.shape
    units = act.shape[2]
    copies, kept = [], []

    def keep(src, dst):
        copy = pltpu.make_async_copy(src, dst, osem.at[len(kept)])
        copy.start()
        kept.append(copy)

    def start(copy):
        copy.start()
        copies.append(copy)
        return copy

    loads = {}
    for k in RISE:
        z, late = (here.z + k) % 4, 4 - k in LATE
        near_up = (z, here.y, slice(None), here.c) if late else (z,)
        near_down = (z, slice(None), here.x, here.c) if late else (z,)
        loads[k] = [
            pltpu.make_async_copy(up_in.at[near_up], up.at[near_up], lsem.at[0, k]),
            pltpu.make_async_copy(down_in.at[near_down], down.at[near_down], lsem.at[1, k]),
        ]
        for load in loads[k]:
            load.start()
    greet(
        [(here.dp, here.sibling), (here.dp, here.across), (here.dp_at(0, 1), here.t)]
    )
    arriving = {}

    def send_late(dz):
        n, z = LATE.index(dz), (here.z + 4 - dz) % 4
        near_up, near_down = (z, here.y, slice(None), here.c), (z, slice(None), here.x, here.c)
        arriving[dz] = [
            start(push(up_in.at[near_up], up.at[near_up], upsem, n, here.dp_at(0, 1), here.t)),
            start(push(down_in.at[near_down], down.at[near_down], downsem, n, here.dp, here.across)),
            start(push(up_in.at[near_up], up.at[near_up], upsem, 2 + n, here.dp, here.sibling)),
            start(push(down_in.at[near_down], down.at[near_down], downsem, 2 + n, here.dp, here.sibling)),
        ]

    send_late(LATE[0])

    def pass_on(dz):
        n, z = LATE.index(dz), (here.z + 4 - dz) % 4
        for copy in arriving[dz][:2]:
            copy.wait_recv()
        far_up, far_down = (z, 1 - here.y, slice(None), here.c), (z, slice(None), 1 - here.x, here.c)
        arriving[dz] = arriving[dz][2:] + [
            start(push(up.at[far_up], up.at[far_up], upsem, 4 + n, here.dp, here.sibling)),
            start(push(down.at[far_down], down.at[far_down], downsem, 4 + n, here.dp, here.sibling)),
        ]

    gain0, gain1 = norms[0:1, :], norms[1:2, :]
    bias0, bias1 = norms[2:3, :], norms[3:4, :]
    width = folded.shape[2] // 2
    for t in range(folded.shape[0]):
        for k in range(2):
            heads[t, k * (block // 2) : (k + 1) * (block // 2), :] = unfold(folded[t], k, width).astype(bf16)
    acc[...] = sum(mm_nt(heads[t], wout[t]) for t in range(heads.shape[0]))

    def first_norm(i, none):
        rows = pl.ds(pl.multiple_of(i * ROWS, ROWS), ROWS)
        n, scale = normalized(x[rows, :].astype(f32) + acc[rows, :])
        now = n * gain0 + bias0
        n1[rows, :] = n
        r1[rows, :] = jnp.broadcast_to(scale, (ROWS, LANES))
        hidden[rows, :] = now
        hlow[rows, :] = now.astype(bf16)
        return none

    lax.fori_loop(0, block // ROWS, first_norm, 0)
    acc[...] = hidden[...]
    flat = (4, units, feat)
    up_of, down_of = up.reshape(flat), down.reshape(flat)
    for k in RISE:
        z = (here.z + k) % 4
        for load in loads[k]:
            load.wait()
        if 4 - k in LATE:
            for copy in arriving[4 - k]:
                copy.wait_recv()
        u = mm_nt(hlow[...], up_of[z])
        cdf = 0.5 * (1.0 + lax.erf(u * math.sqrt(0.5)))
        act[k] = (u * cdf).astype(bf16)
        slope[k] = cdf + u * (jnp.exp(-0.5 * u * u) * (1.0 / math.sqrt(2.0 * math.pi)))
        acc[...] += mm(act[k], down_of[z])
        if k == RISE[0]:
            send_late(LATE[1])
        if k == RISE[1]:
            pass_on(LATE[0])
        if k == RISE[2]:
            pass_on(LATE[1])

    def second_norm(i, sums):
        rows = pl.ds(pl.multiple_of(i * ROWS, ROWS), ROWS)
        n, scale = normalized(acc[rows, :])
        layer_out[rows, :] = (n * gain1 + bias1).astype(bf16)
        c = cot[rows, :].astype(f32)
        g = normalized_back(c * gain1, n, scale)
        gsum[rows, :] = g
        glow[rows, :] = g.astype(bf16)
        return (
            sums[0] + jnp.sum(c * n, axis=0, keepdims=True),
            sums[1] + jnp.sum(c, axis=0, keepdims=True),
        )

    zero = jnp.zeros((1, feat), f32)
    gain_two, bias_two = lax.fori_loop(0, block // ROWS, second_norm, (zero, zero))
    keep(layer_out, layer_to)
    acc[...] = gsum[...]
    core, later = {}, {}

    def after_core(k):
        for copy in core[k]:
            copy.wait_recv()
        cu[k] = cu[k] + gu[k, :, :, here.c]
        cd[k] = cd[k] + gd[k, :, :, here.c]
        if k in FALL[:2]:
            n = FALL.index(k)
            later[k] = (
                start(push(cu.at[k, 1 - here.y], yu.at[n], ysem, n, here.dp_at(0, 1), here.t)),
                start(push(cd.at[k, :, 1 - here.x], xd.at[n], ysem, 2 + n, here.dp, here.across)),
            )
        else:
            n = FALL.index(k) - 2
            keep(cu.at[k], part_up.at[n])
            keep(cd.at[k], part_down.at[n])

    for n, k in enumerate(FALL):
        z = (here.z + k) % 4
        g_act = mm_nt(glow[...], down_of[z])
        g_up = (g_act * slope[k]).astype(bf16)
        gd[k] = mm_tn(act[k], glow[...]).astype(bf16).reshape(gd.shape[1:])
        gu[k] = mm_tn(g_up, hlow[...]).astype(bf16).reshape(gu.shape[1:])
        core[k] = (
            start(push(gd.at[k, :, :, 1 - here.c], cd.at[k], csem, k, here.dp, here.sibling)),
            start(push(gu.at[k, :, :, 1 - here.c], cu.at[k], csem, 4 + k, here.dp, here.sibling)),
        )
        acc[...] += mm(g_up, up_of[z])
        if n > 0:
            after_core(FALL[n - 1])

    def first_back(i, sums):
        rows = pl.ds(pl.multiple_of(i * ROWS, ROWS), ROWS)
        g = acc[rows, :]
        n = n1[rows, :]
        back = normalized_back(g * gain0, n, r1[rows, 0:1])
        gpre[rows, :] = back
        glow[rows, :] = back.astype(bf16)
        return (
            sums[0] + jnp.sum(g * n, axis=0, keepdims=True),
            sums[1] + jnp.sum(g, axis=0, keepdims=True),
        )

    gain_one, bias_one = lax.fori_loop(0, block // ROWS, first_back, (zero, zero))
    keep(gpre, gpre_to)
    gnorm[...] = jnp.concatenate(
        [gain_one, gain_two, bias_one, bias_two, jnp.zeros((4, feat), f32)], axis=0
    )
    after_core(FALL[3])
    for t in range(heads.shape[0]):
        gsend[t] = fold(mm(glow[...], wout[t]), width).astype(bf16)
        grad = mm_tn(glow[...], heads[t]).astype(bf16)
        gout[:, :, t // 2, t % 2] = grad.reshape((4, 2) + gout.shape[4:])
    for n, k in enumerate(FALL[:2]):
        for copy in later[k]:
            copy.wait_recv()
        yu[n] = cu[k, here.y] + yu[n]
        keep(yu.at[n], sum_up.at[n])
        xd[n] = cd[k, :, here.x] + xd[n]
        keep(xd.at[n], sum_down.at[n])
    for copy in copies:
        copy.wait_send()
    for copy in kept:
        copy.wait()


def feed_direct(x, cot, heads, norms, wout, up_in, down_in, depth):
    block, feat = x.shape
    blocks, wide = heads.shape[0], wout.shape[2]
    owners = up_in.shape
    hidden_n = owners[4]
    units = 8 * hidden_n
    shape = jax.ShapeDtypeStruct
    outs = (
        shape((block, feat), bf16),
        shape(heads.shape, bf16),
        shape((block, feat), f32),
        shape((8, feat), f32),
        shape((4, 2, 2, 2, depth, wide), bf16),
        shape((2, 2, hidden_n, feat), bf16),
        shape((2, 2, hidden_n, feat), bf16),
        shape((2, 2, 2, hidden_n, feat), bf16),
        shape((2, 2, 2, hidden_n, feat), bf16),
    )
    scratch = [
        pltpu.VMEM((block, feat), bf16),
        pltpu.VMEM((block, feat), f32),
        pltpu.VMEM((blocks, block, wide), bf16),
        pltpu.VMEM(owners, bf16),
        pltpu.VMEM(owners, bf16),
        pltpu.VMEM((4, block, units), bf16),
        pltpu.VMEM((4, block, units), f32),
        pltpu.VMEM((block, feat), f32),
        pltpu.VMEM((block, feat), bf16),
        pltpu.VMEM((block, feat), f32),
        pltpu.VMEM((block, LANES), f32),
        pltpu.VMEM((block, feat), f32),
        pltpu.VMEM((block, feat), bf16),
        pltpu.VMEM((block, feat), f32),
        pltpu.VMEM(owners, bf16),
        pltpu.VMEM(owners, bf16),
        pltpu.VMEM((4, 2, 2, hidden_n, feat), bf16),
        pltpu.VMEM((4, 2, 2, hidden_n, feat), bf16),
        pltpu.VMEM((2, 2, hidden_n, feat), bf16),
        pltpu.VMEM((2, 2, hidden_n, feat), bf16),
        dma(2, 4),
        dma(2, 8),
        dma(2, 4),
        dma(2, 6),
        dma(2, 6),
        dma(10),
    ]
    return pl.pallas_call(
        feed_direct_body,
        out_shape=outs,
        in_specs=[VMEM] * 5 + [ANY, ANY],
        out_specs=(ANY, VMEM, ANY, VMEM, VMEM) + (ANY,) * 4,
        scratch_shapes=scratch,
        compiler_params=pltpu.CompilerParams(
            vmem_limit_bytes=LIMIT, collective_id=5, has_side_effects=True
        ),
        name="feed_forward",
    )(x, cot, heads, norms, wout, up_in, down_in)


def feed_forward(direct, x, cot, heads, norms, wout, up_in, down_in, depth):
    block, feat = x.shape
    blocks, wide = heads.shape[0], wout.shape[2]
    hidden_n = up_in.shape[0]
    chunks = hidden_n // FF_CHUNK
    shape = jax.ShapeDtypeStruct
    outs = (
        shape((block, feat), bf16),
        shape(heads.shape, bf16),
        shape((block, feat), f32),
        shape((8, feat), f32),
        shape((4, 2, 2, 2, depth, wide) if direct else (blocks, feat, wide), bf16),
        shape((hidden_n, feat), bf16),
        shape((hidden_n, feat), bf16),
    )
    scratch = [
        pltpu.VMEM((blocks, block, wide), bf16),
        pltpu.VMEM((chunks, FF_CHUNK, feat), bf16),
        pltpu.VMEM((chunks, FF_CHUNK, feat), bf16),
        pltpu.VMEM((chunks, block, FF_CHUNK), bf16),
        pltpu.VMEM((chunks, block, FF_CHUNK), f32),
        pltpu.VMEM((block, feat), f32),
        pltpu.VMEM((block, feat), bf16),
        pltpu.VMEM((block, feat), f32),
        pltpu.VMEM((block, LANES), f32),
        pltpu.VMEM((block, feat), f32),
        pltpu.VMEM((block, feat), bf16),
        pltpu.VMEM((block, feat), f32),
        pltpu.VMEM((chunks, FF_CHUNK, feat), bf16),
        pltpu.VMEM((chunks, FF_CHUNK, feat), bf16),
        dma(4, chunks),
    ]
    return pl.pallas_call(
        functools.partial(feed_body, direct),
        out_shape=outs,
        in_specs=[VMEM] * 5 + [ANY, ANY],
        out_specs=tuple([VMEM] * 5 + [ANY, ANY]),
        scratch_shapes=scratch,
        compiler_params=pltpu.CompilerParams(vmem_limit_bytes=LIMIT),
        name="feed_forward",
    )(x, cot, heads, norms, wout, up_in, down_in)


class Summer:
    def __init__(self, here, source, first, count, own, from_core, from_y, from_z, from_x, sems, local):
        self.here, self.source, self.rows = here, source, pl.ds(first, count)
        self.own, self.from_core, self.from_y, self.from_z, self.from_x = (
            own, from_core, from_y, from_z, from_x,
        )
        self.sems, self.local = sems, local
        self.copies = []

    def push(self, src, dst, index, dp, t):
        copy = push(src, dst, self.sems, index, dp, t)
        copy.start()
        self.copies.append(copy)
        return copy

    def begin(self):
        here = self.here
        self.loaded = pltpu.make_async_copy(
            self.source.at[:, :, :, here.c, self.rows], self.own, self.local
        )
        self.loaded.start()
        self.core = self.push(
            self.source.at[:, :, :, 1 - here.c, self.rows], self.from_core, 0, here.dp, here.sibling
        )

    def along_y(self):
        here = self.here
        self.loaded.wait()
        self.core.wait_recv()

        def one(n, none):
            z, x = n // 2, n % 2
            y = 1 - here.y
            self.from_core[z, y, x] = self.from_core[z, y, x] + self.own[z, y, x]
            return none

        lax.fori_loop(0, 8, one, 0)
        self.y = self.push(
            self.from_core.at[:, 1 - here.y], self.from_y, 1, here.dp_at(0, 1), here.t
        )

    def along_z(self):
        here = self.here
        self.y.wait_recv()

        def one(n, none):
            z, x = n // 2, n % 2
            total = self.from_core[z, here.y, x].astype(f32) + self.own[z, here.y, x].astype(f32)
            total = total + self.from_y[z, x].astype(f32)
            self.from_y[z, x] = total.astype(self.own.dtype)
            return none

        lax.fori_loop(0, 8, one, 0)
        self.z = [
            self.push(
                self.from_y.at[(here.z + dz) % 4], self.from_z.at[dz - 1], 1 + dz, here.dp_at(dz, 0), here.t
            )
            for dz in (1, 2, 3)
        ]

    def along_x(self):
        here = self.here
        for copy in self.z:
            copy.wait_recv()
        for x in range(2):
            total = self.from_y[here.z, x].astype(f32)
            for n in range(3):
                total = total + self.from_z[n, x].astype(f32)
            self.from_y[here.z, x] = total.astype(self.own.dtype)
        self.x = self.push(
            self.from_y.at[here.z, 1 - here.x], self.from_x, 5, here.dp, here.across
        )

    def finish(self, out):
        self.x.wait_recv()
        here = self.here
        out[self.rows, :] = self.from_y[here.z, here.x].astype(f32) + self.from_x[...].astype(f32)
        for copy in self.copies:
            copy.wait_send()


class UpSum:
    def __init__(self, here, sums, parts, parts_far, from_y, from_z, from_x, sems, sums_far=None):
        self.here, self.sums, self.parts = here, sums, parts
        self.parts_far, self.sums_far = parts_far, sums_far
        self.from_y, self.from_z, self.from_x, self.sems = from_y, from_z, from_x, sems
        self.copies = []

    def push(self, src, dst, index, dp, t):
        copy = push(src, dst, self.sems, index, dp, t)
        copy.start()
        self.copies.append(copy)
        return copy

    def along_z(self, src, k):
        here = self.here
        return self.push(src, self.from_z.at[k - 1], k - 1, here.dp_at(k, 0), here.t)

    def begin(self):
        here = self.here
        self.y = [
            self.push(self.parts_far.at[n, 1 - here.y], self.from_y.at[n], 3 + n, here.dp_at(0, 1), here.t)
            for n in range(2)
        ]
        self.z = [self.along_z(self.sums.at[n], FALL[n]) for n in range(2)]

    def second(self):
        for n in range(2):
            self.y[n].wait_recv()
            self.from_y[n] = self.from_y[n] + self.parts[n, self.here.y]
        self.z.append(self.along_z(self.from_y.at[0], FALL[2]))

    def third(self):
        here = self.here
        for copy in self.z:
            copy.wait_recv()
        total = self.from_y[1].astype(f32)
        for n in range(3):
            total = total + self.from_z[n].astype(f32)
        self.from_y[1] = total.astype(bf16)
        self.x = self.push(self.from_y.at[1, 1 - here.x], self.from_x, 5, here.dp, here.across)

    def finish(self, out):
        self.x.wait_recv()
        out[...] = self.from_y[1, self.here.x].astype(f32) + self.from_x[...].astype(f32)
        for copy in self.copies:
            copy.wait_send()


class DownSum(UpSum):
    def begin(self):
        here = self.here
        self.x = [
            self.push(self.parts_far.at[n, :, 1 - here.x], self.from_x.at[n], 3 + n, here.dp, here.across)
            for n in range(2)
        ]
        self.y = [self.along_y(self.sums_far.at[n, 1 - here.y], n) for n in range(2)]

    def along_y(self, src, n):
        here = self.here
        return self.push(src, self.from_y.at[n], 5 + n, here.dp_at(0, 1), here.t)

    def second(self):
        self.z = []
        for n in range(2):
            self.y[n].wait_recv()
            self.from_y[n] = self.from_y[n] + self.sums[n, self.here.y]
            self.z.append(self.along_z(self.from_y.at[n], FALL[n]))

    def third(self):
        here = self.here
        for n in range(2):
            self.x[n].wait_recv()
            self.from_x[n] = self.from_x[n] + self.parts[n, :, here.x]
            self.y.append(self.along_y(self.from_x.at[n, 1 - here.y], 2 + n))

    def fourth(self):
        for n in range(2):
            self.y[2 + n].wait_recv()
            self.from_y[2 + n] = self.from_y[2 + n] + self.from_x[n, self.here.y]
        self.z.append(self.along_z(self.from_y.at[2], FALL[2]))

    def finish(self, out):
        for copy in self.z:
            copy.wait_recv()
        total = self.from_y[3].astype(f32)
        for n in range(3):
            total = total + self.from_z[n].astype(f32)
        out[...] = total
        for copy in self.copies:
            copy.wait_send()


SUMMER_SEMS = 6


def backward_body(gather, taps_total, *refs):
    (
        gsend, xall_in, wfull_in, tokc_in, segw, qk_in, v_in, kern1_in, kern3_in,
        land, counts, Ain, mixed, carried, conv, slot_live, gpre_in, hist_in,
    ) = refs[:18]
    refs = refs[18:]
    if gather:
        (sum_up, sum_down_in, part_up_in, part_down_in, out_in, norm_in), refs = refs[:6], refs[6:]
    (input_grad, gw, gconv), refs = refs[:3], refs[3:]
    if gather:
        (up_out, down_out, out_out, gain_out, bias_out), refs = refs[:5], refs[5:]
    (
        go_in, wfull, tokc, qk, v, gpre, taps, gl1, gl3, xall, xT, gopad, gqk, gv, gband, bands, gmixedT, glandT, hist, gstate, gcar, wback,
        part_out, part_in, part_sum, part_x, piece_v, piece_q, in_v, in_q, in_conv, conv_out,
        land_sum, x_land, g_high, g_low, land_own, land_out, land_in, land_all,
        gsem, lsem, psem, csem,
    ) = refs[:44]
    refs = refs[44:]

    here = Place()
    blocks, block, wide = gsend.shape[0], 2 * gsend.shape[1], gcar.shape[2]
    seq = blocks * block
    heads_n = gl1.shape[0]
    width = heads_n * HEAD_DIM
    nslot = land.shape[0]
    nchunk = seq // CHUNK
    per_block = block // CHUNK
    tiles_n = nslot // TILE
    all_tiles = heads_n * tiles_n
    feat = wfull.shape[0]
    doc_row = iota((1, nslot), 1) // LANDMARKS
    live_row = slot_live[...]
    live_cols = [column(live_row[:, g * TILE : (g + 1) * TILE].astype(f32)) for g in range(tiles_n)]
    scaling = 1.0 / math.sqrt(HEAD_DIM)
    same = tile_same()
    masks = lane_masks()

    pairs = [
        (tokc_in, tokc), (xall_in, xall), (kern1_in, gl1), (hist_in, hist), (kern3_in, gl3), (qk_in, qk),
        (v_in, v), (wfull_in, wfull), (gpre_in, gpre),
    ]
    if gather:
        sum_down, part_up, part_down = refs[:3]
        refs = refs[3:]
        pairs += [(sum_down_in, sum_down), (part_up_in, part_up), (part_down_in, part_down)]
    loads = [pltpu.make_async_copy(src, dst, lsem.at[n]) for n, (src, dst) in enumerate(pairs)]
    for load in loads:
        load.start()

    peers = here.tensor_peers()
    if gather:
        peers = peers + [
            (here.dp_at(dz, dy), here.t) for dz in range(4) for dy in range(2) if dz or dy
        ]
    greet(peers)
    copies = []

    def start(copy):
        copy.start()
        copies.append(copy)
        return copy

    gopad[0:HALO, :] = jnp.zeros((HALO, wide), bf16)
    gopad[seq + HALO : seq + 2 * HALO, :] = jnp.zeros((HALO, wide), bf16)
    arriving = [
        start(push(gsend.at[to], go_in.at[here.t], gsem, k, here.dp, to))
        for k, to in enumerate((here.across, here.diagonal, here.sibling))
    ]
    go_in[here.t] = gsend[here.t]

    if gather:
        out_sum, norm_sum, norm_pieces, q_sems, v_sems, in_vz, in_qz = refs[:7]
        refs = refs[7:]
        ups = UpSum(here, sum_up, part_up, part_up_in, *refs[:4])
        downs = DownSum(here, sum_down, part_down, part_down_in, *refs[4:8], sum_down_in)
        refs = refs[8:]
        ups.begin()
        downs.begin()
        length = gain_out.shape[1]
        far = spread_lanes(length, feat).astype(bf16)
        owner = iota((32, feat), 1) // length == iota((32, feat), 0)
        for r in range(4):
            high, low = split(jnp.where(owner, norm_in[r : r + 1, :], 0.0))
            norm_pieces[:, r, :] = mm_nt(high, far) + mm_nt(low, far)
        for r in range(4, 8):
            norm_pieces[:, r, :] = jnp.zeros((32, LANES), f32)
        norm_view = norm_pieces.reshape(4, 2, 2, 2, 8, LANES)
        smalls = []
        for source, count in ((out_in, out_in.shape[4]), (norm_view, 8)):
            buffers, refs = refs[:7], refs[7:]
            smalls.append(Summer(here, source, 0, count, *buffers))
        for summer in smalls:
            summer.begin()

    taps[...] = jnp.zeros_like(taps)
    taps[:heads_n, :taps_total] = conv[...]
    moved = pltpu.roll(taps[...], HALO - taps_total // 2, 1)
    far_rows = (iota((TILE, TILE), 0) + iota((TILE, TILE), 1) == TILE - 1).astype(f32).astype(bf16)
    turn_cols = iota((2 * TILE, 2 * TILE), 0) + iota((2 * TILE, 2 * TILE), 1) == 2 * TILE - 1
    turn_cols = turn_cols.astype(f32).astype(bf16)
    for h in range(heads_n):
        bands[h] = band_from(moved[h : h + 1, :])
        bands[heads_n + h] = mm(mm(far_rows, bands[h].astype(bf16)).astype(bf16), turn_cols)
    gmixedT[...] = jnp.zeros_like(gmixedT)
    glandT[...] = jnp.zeros_like(glandT)
    gband[...] = jnp.zeros_like(gband)
    loads[0].wait()
    loads[1].wait()

    def turn(b, none):
        for i in range(block // TILE):
            rows = slice(i * TILE, i * TILE + TILE)
            col = pl.ds(pl.multiple_of(b * block + i * TILE, TILE), TILE)
            xT[:, col] = xall[b, rows, :].astype(f32).T.astype(bf16)
            slot_now = slot_of(tokc[col, 0:1])
            hot = (slot_now == iota((TILE, nslot), 1)).astype(f32).astype(bf16)
            x_land[...] += mm(xT[:, col], hot)
        return none

    x_land[...] = jnp.zeros_like(x_land)
    lax.fori_loop(0, blocks, turn, 0)
    for h in range(heads_n):
        k0, q1, _ = landmark_parts(land[:, LANES * h : LANES * h + LANES])
        wback[h, :nslot, :] = jnp.concatenate(split(k0 * scaling), axis=1)
        wback[h, nslot:, :] = jnp.concatenate(split(q1 * scaling), axis=1)
    if gather:
        for summer in smalls:
            summer.along_y()
    for copy in arriving:
        copy.wait_recv()
    for load in loads[2:]:
        load.wait()

    def one(b, k):
        c = b * per_block + k
        rows = pl.ds(pl.multiple_of(c * CHUNK, CHUNK), CHUNK)
        inner = pl.ds(pl.multiple_of(c * CHUNK + HALO, HALO), CHUNK)
        alive = (live_of(tokc[rows, 0:1]) > 0) & (iota((CHUNK, wide), 1) < width)
        g_now = jnp.where(alive, unfold(go_in[b], k, width).astype(f32), 0.0).astype(bf16)
        gopad[inner, :] = g_now
        gT = g_now.astype(f32).T.astype(bf16)
        for h in range(heads_n):
            k1 = gl1[h, rows, :]
            gk = mm_nt(g_now, mixed[h])
            k1w = k1.astype(f32)
            gl1[h, rows, :] = (k1w * (gk - jnp.sum(gk * k1w, axis=1, keepdims=True))).astype(bf16)
            e = slice(HEAD_DIM * h, HEAD_DIM * h + HEAD_DIM)
            gmixedT[e, :] += mm(gT[e, :], k1)

    def one_block(b, none):
        for k in range(per_block):
            one(b, k)
        return none

    lax.fori_loop(0, blocks, one_block, 0)
    if gather:
        downs.second()
        ups.second()
    gmixed = gmixedT[...].T
    carried_all = carried[...]
    lane = iota((TILE, wide), 1) // HEAD_DIM
    delta = []
    for h in range(heads_n):
        rows_delta = []
        for g in range(tiles_n):
            n = h * tiles_n + g
            rows = slice(g * TILE, g * TILE + TILE)
            Z = unpack(hist[NEWTON, 1, n])
            gm = split(jnp.where(lane == h, gmixed[rows], 0.0))
            near = jnp.where(lane == h, carried_all[rows], 0.0)
            gstate[0, n] = jnp.zeros((LANDMARKS, TILE), f32)
            gstate[1, n] = pack(jnp.where(same, mm3(gm, split(near), mm_nt), 0.0))
            gc = mm3(split(Z.T), gm).astype(bf16)
            gcar[h, rows, :] = gc
            rows_delta.append(jnp.sum((gc.astype(f32) * near).T, axis=0, keepdims=True))
        delta.append(jnp.concatenate(rows_delta, axis=1))
    def three(c, emit, between=lambda: None):
        rows = pl.ds(pl.multiple_of(c * CHUNK, CHUNK), CHUNK)
        v_now = v[pl.ds(pl.multiple_of(c * CHUNK + HALO, HALO), CHUNK), :]
        total = jnp.zeros((CHUNK, wide), f32)
        for h in range(heads_n):
            gc = gcar[h]
            k3 = gl3[h, rows, :]
            gk = mm_nt(v_now, gc)
            gl = (k3.astype(f32) * (gk - delta[h])).astype(bf16)
            gl3[h, rows, :] = gl
            total = total + mm(k3, gc)
            partT = qk[rows, LANES * h : LANES * h + LANES].astype(f32).T.astype(bf16)
            glandT[h, :HEAD_DIM, :] += mm(partT[:HEAD_DIM, :], gl1[h, rows, :])
            glandT[h, HEAD_DIM:, :] += mm(partT[HEAD_DIM:, :], gl)
            between()
        for part in range(CHUNK // TILE):
            i = c * (CHUNK // TILE) + part
            at = pl.ds(pl.multiple_of(i * TILE, TILE), TILE)
            now = tokc[at, 0:1]
            seg_now = seg_of(now)
            near = seg_now == segw[pl.ds(i, 1), :]
            near_back = (seg_now == segw[pl.ds(seq // TILE + i, 1), :]) & (live_of(now) > 0)
            g_window = gopad[pl.ds(pl.multiple_of(i * TILE, TILE), 2 * TILE), :]
            v_window = v[pl.ds(pl.multiple_of(i * TILE, TILE), 2 * TILE), :]
            g_tile = gopad[pl.ds(pl.multiple_of(i * TILE + HALO, HALO), TILE), :].astype(f32)
            conv = jnp.zeros((TILE, wide), f32)
            for h in range(heads_n):
                back = mm(jnp.where(near_back, bands[heads_n + h], 0.0).astype(bf16), g_window)
                conv = jnp.where(lane == h, back, conv)
                mine = jnp.where(lane == h, g_tile, 0.0).astype(bf16)
                gband[h] += jnp.where(near, mm_nt(mine, v_window), 0.0)
            gv[at, :] = (total[part * TILE : (part + 1) * TILE, :] + conv).astype(bf16)
        for h in range(heads_n):
            both = mm(gl1[h, rows, :], wback[h, :nslot, :]) + mm(gl3[h, rows, :], wback[h, nslot:, :])
            gqk[rows, LANES * h : LANES * h + LANES] = (both[:, :LANES] + both[:, LANES:]).astype(bf16)
        emit(
            mm_nt(gqk[rows, :], wfull[:, : LANES * heads_n])
            + mm_nt(gv[rows, :], wfull[:, LANES * heads_n :])
        )

    def dyn_rows(k):
        return pl.ds(pl.multiple_of(k * CHUNK, CHUNK), CHUNK)

    def chunk_rows(k):
        return pl.ds(k * CHUNK, CHUNK)

    def landmark_stages():
        tiles = range(all_tiles)
        A = [Ain[n] for n in tiles]
        starts = [newton_start(a) for a in A]
        gW = [unpack(gstate[1, n]).T for n in tiles]
        gP = [unpack(gstate[0, n]) for n in tiles]
        GA = [tt(left_of(gP[n] + gP[n].T), right_of(A[n])) for n in tiles]
        yield
        gl2 = []
        for n in tiles:
            factor, colsum, tops = starts[n]
            gf_cols = jnp.sum((0.5 * GA[n] + gW[n]) * A[n], axis=0, keepdims=True)
            first = iota(colsum.shape, 1) < LANDMARKS
            gcol = jnp.zeros_like(colsum)
            for k in range(2):
                mine = first if k == 0 else jnp.logical_not(first)
                gf = jnp.sum(jnp.where(mine, gf_cols, 0.0), axis=1, keepdims=True)
                top = tops[k]
                is_top = mine & (colsum == top)
                ties = jnp.sum(is_top.astype(f32), axis=1, keepdims=True)
                share = jnp.where(top > 1.0, 1.0, jnp.where(top == 1.0, 0.5, 0.0))
                floor = jnp.maximum(top, 1.0)
                gcol = jnp.where(is_top, -gf * share / (floor * floor * ties), gcol)
            gA = (factor * (GA[n] + gW[n]) + gcol) * live_cols[n % tiles_n]
            one = A[n] * (gA - jnp.sum(gA * A[n], axis=1, keepdims=True)) * scaling
            rows = slice((n % tiles_n) * TILE, (n % tiles_n) * TILE + TILE)
            gl2.append(jnp.where(same & (live_row[:, rows] > 0), one, 0.0))
        yield
        for n in tiles:
            h, g = n // tiles_n, n % tiles_n
            rows = slice(g * TILE, g * TILE + TILE)
            k0, q1, _ = landmark_parts(land[rows, LANES * h : LANES * h + LANES])
            land_sum[h, rows, :] = mm3(split(gl2[n]), split(k0)) + mm3(split(gl2[n].T), split(q1))
        yield

    def walk(q, b, emit):
        def both(k, none):
            stages = newton_back_stages(hist, gstate, NEWTON - 1 - q * per_block - k, masks)
            next(stages)
            three(b * per_block + k, functools.partial(emit, k), lambda: next(stages, None))
            return none

        def alone(k, none):
            three(b * per_block + k, functools.partial(emit, k))
            return none

        ends = min(max(NEWTON - q * per_block, 0), per_block)
        lax.fori_loop(0, ends, both, 0)
        if NEWTON <= q * per_block < NEWTON + per_block:
            stages = landmark_stages()
            next(stages)
            three(b * per_block, functools.partial(emit, 0), lambda: next(stages, None))
            ends = 1
        lax.fori_loop(ends, per_block, alone, 0)

    def to_part(n, k, value):
        part_out[n, dyn_rows(k), :] = value.astype(bf16)

    def to_grad(k, value):
        input_grad[dyn_rows(k), :] = value

    def to_own_grad(k, value):
        input_grad[dyn_rows(k), :] = value + gpre[dyn_rows(k), :]

    walk(0, here.diagonal, functools.partial(to_part, 0))
    from_sibling = start(push(part_out.at[0], part_in.at[0], psem, 0, here.dp, here.sibling))
    walk(1, here.across, to_grad)
    from_sibling.wait_recv()
    from_across = []
    for k in range(per_block):
        total = input_grad[chunk_rows(k), :] + part_in[0, chunk_rows(k), :].astype(f32)
        part_sum[chunk_rows(k), :] = total.astype(bf16)
        from_across.append(
            start(push(part_sum.at[chunk_rows(k)], part_x.at[chunk_rows(k)], psem, 1 + k, here.dp, here.across))
        )
    if gather:
        downs.third()
        for summer in smalls:
            summer.along_z()
    walk(2, here.sibling, functools.partial(to_part, 1))
    own_from_sibling = start(push(part_out.at[1], part_in.at[1], psem, 1 + per_block, here.dp, here.sibling))
    walk(3, here.t, to_own_grad)
    if gather:
        downs.fourth()
        ups.third()

    conv_out[...] = jnp.zeros_like(conv_out)
    for h in range(heads_n):
        conv_out[h : h + 1, :] = diagonal_sums(gband[h])
    piece_v[...] = mm(xT[...], gv[...]).astype(bf16)
    others = [(dz, dy) for dz in range(4) for dy in range(2) if dz or dy] if gather else []
    sent_conv = []
    for k, (dz, dy) in enumerate(others):
        sent_conv.append(start(push(conv_out, in_conv.at[k], csem, k, here.dp_at(dz, dy), here.t)))

    def piece_along_y(piece, landing, sems):
        view = piece.reshape((4, 2) + landing.shape[1:])
        return start(push(view.at[:, 1 - here.y], landing, sems, 0, here.dp_at(0, 1), here.t))

    def piece_along_z(copy, piece, landing, last_landing, sems):
        view = piece.reshape((4, 2) + landing.shape[1:])
        copy.wait_recv()
        for z in range(4):
            landing[z] = landing[z] + view[z, here.y]
        return [
            start(push(landing.at[(here.z + dz) % 4], last_landing.at[dz - 1], sems, dz, here.dp_at(dz, 0), here.t))
            for dz in (1, 2, 3)
        ]

    if gather:
        v_along_y = piece_along_y(piece_v, in_v, v_sems)

    for h in range(heads_n):
        sums_land = pltpu.roll(glandT[h].T * scaling, HEAD_DIM, 1)
        lanes = slice(LANES * h, LANES * h + LANES)
        total = (land_sum[h] + sums_land) / counts[...]
        g_high[:, lanes], g_low[:, lanes] = split(total)

    weights_qk = wfull[:, : LANES * heads_n]
    spread_land = mm_nt(g_high[...], weights_qk) + mm_nt(g_low[...], weights_qk)
    half = nslot // 2
    land_own[...] = spread_land
    land_out[0] = land_own[pl.ds(pl.multiple_of((1 - here.c) * half, half), half), :].astype(bf16)
    own_half = pl.ds(pl.multiple_of(here.c * half, half), half)
    first = start(push(land_out.at[0], land_in.at[0], psem, 2 + per_block, here.dp, here.sibling))
    high, low = split(x_land[...])
    piece_q[...] = (
        mm(xT[...], gqk[...])
        + (mm(high, g_high[...]) + (mm(high, g_low[...]) + mm(low, g_high[...])))
    ).astype(bf16)
    if gather:
        q_along_y = piece_along_y(piece_q, in_q, q_sems)
    if gather:
        for summer in smalls:
            summer.along_x()
        sent_v = piece_along_z(v_along_y, piece_v, in_v, in_vz, v_sems)
    first.wait_recv()
    mine = land_own[own_half, :] + land_in[0].astype(f32)
    land_out[1] = mine.astype(bf16)
    second = start(push(land_out.at[1], land_in.at[1], psem, 3 + per_block, here.dp, here.across))
    if gather:
        sent_q = piece_along_z(q_along_y, piece_q, in_q, in_qz, q_sems)
    second.wait_recv()
    mine = mine + land_in[1].astype(f32)
    land_all[own_half, :] = mine.astype(bf16)
    third = start(
        push(land_all.at[own_half], land_all.at[own_half], psem, 4 + per_block, here.dp, here.sibling)
    )
    if gather:
        ups.finish(up_out)
        downs.finish(down_out)
    own_from_sibling.wait_recv()
    third.wait_recv()
    for k in range(per_block):
        from_across[k].wait_recv()
        rows = pl.ds(pl.multiple_of(here.t * block + k * CHUNK, CHUNK), CHUNK)
        hot = (slot_of(tokc[rows, 0:1]) == iota((CHUNK, nslot), 1)).astype(f32).astype(bf16)
        input_grad[chunk_rows(k), :] += (
            part_in[1, chunk_rows(k), :].astype(f32)
            + part_x[chunk_rows(k), :].astype(f32)
            + mm(hot, land_all[...])
        )
    if gather:
        for copy in sent_v + sent_q + sent_conv:
            copy.wait_recv()
        total_v = in_v[here.z].astype(f32)
        total_q = in_q[here.z].astype(f32)
        for k in range(3):
            total_v = total_v + in_vz[k].astype(f32)
            total_q = total_q + in_qz[k].astype(f32)
        total_conv = conv_out[...]
        for k in range(len(others)):
            total_conv = total_conv + in_conv[k]
        for h in range(heads_n):
            e = slice(HEAD_DIM * h, HEAD_DIM * h + HEAD_DIM)
            one = total_q[:, LANES * h : LANES * h + LANES]
            gw[0, :, e] = one[:, :HEAD_DIM]
            gw[1, :, e] = one[:, HEAD_DIM:]
        gw[2] = total_v[:, : heads_n * HEAD_DIM]
        first = HALO - taps_total // 2
        turned = pltpu.roll(total_conv, 2 * TILE - first, 1)
        gconv[...] = turned[:heads_n, :taps_total]
        smalls[0].finish(out_sum)
        out_out[...] = out_sum[:, : heads_n * HEAD_DIM].T
        smalls[1].finish(norm_sum)
        gain_out[...] = norm_sum[0:2, :length]
        bias_out[...] = norm_sum[2:4, :length]
    else:
        gw[:, : LANES * heads_n] = piece_q[...].astype(f32)
        gw[:, LANES * heads_n :] = piece_v[...].astype(f32)
        gconv[...] = conv_out[...]
    for copy in copies:
        copy.wait_send()


def attention_backward(gsend, xall, wfull, tokc, segw, qk, v, kern1, kern3, land, counts, weights,
                       mixed, carried, conv, slot_live, gpre, hist, sources, taps_total, depth):
    blocks, block, wide = gsend.shape[0], 2 * gsend.shape[1], v.shape[1]
    heads_n, seq, nslot = kern1.shape
    feat = wfull.shape[0]
    all_tiles = weights.shape[0]
    shape = jax.ShapeDtypeStruct
    gather = len(sources) > 0
    width = heads_n * HEAD_DIM
    outs = [shape((block, feat), f32)]
    if gather:
        hidden_n = sources[0].shape[2]
        outs += [
            shape((3, depth, width), f32),
            shape((heads_n, taps_total), f32),
            shape((hidden_n, feat), f32),
            shape((hidden_n, feat), f32),
            shape((width, depth), f32),
            shape((2, feat // 32), f32),
            shape((2, feat // 32), f32),
        ]
    else:
        outs += [shape((feat, wfull.shape[1]), f32), shape((8, 2 * TILE), f32)]
    others = 7 if gather else 1
    per_block = block // CHUNK
    scratch = [
        pltpu.VMEM(gsend.shape, bf16),
        pltpu.VMEM(wfull.shape, bf16),
        pltpu.VMEM(tokc.shape, i32),
        pltpu.VMEM(qk.shape, bf16),
        pltpu.VMEM(v.shape, bf16),
        pltpu.VMEM(gpre.shape, f32),
        pltpu.VMEM((8, 2 * TILE), f32),
        pltpu.VMEM((heads_n, seq, nslot), bf16),
        pltpu.VMEM((heads_n, seq, nslot), bf16),
        pltpu.VMEM(xall.shape, bf16),
        pltpu.VMEM((feat, seq), bf16),
        pltpu.VMEM((seq + 2 * HALO, wide), bf16),
        pltpu.VMEM((seq, LANES * heads_n), bf16),
        pltpu.VMEM((seq, wide), bf16),
        pltpu.VMEM((heads_n, TILE, 2 * TILE), f32),
        pltpu.VMEM((2 * heads_n, TILE, 2 * TILE), f32),
        pltpu.VMEM((wide, nslot), f32),
        pltpu.VMEM((heads_n, LANES, nslot), f32),
        pltpu.VMEM((NEWTON + 1, 4, all_tiles, LANDMARKS, TILE), f32),
        pltpu.VMEM((2, all_tiles, LANDMARKS, TILE), f32),
        pltpu.VMEM((heads_n, nslot, wide), bf16),
        pltpu.VMEM((heads_n, 2 * nslot, 256), bf16),
        pltpu.VMEM((2, block, feat), bf16),
        pltpu.VMEM((2, block, feat), bf16),
        pltpu.VMEM((block, feat), bf16),
        pltpu.VMEM((block, feat), bf16),
        pltpu.VMEM((feat, wide), bf16),
        pltpu.VMEM((feat, LANES * heads_n), bf16),
        pltpu.VMEM((4, depth if gather else 16, wide), bf16),
        pltpu.VMEM((4, depth if gather else 16, LANES * heads_n), bf16),
        pltpu.VMEM((others, 8, 2 * TILE), f32),
        pltpu.VMEM((8, 2 * TILE), f32),
        pltpu.VMEM((heads_n, nslot, LANES), f32),
        pltpu.VMEM((feat, nslot), f32),
        pltpu.VMEM((nslot, LANES * heads_n), bf16),
        pltpu.VMEM((nslot, LANES * heads_n), bf16),
        pltpu.VMEM((nslot, feat), f32),
        pltpu.VMEM((2, nslot // 2, feat), bf16),
        pltpu.VMEM((2, nslot // 2, feat), bf16),
        pltpu.VMEM((nslot, feat), bf16),
        dma(2, 3),
        dma(12),
        dma(2, 5 + per_block),
        dma(2, others),
    ]
    if gather:
        scratch += [pltpu.VMEM(source.shape, bf16) for source in sources[1:4]]
        scratch += [
            pltpu.VMEM((depth, wide), f32),
            pltpu.VMEM((8, LANES), f32),
            pltpu.VMEM((32, 8, LANES), f32),
            dma(2, 4),
            dma(2, 4),
            pltpu.VMEM((3, depth, wide), bf16),
            pltpu.VMEM((3, depth, LANES * heads_n), bf16),
            pltpu.VMEM((2, 2, hidden_n, feat), bf16),
            pltpu.VMEM((3, 2, hidden_n, feat), bf16),
            pltpu.VMEM((hidden_n, feat), bf16),
            dma(2, 6),
            pltpu.VMEM((4, hidden_n, feat), bf16),
            pltpu.VMEM((3, hidden_n, feat), bf16),
            pltpu.VMEM((2, 2, hidden_n, feat), bf16),
            dma(2, 9),
        ]
        for count, lanes, kind in ((depth, wide, bf16), (8, LANES, f32)):
            scratch += [
                pltpu.VMEM((4, 2, 2, count, lanes), kind),
                pltpu.VMEM((4, 2, 2, count, lanes), kind),
                pltpu.VMEM((4, 2, count, lanes), kind),
                pltpu.VMEM((3, 2, count, lanes), kind),
                pltpu.VMEM((count, lanes), kind),
                dma(2, SUMMER_SEMS),
                pltpu.SemaphoreType.DMA,
            ]
    specs = [VMEM, ANY, ANY, ANY, VMEM] + [ANY] * 4 + [VMEM] * 7 + [ANY, ANY]
    if gather:
        specs += [ANY] * 5 + [VMEM]
    return pl.pallas_call(
        functools.partial(backward_body, gather, taps_total),
        out_shape=tuple(outs),
        in_specs=specs,
        out_specs=tuple([VMEM] * len(outs)),
        scratch_shapes=scratch,
        compiler_params=pltpu.CompilerParams(
            vmem_limit_bytes=LIMIT, collective_id=3 if gather else 4, has_side_effects=True
        ),
        name="attention_backward",
    )(gsend, xall, wfull, tokc, segw, qk, v, kern1, kern3, land, counts, weights, mixed, carried,
      conv, slot_live, gpre, hist, *sources)


def hand_over_body(*refs):
    half = len(refs) // 2
    for src, dst in zip(refs[:half], refs[half:]):
        dst[...] = src[...]


def hand_over(*arrays):
    return pl.pallas_call(
        hand_over_body,
        out_shape=tuple(jax.ShapeDtypeStruct(a.shape, a.dtype) for a in arrays),
        in_specs=[VMEM] * len(arrays),
        out_specs=tuple([VMEM] * len(arrays)),
        name="hand_over",
    )(*arrays)


def split_up(shard, dim, length):
    before, after = (shard.shape[:dim], shard.shape[dim + 1 :])
    return jnp.moveaxis(shard.reshape(*before, length, -1, *after), dim, 0)


def exchange(pieces, axis):
    return lax.all_to_all(pieces, axis, split_axis=0, concat_axis=0, tiled=True)


def per_device(
    tokens,
    w_qkv,
    w_out,
    conv_weight,
    w_up,
    w_down,
    norm_gain,
    norm_bias,
    cotangent,
    seg_ids,
    landmark_slot,
    token_live,
    slot_live,
):
    both = ("dp", "tensor")
    dp_size, blocks = lax.axis_size("dp"), lax.axis_size("tensor")
    devices = dp_size * blocks
    heads_n, taps_total = conv_weight.shape
    block, feat = tokens.shape
    depth = w_qkv.shape[1]
    width = heads_n * HEAD_DIM
    wide = -(-width // 256) * 256
    hidden_n = w_up.shape[1]
    docs = slot_live.shape[1] // LANDMARKS
    direct = dp_size == 8 and blocks == 4 and depth % 16 == 0 and hidden_n % 32 == 0

    first = HALO - taps_total // 2
    weight = w_qkv if direct else lax.all_gather(w_qkv, "dp", axis=1, tiled=True)
    extra = (w_up.T, w_down, w_out, norm_gain, norm_bias) if direct else ()
    got = attention_forward(
        tokens, weight, conv_weight, seg_ids, landmark_slot, token_live, slot_live,
        extra, heads_n, blocks, taps_total,
    )
    (
        xall, wfull, tokc, segw, qk, v, kern1, kern3, land, counts, weights, mixed, carried, heads, proxies,
        hist,
    ) = got[:16]
    if direct:
        up_all, down_all, out_all, norms = got[16:]
        out_all = out_all.reshape(blocks, feat, wide)
    else:
        up_all = lax.all_gather(w_up.T, both, axis=0, tiled=True)
        down_all = lax.all_gather(w_down, both, axis=0, tiled=True)
        out_all = lax.all_gather(lax.all_gather(w_out.T, "dp", axis=0, tiled=True), "tensor", axis=0)
        out_all = jnp.pad(out_all, ((0, 0), (0, 0), (0, wide - width)))
        norms = jnp.concatenate([norm_gain, norm_bias, jnp.zeros_like(norm_gain), jnp.zeros_like(norm_bias)])
        norms = lax.all_gather(norms, both, axis=1, tiled=True).astype(f32)
    if direct:
        got = feed_direct(tokens, cotangent, heads, norms, out_all, up_all, down_all, depth)
        layer_out, gsend, grad_pre, norm_grads, out_pieces = got[:5]
        sources = got[5:] + (out_pieces, norm_grads)
    else:
        layer_out, gsend, grad_pre, norm_grads, out_pieces, up_pieces, down_pieces = feed_forward(
            direct, tokens, cotangent, heads, norms, out_all, up_all, down_all, depth
        )
        sources = ()
    got = attention_backward(
        gsend, xall, wfull, tokc, segw, qk, v, kern1, kern3, land, counts, weights,
        mixed, carried, conv_weight, slot_live, grad_pre, hist, sources, taps_total, depth,
    )
    if direct:
        (
            input_grad, grad_qkv, grad_conv, grad_up, grad_down, grad_out, grad_gain, grad_bias, proxies,
            layer_out,
        ) = hand_over(*got, proxies, layer_out)
        grad_up = grad_up.T
    else:
        input_grad, grad_w, grad_conv = got
        grad_w = exchange(grad_w.astype(bf16).reshape(dp_size, depth, -1), "dp").astype(f32).sum(axis=0)
        pairs = grad_w[:, : LANES * heads_n].reshape(depth, heads_n, 2, HEAD_DIM)
        grad_qkv = jnp.concatenate(
            [
                jnp.moveaxis(pairs, 2, 0).reshape(2, depth, width),
                grad_w[None, :, LANES * heads_n : LANES * heads_n + width],
            ]
        )
        grad_conv = lax.psum(grad_conv, "dp")[:heads_n, first : first + taps_total]
        grad_up = lax.psum_scatter(up_pieces, both, scatter_dimension=0, tiled=True).astype(f32).T
        grad_down = lax.psum_scatter(down_pieces, both, scatter_dimension=0, tiled=True).astype(f32)
        out_pieces = out_pieces[:, :, :width].reshape(blocks, dp_size, depth, width)
        out_pieces = jnp.swapaxes(out_pieces, 0, 1).reshape(devices, depth, width)
        grad_out = lax.psum_scatter(out_pieces, both, scatter_dimension=0, tiled=False).astype(f32).T
        norm_sum = exchange(split_up(norm_grads[:4], 1, devices), both).sum(axis=0)
        grad_gain, grad_bias = norm_sum[:2], norm_sum[2:]
    return (
        layer_out,
        input_grad,
        grad_qkv,
        grad_out,
        grad_conv,
        grad_up,
        grad_down,
        grad_gain,
        grad_bias,
        jnp.transpose(proxies, (1, 2, 0)),
    )


def solution(mesh):
    return jax.shard_map(
        per_device,
        mesh=mesh,
        in_specs=(
            P(("dp", "tensor"), None),
            P(None, "dp", "tensor"),
            P("tensor", "dp"),
            P("tensor", None),
            P(None, ("dp", "tensor")),
            P(("dp", "tensor"), None),
            P(None, ("dp", "tensor")),
            P(None, ("dp", "tensor")),
            P(("dp", "tensor"), None),
            P("dp", None),
            P("dp", None),
            P("dp", None),
            P("dp", None),
        ),
        out_specs=(
            P(("dp", "tensor"), None),
            P(("dp", "tensor"), None),
            P(None, "dp", "tensor"),
            P("tensor", "dp"),
            P("tensor", None),
            P(None, ("dp", "tensor")),
            P(("dp", "tensor"), None),
            P(None, ("dp", "tensor")),
            P(None, ("dp", "tensor")),
            P("dp", None, "tensor"),
        ),
        check_vma=False,
    )
```
